32 devices in a mesh: samp: 4 (over z), seq: 8 (over y, x, core).
Axes of the slice: x: 2, y: 2, z: 4, core: 2. Of those that a mesh axis runs over, the one named last changes fastest.
Arguments:
- atom_input: bfloat16 [32, 4096, 128], P('samp', 'seq'), may hold values from -6 to 6
- token_input: bfloat16 [32, 512, 768], P('samp', 'seq'), may hold values from -6 to 6
- atom_counts: int32 [512], replicated, may hold values from 1 to 8
- key_offsets: int32 [128], P('seq'), may hold values from -96 to 0, as said below
- atom_pairs: bfloat16 [128, 32, 128, 16], P('seq'), may hold values from -6 to 6
- pair_features: bfloat16 [512, 512, 128], P('seq'), may hold values from -6 to 6
- single_features: bfloat16 [512, 384], P('seq'), may hold values from -6 to 6
- noise_levels: float32 [32], P('samp'), may hold values from 0.5 to 160
- noise_direction: float32 [384], replicated, may hold values from -6 to 6
- atom_proj: bfloat16 [128, 512], P('samp'), may hold values from -0.5 to 0.5
- atom_qbias: bfloat16 [128], P('samp'), may hold values from -4 to 4
- atom_pairw: bfloat16 [16, 4], P('samp'), may hold values from -1.5 to 1.5
- atom_outw: bfloat16 [128, 128], P('samp'), may hold values from -1 to 1
- atom_upw: bfloat16 [128, 512], P('samp'), may hold values from -0.5 to 0.5
- atom_downw: bfloat16 [256, 128], P('samp'), may hold values from -0.375 to 0.375
- pool_weight: bfloat16 [128, 768], P('samp'), may hold values from -0.5 to 0.5
- cond_weight: bfloat16 [384, 4608], P('samp'), may hold values from -0.3125 to 0.3125
- cond_bias: bfloat16 [4608], P('samp'), may hold values from -4 to 4
- token_proj: bfloat16 [768, 3072], P('samp'), may hold values from -0.21875 to 0.21875
- token_qbias: bfloat16 [768], P('samp'), may hold values from -4 to 4
- token_pairw: bfloat16 [128, 16], P('samp'), may hold values from -0.5 to 0.5
- token_outw: bfloat16 [768, 768], P('samp'), may hold values from -0.875 to 0.875
- token_upw: bfloat16 [768, 3072], P('samp'), may hold values from -0.21875 to 0.21875
- token_downw: bfloat16 [1536, 768], P('samp'), may hold values from -0.15625 to 0.15625
- cotangent: bfloat16 [32, 512, 768], P('samp', 'seq'), may hold values from -6 to 6
Outputs:
- block_out: bfloat16 [32, 512, 768], P('samp', 'seq')
- atom_grad: float32 [32, 4096, 128], P('samp', 'seq')
- token_grad: float32 [32, 512, 768], P('samp', 'seq')
- grad_atom_proj: float32 [128, 512], P('samp')
- grad_atom_qbias: float32 [128], P('samp')
- grad_atom_pairw: float32 [16, 4], P('samp')
- grad_atom_outw: float32 [128, 128], P('samp')
- grad_atom_upw: float32 [128, 512], P('samp')
- grad_atom_downw: float32 [256, 128], P('samp')
- grad_pool_weight: float32 [128, 768], P('samp')
- grad_cond_weight: float32 [384, 4608], P('samp')
- grad_cond_bias: float32 [4608], P('samp')
- grad_token_proj: float32 [768, 3072], P('samp')
- grad_token_qbias: float32 [768], P('samp')
- grad_token_pairw: float32 [128, 16], P('samp')
- grad_token_outw: float32 [768, 768], P('samp')
- grad_token_upw: float32 [768, 3072], P('samp')
- grad_token_downw: float32 [1536, 768], P('samp')
The draws below stay inside these ranges and needn't reach their ends.
Inputs may be any that keep to these rules, and one draw needn't show every extreme that they name: `key_offsets`: both ends of the range occur.
All inputs are finite; a program needn't handle non-finite values.
Results may differ from the reference program's by a relative error of at most 0.03.
Values may be sent and summed in bfloat16 or wider, within the bound.
A program may use at most 384 MiB of HBM per device.

```python
import math
import jax
import jax.numpy as jnp
from jax import lax

MAX_ATOMS = 8
WIN_Q = 32
WIN_K = 128
ATOM_W = 128
ATOM_HEADS = 4
ATOM_PAIR = 16
ATOM_FF = 256
WIDTH = 768
HEADS = 16
PAIR_W = 128
SINGLE_W = 384
FF = 1536
SEQ_LEN = 512
SAMPLES = 32
ATOMS = 4096
NWIN = 128
RIM = 96


def draw_key_offsets(key, part):
    key = jax.random.fold_in(key, 11)
    first_key, second_key, third_key = jax.random.split(key, 3)
    offsets = jax.random.randint(first_key, (NWIN,), -RIM, 1)
    lowest = jax.random.randint(second_key, (), 0, NWIN)
    highest = (lowest + 1 + jax.random.randint(third_key, (), 0, NWIN - 1)) % NWIN
    places = jnp.arange(NWIN)
    offsets = jnp.where(places == lowest, -RIM, offsets)
    offsets = jnp.where(places == highest, 0, offsets)
    return offsets.astype(jnp.int32)


def with_ends(entries, key, smallest, top_value):
    longest = entries.shape.index(max(entries.shape))
    spots = []
    for shift in (0, 1):
        where = [jax.random.randint(jax.random.fold_in(key, axis), (), 0, length) for axis, length in enumerate(entries.shape)]
        where[longest] = (where[longest] + shift) % entries.shape[longest]
        spots.append(tuple(where))
    return entries.at[spots[0]].set(smallest).at[spots[1]].set(top_value)


def shard_levels(own_key, shape, cuts, least, high):
    loudness, own = 1.0, jax.random.fold_in(own_key, 6)
    for position, shards_of in cuts:
        heights = jnp.exp(jax.random.uniform(jax.random.fold_in(own, position), (shards_of,), jnp.float32, least / len(cuts), high / len(cuts)))
        loudness = loudness * jnp.repeat(heights, shape[position] // shards_of).reshape([-1 if axis == position else 1 for axis in range(len(shape))])
    return loudness


def normal_values(stream_key, extent, width, bound, cuts=(), kind=jnp.bfloat16):
    result = jax.random.normal(stream_key, extent, jnp.float32) * width
    if len(cuts) > 0:
        result = shard_levels(stream_key, extent, cuts, -0.22, 0.18) * result
    return jnp.clip(result, min=-bound, max=bound).astype(kind)


def setup_inputs(seed: int = 0) -> dict:
    key_of = jax.random.split(jax.random.key(seed), 26)
    atom_input = normal_values(key_of[0], (SAMPLES, ATOMS, ATOM_W), 1.0, 6.0, ((0, 4), (1, 8)))
    token_input = normal_values(key_of[1], (SAMPLES, SEQ_LEN, WIDTH), 1.0, 6.0, ((0, 4), (1, 8)))
    atom_counts = with_ends(jax.random.randint(key_of[2], (SEQ_LEN,), 1, MAX_ATOMS + 1), jax.random.fold_in(key_of[2], 1), 1, MAX_ATOMS).astype(jnp.int32)
    key_offsets = draw_key_offsets(jax.random.fold_in(key_of[25], 71), 0)
    atom_pairs = normal_values(key_of[4], (NWIN, WIN_Q, WIN_K, ATOM_PAIR), 1.0, 6.0, ((0, 8),))
    pair_features = normal_values(key_of[5], (SEQ_LEN, SEQ_LEN, PAIR_W), 1.0, 6.0, ((0, 8),))
    single_features = normal_values(key_of[6], (SEQ_LEN, SINGLE_W), 1.0, 6.0, ((0, 8),))
    noise_levels = jnp.clip(jnp.exp(math.log(160.0) - 5.768321 * jax.random.uniform(key_of[7], (SAMPLES,), jnp.float32) ** shard_levels(key_of[7], (SAMPLES,), ((0, 4),), -0.2, 0.2)), 0.5, 160.0)
    noise_direction = normal_values(key_of[8], (SINGLE_W,), 1.0, 6.0, (), jnp.float32)
    atom_proj = normal_values(key_of[9], (ATOM_W, 4 * ATOM_W), ATOM_W ** -0.5, 0.5, ((0, 4),))
    atom_qbias = normal_values(key_of[10], (ATOM_W,), 1.0, 4.0, ((0, 4),))
    atom_pairw = normal_values(key_of[11], (ATOM_PAIR, ATOM_HEADS), ATOM_PAIR ** -0.5, 1.5, ((0, 4),))
    atom_outw = normal_values(key_of[12], (ATOM_W, ATOM_W), (ATOM_W // 4) ** -0.5, 1.0, ((0, 4),))
    atom_upw = normal_values(key_of[13], (ATOM_W, 2 * ATOM_FF), ATOM_W ** -0.5, 0.5, ((0, 4),))
    atom_downw = normal_values(key_of[14], (ATOM_FF, ATOM_W), ATOM_FF ** -0.5, 0.375, ((0, 4),))
    pool_weight = normal_values(key_of[15], (ATOM_W, WIDTH), ATOM_W ** -0.5, 0.5, ((0, 4),))
    cond_weight = normal_values(key_of[16], (SINGLE_W, 6 * WIDTH), SINGLE_W ** -0.5, 0.3125, ((0, 4),))
    cond_bias = normal_values(key_of[17], (6 * WIDTH,), 1.0, 4.0, ((0, 4),))
    token_proj = normal_values(key_of[18], (WIDTH, 4 * WIDTH), WIDTH ** -0.5, 0.21875, ((0, 4),))
    token_qbias = normal_values(key_of[19], (WIDTH,), 1.0, 4.0, ((0, 4),))
    token_pairw = normal_values(key_of[20], (PAIR_W, HEADS), PAIR_W ** -0.5, 0.5, ((0, 4),))
    token_outw = normal_values(key_of[21], (WIDTH, WIDTH), (WIDTH // 16) ** -0.5, 0.875, ((0, 4),))
    token_upw = normal_values(key_of[22], (WIDTH, 2 * FF), WIDTH ** -0.5, 0.21875, ((0, 4),))
    token_downw = normal_values(key_of[23], (FF, WIDTH), FF ** -0.5, 0.15625, ((0, 4),))
    cotangent = normal_values(key_of[24], (SAMPLES, SEQ_LEN, WIDTH), 1.0, 6.0, ((0, 4), (1, 8)))
    return {"atom_input": atom_input, "token_input": token_input, "atom_counts": atom_counts, "key_offsets": key_offsets, "atom_pairs": atom_pairs, "pair_features": pair_features, "single_features": single_features, "noise_levels": noise_levels, "noise_direction": noise_direction, "atom_proj": atom_proj, "atom_qbias": atom_qbias, "atom_pairw": atom_pairw, "atom_outw": atom_outw, "atom_upw": atom_upw, "atom_downw": atom_downw, "pool_weight": pool_weight, "cond_weight": cond_weight, "cond_bias": cond_bias, "token_proj": token_proj, "token_qbias": token_qbias, "token_pairw": token_pairw, "token_outw": token_outw, "token_upw": token_upw, "token_downw": token_downw, "cotangent": cotangent}


high = lax.Precision.HIGHEST
norm_eps = 1e-05
sigma_data = 16.0
masked_score = -1000000000.0

@jax.custom_vjp
def low(v):
    return lax.optimization_barrier(v.astype(jnp.bfloat16)).astype(jnp.float32)

@jax.custom_vjp
def low_back(v):
    return v

def low_keep(v):
    return (low(v), None)

def low_pass(kept, grad):
    return (grad,)

def back_keep(v):
    return (v, None)

def back_low(kept, grad):
    return (low(grad),)
low.defvjp(low_keep, low_pass)
low_back.defvjp(back_keep, back_low)

def layer_norm(operand):
    center = operand - lax.optimization_barrier(jnp.mean(operand, -1, keepdims=True))
    return center * lax.rsqrt(lax.optimization_barrier(jnp.mean(center * center, -1, keepdims=True)) + norm_eps)

def matmul(left_op, right_op):
    return jnp.matmul(left_op, right_op, precision=high)

def silu(operand):
    return operand * jax.nn.sigmoid(operand)

def softmax(scores):
    row_top = lax.optimization_barrier(jnp.max(scores, -1, keepdims=True))
    exp_scores = jnp.exp(scores - row_top)
    return exp_scores / lax.optimization_barrier(jnp.sum(exp_scores, -1, keepdims=True))

def expand(normed_low, up_weight, down_weight):
    hidden_width = down_weight.shape[0]
    upper_pair = low_back(matmul(normed_low, up_weight))
    hidden = low(silu(upper_pair[:, :hidden_width]) * upper_pair[:, hidden_width:])
    return low_back(matmul(hidden, down_weight))

def atom_block(atom_rows, win_index, win_usable, atom_bias, params):
    proj_weight, query_bias, out_weight, up_weight, down_weight = params
    atom_width = atom_rows.shape[-1]
    win_count = win_index.shape[0]
    head_dim = atom_width // ATOM_HEADS
    normed = low(layer_norm(atom_rows))
    mix_rows = low_back(matmul(normed, proj_weight))
    queries = low(mix_rows[:, :atom_width] + query_bias)
    key_rows = low(mix_rows[:, atom_width:2 * atom_width])
    value_rows = low(mix_rows[:, 2 * atom_width:3 * atom_width])
    gating = mix_rows[:, 3 * atom_width:]
    win_query = queries.reshape(win_count, WIN_Q, ATOM_HEADS, head_dim)
    win_key = key_rows[win_index.reshape(-1)].reshape(win_count, WIN_K, ATOM_HEADS, head_dim)
    win_value = value_rows[win_index.reshape(-1)].reshape(win_count, WIN_K, ATOM_HEADS, head_dim)
    scores = jnp.einsum('wqhd,wkhd->whqk', win_query, win_key, precision=high) * float(head_dim) ** (-0.5) + atom_bias
    scores = low_back(jnp.where(win_usable[:, None, None, :], scores, masked_score))
    probs_low = low(softmax(scores))
    attend = low_back(jnp.einsum('whqk,wkhd->wqhd', probs_low, win_value, precision=high)).reshape(-1, atom_width)
    gated_low = low(attend * jax.nn.sigmoid(gating))
    mid_rows = atom_rows + low_back(matmul(gated_low, out_weight))
    return mid_rows + expand(low(layer_norm(mid_rows)), up_weight, down_weight)

def token_block(block_in, cond_all, pair_bias, params):
    proj_weight, query_bias, out_weight, up_weight, down_weight = params
    model_width = block_in.shape[-1]
    head_count = pair_bias.shape[0]
    head_dim = model_width // head_count
    cond_parts = [cond_all[:, part_index * model_width:(part_index + 1) * model_width] for part_index in range(6)]
    attn_in = low(jax.nn.sigmoid(cond_parts[0]) * layer_norm(block_in) + cond_parts[1])
    mix_rows = low_back(matmul(attn_in, proj_weight))
    queries = low(mix_rows[:, :model_width] + query_bias).reshape(-1, head_count, head_dim)
    key_rows = low(mix_rows[:, model_width:2 * model_width]).reshape(-1, head_count, head_dim)
    value_rows = low(mix_rows[:, 2 * model_width:3 * model_width]).reshape(-1, head_count, head_dim)
    gating = mix_rows[:, 3 * model_width:]
    scores = jnp.einsum('qhd,khd->hqk', queries, key_rows, precision=high) * float(head_dim) ** (-0.5) + pair_bias
    scores = low_back(scores)
    probs_low = low(softmax(scores))
    attend = low_back(jnp.einsum('hqk,khd->qhd', probs_low, value_rows, precision=high)).reshape(-1, model_width)
    gated_low = low(attend * jax.nn.sigmoid(gating))
    mid_rows = block_in + jax.nn.sigmoid(cond_parts[2]) * low_back(matmul(gated_low, out_weight))
    ffn_in = low(jax.nn.sigmoid(cond_parts[3]) * layer_norm(mid_rows) + cond_parts[4])
    return mid_rows + jax.nn.sigmoid(cond_parts[5]) * expand(ffn_in, up_weight, down_weight)

def reference(atom_input, token_input, atom_counts, key_offsets, atom_pairs, pair_features, single_features, noise_levels, noise_direction, atom_proj, atom_qbias, atom_pairw, atom_outw, atom_upw, atom_downw, pool_weight, cond_weight, cond_bias, token_proj, token_qbias, token_pairw, token_outw, token_upw, token_downw, cotangent):
    seq_len = atom_counts.shape[0]
    slot_used = jnp.arange(MAX_ATOMS, dtype=jnp.int32)[None, :] < atom_counts[:, None]
    slot_weight = slot_used.astype(jnp.float32) / atom_counts[:, None].astype(jnp.float32)
    flat_used = slot_used.reshape(-1)
    slot_total = flat_used.shape[0]
    win_count = key_offsets.shape[0]
    raw_index = (jnp.arange(win_count, dtype=jnp.int32) * WIN_Q + key_offsets)[:, None] + jnp.arange(WIN_K, dtype=jnp.int32)[None, :]
    win_index = jnp.clip(raw_index, 0, slot_total - 1).astype(jnp.int32)
    win_usable = (raw_index >= 0) & (raw_index < slot_total) & flat_used[win_index]
    noise_feature = 0.25 * jnp.log(noise_levels / sigma_data)
    cond_rows = single_features.astype(jnp.float32)[None] + noise_feature[:, None, None] * noise_direction[None, None, :]
    cond_low = low(layer_norm(cond_rows))
    atom_pair_normed = layer_norm(atom_pairs.astype(jnp.float32))
    pair_normed = layer_norm(pair_features.astype(jnp.float32))

    def forward(atom_rows, token_rows, params):
        atom_proj, atom_qbias, atom_pairw, atom_outw, atom_upw, atom_downw, pool_weight, cond_weight, cond_bias, token_proj, token_qbias, token_pairw, token_outw, token_upw, token_downw = params
        atom_bias = jnp.einsum('wqkc,ch->whqk', atom_pair_normed, atom_pairw, precision=high)
        pair_bias = jnp.einsum('qkc,ch->hqk', pair_normed, token_pairw, precision=high)

        def one_sample(inputs):
            atoms_one, tokens_one, cond_one = inputs
            atom_final = atom_block(atoms_one, win_index, win_usable, atom_bias, (atom_proj, atom_qbias, atom_outw, atom_upw, atom_downw))
            pool_pre = low_back(matmul(low(atom_final), pool_weight))
            pooled = lax.optimization_barrier(jnp.sum(silu(pool_pre).reshape(seq_len, MAX_ATOMS, -1) * slot_weight[:, :, None], 1))
            block_in = tokens_one + pooled
            cond_all = low_back(matmul(cond_one, cond_weight) + cond_bias)
            return token_block(block_in, cond_all, pair_bias, (token_proj, token_qbias, token_outw, token_upw, token_downw))
        return lax.map(jax.checkpoint(one_sample), (atom_rows, token_rows, cond_low))
    params = tuple((weight.astype(jnp.float32) for weight in (atom_proj, atom_qbias, atom_pairw, atom_outw, atom_upw, atom_downw, pool_weight, cond_weight, cond_bias, token_proj, token_qbias, token_pairw, token_outw, token_upw, token_downw)))
    block_out, pullback = jax.vjp(forward, atom_input.astype(jnp.float32), token_input.astype(jnp.float32), params)
    atom_grad, token_grad, grads = pullback(cotangent.astype(jnp.float32))
    return (block_out.astype(jnp.bfloat16), atom_grad, token_grad, grads[0], grads[1], grads[2], grads[3], grads[4], grads[5], grads[6], grads[7], grads[8], grads[9], grads[10], grads[11], grads[12], grads[13], grads[14])
```

```python
import functools

import jax
import jax.numpy as jnp
from jax import lax
from jax.experimental import pallas as pl
from jax.experimental.pallas import tpu as pltpu
from jax.sharding import PartitionSpec as P

MAX_ATOMS = 8
WIN_Q = 32
WIN_K = 128
ATOM_HEADS = 4
RIM = 96
LANES = 128

norm_eps = 1e-05
sigma_data = 16.0
masked_score = -1000000000.0
bf16 = jnp.bfloat16
f32 = jnp.float32
vmem_bytes = 56 << 20


def dot_last(left_op, right_op):
    return jnp.einsum("...k,kn->...n", left_op, right_op, preferred_element_type=f32)


def dot_back(grad_op, weight):
    return jnp.einsum("...n,kn->...k", grad_op, weight, preferred_element_type=f32)


def weight_grad(left_op, grad_op):
    flat_left = left_op.reshape(-1, left_op.shape[-1])
    flat_grad = grad_op.reshape(-1, grad_op.shape[-1])
    return jnp.einsum("rk,rn->kn", flat_left, flat_grad, preferred_element_type=f32)


def mm(left_op, right_op):
    return lax.dot_general(left_op, right_op, (((1,), (0,)), ((), ())), preferred_element_type=f32)


def mm_nt(left_op, right_op):
    return lax.dot_general(left_op, right_op, (((1,), (1,)), ((), ())), preferred_element_type=f32)


def mm_tn(left_op, right_op):
    return lax.dot_general(left_op, right_op, (((0,), (0,)), ((), ())), preferred_element_type=f32)


def norm_stats(operand):
    center = operand - jnp.mean(operand, -1, keepdims=True)
    inv_std = lax.rsqrt(jnp.mean(center * center, -1, keepdims=True) + norm_eps)
    return (center * inv_std, inv_std)


def norm_back(normed, inv_std, grad_op):
    return inv_std * (
        grad_op
        - jnp.mean(grad_op, -1, keepdims=True)
        - normed * jnp.mean(grad_op * normed, -1, keepdims=True)
    )


def sigmoid(operand):
    return 1.0 / (1.0 + jnp.exp(-operand))


def whole(shape):
    return pl.BlockSpec(shape, lambda *_: (0,) * len(shape))


def per_sample(shape):
    return pl.BlockSpec((1,) + shape, lambda b, *_: (b,) + (0,) * len(shape))


def params():
    return pltpu.CompilerParams(vmem_limit_bytes=vmem_bytes)


def square_sums(ones_op, squares):
    upper = squares.astype(bf16)
    lower = (squares - upper.astype(f32)).astype(bf16)
    return upper, lower


def head_stack(rows, heads, head_dim, first):
    lane = lax.broadcasted_iota(jnp.int32, rows.shape, 1)
    parts = []
    for head in range(heads):
        low = first + head * head_dim
        parts.append(jnp.where((lane >= low) & (lane < low + head_dim), rows, jnp.zeros_like(rows)))
    return jnp.concatenate(parts, 0)


def head_fold(stacked, heads, head_dim, first):
    count = stacked.shape[0] // heads
    lane = lax.broadcasted_iota(jnp.int32, (count, stacked.shape[1]), 1)
    total = jnp.zeros((count, stacked.shape[1]), f32)
    for head in range(heads):
        low = first + head * head_dim
        part = stacked[head * count : (head + 1) * count]
        total = jnp.where((lane >= low) & (lane < low + head_dim), part, total)
    return total


def pair_stats(pairs, fold):
    upper, lower = square_sums(fold, pairs.astype(f32) * pairs.astype(f32))
    features = pairs.shape[0] // WIN_Q
    mean = mm(fold, pairs) * (1.0 / features)
    square = (mm(fold, upper) + mm(fold, lower)) * (1.0 / features)
    var = jnp.maximum(square - mean * mean, 0.0)
    inv_std = lax.rsqrt(var + norm_eps)
    return mean, inv_std


def pair_fold(features):
    shape = (WIN_Q, WIN_Q * features)
    row = lax.broadcasted_iota(jnp.int32, shape, 0)
    column = lax.broadcasted_iota(jnp.int32, shape, 1)
    return jnp.where(column // features == row, 1.0, 0.0).astype(bf16)


def atom_fwd_kernel(
    starts,
    ext_ref,
    pairs_ref,
    spread_ref,
    blocked_ref,
    share_ref,
    wide_ref,
    down_ref,
    qbias_ref,
    pooled_ref,
    query_ref,
    keyval_ref,
    gate_ref,
    probs_ref,
    attend_ref,
    mid_ref,
    bias_s,
    keys_s,
    values_s,
):
    width = ext_ref.shape[-1]
    head_dim = width // ATOM_HEADS
    scale = float(head_dim) ** (-0.5)
    slots = query_ref.shape[1]
    windows = slots // WIN_Q
    hidden_width = down_ref.shape[0]
    model_width = pooled_ref.shape[-1]
    features = pairs_ref.shape[1] // WIN_Q

    @pl.when(pl.program_id(0) == 0)
    def _():
        fold = pair_fold(features)
        spread = spread_ref[...]
        spread_sum = jnp.sum(spread.astype(f32), -1, keepdims=True)
        first_lane = jnp.where(
            lax.broadcasted_iota(jnp.int32, (ATOM_HEADS * WIN_Q, LANES), 1) == 0, 1.0, 0.0
        ).astype(bf16)

        def one(win, carry):
            pairs = pairs_ref[win]
            mean, inv_std = pair_stats(pairs, fold)
            mean = jnp.concatenate([mean] * ATOM_HEADS, 0)
            inv_std = jnp.concatenate([inv_std] * ATOM_HEADS, 0)
            blocked = blocked_ref[pl.ds(starts[win], WIN_K), :].astype(bf16)
            bias = inv_std * (mm(spread, pairs) - mean * spread_sum)
            bias_s[win] = bias + mm_nt(first_lane, blocked)
            return carry

        lax.fori_loop(0, windows, one, 0)

    rows = ext_ref[0].astype(f32)
    normed_low = norm_stats(rows)[0].astype(bf16)
    key_val = mm(normed_low, wide_ref[:, width : 3 * width]).astype(bf16)
    keyval_ref[0] = key_val
    keys_s[...] = key_val[:, :width].astype(f32)
    values_s[...] = key_val[:, width:].astype(f32)
    own_low = normed_low[RIM : RIM + slots]
    query_ref[0] = (mm(own_low, wide_ref[:, :width]) + qbias_ref[...]).astype(bf16)
    gate_ref[0] = mm(own_low, wide_ref[:, 3 * width : 4 * width])

    def one_window(win):
        first = pl.multiple_of(win * WIN_Q, WIN_Q)
        keys = keys_s[pl.ds(starts[win], WIN_K), :].astype(bf16)
        values = values_s[pl.ds(starts[win], WIN_K), :].astype(bf16)
        stacked = head_stack(query_ref[0, pl.ds(first, WIN_Q), :], ATOM_HEADS, head_dim, 0)
        scores = mm_nt(stacked, keys) * scale + bias_s[win]
        exp_scores = jnp.exp(scores - jnp.max(scores, -1, keepdims=True))
        probs = exp_scores * (1.0 / jnp.sum(exp_scores, -1, keepdims=True))
        probs_low = probs.astype(bf16)
        probs_ref[0, win] = probs_low
        attend = head_fold(mm(probs_low, values), ATOM_HEADS, head_dim, 0)
        attend_ref[0, pl.ds(first, WIN_Q), :] = attend

    def some_windows(step, carry):
        for part in range(4):
            one_window(step * 4 + part)
        return carry

    lax.fori_loop(0, windows // 4, some_windows, 0)

    gated_low = (attend_ref[0] * sigmoid(gate_ref[0])).astype(bf16)
    offset = 4 * width
    upw = wide_ref[:, offset : offset + 2 * hidden_width]
    offset += 2 * hidden_width
    pool_weight = wide_ref[:, offset : offset + model_width]
    outw = wide_ref[:, offset + model_width : offset + model_width + width]
    mid = rows[RIM : RIM + slots] + mm(gated_low, outw)
    mid_ref[0] = mid
    ffn_low = norm_stats(mid)[0].astype(bf16)
    upper = mm(ffn_low, upw)
    first_half, second_half = upper[:, :hidden_width], upper[:, hidden_width:]
    hidden = (first_half * sigmoid(first_half) * second_half).astype(bf16)
    final_low = (mid + mm(hidden, down_ref[...])).astype(bf16)
    pool_pre = mm(final_low, pool_weight)
    share = share_ref[...]
    for lane in range(0, model_width, LANES):
        part = pool_pre[:, lane : lane + LANES]
        part = part * sigmoid(part) * share
        pooled_ref[0, :, lane : lane + LANES] = jnp.sum(
            part.reshape(slots // MAX_ATOMS, MAX_ATOMS, LANES), 1
        )


def atom_forward(ext, starts, pairs, spread, blocked, share, wide, down, qbias):
    samples, ext_slots, width = ext.shape
    slots = ext_slots - 2 * RIM
    tokens = slots // MAX_ATOMS
    windows = slots // WIN_Q
    model_width = wide.shape[1] - 5 * width - 2 * down.shape[0]
    stack = ATOM_HEADS * WIN_Q
    outs = (
        ((tokens, model_width), f32),
        ((slots, width), bf16),
        ((ext_slots, 2 * width), bf16),
        ((slots, width), f32),
        ((windows, stack, WIN_K), bf16),
        ((slots, width), f32),
        ((slots, width), f32),
    )
    return pl.pallas_call(
        atom_fwd_kernel,
        out_shape=[jax.ShapeDtypeStruct((samples,) + shape, kind) for shape, kind in outs],
        grid_spec=pltpu.PrefetchScalarGridSpec(
            num_scalar_prefetch=1,
            grid=(samples,),
            in_specs=[
                per_sample((ext_slots, width)),
                whole(pairs.shape),
                whole(spread.shape),
                whole(blocked.shape),
                whole(share.shape),
                whole(wide.shape),
                whole(down.shape),
                whole(qbias.shape),
            ],
            out_specs=[per_sample(shape) for shape, _ in outs],
            scratch_shapes=[
                pltpu.VMEM((windows, stack, WIN_K), f32),
                pltpu.VMEM((ext_slots, width), f32),
                pltpu.VMEM((ext_slots, width), f32),
            ],
        ),
        compiler_params=params(),
        name="atom_forward",
    )(starts, ext, pairs, spread, blocked, share, wide, down, qbias)


def atom_bwd_kernel(
    starts,
    grad_ref,
    query_ref,
    keyval_ref,
    gate_ref,
    probs_ref,
    attend_ref,
    mid_ref,
    pairs_ref,
    share_ref,
    wide_ref,
    down_ref,
    mix_ref,
    own_ref,
    left_ref,
    right_ref,
    midgrad_ref,
    qbias_ref,
    outw_ref,
    upw_ref,
    downw_ref,
    pool_ref,
    pairw_ref,
    pairm_ref,
    keys_s,
    values_s,
    acck_s,
    accv_s,
    bias_s,
    attlow_s,
    dq_s,
):
    width = query_ref.shape[-1]
    head_dim = width // ATOM_HEADS
    scale = float(head_dim) ** (-0.5)
    slots = query_ref.shape[1]
    windows = slots // WIN_Q
    hidden_width = down_ref.shape[0]
    model_width = grad_ref.shape[-1]
    tokens = grad_ref.shape[1]
    sample = pl.program_id(0)

    @pl.when(sample == 0)
    def _():
        for ref in (qbias_ref, outw_ref, upw_ref, downw_ref, pool_ref, pairw_ref, pairm_ref, bias_s):
            ref[...] = jnp.zeros_like(ref)

    offset = 4 * width
    upw = wide_ref[:, offset : offset + 2 * hidden_width]
    offset += 2 * hidden_width
    pool_weight = wide_ref[:, offset : offset + model_width]
    outw = wide_ref[:, offset + model_width : offset + model_width + width]
    down = down_ref[...]

    mid = mid_ref[0]
    normed_mid, inv_mid = norm_stats(mid)
    ffn_low = normed_mid.astype(bf16)
    upper = mm(ffn_low, upw)
    first_half, second_half = upper[:, :hidden_width], upper[:, hidden_width:]
    sig_first = sigmoid(first_half)
    hidden = (first_half * sig_first * second_half).astype(bf16)
    final_low = (mid + mm(hidden, down)).astype(bf16)
    pool_pre = mm(final_low, pool_weight)
    share = share_ref[...]
    pool_parts = []
    for lane in range(0, model_width, LANES):
        part = pool_pre[:, lane : lane + LANES]
        grad = jnp.broadcast_to(
            grad_ref[0, :, lane : lane + LANES][:, None, :], (tokens, MAX_ATOMS, LANES)
        ).reshape(slots, LANES)
        sig_pool = sigmoid(part)
        pool_parts.append((grad * share * sig_pool * (1.0 + part * (1.0 - sig_pool))).astype(bf16))
    pool_grad = jnp.concatenate(pool_parts, 1)
    final_grad = mm_nt(pool_grad, pool_weight)
    pool_ref[...] += mm_tn(final_low, pool_grad)
    branch_low = final_grad.astype(bf16)
    hidden_grad = mm_nt(branch_low, down)
    first_grad = hidden_grad * second_half * sig_first * (1.0 + first_half * (1.0 - sig_first))
    second_grad = hidden_grad * first_half * sig_first
    upper_grad = jnp.concatenate([first_grad.astype(bf16), second_grad.astype(bf16)], 1)
    downw_ref[...] += mm_tn(hidden, branch_low)
    upw_ref[...] += mm_tn(ffn_low, upper_grad)
    mid_grad = final_grad + norm_back(normed_mid, inv_mid, mm_nt(upper_grad, upw))
    midgrad_ref[0] = mid_grad
    out_low = mid_grad.astype(bf16)
    gated_grad = mm_nt(out_low, outw)
    sig_gate = sigmoid(gate_ref[0])
    attend = attend_ref[0]
    gated_low = (attend * sig_gate).astype(bf16)
    outw_ref[...] += mm_tn(gated_low, out_low)
    attlow_s[...] = (gated_grad * sig_gate).astype(bf16)
    mix_ref[0, :, width:] = (gated_grad * attend * sig_gate * (1.0 - sig_gate)).astype(bf16)

    keys_s[...] = keyval_ref[0, :, :width].astype(f32)
    values_s[...] = keyval_ref[0, :, width:].astype(f32)
    acck_s[...] = jnp.zeros_like(acck_s)
    accv_s[...] = jnp.zeros_like(accv_s)

    def one_window(win):
        first = pl.multiple_of(win * WIN_Q, WIN_Q)
        start = starts[win]
        keys = keys_s[pl.ds(start, WIN_K), :].astype(bf16)
        values = values_s[pl.ds(start, WIN_K), :].astype(bf16)
        queries = head_stack(query_ref[0, pl.ds(first, WIN_Q), :], ATOM_HEADS, head_dim, 0)
        att = head_stack(attlow_s[pl.ds(first, WIN_Q), :], ATOM_HEADS, head_dim, 0)
        probs_low = probs_ref[0, win]
        probs = probs_low.astype(f32)
        prob_grad = mm_nt(att, values)
        delta = jnp.sum(prob_grad * probs, -1, keepdims=True)
        score_low = (probs * (prob_grad - delta)).astype(bf16)
        bias_s[win] += score_low.astype(f32)
        dq_s[pl.ds(first, WIN_Q), :] = (
            head_fold(mm(score_low, keys), ATOM_HEADS, head_dim, 0) * scale
        )
        acck_s[pl.ds(start, WIN_K), :] += mm_tn(score_low, queries) * scale
        accv_s[pl.ds(start, WIN_K), :] += mm_tn(probs_low, att)

    def some_windows(step, carry):
        for part in range(4):
            one_window(step * 4 + part)
        return carry

    lax.fori_loop(0, windows // 4, some_windows, 0)

    query_grad = dq_s[...]
    qbias_ref[...] += jnp.sum(query_grad, 0, keepdims=True)
    mix_ref[0, :, :width] = query_grad.astype(bf16)
    for ref, low, high in ((own_ref, RIM, RIM + slots), (left_ref, 0, RIM), (right_ref, RIM + slots, slots + 2 * RIM)):
        ref[0, :, :width] = acck_s[low:high, :].astype(ref.dtype)
        ref[0, :, width:] = accv_s[low:high, :].astype(ref.dtype)

    @pl.when(sample == pl.num_programs(0) - 1)
    def _():
        fold = pair_fold(pairs_ref.shape[1] // WIN_Q)

        def one(win, carry):
            pairs = pairs_ref[win]
            mean, inv_std = pair_stats(pairs, fold)
            scaled = bias_s[win] * jnp.concatenate([inv_std] * ATOM_HEADS, 0)
            pairm_ref[...] += scaled * jnp.concatenate([mean] * ATOM_HEADS, 0)
            upper = scaled.astype(bf16)
            lower = (scaled - upper.astype(f32)).astype(bf16)
            pairw_ref[...] += mm_nt(upper, pairs) + mm_nt(lower, pairs)
            return carry

        lax.fori_loop(0, windows, one, 0)


def atom_backward(grad, starts, stored, pairs, share, wide, down):
    query, keyval, gate, probs, attend, mid = stored
    samples, slots, width = query.shape
    ext_slots = slots + 2 * RIM
    windows = slots // WIN_Q
    model_width = grad.shape[-1]
    hidden_width = down.shape[0]
    stack = ATOM_HEADS * WIN_Q
    outs = (
        ((slots, 2 * width), bf16),
        ((slots, 2 * width), f32),
        ((RIM, 2 * width), bf16),
        ((RIM, 2 * width), bf16),
        ((slots, width), f32),
    )
    totals = (
        (1, width),
        (width, width),
        (width, 2 * hidden_width),
        (hidden_width, width),
        (width, model_width),
        (stack, pairs.shape[1]),
        (stack, WIN_K),
    )
    return pl.pallas_call(
        atom_bwd_kernel,
        out_shape=[jax.ShapeDtypeStruct((samples,) + shape, kind) for shape, kind in outs]
        + [jax.ShapeDtypeStruct(shape, f32) for shape in totals],
        grid_spec=pltpu.PrefetchScalarGridSpec(
            num_scalar_prefetch=1,
            grid=(samples,),
            in_specs=[per_sample(grad.shape[1:])]
            + [per_sample(part.shape[1:]) for part in stored]
            + [whole(part.shape) for part in (pairs, share, wide, down)],
            out_specs=[per_sample(shape) for shape, _ in outs] + [whole(shape) for shape in totals],
            scratch_shapes=[
                pltpu.VMEM((ext_slots, width), f32),
                pltpu.VMEM((ext_slots, width), f32),
                pltpu.VMEM((ext_slots, width), f32),
                pltpu.VMEM((ext_slots, width), f32),
                pltpu.VMEM((windows, stack, WIN_K), f32),
                pltpu.VMEM((slots, width), bf16),
                pltpu.VMEM((slots, width), f32),
            ],
        ),
        compiler_params=params(),
        name="atom_backward",
    )(starts, grad, *stored, pairs, share, wide, down)


def atom_input_kernel(
    rows_ref, mix_ref, own_ref, left_ref, right_ref, midgrad_ref, wide_ref, grad_ref, proj_ref
):
    width = rows_ref.shape[-1]

    @pl.when(pl.program_id(0) == 0)
    def _():
        proj_ref[...] = jnp.zeros_like(proj_ref)

    normed, inv_std = norm_stats(rows_ref[0].astype(f32))
    slots = normed.shape[0]
    own = own_ref[0]
    head = own[:RIM] + left_ref[0].astype(f32)
    tail = own[slots - RIM :] + right_ref[0].astype(f32)
    own = jnp.concatenate([head, own[RIM : slots - RIM], tail], 0).astype(bf16)
    mix = jnp.concatenate([mix_ref[0, :, :width], own, mix_ref[0, :, width:]], 1)
    proj_ref[...] += mm_tn(normed.astype(bf16), mix)
    normed_grad = mm_nt(mix, wide_ref[:, : 4 * width])
    grad_ref[0] = midgrad_ref[0] + norm_back(normed, inv_std, normed_grad)


def atom_input_backward(rows, mix, own, left, right, midgrad, wide):
    samples, slots, width = rows.shape
    return pl.pallas_call(
        atom_input_kernel,
        out_shape=[
            jax.ShapeDtypeStruct(rows.shape, f32),
            jax.ShapeDtypeStruct((width, 4 * width), f32),
        ],
        grid=(samples,),
        in_specs=[per_sample(part.shape[1:]) for part in (rows, mix, own, left, right, midgrad)]
        + [whole(wide.shape)],
        out_specs=[per_sample((slots, width)), whole((width, 4 * width))],
        compiler_params=params(),
        name="atom_input_backward",
    )(rows, mix, own, left, right, midgrad, wide)


def row_stats(pairs, ones_op, weights):
    count = weights.shape[0]
    both = mm_nt(jnp.concatenate([weights, ones_op], 0), pairs)
    upper, lower = square_sums(ones_op, pairs.astype(f32) * pairs.astype(f32))
    features = pairs.shape[1]
    mean = both[count : count + 1] * (1.0 / features)
    square = (mm_nt(ones_op, upper) + mm_nt(ones_op, lower))[:1] * (1.0 / features)
    var = jnp.maximum(square - mean * mean, 0.0)
    return both[:count], mean, lax.rsqrt(var + norm_eps)


def pair_bias_kernel(pair_ref, weight_ref, bias_ref):
    weights = weight_ref[...]
    ones_op = jnp.ones((16, weights.shape[1]), bf16)
    weight_sum = jnp.sum(weights.astype(f32), -1, keepdims=True)
    for row in range(pair_ref.shape[0]):
        product, mean, inv_std = row_stats(pair_ref[row], ones_op, weights)
        bias_ref[:, row, :] = inv_std * (product - mean * weight_sum)


def pair_bias(pairs, weights):
    rows, keys, features = pairs.shape
    heads = weights.shape[0]
    return pl.pallas_call(
        pair_bias_kernel,
        out_shape=jax.ShapeDtypeStruct((heads, rows, keys), f32),
        grid=(rows // 8,),
        in_specs=[pl.BlockSpec((8, keys, features), lambda i: (i, 0, 0)), whole(weights.shape)],
        out_specs=pl.BlockSpec((heads, 8, keys), lambda i: (0, i, 0)),
        compiler_params=params(),
        name="pair_bias",
    )(pairs, weights)


def pair_grad_kernel(pair_ref, grad_ref, weight_ref, total_ref, mean_ref):
    @pl.when(pl.program_id(0) == 0)
    def _():
        total_ref[...] = jnp.zeros_like(total_ref)
        mean_ref[...] = jnp.zeros_like(mean_ref)

    heads = grad_ref.shape[0]
    ones_op = jnp.ones((16, pair_ref.shape[2]), bf16)
    total = jnp.zeros(total_ref.shape, f32)
    means = jnp.zeros(mean_ref.shape, f32)
    for row in range(pair_ref.shape[0]):
        pairs = pair_ref[row]
        _, mean, inv_std = row_stats(pairs, ones_op, weight_ref[...])
        scaled = grad_ref[:, row, :] * inv_std
        means += scaled * mean
        upper = scaled.astype(bf16)
        lower = (scaled - upper.astype(f32)).astype(bf16)
        both = mm(jnp.concatenate([upper, lower], 0), pairs)
        total += both[:heads] + both[heads:]
    total_ref[...] += total
    mean_ref[...] += means


def pair_grad(pairs, grads, weights):
    rows, keys, features = pairs.shape
    heads = grads.shape[0]
    total, means = pl.pallas_call(
        pair_grad_kernel,
        out_shape=[
            jax.ShapeDtypeStruct((heads, features), f32),
            jax.ShapeDtypeStruct((heads, keys), f32),
        ],
        grid=(rows // 8,),
        in_specs=[
            pl.BlockSpec((8, keys, features), lambda i: (i, 0, 0)),
            pl.BlockSpec((heads, 8, keys), lambda i: (0, i, 0)),
            whole(weights.shape),
        ],
        out_specs=[whole((heads, features)), whole((heads, keys))],
        compiler_params=params(),
        name="pair_grad",
    )(pairs, grads, weights)
    return total - jnp.sum(means, -1, keepdims=True)


def head_groups(width, heads):
    head_dim = width // heads
    groups = []
    for head in range(0, heads, 4):
        low = head * head_dim
        base = low // LANES * LANES
        groups.append((head, base, low - base))
    return head_dim, groups


def token_fwd_kernel(query_ref, keyval_ref, bias_ref, attend_ref, probs_ref, fold_s):
    tokens, width = query_ref.shape[1:]
    heads = bias_ref.shape[0]
    keys = bias_ref.shape[2]
    head_dim, groups = head_groups(width, heads)
    scale = float(head_dim) ** (-0.5)
    fold_s[...] = jnp.zeros_like(fold_s)
    for head, base, first in groups:
        span = slice(base, base + 256)
        key_rows = keyval_ref[:, 0, :, base : base + 256].reshape(keys, 256)
        value_rows = keyval_ref[:, 0, :, width + base : width + base + 256].reshape(keys, 256)
        stacked = head_stack(query_ref[0, :, span], 4, head_dim, first)
        bias = bias_ref[head : head + 4].reshape(4 * tokens, keys)
        scores = mm_nt(stacked, key_rows) * scale + bias
        exp_scores = jnp.exp(scores - jnp.max(scores, -1, keepdims=True))
        probs = exp_scores * (1.0 / jnp.sum(exp_scores, -1, keepdims=True))
        probs_low = probs.astype(bf16)
        probs_ref[0, head : head + 4] = probs_low.reshape(4, tokens, keys)
        fold_s[:, span] += head_fold(mm(probs_low, value_rows), 4, head_dim, first)
    attend_ref[0] = fold_s[...]


def token_attention(query, keyval, bias):
    samples, tokens, width = query.shape
    heads, _, keys = bias.shape
    devices = keyval.shape[0]
    return pl.pallas_call(
        token_fwd_kernel,
        out_shape=[
            jax.ShapeDtypeStruct(query.shape, f32),
            jax.ShapeDtypeStruct((samples, heads, tokens, keys), bf16),
        ],
        grid=(samples,),
        in_specs=[
            per_sample((tokens, width)),
            pl.BlockSpec((devices, 1, tokens, 2 * width), lambda b: (0, b, 0, 0)),
            whole(bias.shape),
        ],
        out_specs=[per_sample((tokens, width)), per_sample((heads, tokens, keys))],
        scratch_shapes=[pltpu.VMEM((tokens, width), f32)],
        compiler_params=params(),
        name="token_attention",
    )(query, keyval, bias)


def token_bwd_kernel(
    query_ref, keyval_ref, probs_ref, att_ref, dq_ref, dkv_ref, bias_ref, fold_s, grad_s
):
    tokens, width = query_ref.shape[1:]
    heads, _, keys = bias_ref.shape
    devices = keyval_ref.shape[0]
    head_dim, groups = head_groups(width, heads)
    scale = float(head_dim) ** (-0.5)

    @pl.when(pl.program_id(0) == 0)
    def _():
        bias_ref[...] = jnp.zeros_like(bias_ref)

    fold_s[...] = jnp.zeros_like(fold_s)
    grad_s[...] = jnp.zeros_like(grad_s)
    for head, base, first in groups:
        span = slice(base, base + 256)
        key_rows = keyval_ref[:, 0, :, base : base + 256].reshape(keys, 256)
        value_rows = keyval_ref[:, 0, :, width + base : width + base + 256].reshape(keys, 256)
        queries = head_stack(query_ref[0, :, span], 4, head_dim, first)
        att = head_stack(att_ref[0, :, span], 4, head_dim, first)
        probs_low = probs_ref[0, head : head + 4].reshape(4 * tokens, keys)
        probs = probs_low.astype(f32)
        prob_grad = mm_nt(att, value_rows)
        delta = jnp.sum(prob_grad * probs, -1, keepdims=True)
        score_low = (probs * (prob_grad - delta)).astype(bf16)
        bias_ref[head : head + 4] += score_low.astype(f32).reshape(4, tokens, keys)
        fold_s[:, span] += head_fold(mm(score_low, key_rows), 4, head_dim, first) * scale
        grad_s[:, span] += mm_tn(score_low, queries) * scale
        grad_s[:, width + base : width + base + 256] += mm_tn(probs_low, att)
    dq_ref[0] = fold_s[...]
    dkv_ref[:, 0] = grad_s[...].astype(bf16).reshape(devices, tokens, 2 * width)


def token_attention_back(query, keyval, probs, att):
    samples, tokens, width = query.shape
    heads, _, keys = probs.shape[1:]
    devices = keyval.shape[0]
    return pl.pallas_call(
        token_bwd_kernel,
        out_shape=[
            jax.ShapeDtypeStruct(query.shape, f32),
            jax.ShapeDtypeStruct(keyval.shape, bf16),
            jax.ShapeDtypeStruct((heads, tokens, keys), f32),
        ],
        grid=(samples,),
        in_specs=[
            per_sample((tokens, width)),
            pl.BlockSpec((devices, 1, tokens, 2 * width), lambda b: (0, b, 0, 0)),
            per_sample((heads, tokens, keys)),
            per_sample((tokens, width)),
        ],
        out_specs=[
            per_sample((tokens, width)),
            pl.BlockSpec((devices, 1, tokens, 2 * width), lambda b: (0, b, 0, 0)),
            whole((heads, tokens, keys)),
        ],
        scratch_shapes=[
            pltpu.VMEM((tokens, width), f32),
            pltpu.VMEM((keys, 2 * width), f32),
        ],
        compiler_params=params(),
        name="token_attention_back",
    )(query, keyval, probs, att)


def to_blocks(array, width):
    return [array[:, low : low + width] for low in range(0, array.shape[1], width)]


def pack_blocks(arrays, width):
    parts = []
    for array in arrays:
        parts += to_blocks(array, width)
    return jnp.concatenate(parts, 0)


def unpack_blocks(packed, shapes, width):
    arrays, low = [], 0
    for rows, columns in shapes:
        parts = []
        for _ in range(columns // width):
            parts.append(packed[low : low + rows])
            low += rows
        arrays.append(jnp.concatenate(parts, 1) if len(parts) > 1 else parts[0])
    return arrays


def sum_shares(grads, extra):
    samp, seq = lax.axis_size("samp"), lax.axis_size("seq")
    width = grads[2].shape[1]
    shapes = [(grad.shape[0] // samp, grad.shape[1]) for grad in grads]
    packed = jnp.concatenate(
        [
            block.astype(bf16).reshape(samp, -1, width)
            for grad in grads
            for block in to_blocks(grad, width)
        ]
        + [extra.astype(bf16).reshape(samp, -1, width)],
        1,
    )
    rows = packed.shape[1]
    packed = packed.reshape(samp, seq, rows // seq, width).transpose(1, 0, 2, 3)
    part = lax.psum_scatter(packed, "seq", scatter_dimension=0, tiled=False)
    part = lax.psum_scatter(part, "samp", scatter_dimension=0, tiled=False)
    packed = lax.all_gather(part, "seq", axis=0, tiled=True).astype(f32)
    shares = unpack_blocks(packed, shapes, width)
    return shares, packed[sum(r * (c // width) for r, c in shapes) :]


def local(
    atom_input,
    token_input,
    atom_counts,
    key_offsets,
    atom_pairs,
    pair_features,
    single_features,
    noise_levels,
    noise_direction,
    atom_proj,
    atom_qbias,
    atom_pairw,
    atom_outw,
    atom_upw,
    atom_downw,
    pool_weight,
    cond_weight,
    cond_bias,
    token_proj,
    token_qbias,
    token_pairw,
    token_outw,
    token_upw,
    token_downw,
    cotangent,
):
    samp, seq = lax.axis_size("samp"), lax.axis_size("seq")
    seq_pos = lax.axis_index("seq")
    samples, slots, atom_width = atom_input.shape
    tokens, width = token_input.shape[1:]
    features = atom_pairs.shape[-1]

    half = atom_downw.shape[0] // 2
    wide_own = jnp.concatenate(
        [atom_proj, atom_upw, pool_weight, atom_outw, atom_downw[:half], atom_downw[half:]], 1
    )
    tiny_own = jnp.concatenate(
        [
            atom_qbias,
            cond_bias,
            token_qbias,
            atom_pairw.reshape(-1),
            token_pairw.reshape(-1),
        ]
    )
    wide_all = lax.all_gather(wide_own, "samp", axis=0, tiled=True)
    tiny_all = lax.all_gather(tiny_own[None], "samp", axis=0, tiled=True)
    wide = wide_all[:, : -2 * atom_width]
    down = (
        wide_all[:, -2 * atom_width :]
        .reshape(samp, half, 2, atom_width)
        .transpose(0, 2, 1, 3)
        .reshape(-1, atom_width)
    )
    sizes = [atom_qbias.size, cond_bias.size, token_qbias.size, atom_pairw.size, token_pairw.size]
    cuts = [sum(sizes[:i]) for i in range(6)]
    tiny = [tiny_all[:, cuts[i] : cuts[i + 1]] for i in range(5)]
    atom_qb = tiny[0].reshape(1, -1).astype(f32)
    cond_b = tiny[1].reshape(-1)
    token_qb = tiny[2].reshape(-1)
    atom_pw = tiny[3].reshape(features, ATOM_HEADS)
    token_pw = tiny[4].reshape(-1, token_pairw.shape[1])

    cond_w = lax.all_gather(cond_weight, "samp", axis=0, tiled=True)
    proj_w = lax.all_gather(token_proj, "samp", axis=0, tiled=True)
    out_w = lax.all_gather(token_outw, "samp", axis=0, tiled=True)
    up_w = lax.all_gather(token_upw, "samp", axis=0, tiled=True)
    down_w = lax.all_gather(token_downw, "samp", axis=0, tiled=True)

    up_pairs = [(i, i + 1) for i in range(seq - 1)]
    down_pairs = [(i + 1, i) for i in range(seq - 1)]
    before = lax.ppermute(atom_input[:, slots - RIM :], "seq", up_pairs)
    after = lax.ppermute(atom_input[:, :RIM], "seq", down_pairs)
    ext = jnp.concatenate([before, atom_input, after], 1)
    rim_tokens = RIM // MAX_ATOMS
    counts = lax.dynamic_slice_in_dim(
        jnp.pad(atom_counts, (rim_tokens, rim_tokens)), seq_pos * tokens, tokens + 2 * rim_tokens
    )
    place = jnp.arange(MAX_ATOMS, dtype=jnp.int32)
    used = place[None, :] < counts[:, None]
    blocked = jnp.where(used, 0.0, masked_score).astype(f32).reshape(-1, 1)
    blocked = jnp.broadcast_to(blocked, (blocked.shape[0], LANES))
    own_counts = counts[rim_tokens : rim_tokens + tokens]
    share = used[rim_tokens : rim_tokens + tokens].astype(f32) / own_counts[:, None].astype(f32)
    share = jnp.broadcast_to(share.reshape(-1, 1), (slots, LANES))
    windows = slots // WIN_Q
    starts = jnp.arange(windows, dtype=jnp.int32) * WIN_Q + key_offsets + RIM
    pairs_t = atom_pairs.transpose(0, 1, 3, 2).reshape(windows, WIN_Q * features, WIN_K)
    eye = jnp.eye(WIN_Q, dtype=bool)
    spread = jnp.where(
        eye[None, :, :, None], atom_pw.T[:, None, None, :], jnp.zeros((), bf16)
    ).reshape(ATOM_HEADS * WIN_Q, WIN_Q * features)
    pooled, *stored = atom_forward(
        ext, starts, pairs_t, spread, blocked, share, wide, down, atom_qb
    )
    block_in = token_input.astype(f32) + pooled

    noise_feature = 0.25 * jnp.log(noise_levels / sigma_data)
    cond_rows = (
        single_features.astype(f32)[None]
        + noise_feature[:, None, None] * noise_direction[None, None, :]
    )
    cond_low = norm_stats(cond_rows)[0].astype(bf16)
    cond_all = dot_last(cond_low, cond_w) + cond_b.astype(f32)
    parts = [cond_all[..., i * width : (i + 1) * width] for i in range(6)]

    pair_w = token_pw.T
    bias = pair_bias(pair_features, pair_w)
    normed_in, inv_in = norm_stats(block_in)
    attn_in = (jax.nn.sigmoid(parts[0]) * normed_in + parts[1]).astype(bf16)
    mix = dot_last(attn_in, proj_w)
    queries = (mix[..., :width] + token_qb.astype(f32)).astype(bf16)
    keyval_own = mix[..., width : 3 * width].astype(bf16)
    gating = mix[..., 3 * width :]
    keyval = lax.all_gather(keyval_own, "seq", axis=0, tiled=False)
    attend, probs = token_attention(queries, keyval, bias)
    sig_gate = jax.nn.sigmoid(gating)
    gated_low = (attend * sig_gate).astype(bf16)
    branch = dot_last(gated_low, out_w)
    gate_one = jax.nn.sigmoid(parts[2])
    mid = block_in + gate_one * branch
    normed_mid, inv_mid = norm_stats(mid)
    scale_two = jax.nn.sigmoid(parts[3])
    ffn_in = (scale_two * normed_mid + parts[4]).astype(bf16)
    upper = dot_last(ffn_in, up_w)
    hidden_width = down_w.shape[0]
    first_half, second_half = upper[..., :hidden_width], upper[..., hidden_width:]
    sig_first = jax.nn.sigmoid(first_half)
    hidden = (first_half * sig_first * second_half).astype(bf16)
    branch_two = dot_last(hidden, down_w)
    gate_two = jax.nn.sigmoid(parts[5])
    block_out = (mid + gate_two * branch_two).astype(bf16)

    out_grad = cotangent.astype(f32)
    branch_two_low = (out_grad * gate_two).astype(bf16)
    gate_two_grad = out_grad * branch_two * gate_two * (1.0 - gate_two)
    hidden_grad = dot_back(branch_two_low, down_w)
    first_grad = hidden_grad * second_half * sig_first * (1.0 + first_half * (1.0 - sig_first))
    second_grad = hidden_grad * first_half * sig_first
    upper_grad = jnp.concatenate([first_grad, second_grad], -1).astype(bf16)
    ffn_grad = dot_back(upper_grad, up_w)
    scale_two_grad = ffn_grad * normed_mid * scale_two * (1.0 - scale_two)
    mid_grad = out_grad + norm_back(normed_mid, inv_mid, ffn_grad * scale_two)
    branch_low = (mid_grad * gate_one).astype(bf16)
    gate_one_grad = mid_grad * branch * gate_one * (1.0 - gate_one)
    gated_grad = dot_back(branch_low, out_w)
    attend_low = (gated_grad * sig_gate).astype(bf16)
    gating_grad = gated_grad * attend * sig_gate * (1.0 - sig_gate)
    query_grad, keyval_part, bias_grad = token_attention_back(queries, keyval, probs, attend_low)
    keyval_grad = lax.psum_scatter(keyval_part, "seq", scatter_dimension=0, tiled=False)
    pairw_grad = pair_grad(pair_features, bias_grad, pair_w).T
    mix_grad = jnp.concatenate(
        [query_grad.astype(bf16), keyval_grad, gating_grad.astype(bf16)], -1
    )
    token_qb_grad = jnp.sum(query_grad, (0, 1))
    attn_in_grad = dot_back(mix_grad, proj_w)
    scale_one = jax.nn.sigmoid(parts[0])
    scale_one_grad = attn_in_grad * normed_in * scale_one * (1.0 - scale_one)
    token_grad = mid_grad + norm_back(normed_in, inv_in, attn_in_grad * scale_one)
    cond_grad = jnp.concatenate(
        [scale_one_grad, attn_in_grad, gate_one_grad, scale_two_grad, ffn_grad, gate_two_grad], -1
    ).astype(bf16)
    cond_b_grad = jnp.sum(cond_grad.astype(f32), (0, 1))

    mix_part, own, left, right, atom_mid_grad, *atom_totals = atom_backward(
        token_grad, starts, stored, pairs_t, share, wide, down
    )
    from_right = lax.ppermute(left, "seq", down_pairs)
    from_left = lax.ppermute(right, "seq", up_pairs)
    atom_grad, atom_proj_grad = atom_input_backward(
        atom_input, mix_part, own, from_left, from_right, atom_mid_grad, wide
    )
    qb_grad, outw_grad, upw_grad, downw_grad, pool_grad, pairw_stack, pairw_mean = atom_totals
    diagonal = pairw_stack.reshape(ATOM_HEADS, WIN_Q, WIN_Q, features)
    atom_pw_grad = (
        jnp.sum(jnp.where(eye[None, :, :, None], diagonal, 0.0), (1, 2)).T
        - jnp.sum(pairw_mean.reshape(ATOM_HEADS, -1), 1)[None, :]
    )

    grads = [
        weight_grad(hidden, branch_two_low),
        weight_grad(attn_in, mix_grad),
        weight_grad(gated_low, branch_low),
        weight_grad(ffn_in, upper_grad),
        weight_grad(cond_low, cond_grad),
    ]
    small = [
        atom_proj_grad,
        qb_grad.reshape(-1),
        atom_pw_grad,
        outw_grad,
        upw_grad,
        downw_grad,
        pool_grad,
        cond_b_grad,
        token_qb_grad,
        pairw_grad,
    ]
    flat = jnp.concatenate([part.reshape(samp, -1) for part in small], 1)
    unit = 16 * seq * width
    flat = jnp.pad(flat, ((0, 0), (0, -flat.shape[1] % unit))).reshape(-1, width)
    shares, rest = sum_shares(grads, flat)
    rest = rest.reshape(-1)
    out, low = [], 0
    for part in small:
        size = part.size // samp
        out.append(rest[low : low + size].reshape((part.shape[0] // samp,) + part.shape[1:]))
        low += size
    return (
        block_out,
        atom_grad,
        token_grad,
        out[0],
        out[1],
        out[2],
        out[3],
        out[4],
        out[5],
        out[6],
        shares[4],
        out[7],
        shares[1],
        out[8],
        out[9],
        shares[2],
        shares[3],
        shares[0],
    )


def solution(mesh):
    in_specs = (
        P("samp", "seq", None),
        P("samp", "seq", None),
        P(),
        P("seq"),
        P("seq", None, None, None),
        P("seq", None, None),
        P("seq", None),
        P("samp"),
        P(),
        P("samp", None),
        P("samp"),
        P("samp", None),
        P("samp", None),
        P("samp", None),
        P("samp", None),
        P("samp", None),
        P("samp", None),
        P("samp"),
        P("samp", None),
        P("samp"),
        P("samp", None),
        P("samp", None),
        P("samp", None),
        P("samp", None),
        P("samp", "seq", None),
    )
    out_specs = (
        P("samp", "seq", None),
        P("samp", "seq", None),
        P("samp", "seq", None),
        P("samp", None),
        P("samp"),
        P("samp", None),
        P("samp", None),
        P("samp", None),
        P("samp", None),
        P("samp", None),
        P("samp", None),
        P("samp"),
        P("samp", None),
        P("samp"),
        P("samp", None),
        P("samp", None),
        P("samp", None),
        P("samp", None),
    )
    return jax.shard_map(local, mesh=mesh, in_specs=in_specs, out_specs=out_specs, check_vma=False)
```

```python
import functools

import jax
import jax.numpy as jnp
from jax import lax
from jax.experimental import pallas as pl
from jax.experimental.pallas import tpu as pltpu
from jax.sharding import PartitionSpec as P

MAX_ATOMS = 8
WIN_Q = 32
WIN_K = 128
ATOM_HEADS = 4
RIM = 96
LANES = 128

norm_eps = 1e-05
sigma_data = 16.0
masked_score = -1000000000.0
bf16 = jnp.bfloat16
f32 = jnp.float32
vmem_bytes = 56 << 20


def dot_last(left_op, right_op):
    return jnp.einsum("...k,kn->...n", left_op, right_op, preferred_element_type=f32)


def dot_back(grad_op, weight):
    return jnp.einsum("...n,kn->...k", grad_op, weight, preferred_element_type=f32)


def weight_grad(left_op, grad_op):
    flat_left = left_op.reshape(-1, left_op.shape[-1])
    flat_grad = grad_op.reshape(-1, grad_op.shape[-1])
    return jnp.einsum("rk,rn->kn", flat_left, flat_grad, preferred_element_type=f32)


def mm(left_op, right_op):
    return lax.dot_general(left_op, right_op, (((1,), (0,)), ((), ())), preferred_element_type=f32)


def mm_nt(left_op, right_op):
    return lax.dot_general(left_op, right_op, (((1,), (1,)), ((), ())), preferred_element_type=f32)


def mm_tn(left_op, right_op):
    return lax.dot_general(left_op, right_op, (((0,), (0,)), ((), ())), preferred_element_type=f32)


def norm_stats(operand):
    center = operand - jnp.mean(operand, -1, keepdims=True)
    inv_std = lax.rsqrt(jnp.mean(center * center, -1, keepdims=True) + norm_eps)
    return (center * inv_std, inv_std)


def norm_back(normed, inv_std, grad_op):
    return inv_std * (
        grad_op
        - jnp.mean(grad_op, -1, keepdims=True)
        - normed * jnp.mean(grad_op * normed, -1, keepdims=True)
    )


def sigmoid(operand):
    return 1.0 / (1.0 + jnp.exp(-operand))


def whole(shape):
    return pl.BlockSpec(shape, lambda *_: (0,) * len(shape))


def per_sample(shape):
    return pl.BlockSpec((1,) + shape, lambda b, *_: (b,) + (0,) * len(shape))


def params():
    return pltpu.CompilerParams(vmem_limit_bytes=vmem_bytes)


def square_sums(ones_op, squares):
    upper = squares.astype(bf16)
    lower = (squares - upper.astype(f32)).astype(bf16)
    return upper, lower


def head_stack(rows, heads, head_dim, first):
    lane = lax.broadcasted_iota(jnp.int32, rows.shape, 1)
    parts = []
    for head in range(heads):
        low = first + head * head_dim
        parts.append(jnp.where((lane >= low) & (lane < low + head_dim), rows, jnp.zeros_like(rows)))
    return jnp.concatenate(parts, 0)


def head_fold(stacked, heads, head_dim, first):
    count = stacked.shape[0] // heads
    lane = lax.broadcasted_iota(jnp.int32, (count, stacked.shape[1]), 1)
    total = jnp.zeros((count, stacked.shape[1]), f32)
    for head in range(heads):
        low = first + head * head_dim
        part = stacked[head * count : (head + 1) * count]
        total = jnp.where((lane >= low) & (lane < low + head_dim), part, total)
    return total


MESH = pl.DeviceIdType.MESH


def places():
    samp_pos, seq_pos = lax.axis_index("samp"), lax.axis_index("seq")
    core, across, along = seq_pos % 2, seq_pos // 2 % 2, seq_pos // 4

    def index(along, across, core):
        return (along * 2 + across) * 2 + core

    return (
        samp_pos,
        seq_pos,
        index(along, across, 1 - core),
        index(along, 1 - across, core),
        index(1 - along, across, core),
        index(1 - along, 1 - across, core),
    )


def remote(source, target, send_sem, recv_sem, device):
    return pltpu.make_async_remote_copy(
        src_ref=source,
        dst_ref=target,
        send_sem=send_sem,
        recv_sem=recv_sem,
        device_id=device,
        device_id_type=MESH,
    )


def greet(devices):
    barrier = pltpu.get_barrier_semaphore()
    for device in devices:
        pl.semaphore_signal(barrier, inc=1, device_id=device, device_id_type=MESH)
    pl.semaphore_wait(barrier, len(devices))


def pick(position, values):
    chosen = values[0]
    for index, value in enumerate(values[1:], 1):
        chosen = jnp.where(position == index, value, chosen)
    return chosen


class WeightGather:
    def __init__(self, shapes, samp, seq):
        self.shapes, self.samp, self.seq = shapes, samp, seq
        self.splits = [self.split(shape, seq) for shape in shapes]

    @staticmethod
    def split(shape, parts):
        rows, columns = shape
        for down in (1, 2, 4, 8):
            across = parts // down
            if rows % (16 * down) == 0 and columns % (LANES * across) == 0:
                return (down, across)
        return None

    @staticmethod
    def fits(shapes, samp, seq):
        return (
            samp == 4
            and seq == 8
            and len(shapes) == 5
            and all(WeightGather.split(shape, seq) for shape in shapes)
        )

    def full_shapes(self):
        return [(rows * self.samp, columns) for rows, columns in self.shapes]

    def scratch(self):
        count = len(self.shapes)
        return [
            pltpu.SemaphoreType.DMA((9, self.samp, count)),
            pltpu.SemaphoreType.DMA((8, self.samp, count)),
            pltpu.SemaphoreType.DMA((2, count)),
        ] + [pltpu.VMEM(shape, bf16) for shape in self.shapes]

    def params(self):
        return pltpu.CompilerParams(
            vmem_limit_bytes=vmem_bytes, collective_id=1, has_side_effects=True
        )

    def cell(self, ref, weight, origin, part):
        rows, columns = self.shapes[weight]
        down, across = self.splits[weight]
        height, width = rows // down, columns // across
        low = origin * rows + part // across * height
        left = part % across * width
        return ref.at[
            pl.ds(pl.multiple_of(low, 16), height), pl.ds(pl.multiple_of(left, LANES), width)
        ]

    def origin(self, position, turn):
        order = [sorted(range(self.samp), key=lambda o: (abs(o - z), o)) for z in range(self.samp)]
        if isinstance(turn, int):
            return pick(position, [order[z][turn] for z in range(self.samp)])
        return pick(
            position, [pick(turn, [order[z][t] for t in range(self.samp)]) for z in range(self.samp)]
        )

    def own_copies(self, shards, fulls, own, held, stage):
        z = places()[0]
        copies = []
        for w, shard in enumerate(shards):
            rows = self.shapes[w][0]
            target = fulls[w].at[pl.ds(pl.multiple_of(z * rows, 16), rows), :]
            ends = (shard, held[w]) if stage == 0 else (held[w], target)
            copies.append(pltpu.make_async_copy(*ends, own.at[stage, w]))
        return copies

    def start(self, shards, fulls, send, recv, own, held):
        z, me, sib, xn, yn, dg = places()
        above, below = lax.rem(z + 1, self.samp), lax.rem(z + self.samp - 1, self.samp)
        greet([(z, sib), (z, xn), (z, yn), (above, me), (below, me)])
        for w, shard in enumerate(shards):
            source = self.cell(shard, w, 0, me)
            target = self.cell(fulls[w], w, z, me)

            @pl.when(z < self.samp - 1)
            def _():
                remote(source, target, send.at[0, 0, w], recv.at[0, z, w], (z + 1, me)).start()

            @pl.when(z > 0)
            def _():
                remote(source, target, send.at[1, 0, w], recv.at[0, z, w], (z - 1, me)).start()

        for copy in self.own_copies(shards, fulls, own, held, 0):
            copy.start()

    def place_own(self, shards, fulls, own, held):
        for copy in self.own_copies(shards, fulls, own, held, 0):
            copy.wait()
        for copy in self.own_copies(shards, fulls, own, held, 1):
            copy.start()

    def share_own(self, turn, origin, sources, fulls, send, recv):
        z, me, sib, xn, yn, dg = places()
        for kind, part in ((2, xn), (3, yn), (5, sib)):
            for w, source in enumerate(sources):
                target = self.cell(fulls[w], w, origin, me)
                arrival = {2: 1, 3: 2, 5: 4}[kind]
                remote(
                    source, target, send.at[kind, turn, w], recv.at[arrival, origin, w], (z, part)
                ).start()

    def wait_cell(self, fulls, recv, kind, w, origin, part, device):
        target = self.cell(fulls[w], w, origin, part)
        remote(target, target, recv.at[kind, origin, w], recv.at[kind, origin, w], device).wait_recv()

    def issue(self, turn, fulls, send, recv):
        z, me, sib, xn, yn, dg = places()
        origin = self.origin(z, turn)
        count = len(self.shapes)
        for w in range(count):
            self.wait_cell(fulls, recv, 0, w, origin, me, (z, sib))
        for w in range(count):
            cell = self.cell(fulls[w], w, origin, me)

            @pl.when((origin < z) & (z < self.samp - 1))
            def _():
                remote(cell, cell, send.at[0, turn, w], recv.at[0, origin, w], (z + 1, me)).start()

            @pl.when((origin > z) & (z > 0))
            def _():
                remote(cell, cell, send.at[1, turn, w], recv.at[0, origin, w], (z - 1, me)).start()

        cells = [self.cell(fulls[w], w, origin, me) for w in range(count)]
        self.share_own(turn, origin, cells, fulls, send, recv)

    def passed_on(self, w):
        return w in (0, 3)

    def finish(self, turn, fulls, send, recv):
        z, me, sib, xn, yn, dg = places()
        origin = self.origin(z, turn)
        count = len(self.shapes)
        for kind, part, other, by in ((1, xn, yn, True), (2, yn, xn, False)):
            for w in range(count):
                self.wait_cell(fulls, recv, kind, w, origin, part, (z, part))
                cell = self.cell(fulls[w], w, origin, part)
                if self.passed_on(w) == by:
                    remote(
                        cell, cell, send.at[4, turn, w], recv.at[3, origin, w], (z, other)
                    ).start()
                remote(
                    cell, cell, send.at[5 + kind, turn, w], recv.at[4 + kind, origin, w], (z, sib)
                ).start()

    def diagonal(self, turn, fulls, send, recv):
        z, me, sib, xn, yn, dg = places()
        origin = self.origin(z, turn)
        for w in range(len(self.shapes)):
            self.wait_cell(fulls, recv, 3, w, origin, dg, (z, yn))
            cell = self.cell(fulls[w], w, origin, dg)
            remote(cell, cell, send.at[8, turn, w], recv.at[7, origin, w], (z, sib)).start()

    def drain(self, shards, fulls, send, recv, own, held):
        z, me, sib, xn, yn, dg = places()
        count = len(self.shapes)

        def sent(kind, turn, w):
            cell = self.cell(fulls[w], w, 0, me)
            remote(cell, cell, send.at[kind, turn, w], recv.at[0, 0, w], (z, sib)).wait_send()

        def one(turn, carry):
            origin = self.origin(z, turn)
            for w in range(count):
                for kind in range(2, 9):
                    sent(kind, turn, w)

                @pl.when((z < self.samp - 1) & (origin < z))
                def _():
                    sent(0, turn, w)

                @pl.when((z > 0) & (origin > z))
                def _():
                    sent(1, turn, w)

                for kind in range(4, 8):
                    self.wait_cell(fulls, recv, kind, w, origin, sib, (z, sib))
            return carry

        lax.fori_loop(1, self.samp, one, 0)
        for w in range(count):

            @pl.when(z < self.samp - 1)
            def _():
                sent(0, 0, w)

            @pl.when(z > 0)
            def _():
                sent(1, 0, w)

        for copy in self.own_copies(shards, fulls, own, held, 1):
            copy.wait()

    def step(self, sample, shards, fulls, send, recv, own, *held):
        @pl.when(sample == 0)
        def _():
            self.start(shards, fulls, send, recv, own, held)

        @pl.when(sample == 1)
        def _():
            self.place_own(shards, fulls, own, held)

        for at, turn in ((2, 1), (3, 2), (5, 3)):

            @pl.when(sample == at)
            def _():
                self.issue(turn, fulls, send, recv)

        for at, turn in ((4, 1), (5, 2), (7, 3)):

            @pl.when(sample == at)
            def _():
                self.finish(turn, fulls, send, recv)

        for at, turn in ((5, 1), (7, 2)):

            @pl.when(sample == at)
            def _():
                self.diagonal(turn, fulls, send, recv)

    def last(self, sample, shards, fulls, send, recv, own, *held):
        @pl.when(sample == pl.num_programs(0) - 1)
        def _():
            self.diagonal(3, fulls, send, recv)
            self.drain(shards, fulls, send, recv, own, held)


def edge_kernel(samp, seq, wide_ref, tiny_ref, rows_ref, wide_out, tiny_out, ext_out, send, recv):
    z, me = lax.axis_index("samp"), lax.axis_index("seq")
    samples, slots, width = rows_ref.shape
    right, left = lax.rem(me + 1, seq), lax.rem(me + seq - 1, seq)
    others = [(lax.rem(z + hop, samp), me) for hop in range(1, samp)]
    greet(others + [(z, right), (z, left)])
    copies = []
    for hop, device in enumerate(others):
        for kind, (ref, out) in enumerate(((wide_ref, wide_out), (tiny_ref, tiny_out))):
            rows = ref.shape[0]
            target = out.at[pl.ds(pl.multiple_of(z * rows, 16), rows), :]
            copy = remote(ref, target, send.at[kind, hop], recv.at[kind, hop], device)
            copy.start()
            copies.append(copy)
    before, after = ext_out.at[:, :RIM, :], ext_out.at[:, RIM + slots :, :]
    to_right = remote(rows_ref.at[:, slots - RIM :, :], before, send.at[2, 0], recv.at[2, 0], (z, right))
    to_left = remote(rows_ref.at[:, :RIM, :], after, send.at[2, 1], recv.at[2, 1], (z, left))
    first, last = me == 0, me == seq - 1

    @pl.when(~last)
    def _():
        to_right.start()

    @pl.when(~first)
    def _():
        to_left.start()

    @pl.when(first)
    def _():
        ext_out[:, :RIM, :] = jnp.zeros((samples, RIM, width), bf16)

    @pl.when(last)
    def _():
        ext_out[:, RIM + slots :, :] = jnp.zeros((samples, RIM, width), bf16)

    def move(sample, carry):
        ext_out[sample, RIM : RIM + slots, :] = rows_ref[sample]
        return carry

    lax.fori_loop(0, samples, move, 0)
    for ref, out in ((wide_ref, wide_out), (tiny_ref, tiny_out)):
        rows = ref.shape[0]
        out[pl.ds(pl.multiple_of(z * rows, 16), rows), :] = ref[...]
    for copy in copies:
        copy.wait()

    @pl.when(~last)
    def _():
        to_right.wait_send()
        to_left.wait_recv()

    @pl.when(~first)
    def _():
        to_left.wait_send()
        to_right.wait_recv()


def edges(wide_own, tiny_own, rows):
    samp, seq = lax.axis_size("samp"), lax.axis_size("seq")
    samples, slots, width = rows.shape
    place = pl.BlockSpec(memory_space=pltpu.VMEM)
    return pl.pallas_call(
        functools.partial(edge_kernel, samp, seq),
        out_shape=[
            jax.ShapeDtypeStruct((samp * wide_own.shape[0], wide_own.shape[1]), bf16),
            jax.ShapeDtypeStruct((samp * tiny_own.shape[0], tiny_own.shape[1]), bf16),
            jax.ShapeDtypeStruct((samples, slots + 2 * RIM, width), bf16),
        ],
        in_specs=[place] * 3,
        out_specs=[place] * 3,
        scratch_shapes=[
            pltpu.SemaphoreType.DMA((3, samp)),
            pltpu.SemaphoreType.DMA((3, samp)),
        ],
        compiler_params=pltpu.CompilerParams(
            vmem_limit_bytes=vmem_bytes, collective_id=0, has_side_effects=True
        ),
        name="edges",
    )(wide_own, tiny_own, rows)


UNIT = 352


def weight_grad_kernel(
    attn_ref,
    mix_ref,
    ffn_ref,
    upper_ref,
    hidden_ref,
    two_ref,
    cond_ref,
    condgrad_ref,
    gated_ref,
    branch_ref,
    small_ref,
    out_ref,
    down_s,
    cond_s,
    outw_s,
):
    part = pl.program_id(0)
    samp = out_ref.shape[1]

    @pl.when(part == 0)
    def _():
        down_s[...] = mm_tn(hidden_ref[...], two_ref[...]).astype(bf16)
        outw_s[...] = mm_tn(gated_ref[...], branch_ref[...]).astype(bf16)
        for low in range(0, cond_s.shape[1], 768):
            cond_s[:, low : low + 768] = mm_tn(
                cond_ref[...], condgrad_ref[:, low : low + 768]
            ).astype(bf16)

    proj = mm_tn(attn_ref[...], mix_ref[...]).astype(bf16)
    upw = mm_tn(ffn_ref[...], upper_ref[...]).astype(bf16)
    rows = proj.shape[0] // samp
    for z in range(samp):
        out_ref[0, z, :rows, :384] = proj[z * rows : (z + 1) * rows]
        out_ref[0, z, :rows, 384:] = upw[z * rows : (z + 1) * rows]
        out_ref[0, z, 192:240, :] = down_s[pl.ds(pl.multiple_of(z * 384 + part * 48, 16), 48), :]
        low = pl.multiple_of(z * 96 + part // 4 * 48, 16)
        left = pl.multiple_of(part % 4 * 1152, LANES)
        out_ref[0, z, 240:288, :] = cond_s[pl.ds(low, 48), pl.ds(left, 768)]
        left = pl.multiple_of(part % 4 * 1152 + 768, LANES)
        out_ref[0, z, 288:336, :384] = cond_s[pl.ds(low, 48), pl.ds(left, 384)]
        low = pl.multiple_of(z * 192 + part // 2 * 48, 16)
        left = pl.multiple_of(part % 2 * 384, LANES)
        out_ref[0, z, 288:336, 384:] = outw_s[pl.ds(low, 48), pl.ds(left, 384)]
        out_ref[0, z, 336:, :] = small_ref[0, z]


def weight_grads(pairs, small, samp, seq):
    flat = [array.reshape(-1, array.shape[-1]) for pair in pairs for array in pair]
    rows = flat[0].shape[0]
    columns = pl.BlockSpec((rows, 384), lambda s: (0, s))
    specs = [whole(array.shape) for array in flat]
    specs[1] = columns
    specs[3] = columns
    return pl.pallas_call(
        weight_grad_kernel,
        out_shape=jax.ShapeDtypeStruct((seq, samp, UNIT, 768), bf16),
        grid=(seq,),
        in_specs=specs + [pl.BlockSpec((1, samp, 16, 768), lambda s: (s, 0, 0, 0))],
        out_specs=pl.BlockSpec((1, samp, UNIT, 768), lambda s: (s, 0, 0, 0)),
        scratch_shapes=[
            pltpu.VMEM((1536, 768), bf16),
            pltpu.VMEM((384, 4608), bf16),
            pltpu.VMEM((768, 768), bf16),
        ],
        compiler_params=params(),
        name="weight_grads",
    )(*flat, small)


def add_into(target, source, lanes=slice(None)):
    def one(step, carry):
        rows = pl.ds(pl.multiple_of(step * 32, 32), 32)
        both = target[rows, lanes].astype(f32) + source[rows, :].astype(f32)
        target[rows, lanes] = both.astype(bf16)
        return carry

    lax.fori_loop(0, UNIT // 32, one, 0)


def grad_sum_kernel(
    grads,
    proj_ref,
    up_ref,
    down_ref,
    cond_ref,
    outw_ref,
    small_ref,
    mine,
    theirs,
    from_x,
    from_y,
    last_x,
    last_y,
    planes,
    shares,
    s_sib,
    r_sib,
    s_own,
    s_one,
    r_one,
    s_two,
    r_two,
    s_z,
    r_z,
    s_share,
    r_share,
):
    z, me, sib, xn, yn, dg = places()
    core, chip = me % 2, me // 2
    chip_x, chip_y, chip_d = xn // 2, yn // 2, dg // 2
    order = [[p ^ hop for hop in (2, 3, 1, 0)] for p in range(4)]
    planes_of = [pick(z, [order[p][r] for p in range(4)]) for r in range(4)]
    greet([(z, sib), (z, xn), (z, yn)] + [(planes_of[r], me) for r in range(3)])
    head, tail = slice(0, 384), slice(384, 768)

    def pair_copies(r, j):
        return (
            remote(
                grads.at[2 * j + 1 - core, planes_of[r]],
                theirs.at[r, j],
                s_sib.at[r, j],
                r_sib.at[r, j],
                (z, sib),
            ),
            pltpu.make_async_copy(grads.at[2 * j + core, planes_of[r]], mine.at[r, j], s_own.at[r, j]),
        )

    def begin(r):
        for j in range(4):
            for copy in pair_copies(r, j):
                copy.start()

    def ones(r):
        return (
            remote(mine.at[r, chip_x, :, head], from_x.at[r, 0], s_one.at[r, 0], r_one.at[r, 0], (z, xn)),
            remote(mine.at[r, chip_d, :, head], from_x.at[r, 1], s_one.at[r, 1], r_one.at[r, 1], (z, xn)),
            remote(mine.at[r, chip_y, :, tail], from_y.at[r, 0], s_one.at[r, 2], r_one.at[r, 2], (z, yn)),
            remote(mine.at[r, chip_d, :, tail], from_y.at[r, 1], s_one.at[r, 3], r_one.at[r, 3], (z, yn)),
        )

    def twos(r):
        return (
            remote(mine.at[r, chip_y, :, head], last_y.at[r], s_two.at[r, 0], r_two.at[r, 0], (z, yn)),
            remote(mine.at[r, chip_x, :, tail], last_x.at[r], s_two.at[r, 1], r_two.at[r, 1], (z, xn)),
        )

    def across(r):
        return remote(mine.at[r, chip], planes.at[r], s_z.at[r], r_z.at[r], (planes_of[r], me))

    def pairs(r):
        for j in range(4):
            there, here = pair_copies(r, j)
            there.wait_recv()
            here.wait()
        for j in range(4):
            add_into(mine.at[r, j], theirs.at[r, j])
        for copy in ones(r):
            copy.start()

    def middle(r):
        one = ones(r)
        two = twos(r)
        one[1].wait_recv()
        add_into(mine.at[r, chip_y], from_x.at[r, 1], head)
        two[0].start()
        one[3].wait_recv()
        add_into(mine.at[r, chip_x], from_y.at[r, 1], tail)
        two[1].start()
        one[0].wait_recv()
        add_into(mine.at[r, chip], from_x.at[r, 0], head)
        one[2].wait_recv()
        add_into(mine.at[r, chip], from_y.at[r, 0], tail)

    def finish(r):
        two = twos(r)
        two[0].wait_recv()
        add_into(mine.at[r, chip], last_y.at[r], head)
        two[1].wait_recv()
        add_into(mine.at[r, chip], last_x.at[r], tail)
        if r < 3:
            across(r).start()

    begin(0)
    for r in range(6):
        if r < 4:
            if r < 3:
                begin(r + 1)
            pairs(r)
        if 1 <= r < 5:
            middle(r - 1)
        if r >= 2:
            finish(r - 2)
    for r in range(3):
        across(r).wait_recv()

    def total(step, carry):
        rows = pl.ds(pl.multiple_of(step * 32, 32), 32)
        both = mine[3, chip, rows, :].astype(f32)
        for r in range(3):
            both += planes[r, rows, :].astype(f32)
        shares[me, rows, :] = both.astype(bf16)
        return carry

    lax.fori_loop(0, UNIT // 32, total, 0)

    def share(part, lanes, kind, device):
        ref = shares.at[part, :, lanes]
        return remote(ref, ref, s_share.at[kind], r_share.at[kind], (z, device))

    full = slice(0, 768)
    sends = [share(me, full, 0, xn), share(me, full, 1, yn), share(me, full, 4, sib)]
    for copy in sends:
        copy.start()
    share(xn, full, 0, xn).wait_recv()
    more = [share(xn, head, 2, yn), share(xn, full, 5, sib)]
    for copy in more:
        copy.start()
    share(yn, full, 1, yn).wait_recv()
    more += [share(yn, tail, 3, xn), share(yn, full, 6, sib)]
    for copy in more[2:]:
        copy.start()
    share(dg, head, 2, yn).wait_recv()
    share(dg, tail, 3, xn).wait_recv()
    more.append(share(dg, full, 7, sib))
    more[-1].start()
    for kind in range(4, 8):
        share(sib, full, kind, sib).wait_recv()
    for copy in sends + more:
        copy.wait_send()
    for r in range(4):
        for j in range(4):
            pair_copies(r, j)[0].wait_send()
        for copy in ones(r) + twos(r):
            copy.wait_send()
        if r < 3:
            across(r).wait_send()

    for part in range(8):
        proj_ref[:, part * 384 : (part + 1) * 384] = shares[part, :192, head].astype(f32)
        up_ref[:, part * 384 : (part + 1) * 384] = shares[part, :192, tail].astype(f32)
        down_ref[part * 48 : (part + 1) * 48, :] = shares[part, 192:240, :].astype(f32)
        low, left = part // 4 * 48, part % 4 * 1152
        cond_ref[low : low + 48, left : left + 768] = shares[part, 240:288, :].astype(f32)
        cond_ref[low : low + 48, left + 768 : left + 1152] = shares[part, 288:336, head].astype(f32)
        low, left = part // 2 * 48, part % 2 * 384
        outw_ref[low : low + 48, left : left + 384] = shares[part, 288:336, tail].astype(f32)
        small_ref[part] = shares[part, 336:, :].astype(f32)


def grad_sums(grads, shapes):
    seq = grads.shape[0]
    outs = list(shapes) + [(seq, 16, 768)]
    half = (UNIT, 384)
    dma = pltpu.SemaphoreType.DMA
    return pl.pallas_call(
        grad_sum_kernel,
        out_shape=[jax.ShapeDtypeStruct(shape, f32) for shape in outs],
        in_specs=[pl.BlockSpec(memory_space=pl.ANY)],
        out_specs=[pl.BlockSpec(memory_space=pltpu.VMEM)] * 6,
        scratch_shapes=[
            pltpu.VMEM((4, 4, UNIT, 768), bf16),
            pltpu.VMEM((4, 4, UNIT, 768), bf16),
            pltpu.VMEM((4, 2) + half, bf16),
            pltpu.VMEM((4, 2) + half, bf16),
            pltpu.VMEM((4,) + half, bf16),
            pltpu.VMEM((4,) + half, bf16),
            pltpu.VMEM((3, UNIT, 768), bf16),
            pltpu.VMEM((8, UNIT, 768), bf16),
            dma((4, 4)),
            dma((4, 4)),
            dma((4, 4)),
            dma((4, 4)),
            dma((4, 4)),
            dma((4, 2)),
            dma((4, 2)),
            dma((3,)),
            dma((3,)),
            dma((8,)),
            dma((8,)),
        ],
        compiler_params=pltpu.CompilerParams(
            vmem_limit_bytes=vmem_bytes, collective_id=2, has_side_effects=True
        ),
        name="grad_sums",
    )(grads)


def pair_stats(pairs, fold):
    upper, lower = square_sums(fold, pairs.astype(f32) * pairs.astype(f32))
    features = pairs.shape[0] // WIN_Q
    mean = mm(fold, pairs) * (1.0 / features)
    square = (mm(fold, upper) + mm(fold, lower)) * (1.0 / features)
    var = jnp.maximum(square - mean * mean, 0.0)
    inv_std = lax.rsqrt(var + norm_eps)
    return mean, inv_std


def pair_fold(features):
    shape = (WIN_Q, WIN_Q * features)
    row = lax.broadcasted_iota(jnp.int32, shape, 0)
    column = lax.broadcasted_iota(jnp.int32, shape, 1)
    return jnp.where(column // features == row, 1.0, 0.0).astype(bf16)


def atom_fwd_kernel(
    gather,
    starts,
    ext_ref,
    pairs_ref,
    spread_ref,
    blocked_ref,
    share_ref,
    wide_ref,
    down_ref,
    qbias_ref,
    *refs,
):
    count = len(gather.shapes) if gather is not None else 0
    shards, refs = refs[:count], refs[count:]
    (
        pooled_ref,
        query_ref,
        keyval_ref,
        gate_ref,
        probs_ref,
        attend_ref,
        mid_ref,
    ), refs = refs[:7], refs[7:]
    fulls, refs = refs[:count], refs[count:]
    (bias_s, keys_s, values_s), sems = refs[:3], refs[3:]
    width = ext_ref.shape[-1]
    head_dim = width // ATOM_HEADS
    scale = float(head_dim) ** (-0.5)
    slots = query_ref.shape[1]
    windows = slots // WIN_Q
    hidden_width = down_ref.shape[0]
    model_width = pooled_ref.shape[-1]
    features = pairs_ref.shape[1] // WIN_Q
    sample = pl.program_id(0)
    if gather is not None:
        gather.step(sample, shards, fulls, *sems)

    @pl.when(sample == 0)
    def _():
        fold = pair_fold(features)
        spread = spread_ref[...]
        spread_sum = jnp.sum(spread.astype(f32), -1, keepdims=True)
        first_lane = jnp.where(
            lax.broadcasted_iota(jnp.int32, (ATOM_HEADS * WIN_Q, LANES), 1) == 0, 1.0, 0.0
        ).astype(bf16)

        def one(win, carry):
            pairs = pairs_ref[win]
            mean, inv_std = pair_stats(pairs, fold)
            mean = jnp.concatenate([mean] * ATOM_HEADS, 0)
            inv_std = jnp.concatenate([inv_std] * ATOM_HEADS, 0)
            blocked = blocked_ref[pl.ds(starts[win], WIN_K), :].astype(bf16)
            bias = inv_std * (mm(spread, pairs) - mean * spread_sum)
            bias_s[win] = bias + mm_nt(first_lane, blocked)
            return carry

        lax.fori_loop(0, windows, one, 0)

    rows = ext_ref[0].astype(f32)
    normed_low = norm_stats(rows)[0].astype(bf16)
    key_val = mm(normed_low, wide_ref[:, width : 3 * width]).astype(bf16)
    keyval_ref[0] = key_val
    keys_s[...] = key_val[:, :width].astype(f32)
    values_s[...] = key_val[:, width:].astype(f32)
    own_low = normed_low[RIM : RIM + slots]
    query_ref[0] = (mm(own_low, wide_ref[:, :width]) + qbias_ref[...]).astype(bf16)
    gate_ref[0] = mm(own_low, wide_ref[:, 3 * width : 4 * width])

    def one_window(win):
        first = pl.multiple_of(win * WIN_Q, WIN_Q)
        keys = keys_s[pl.ds(starts[win], WIN_K), :].astype(bf16)
        values = values_s[pl.ds(starts[win], WIN_K), :].astype(bf16)
        stacked = head_stack(query_ref[0, pl.ds(first, WIN_Q), :], ATOM_HEADS, head_dim, 0)
        scores = mm_nt(stacked, keys) * scale + bias_s[win]
        exp_scores = jnp.exp(scores - jnp.max(scores, -1, keepdims=True))
        probs = exp_scores * (1.0 / jnp.sum(exp_scores, -1, keepdims=True))
        probs_low = probs.astype(bf16)
        probs_ref[0, win] = probs_low
        attend = head_fold(mm(probs_low, values), ATOM_HEADS, head_dim, 0)
        attend_ref[0, pl.ds(first, WIN_Q), :] = attend

    def some_windows(step, carry):
        for part in range(4):
            one_window(step * 4 + part)
        return carry

    lax.fori_loop(0, windows // 4, some_windows, 0)

    gated_low = (attend_ref[0] * sigmoid(gate_ref[0])).astype(bf16)
    offset = 4 * width
    upw = wide_ref[:, offset : offset + 2 * hidden_width]
    offset += 2 * hidden_width
    pool_weight = wide_ref[:, offset : offset + model_width]
    outw = wide_ref[:, offset + model_width : offset + model_width + width]
    mid = rows[RIM : RIM + slots] + mm(gated_low, outw)
    mid_ref[0] = mid
    ffn_low = norm_stats(mid)[0].astype(bf16)
    upper = mm(ffn_low, upw)
    first_half, second_half = upper[:, :hidden_width], upper[:, hidden_width:]
    hidden = (first_half * sigmoid(first_half) * second_half).astype(bf16)
    final_low = (mid + mm(hidden, down_ref[...])).astype(bf16)
    pool_pre = mm(final_low, pool_weight)
    share = share_ref[...]
    for lane in range(0, model_width, LANES):
        part = pool_pre[:, lane : lane + LANES]
        part = part * sigmoid(part) * share
        pooled_ref[0, :, lane : lane + LANES] = jnp.sum(
            part.reshape(slots // MAX_ATOMS, MAX_ATOMS, LANES), 1
        )
    if gather is not None:
        gather.last(sample, shards, fulls, *sems)


def atom_forward(ext, starts, pairs, spread, blocked, share, wide, down, qbias, gather, shards):
    samples, ext_slots, width = ext.shape
    slots = ext_slots - 2 * RIM
    tokens = slots // MAX_ATOMS
    windows = slots // WIN_Q
    model_width = wide.shape[1] - 5 * width - 2 * down.shape[0]
    stack = ATOM_HEADS * WIN_Q
    outs = (
        ((tokens, model_width), f32),
        ((slots, width), bf16),
        ((ext_slots, 2 * width), bf16),
        ((slots, width), f32),
        ((windows, stack, WIN_K), bf16),
        ((slots, width), f32),
        ((slots, width), f32),
    )
    place = pl.BlockSpec(memory_space=pl.ANY)
    results = pl.pallas_call(
        functools.partial(atom_fwd_kernel, gather),
        out_shape=[jax.ShapeDtypeStruct((samples,) + shape, kind) for shape, kind in outs]
        + [jax.ShapeDtypeStruct(shape, bf16) for shape in (gather.full_shapes() if gather else [])],
        grid=(samples,),
        in_specs=[
            pl.BlockSpec(memory_space=pltpu.SMEM),
            per_sample((ext_slots, width)),
            whole(pairs.shape),
            whole(spread.shape),
            whole(blocked.shape),
            whole(share.shape),
            whole(wide.shape),
            whole(down.shape),
            whole(qbias.shape),
        ]
        + [place] * len(shards),
        out_specs=[per_sample(shape) for shape, _ in outs] + [place] * len(shards),
        scratch_shapes=[
            pltpu.VMEM((windows, stack, WIN_K), f32),
            pltpu.VMEM((ext_slots, width), f32),
            pltpu.VMEM((ext_slots, width), f32),
        ]
        + (gather.scratch() if gather else []),
        compiler_params=gather.params() if gather else params(),
        name="atom_forward",
    )(starts, ext, pairs, spread, blocked, share, wide, down, qbias, *shards)
    return results[0], results[1:7], results[7:]


def atom_bwd_kernel(
    starts,
    grad_ref,
    query_ref,
    keyval_ref,
    gate_ref,
    probs_ref,
    attend_ref,
    mid_ref,
    pairs_ref,
    share_ref,
    wide_ref,
    down_ref,
    mix_ref,
    own_ref,
    left_ref,
    right_ref,
    midgrad_ref,
    qbias_ref,
    outw_ref,
    upw_ref,
    downw_ref,
    pool_ref,
    pairw_ref,
    pairm_ref,
    keys_s,
    values_s,
    acck_s,
    accv_s,
    bias_s,
    attlow_s,
    dq_s,
):
    width = query_ref.shape[-1]
    head_dim = width // ATOM_HEADS
    scale = float(head_dim) ** (-0.5)
    slots = query_ref.shape[1]
    windows = slots // WIN_Q
    hidden_width = down_ref.shape[0]
    model_width = grad_ref.shape[-1]
    tokens = grad_ref.shape[1]
    sample = pl.program_id(0)

    @pl.when(sample == 0)
    def _():
        for ref in (qbias_ref, outw_ref, upw_ref, downw_ref, pool_ref, pairw_ref, pairm_ref, bias_s):
            ref[...] = jnp.zeros_like(ref)

    offset = 4 * width
    upw = wide_ref[:, offset : offset + 2 * hidden_width]
    offset += 2 * hidden_width
    pool_weight = wide_ref[:, offset : offset + model_width]
    outw = wide_ref[:, offset + model_width : offset + model_width + width]
    down = down_ref[...]

    mid = mid_ref[0]
    normed_mid, inv_mid = norm_stats(mid)
    ffn_low = normed_mid.astype(bf16)
    upper = mm(ffn_low, upw)
    first_half, second_half = upper[:, :hidden_width], upper[:, hidden_width:]
    sig_first = sigmoid(first_half)
    hidden = (first_half * sig_first * second_half).astype(bf16)
    final_low = (mid + mm(hidden, down)).astype(bf16)
    pool_pre = mm(final_low, pool_weight)
    share = share_ref[...]
    pool_parts = []
    for lane in range(0, model_width, LANES):
        part = pool_pre[:, lane : lane + LANES]
        grad = jnp.broadcast_to(
            grad_ref[0, :, lane : lane + LANES][:, None, :], (tokens, MAX_ATOMS, LANES)
        ).reshape(slots, LANES)
        sig_pool = sigmoid(part)
        pool_parts.append((grad * share * sig_pool * (1.0 + part * (1.0 - sig_pool))).astype(bf16))
    pool_grad = jnp.concatenate(pool_parts, 1)
    final_grad = mm_nt(pool_grad, pool_weight)
    pool_ref[...] += mm_tn(final_low, pool_grad)
    branch_low = final_grad.astype(bf16)
    hidden_grad = mm_nt(branch_low, down)
    first_grad = hidden_grad * second_half * sig_first * (1.0 + first_half * (1.0 - sig_first))
    second_grad = hidden_grad * first_half * sig_first
    upper_grad = jnp.concatenate([first_grad.astype(bf16), second_grad.astype(bf16)], 1)
    downw_ref[...] += mm_tn(hidden, branch_low)
    upw_ref[...] += mm_tn(ffn_low, upper_grad)
    mid_grad = final_grad + norm_back(normed_mid, inv_mid, mm_nt(upper_grad, upw))
    midgrad_ref[0] = mid_grad
    out_low = mid_grad.astype(bf16)
    gated_grad = mm_nt(out_low, outw)
    sig_gate = sigmoid(gate_ref[0])
    attend = attend_ref[0]
    gated_low = (attend * sig_gate).astype(bf16)
    outw_ref[...] += mm_tn(gated_low, out_low)
    attlow_s[...] = (gated_grad * sig_gate).astype(bf16)
    mix_ref[0, :, width:] = (gated_grad * attend * sig_gate * (1.0 - sig_gate)).astype(bf16)

    keys_s[...] = keyval_ref[0, :, :width].astype(f32)
    values_s[...] = keyval_ref[0, :, width:].astype(f32)
    acck_s[...] = jnp.zeros_like(acck_s)
    accv_s[...] = jnp.zeros_like(accv_s)

    def one_window(win):
        first = pl.multiple_of(win * WIN_Q, WIN_Q)
        start = starts[win]
        keys = keys_s[pl.ds(start, WIN_K), :].astype(bf16)
        values = values_s[pl.ds(start, WIN_K), :].astype(bf16)
        queries = head_stack(query_ref[0, pl.ds(first, WIN_Q), :], ATOM_HEADS, head_dim, 0)
        att = head_stack(attlow_s[pl.ds(first, WIN_Q), :], ATOM_HEADS, head_dim, 0)
        probs_low = probs_ref[0, win]
        probs = probs_low.astype(f32)
        prob_grad = mm_nt(att, values)
        delta = jnp.sum(prob_grad * probs, -1, keepdims=True)
        score_low = (probs * (prob_grad - delta)).astype(bf16)
        bias_s[win] += score_low.astype(f32)
        dq_s[pl.ds(first, WIN_Q), :] = (
            head_fold(mm(score_low, keys), ATOM_HEADS, head_dim, 0) * scale
        )
        acck_s[pl.ds(start, WIN_K), :] += mm_tn(score_low, queries) * scale
        accv_s[pl.ds(start, WIN_K), :] += mm_tn(probs_low, att)

    def some_windows(step, carry):
        for part in range(4):
            one_window(step * 4 + part)
        return carry

    lax.fori_loop(0, windows // 4, some_windows, 0)

    query_grad = dq_s[...]
    qbias_ref[...] += jnp.sum(query_grad, 0, keepdims=True)
    mix_ref[0, :, :width] = query_grad.astype(bf16)
    for ref, low, high in ((own_ref, RIM, RIM + slots), (left_ref, 0, RIM), (right_ref, RIM + slots, slots + 2 * RIM)):
        ref[0, :, :width] = acck_s[low:high, :].astype(ref.dtype)
        ref[0, :, width:] = accv_s[low:high, :].astype(ref.dtype)

    @pl.when(sample == pl.num_programs(0) - 1)
    def _():
        fold = pair_fold(pairs_ref.shape[1] // WIN_Q)

        def one(win, carry):
            pairs = pairs_ref[win]
            mean, inv_std = pair_stats(pairs, fold)
            scaled = bias_s[win] * jnp.concatenate([inv_std] * ATOM_HEADS, 0)
            pairm_ref[...] += scaled * jnp.concatenate([mean] * ATOM_HEADS, 0)
            upper = scaled.astype(bf16)
            lower = (scaled - upper.astype(f32)).astype(bf16)
            pairw_ref[...] += mm_nt(upper, pairs) + mm_nt(lower, pairs)
            return carry

        lax.fori_loop(0, windows, one, 0)


def atom_backward(grad, starts, stored, pairs, share, wide, down):
    query, keyval, gate, probs, attend, mid = stored
    samples, slots, width = query.shape
    ext_slots = slots + 2 * RIM
    windows = slots // WIN_Q
    model_width = grad.shape[-1]
    hidden_width = down.shape[0]
    stack = ATOM_HEADS * WIN_Q
    outs = (
        ((slots, 2 * width), bf16),
        ((slots, 2 * width), f32),
        ((RIM, 2 * width), bf16),
        ((RIM, 2 * width), bf16),
        ((slots, width), f32),
    )
    totals = (
        (1, width),
        (width, width),
        (width, 2 * hidden_width),
        (hidden_width, width),
        (width, model_width),
        (stack, pairs.shape[1]),
        (stack, WIN_K),
    )
    return pl.pallas_call(
        atom_bwd_kernel,
        out_shape=[jax.ShapeDtypeStruct((samples,) + shape, kind) for shape, kind in outs]
        + [jax.ShapeDtypeStruct(shape, f32) for shape in totals],
        grid_spec=pltpu.PrefetchScalarGridSpec(
            num_scalar_prefetch=1,
            grid=(samples,),
            in_specs=[per_sample(grad.shape[1:])]
            + [per_sample(part.shape[1:]) for part in stored]
            + [whole(part.shape) for part in (pairs, share, wide, down)],
            out_specs=[per_sample(shape) for shape, _ in outs] + [whole(shape) for shape in totals],
            scratch_shapes=[
                pltpu.VMEM((ext_slots, width), f32),
                pltpu.VMEM((ext_slots, width), f32),
                pltpu.VMEM((ext_slots, width), f32),
                pltpu.VMEM((ext_slots, width), f32),
                pltpu.VMEM((windows, stack, WIN_K), f32),
                pltpu.VMEM((slots, width), bf16),
                pltpu.VMEM((slots, width), f32),
            ],
        ),
        compiler_params=params(),
        name="atom_backward",
    )(starts, grad, *stored, pairs, share, wide, down)


def atom_input_kernel(
    rows_ref, mix_ref, own_ref, left_ref, right_ref, midgrad_ref, wide_ref, grad_ref, proj_ref
):
    width = rows_ref.shape[-1]

    @pl.when(pl.program_id(0) == 0)
    def _():
        proj_ref[...] = jnp.zeros_like(proj_ref)

    normed, inv_std = norm_stats(rows_ref[0].astype(f32))
    slots = normed.shape[0]
    own = own_ref[0]
    head = own[:RIM] + left_ref[0].astype(f32)
    tail = own[slots - RIM :] + right_ref[0].astype(f32)
    own = jnp.concatenate([head, own[RIM : slots - RIM], tail], 0).astype(bf16)
    mix = jnp.concatenate([mix_ref[0, :, :width], own, mix_ref[0, :, width:]], 1)
    proj_ref[...] += mm_tn(normed.astype(bf16), mix)
    normed_grad = mm_nt(mix, wide_ref[:, : 4 * width])
    grad_ref[0] = midgrad_ref[0] + norm_back(normed, inv_std, normed_grad)


def atom_input_backward(rows, mix, own, left, right, midgrad, wide):
    samples, slots, width = rows.shape
    return pl.pallas_call(
        atom_input_kernel,
        out_shape=[
            jax.ShapeDtypeStruct(rows.shape, f32),
            jax.ShapeDtypeStruct((width, 4 * width), f32),
        ],
        grid=(samples,),
        in_specs=[per_sample(part.shape[1:]) for part in (rows, mix, own, left, right, midgrad)]
        + [whole(wide.shape)],
        out_specs=[per_sample((slots, width)), whole((width, 4 * width))],
        compiler_params=params(),
        name="atom_input_backward",
    )(rows, mix, own, left, right, midgrad, wide)


def row_stats(pairs, ones_op, weights):
    count = weights.shape[0]
    both = mm_nt(jnp.concatenate([weights, ones_op], 0), pairs)
    upper, lower = square_sums(ones_op, pairs.astype(f32) * pairs.astype(f32))
    features = pairs.shape[1]
    mean = both[count : count + 1] * (1.0 / features)
    square = (mm_nt(ones_op, upper) + mm_nt(ones_op, lower))[:1] * (1.0 / features)
    var = jnp.maximum(square - mean * mean, 0.0)
    return both[:count], mean, lax.rsqrt(var + norm_eps)


def pair_bias_kernel(pair_ref, weight_ref, bias_ref):
    weights = weight_ref[...]
    ones_op = jnp.ones((16, weights.shape[1]), bf16)
    weight_sum = jnp.sum(weights.astype(f32), -1, keepdims=True)
    for row in range(pair_ref.shape[0]):
        product, mean, inv_std = row_stats(pair_ref[row], ones_op, weights)
        bias_ref[:, row, :] = inv_std * (product - mean * weight_sum)


def pair_bias(pairs, weights):
    rows, keys, features = pairs.shape
    heads = weights.shape[0]
    return pl.pallas_call(
        pair_bias_kernel,
        out_shape=jax.ShapeDtypeStruct((heads, rows, keys), f32),
        grid=(rows // 8,),
        in_specs=[pl.BlockSpec((8, keys, features), lambda i: (i, 0, 0)), whole(weights.shape)],
        out_specs=pl.BlockSpec((heads, 8, keys), lambda i: (0, i, 0)),
        compiler_params=params(),
        name="pair_bias",
    )(pairs, weights)


def pair_grad_kernel(pair_ref, grad_ref, weight_ref, total_ref, mean_ref):
    @pl.when(pl.program_id(0) == 0)
    def _():
        total_ref[...] = jnp.zeros_like(total_ref)
        mean_ref[...] = jnp.zeros_like(mean_ref)

    heads = grad_ref.shape[0]
    ones_op = jnp.ones((16, pair_ref.shape[2]), bf16)
    total = jnp.zeros(total_ref.shape, f32)
    means = jnp.zeros(mean_ref.shape, f32)
    for row in range(pair_ref.shape[0]):
        pairs = pair_ref[row]
        _, mean, inv_std = row_stats(pairs, ones_op, weight_ref[...])
        scaled = grad_ref[:, row, :] * inv_std
        means += scaled * mean
        upper = scaled.astype(bf16)
        lower = (scaled - upper.astype(f32)).astype(bf16)
        both = mm(jnp.concatenate([upper, lower], 0), pairs)
        total += both[:heads] + both[heads:]
    total_ref[...] += total
    mean_ref[...] += means


def pair_grad(pairs, grads, weights):
    rows, keys, features = pairs.shape
    heads = grads.shape[0]
    total, means = pl.pallas_call(
        pair_grad_kernel,
        out_shape=[
            jax.ShapeDtypeStruct((heads, features), f32),
            jax.ShapeDtypeStruct((heads, keys), f32),
        ],
        grid=(rows // 8,),
        in_specs=[
            pl.BlockSpec((8, keys, features), lambda i: (i, 0, 0)),
            pl.BlockSpec((heads, 8, keys), lambda i: (0, i, 0)),
            whole(weights.shape),
        ],
        out_specs=[whole((heads, features)), whole((heads, keys))],
        compiler_params=params(),
        name="pair_grad",
    )(pairs, grads, weights)
    return total - jnp.sum(means, -1, keepdims=True)


def head_groups(width, heads):
    head_dim = width // heads
    groups = []
    for head in range(0, heads, 4):
        low = head * head_dim
        base = low // LANES * LANES
        groups.append((head, base, low - base))
    return head_dim, groups


def token_fwd_kernel(query_ref, keyval_ref, bias_ref, attend_ref, probs_ref, fold_s):
    tokens, width = query_ref.shape[1:]
    heads = bias_ref.shape[0]
    keys = bias_ref.shape[2]
    head_dim, groups = head_groups(width, heads)
    scale = float(head_dim) ** (-0.5)
    fold_s[...] = jnp.zeros_like(fold_s)
    for head, base, first in groups:
        span = slice(base, base + 256)
        key_rows = keyval_ref[:, 0, :, base : base + 256].reshape(keys, 256)
        value_rows = keyval_ref[:, 0, :, width + base : width + base + 256].reshape(keys, 256)
        stacked = head_stack(query_ref[0, :, span], 4, head_dim, first)
        bias = bias_ref[head : head + 4].reshape(4 * tokens, keys)
        scores = mm_nt(stacked, key_rows) * scale + bias
        exp_scores = jnp.exp(scores - jnp.max(scores, -1, keepdims=True))
        probs = exp_scores * (1.0 / jnp.sum(exp_scores, -1, keepdims=True))
        probs_low = probs.astype(bf16)
        probs_ref[0, head : head + 4] = probs_low.reshape(4, tokens, keys)
        fold_s[:, span] += head_fold(mm(probs_low, value_rows), 4, head_dim, first)
    attend_ref[0] = fold_s[...]


def token_attention(query, keyval, bias):
    samples, tokens, width = query.shape
    heads, _, keys = bias.shape
    devices = keyval.shape[0]
    return pl.pallas_call(
        token_fwd_kernel,
        out_shape=[
            jax.ShapeDtypeStruct(query.shape, f32),
            jax.ShapeDtypeStruct((samples, heads, tokens, keys), bf16),
        ],
        grid=(samples,),
        in_specs=[
            per_sample((tokens, width)),
            pl.BlockSpec((devices, 1, tokens, 2 * width), lambda b: (0, b, 0, 0)),
            whole(bias.shape),
        ],
        out_specs=[per_sample((tokens, width)), per_sample((heads, tokens, keys))],
        scratch_shapes=[pltpu.VMEM((tokens, width), f32)],
        compiler_params=params(),
        name="token_attention",
    )(query, keyval, bias)


def token_bwd_kernel(
    query_ref, keyval_ref, probs_ref, att_ref, dq_ref, dkv_ref, bias_ref, fold_s, grad_s
):
    tokens, width = query_ref.shape[1:]
    heads, _, keys = bias_ref.shape
    devices = keyval_ref.shape[0]
    head_dim, groups = head_groups(width, heads)
    scale = float(head_dim) ** (-0.5)

    @pl.when(pl.program_id(0) == 0)
    def _():
        bias_ref[...] = jnp.zeros_like(bias_ref)

    fold_s[...] = jnp.zeros_like(fold_s)
    grad_s[...] = jnp.zeros_like(grad_s)
    for head, base, first in groups:
        span = slice(base, base + 256)
        key_rows = keyval_ref[:, 0, :, base : base + 256].reshape(keys, 256)
        value_rows = keyval_ref[:, 0, :, width + base : width + base + 256].reshape(keys, 256)
        queries = head_stack(query_ref[0, :, span], 4, head_dim, first)
        att = head_stack(att_ref[0, :, span], 4, head_dim, first)
        probs_low = probs_ref[0, head : head + 4].reshape(4 * tokens, keys)
        probs = probs_low.astype(f32)
        prob_grad = mm_nt(att, value_rows)
        delta = jnp.sum(prob_grad * probs, -1, keepdims=True)
        score_low = (probs * (prob_grad - delta)).astype(bf16)
        bias_ref[head : head + 4] += score_low.astype(f32).reshape(4, tokens, keys)
        fold_s[:, span] += head_fold(mm(score_low, key_rows), 4, head_dim, first) * scale
        grad_s[:, span] += mm_tn(score_low, queries) * scale
        grad_s[:, width + base : width + base + 256] += mm_tn(probs_low, att)
    dq_ref[0] = fold_s[...]
    dkv_ref[:, 0] = grad_s[...].astype(bf16).reshape(devices, tokens, 2 * width)


def token_attention_back(query, keyval, probs, att):
    samples, tokens, width = query.shape
    heads, _, keys = probs.shape[1:]
    devices = keyval.shape[0]
    return pl.pallas_call(
        token_bwd_kernel,
        out_shape=[
            jax.ShapeDtypeStruct(query.shape, f32),
            jax.ShapeDtypeStruct(keyval.shape, bf16),
            jax.ShapeDtypeStruct((heads, tokens, keys), f32),
        ],
        grid=(samples,),
        in_specs=[
            per_sample((tokens, width)),
            pl.BlockSpec((devices, 1, tokens, 2 * width), lambda b: (0, b, 0, 0)),
            per_sample((heads, tokens, keys)),
            per_sample((tokens, width)),
        ],
        out_specs=[
            per_sample((tokens, width)),
            pl.BlockSpec((devices, 1, tokens, 2 * width), lambda b: (0, b, 0, 0)),
            whole((heads, tokens, keys)),
        ],
        scratch_shapes=[
            pltpu.VMEM((tokens, width), f32),
            pltpu.VMEM((keys, 2 * width), f32),
        ],
        compiler_params=params(),
        name="token_attention_back",
    )(query, keyval, probs, att)


def to_blocks(array, width):
    return [array[:, low : low + width] for low in range(0, array.shape[1], width)]


def pack_blocks(arrays, width):
    parts = []
    for array in arrays:
        parts += to_blocks(array, width)
    return jnp.concatenate(parts, 0)


def unpack_blocks(packed, shapes, width):
    arrays, low = [], 0
    for rows, columns in shapes:
        parts = []
        for _ in range(columns // width):
            parts.append(packed[low : low + rows])
            low += rows
        arrays.append(jnp.concatenate(parts, 1) if len(parts) > 1 else parts[0])
    return arrays


def sum_shares(grads, extra):
    samp, seq = lax.axis_size("samp"), lax.axis_size("seq")
    width = grads[2].shape[1]
    shapes = [(grad.shape[0] // samp, grad.shape[1]) for grad in grads]
    packed = jnp.concatenate(
        [
            block.astype(bf16).reshape(samp, -1, width)
            for grad in grads
            for block in to_blocks(grad, width)
        ]
        + [extra.astype(bf16).reshape(samp, -1, width)],
        1,
    )
    rows = packed.shape[1]
    packed = packed.reshape(samp, seq, rows // seq, width).transpose(1, 0, 2, 3)
    part = lax.psum_scatter(packed, "seq", scatter_dimension=0, tiled=False)
    part = lax.psum_scatter(part, "samp", scatter_dimension=0, tiled=False)
    packed = lax.all_gather(part, "seq", axis=0, tiled=True).astype(f32)
    shares = unpack_blocks(packed, shapes, width)
    return shares, packed[sum(r * (c // width) for r, c in shapes) :]


def local(
    atom_input,
    token_input,
    atom_counts,
    key_offsets,
    atom_pairs,
    pair_features,
    single_features,
    noise_levels,
    noise_direction,
    atom_proj,
    atom_qbias,
    atom_pairw,
    atom_outw,
    atom_upw,
    atom_downw,
    pool_weight,
    cond_weight,
    cond_bias,
    token_proj,
    token_qbias,
    token_pairw,
    token_outw,
    token_upw,
    token_downw,
    cotangent,
):
    samp, seq = lax.axis_size("samp"), lax.axis_size("seq")
    seq_pos = lax.axis_index("seq")
    samples, slots, atom_width = atom_input.shape
    tokens, width = token_input.shape[1:]
    features = atom_pairs.shape[-1]

    half = atom_downw.shape[0] // 2
    wide_own = jnp.concatenate(
        [atom_proj, atom_upw, pool_weight, atom_outw, atom_downw[:half], atom_downw[half:]], 1
    )
    tiny_own = jnp.concatenate(
        [
            atom_qbias,
            cond_bias,
            token_qbias,
            atom_pairw.reshape(-1),
            token_pairw.reshape(-1),
        ]
    )
    tiny_own = jnp.pad(tiny_own, (0, -tiny_own.size % (16 * LANES))).reshape(-1, LANES)
    large = (token_proj, token_upw, token_downw, cond_weight, token_outw)
    kernels = samples == 8 and WeightGather.fits([part.shape for part in large], samp, seq)
    up_pairs = [(i, i + 1) for i in range(seq - 1)]
    down_pairs = [(i + 1, i) for i in range(seq - 1)]
    if kernels:
        wide_all, tiny_all, ext = edges(wide_own, tiny_own, atom_input)
    else:
        wide_all = lax.all_gather(wide_own, "samp", axis=0, tiled=True)
        tiny_all = lax.all_gather(tiny_own, "samp", axis=0, tiled=True)
        before = lax.ppermute(atom_input[:, slots - RIM :], "seq", up_pairs)
        after = lax.ppermute(atom_input[:, :RIM], "seq", down_pairs)
        ext = jnp.concatenate([before, atom_input, after], 1)
    tiny_all = tiny_all.reshape(samp, -1)
    wide = wide_all[:, : -2 * atom_width]
    down = (
        wide_all[:, -2 * atom_width :]
        .reshape(samp, half, 2, atom_width)
        .transpose(0, 2, 1, 3)
        .reshape(-1, atom_width)
    )
    sizes = [atom_qbias.size, cond_bias.size, token_qbias.size, atom_pairw.size, token_pairw.size]
    cuts = [sum(sizes[:i]) for i in range(6)]
    tiny = [tiny_all[:, cuts[i] : cuts[i + 1]] for i in range(5)]
    atom_qb = tiny[0].reshape(1, -1).astype(f32)
    cond_b = tiny[1].reshape(-1)
    token_qb = tiny[2].reshape(-1)
    atom_pw = tiny[3].reshape(features, ATOM_HEADS)
    token_pw = tiny[4].reshape(-1, token_pairw.shape[1])

    rim_tokens = RIM // MAX_ATOMS
    counts = lax.dynamic_slice_in_dim(
        jnp.pad(atom_counts, (rim_tokens, rim_tokens)), seq_pos * tokens, tokens + 2 * rim_tokens
    )
    place = jnp.arange(MAX_ATOMS, dtype=jnp.int32)
    used = place[None, :] < counts[:, None]
    blocked = jnp.where(used, 0.0, masked_score).astype(f32).reshape(-1, 1)
    blocked = jnp.broadcast_to(blocked, (blocked.shape[0], LANES))
    own_counts = counts[rim_tokens : rim_tokens + tokens]
    share = used[rim_tokens : rim_tokens + tokens].astype(f32) / own_counts[:, None].astype(f32)
    share = jnp.broadcast_to(share.reshape(-1, 1), (slots, LANES))
    windows = slots // WIN_Q
    starts = jnp.arange(windows, dtype=jnp.int32) * WIN_Q + key_offsets + RIM
    pairs_t = atom_pairs.transpose(0, 1, 3, 2).reshape(windows, WIN_Q * features, WIN_K)
    eye = jnp.eye(WIN_Q, dtype=bool)
    spread = jnp.where(
        eye[None, :, :, None], atom_pw.T[:, None, None, :], jnp.zeros((), bf16)
    ).reshape(ATOM_HEADS * WIN_Q, WIN_Q * features)
    gather = WeightGather([part.shape for part in large], samp, seq) if kernels else None
    pooled, stored, fulls = atom_forward(
        ext,
        starts,
        pairs_t,
        spread,
        blocked,
        share,
        wide,
        down,
        atom_qb,
        gather,
        large if kernels else (),
    )
    if not kernels:
        fulls = [lax.all_gather(part, "samp", axis=0, tiled=True) for part in large]
    proj_w, up_w, down_w, cond_w, out_w = fulls
    block_in = token_input.astype(f32) + pooled

    noise_feature = 0.25 * jnp.log(noise_levels / sigma_data)
    cond_rows = (
        single_features.astype(f32)[None]
        + noise_feature[:, None, None] * noise_direction[None, None, :]
    )
    cond_low = norm_stats(cond_rows)[0].astype(bf16)
    cond_all = dot_last(cond_low, cond_w) + cond_b.astype(f32)
    parts = [cond_all[..., i * width : (i + 1) * width] for i in range(6)]

    pair_w = token_pw.T
    bias = pair_bias(pair_features, pair_w)
    normed_in, inv_in = norm_stats(block_in)
    attn_in = (jax.nn.sigmoid(parts[0]) * normed_in + parts[1]).astype(bf16)
    mix = dot_last(attn_in, proj_w)
    queries = (mix[..., :width] + token_qb.astype(f32)).astype(bf16)
    keyval_own = mix[..., width : 3 * width].astype(bf16)
    gating = mix[..., 3 * width :]
    keyval = lax.all_gather(keyval_own, "seq", axis=0, tiled=False)
    attend, probs = token_attention(queries, keyval, bias)
    sig_gate = jax.nn.sigmoid(gating)
    gated_low = (attend * sig_gate).astype(bf16)
    branch = dot_last(gated_low, out_w)
    gate_one = jax.nn.sigmoid(parts[2])
    mid = block_in + gate_one * branch
    normed_mid, inv_mid = norm_stats(mid)
    scale_two = jax.nn.sigmoid(parts[3])
    ffn_in = (scale_two * normed_mid + parts[4]).astype(bf16)
    upper = dot_last(ffn_in, up_w)
    hidden_width = down_w.shape[0]
    first_half, second_half = upper[..., :hidden_width], upper[..., hidden_width:]
    sig_first = jax.nn.sigmoid(first_half)
    hidden = (first_half * sig_first * second_half).astype(bf16)
    branch_two = dot_last(hidden, down_w)
    gate_two = jax.nn.sigmoid(parts[5])
    block_out = (mid + gate_two * branch_two).astype(bf16)

    out_grad = cotangent.astype(f32)
    branch_two_low = (out_grad * gate_two).astype(bf16)
    gate_two_grad = out_grad * branch_two * gate_two * (1.0 - gate_two)
    hidden_grad = dot_back(branch_two_low, down_w)
    first_grad = hidden_grad * second_half * sig_first * (1.0 + first_half * (1.0 - sig_first))
    second_grad = hidden_grad * first_half * sig_first
    upper_grad = jnp.concatenate([first_grad, second_grad], -1).astype(bf16)
    ffn_grad = dot_back(upper_grad, up_w)
    scale_two_grad = ffn_grad * normed_mid * scale_two * (1.0 - scale_two)
    mid_grad = out_grad + norm_back(normed_mid, inv_mid, ffn_grad * scale_two)
    branch_low = (mid_grad * gate_one).astype(bf16)
    gate_one_grad = mid_grad * branch * gate_one * (1.0 - gate_one)
    gated_grad = dot_back(branch_low, out_w)
    attend_low = (gated_grad * sig_gate).astype(bf16)
    gating_grad = gated_grad * attend * sig_gate * (1.0 - sig_gate)
    query_grad, keyval_part, bias_grad = token_attention_back(queries, keyval, probs, attend_low)
    keyval_grad = lax.psum_scatter(keyval_part, "seq", scatter_dimension=0, tiled=False)
    pairw_grad = pair_grad(pair_features, bias_grad, pair_w).T
    mix_grad = jnp.concatenate(
        [query_grad.astype(bf16), keyval_grad, gating_grad.astype(bf16)], -1
    )
    token_qb_grad = jnp.sum(query_grad, (0, 1))
    attn_in_grad = dot_back(mix_grad, proj_w)
    scale_one = jax.nn.sigmoid(parts[0])
    scale_one_grad = attn_in_grad * normed_in * scale_one * (1.0 - scale_one)
    token_grad = mid_grad + norm_back(normed_in, inv_in, attn_in_grad * scale_one)
    cond_grad = jnp.concatenate(
        [scale_one_grad, attn_in_grad, gate_one_grad, scale_two_grad, ffn_grad, gate_two_grad], -1
    ).astype(bf16)
    cond_b_grad = jnp.sum(cond_grad.astype(f32), (0, 1))

    mix_part, own, left, right, atom_mid_grad, *atom_totals = atom_backward(
        token_grad, starts, stored, pairs_t, share, wide, down
    )
    from_right = lax.ppermute(left, "seq", down_pairs)
    from_left = lax.ppermute(right, "seq", up_pairs)
    atom_grad, atom_proj_grad = atom_input_backward(
        atom_input, mix_part, own, from_left, from_right, atom_mid_grad, wide
    )
    qb_grad, outw_grad, upw_grad, downw_grad, pool_grad, pairw_stack, pairw_mean = atom_totals
    diagonal = pairw_stack.reshape(ATOM_HEADS, WIN_Q, WIN_Q, features)
    atom_pw_grad = (
        jnp.sum(jnp.where(eye[None, :, :, None], diagonal, 0.0), (1, 2)).T
        - jnp.sum(pairw_mean.reshape(ATOM_HEADS, -1), 1)[None, :]
    )

    factors = [
        (attn_in, mix_grad),
        (ffn_in, upper_grad),
        (hidden, branch_two_low),
        (cond_low, cond_grad),
        (gated_low, branch_low),
    ]
    rows = atom_width // samp
    tiny_parts = [qb_grad.reshape(-1), atom_pw_grad, cond_b_grad, token_qb_grad, pairw_grad]
    tiny_flat = jnp.concatenate([part.astype(bf16).reshape(samp, -1) for part in tiny_parts], 1)
    spare = width - upw_grad.shape[1] - atom_width
    tiny_flat = jnp.pad(tiny_flat, ((0, 0), (0, rows * spare - tiny_flat.shape[1])))
    lanes = lambda part: part.astype(bf16).reshape(samp, rows, -1)
    downw_two = downw_grad.astype(bf16).reshape(samp, 2, rows, atom_width)
    small = jnp.stack(
        [
            lanes(pool_grad),
            jnp.concatenate([lanes(atom_proj_grad), downw_two[:, 0], downw_two[:, 1]], -1),
            jnp.concatenate(
                [lanes(upw_grad), lanes(outw_grad), tiny_flat.reshape(samp, rows, spare)], -1
            ),
            jnp.zeros((samp, rows, width), bf16),
        ],
        1,
    ).reshape(samp, -1, width)
    if kernels:
        small = small.reshape(samp, seq, 16, width).transpose(1, 0, 2, 3)
        *shares, rest = grad_sums(
            weight_grads(factors, small, samp, seq), [part.shape for part in large]
        )
    else:
        shares, rest = sum_shares(
            [weight_grad(*pair) for pair in factors], small.reshape(-1, width)
        )
    rest = rest.reshape(-1, width)
    pool_out, second, third = rest[:rows], rest[rows : 2 * rows], rest[2 * rows : 3 * rows]
    low = atom_proj_grad.shape[1]
    downw_out = jnp.concatenate(
        [second[:, low : low + atom_width], second[:, low + atom_width :]], 0
    )
    high = upw_grad.shape[1]
    tiny_out = third[:, high + atom_width :].reshape(-1)
    tiny_shares, cut = [], 0
    for part in tiny_parts:
        size = part.size // samp
        shape = (part.shape[0] // samp,) + part.shape[1:]
        tiny_shares.append(tiny_out[cut : cut + size].reshape(shape))
        cut += size
    return (
        block_out,
        atom_grad,
        token_grad,
        second[:, :low],
        tiny_shares[0],
        tiny_shares[1],
        third[:, high : high + atom_width],
        third[:, :high],
        downw_out,
        pool_out,
        shares[3],
        tiny_shares[2],
        shares[0],
        tiny_shares[3],
        tiny_shares[4],
        shares[4],
        shares[1],
        shares[2],
    )


def solution(mesh):
    in_specs = (
        P("samp", "seq", None),
        P("samp", "seq", None),
        P(),
        P("seq"),
        P("seq", None, None, None),
        P("seq", None, None),
        P("seq", None),
        P("samp"),
        P(),
        P("samp", None),
        P("samp"),
        P("samp", None),
        P("samp", None),
        P("samp", None),
        P("samp", None),
        P("samp", None),
        P("samp", None),
        P("samp"),
        P("samp", None),
        P("samp"),
        P("samp", None),
        P("samp", None),
        P("samp", None),
        P("samp", None),
        P("samp", "seq", None),
    )
    out_specs = (
        P("samp", "seq", None),
        P("samp", "seq", None),
        P("samp", "seq", None),
        P("samp", None),
        P("samp"),
        P("samp", None),
        P("samp", None),
        P("samp", None),
        P("samp", None),
        P("samp", None),
        P("samp", None),
        P("samp"),
        P("samp", None),
        P("samp"),
        P("samp", None),
        P("samp", None),
        P("samp", None),
        P("samp", None),
    )
    return jax.shard_map(local, mesh=mesh, in_specs=in_specs, out_specs=out_specs, check_vma=False)
```

```python
import functools

import jax
import jax.numpy as jnp
from jax import lax
from jax.experimental import pallas as pl
from jax.experimental.pallas import tpu as pltpu
from jax.sharding import PartitionSpec as P

MAX_ATOMS = 8
WIN_Q = 32
WIN_K = 128
ATOM_HEADS = 4
RIM = 96
LANES = 128

norm_eps = 1e-05
sigma_data = 16.0
masked_score = -1000000000.0
bf16 = jnp.bfloat16
f32 = jnp.float32
vmem_bytes = 56 << 20


def dot_last(left_op, right_op):
    return jnp.einsum("...k,kn->...n", left_op, right_op, preferred_element_type=f32)


def dot_back(grad_op, weight):
    return jnp.einsum("...n,kn->...k", grad_op, weight, preferred_element_type=f32)


def weight_grad(left_op, grad_op):
    flat_left = left_op.reshape(-1, left_op.shape[-1])
    flat_grad = grad_op.reshape(-1, grad_op.shape[-1])
    return jnp.einsum("rk,rn->kn", flat_left, flat_grad, preferred_element_type=f32)


def mm(left_op, right_op):
    return lax.dot_general(left_op, right_op, (((1,), (0,)), ((), ())), preferred_element_type=f32)


def mm_nt(left_op, right_op):
    return lax.dot_general(left_op, right_op, (((1,), (1,)), ((), ())), preferred_element_type=f32)


def mm_tn(left_op, right_op):
    return lax.dot_general(left_op, right_op, (((0,), (0,)), ((), ())), preferred_element_type=f32)


def norm_stats(operand):
    center = operand - jnp.mean(operand, -1, keepdims=True)
    inv_std = lax.rsqrt(jnp.mean(center * center, -1, keepdims=True) + norm_eps)
    return (center * inv_std, inv_std)


def norm_back(normed, inv_std, grad_op):
    return inv_std * (
        grad_op
        - jnp.mean(grad_op, -1, keepdims=True)
        - normed * jnp.mean(grad_op * normed, -1, keepdims=True)
    )


def sigmoid(operand):
    return 1.0 / (1.0 + jnp.exp(-operand))


def whole(shape):
    return pl.BlockSpec(shape, lambda *_: (0,) * len(shape))


def per_sample(shape):
    return pl.BlockSpec((1,) + shape, lambda b, *_: (b,) + (0,) * len(shape))


def params():
    return pltpu.CompilerParams(vmem_limit_bytes=vmem_bytes)


def square_sums(ones_op, squares):
    upper = squares.astype(bf16)
    lower = (squares - upper.astype(f32)).astype(bf16)
    return upper, lower


def head_stack(rows, heads, head_dim, first):
    lane = lax.broadcasted_iota(jnp.int32, rows.shape, 1)
    parts = []
    for head in range(heads):
        low = first + head * head_dim
        parts.append(jnp.where((lane >= low) & (lane < low + head_dim), rows, jnp.zeros_like(rows)))
    return jnp.concatenate(parts, 0)


def head_fold(stacked, heads, head_dim, first):
    count = stacked.shape[0] // heads
    lane = lax.broadcasted_iota(jnp.int32, (count, stacked.shape[1]), 1)
    total = jnp.zeros((count, stacked.shape[1]), f32)
    for head in range(heads):
        low = first + head * head_dim
        part = stacked[head * count : (head + 1) * count]
        total = jnp.where((lane >= low) & (lane < low + head_dim), part, total)
    return total


MESH = pl.DeviceIdType.MESH


def places():
    samp_pos, seq_pos = lax.axis_index("samp"), lax.axis_index("seq")
    core, across, along = seq_pos % 2, seq_pos // 2 % 2, seq_pos // 4

    def index(along, across, core):
        return (along * 2 + across) * 2 + core

    return (
        samp_pos,
        seq_pos,
        index(along, across, 1 - core),
        index(along, 1 - across, core),
        index(1 - along, across, core),
        index(1 - along, 1 - across, core),
    )


def remote(source, target, send_sem, recv_sem, device):
    return pltpu.make_async_remote_copy(
        src_ref=source,
        dst_ref=target,
        send_sem=send_sem,
        recv_sem=recv_sem,
        device_id=device,
        device_id_type=MESH,
    )


def greet(devices):
    barrier = pltpu.get_barrier_semaphore()
    for device in devices:
        pl.semaphore_signal(barrier, inc=1, device_id=device, device_id_type=MESH)
    pl.semaphore_wait(barrier, len(devices))


def pick(position, values):
    chosen = values[0]
    for index, value in enumerate(values[1:], 1):
        chosen = jnp.where(position == index, value, chosen)
    return chosen


class WeightGather:
    def __init__(self, shapes, samp, seq):
        self.shapes, self.samp, self.seq = shapes, samp, seq
        self.splits = [self.split(shape, seq) for shape in shapes]

    @staticmethod
    def split(shape, parts):
        rows, columns = shape
        for down in (1, 2, 4, 8):
            across = parts // down
            if rows % (16 * down) == 0 and columns % (LANES * across) == 0:
                return (down, across)
        return None

    @staticmethod
    def fits(shapes, samp, seq):
        return (
            samp == 4
            and seq == 8
            and len(shapes) == 5
            and all(WeightGather.split(shape, seq) for shape in shapes)
        )

    def full_shapes(self):
        return [(rows * self.samp, columns) for rows, columns in self.shapes]

    def scratch(self):
        count = len(self.shapes)
        return [
            pltpu.SemaphoreType.DMA((9, self.samp, count)),
            pltpu.SemaphoreType.DMA((8, self.samp, count)),
            pltpu.SemaphoreType.DMA((2, count)),
        ] + [pltpu.VMEM(shape, bf16) for shape in self.shapes]

    def params(self):
        return pltpu.CompilerParams(
            vmem_limit_bytes=vmem_bytes, collective_id=1, has_side_effects=True
        )

    def cell(self, ref, weight, origin, part):
        rows, columns = self.shapes[weight]
        down, across = self.splits[weight]
        height, width = rows // down, columns // across
        low = origin * rows + part // across * height
        left = part % across * width
        return ref.at[
            pl.ds(pl.multiple_of(low, 16), height), pl.ds(pl.multiple_of(left, LANES), width)
        ]

    def origin(self, position, turn):
        order = [sorted(range(self.samp), key=lambda o: (abs(o - z), o)) for z in range(self.samp)]
        if isinstance(turn, int):
            return pick(position, [order[z][turn] for z in range(self.samp)])
        return pick(
            position, [pick(turn, [order[z][t] for t in range(self.samp)]) for z in range(self.samp)]
        )

    def own_copies(self, shards, fulls, own, held, stage):
        z = places()[0]
        copies = []
        for w, shard in enumerate(shards):
            rows = self.shapes[w][0]
            target = fulls[w].at[pl.ds(pl.multiple_of(z * rows, 16), rows), :]
            ends = (shard, held[w]) if stage == 0 else (held[w], target)
            copies.append(pltpu.make_async_copy(*ends, own.at[stage, w]))
        return copies

    def start(self, shards, fulls, send, recv, own, held):
        z, me, sib, xn, yn, dg = places()
        above, below = lax.rem(z + 1, self.samp), lax.rem(z + self.samp - 1, self.samp)
        greet([(z, sib), (z, xn), (z, yn), (above, me), (below, me)])
        for w, shard in enumerate(shards):
            source = self.cell(shard, w, 0, me)
            target = self.cell(fulls[w], w, z, me)

            @pl.when(z < self.samp - 1)
            def _():
                remote(source, target, send.at[0, 0, w], recv.at[0, z, w], (z + 1, me)).start()

            @pl.when(z > 0)
            def _():
                remote(source, target, send.at[1, 0, w], recv.at[0, z, w], (z - 1, me)).start()

        for copy in self.own_copies(shards, fulls, own, held, 0):
            copy.start()

    def place_own(self, shards, fulls, own, held):
        for copy in self.own_copies(shards, fulls, own, held, 0):
            copy.wait()
        for copy in self.own_copies(shards, fulls, own, held, 1):
            copy.start()

    def share_own(self, turn, origin, sources, fulls, send, recv):
        z, me, sib, xn, yn, dg = places()
        for kind, part in ((2, xn), (3, yn), (5, sib)):
            for w, source in enumerate(sources):
                target = self.cell(fulls[w], w, origin, me)
                arrival = {2: 1, 3: 2, 5: 4}[kind]
                remote(
                    source, target, send.at[kind, turn, w], recv.at[arrival, origin, w], (z, part)
                ).start()

    def wait_cell(self, fulls, recv, kind, w, origin, part, device):
        target = self.cell(fulls[w], w, origin, part)
        remote(target, target, recv.at[kind, origin, w], recv.at[kind, origin, w], device).wait_recv()

    def issue(self, turn, fulls, send, recv):
        z, me, sib, xn, yn, dg = places()
        origin = self.origin(z, turn)
        count = len(self.shapes)
        for w in range(count):
            self.wait_cell(fulls, recv, 0, w, origin, me, (z, sib))
        for w in range(count):
            cell = self.cell(fulls[w], w, origin, me)

            @pl.when((origin < z) & (z < self.samp - 1))
            def _():
                remote(cell, cell, send.at[0, turn, w], recv.at[0, origin, w], (z + 1, me)).start()

            @pl.when((origin > z) & (z > 0))
            def _():
                remote(cell, cell, send.at[1, turn, w], recv.at[0, origin, w], (z - 1, me)).start()

        cells = [self.cell(fulls[w], w, origin, me) for w in range(count)]
        self.share_own(turn, origin, cells, fulls, send, recv)

    def passed_on(self, w):
        return w in (0, 3)

    def finish(self, turn, fulls, send, recv):
        z, me, sib, xn, yn, dg = places()
        origin = self.origin(z, turn)
        count = len(self.shapes)
        for kind, part, other, by in ((1, xn, yn, True), (2, yn, xn, False)):
            for w in range(count):
                self.wait_cell(fulls, recv, kind, w, origin, part, (z, part))
                cell = self.cell(fulls[w], w, origin, part)
                if self.passed_on(w) == by:
                    remote(
                        cell, cell, send.at[4, turn, w], recv.at[3, origin, w], (z, other)
                    ).start()
                remote(
                    cell, cell, send.at[5 + kind, turn, w], recv.at[4 + kind, origin, w], (z, sib)
                ).start()

    def diagonal(self, turn, fulls, send, recv):
        z, me, sib, xn, yn, dg = places()
        origin = self.origin(z, turn)
        for w in range(len(self.shapes)):
            self.wait_cell(fulls, recv, 3, w, origin, dg, (z, yn))
            cell = self.cell(fulls[w], w, origin, dg)
            remote(cell, cell, send.at[8, turn, w], recv.at[7, origin, w], (z, sib)).start()

    def drain(self, shards, fulls, send, recv, own, held):
        z, me, sib, xn, yn, dg = places()
        count = len(self.shapes)

        def sent(kind, turn, w):
            cell = self.cell(fulls[w], w, 0, me)
            remote(cell, cell, send.at[kind, turn, w], recv.at[0, 0, w], (z, sib)).wait_send()

        def one(turn, carry):
            origin = self.origin(z, turn)
            for w in range(count):
                for kind in range(2, 9):
                    sent(kind, turn, w)

                @pl.when((z < self.samp - 1) & (origin < z))
                def _():
                    sent(0, turn, w)

                @pl.when((z > 0) & (origin > z))
                def _():
                    sent(1, turn, w)

                for kind in range(4, 8):
                    self.wait_cell(fulls, recv, kind, w, origin, sib, (z, sib))
            return carry

        lax.fori_loop(1, self.samp, one, 0)
        for w in range(count):

            @pl.when(z < self.samp - 1)
            def _():
                sent(0, 0, w)

            @pl.when(z > 0)
            def _():
                sent(1, 0, w)

        for copy in self.own_copies(shards, fulls, own, held, 1):
            copy.wait()

    def step(self, sample, shards, fulls, send, recv, own, *held):
        @pl.when(sample == 0)
        def _():
            self.start(shards, fulls, send, recv, own, held)

        @pl.when(sample == 1)
        def _():
            self.place_own(shards, fulls, own, held)

        for at, turn in ((2, 1), (3, 2), (5, 3)):

            @pl.when(sample == at)
            def _():
                self.issue(turn, fulls, send, recv)

        for at, turn in ((4, 1), (5, 2), (7, 3)):

            @pl.when(sample == at)
            def _():
                self.finish(turn, fulls, send, recv)

        for at, turn in ((5, 1), (7, 2)):

            @pl.when(sample == at)
            def _():
                self.diagonal(turn, fulls, send, recv)

    def last(self, sample, shards, fulls, send, recv, own, *held):
        @pl.when(sample == pl.num_programs(0) - 1)
        def _():
            self.diagonal(3, fulls, send, recv)
            self.drain(shards, fulls, send, recv, own, held)


def edge_kernel(samp, seq, wide_ref, tiny_ref, rows_ref, wide_out, tiny_out, ext_out, send, recv):
    z, me = lax.axis_index("samp"), lax.axis_index("seq")
    samples, slots, width = rows_ref.shape
    right, left = lax.rem(me + 1, seq), lax.rem(me + seq - 1, seq)
    others = [(lax.rem(z + hop, samp), me) for hop in range(1, samp)]
    greet(others + [(z, right), (z, left)])
    copies = []
    for hop, device in enumerate(others):
        for kind, (ref, out) in enumerate(((wide_ref, wide_out), (tiny_ref, tiny_out))):
            rows = ref.shape[0]
            target = out.at[pl.ds(pl.multiple_of(z * rows, 16), rows), :]
            copy = remote(ref, target, send.at[kind, hop], recv.at[kind, hop], device)
            copy.start()
            copies.append(copy)
    before, after = ext_out.at[:, :RIM, :], ext_out.at[:, RIM + slots :, :]
    to_right = remote(rows_ref.at[:, slots - RIM :, :], before, send.at[2, 0], recv.at[2, 0], (z, right))
    to_left = remote(rows_ref.at[:, :RIM, :], after, send.at[2, 1], recv.at[2, 1], (z, left))
    first, last = me == 0, me == seq - 1

    @pl.when(~last)
    def _():
        to_right.start()

    @pl.when(~first)
    def _():
        to_left.start()

    @pl.when(first)
    def _():
        ext_out[:, :RIM, :] = jnp.zeros((samples, RIM, width), bf16)

    @pl.when(last)
    def _():
        ext_out[:, RIM + slots :, :] = jnp.zeros((samples, RIM, width), bf16)

    def move(sample, carry):
        ext_out[sample, RIM : RIM + slots, :] = rows_ref[sample]
        return carry

    lax.fori_loop(0, samples, move, 0)
    for ref, out in ((wide_ref, wide_out), (tiny_ref, tiny_out)):
        rows = ref.shape[0]
        out[pl.ds(pl.multiple_of(z * rows, 16), rows), :] = ref[...]
    for copy in copies:
        copy.wait()

    @pl.when(~last)
    def _():
        to_right.wait_send()
        to_left.wait_recv()

    @pl.when(~first)
    def _():
        to_left.wait_send()
        to_right.wait_recv()


def edges(wide_own, tiny_own, rows):
    samp, seq = lax.axis_size("samp"), lax.axis_size("seq")
    samples, slots, width = rows.shape
    place = pl.BlockSpec(memory_space=pltpu.VMEM)
    return pl.pallas_call(
        functools.partial(edge_kernel, samp, seq),
        out_shape=[
            jax.ShapeDtypeStruct((samp * wide_own.shape[0], wide_own.shape[1]), bf16),
            jax.ShapeDtypeStruct((samp * tiny_own.shape[0], tiny_own.shape[1]), bf16),
            jax.ShapeDtypeStruct((samples, slots + 2 * RIM, width), bf16),
        ],
        in_specs=[place] * 3,
        out_specs=[place] * 3,
        scratch_shapes=[
            pltpu.SemaphoreType.DMA((3, samp)),
            pltpu.SemaphoreType.DMA((3, samp)),
        ],
        compiler_params=pltpu.CompilerParams(
            vmem_limit_bytes=vmem_bytes, collective_id=0, has_side_effects=True
        ),
        name="edges",
    )(wide_own, tiny_own, rows)


UNIT = 336


def weight_grad_kernel(
    attn_ref,
    mix_ref,
    ffn_ref,
    upper_ref,
    hidden_ref,
    two_ref,
    cond_ref,
    condgrad_ref,
    gated_ref,
    branch_ref,
    out_ref,
    down_s,
    cond_s,
    outw_s,
):
    part = pl.program_id(0)
    samp = out_ref.shape[1]

    @pl.when(part == 0)
    def _():
        down_s[...] = mm_tn(hidden_ref[...], two_ref[...]).astype(bf16)
        outw_s[...] = mm_tn(gated_ref[...], branch_ref[...]).astype(bf16)
        for low in range(0, cond_s.shape[1], 768):
            cond_s[:, low : low + 768] = mm_tn(
                cond_ref[...], condgrad_ref[:, low : low + 768]
            ).astype(bf16)

    proj = mm_tn(attn_ref[...], mix_ref[...]).astype(bf16)
    upw = mm_tn(ffn_ref[...], upper_ref[...]).astype(bf16)
    rows = proj.shape[0] // samp
    for z in range(samp):
        out_ref[0, z, :rows, :384] = proj[z * rows : (z + 1) * rows]
        out_ref[0, z, :rows, 384:] = upw[z * rows : (z + 1) * rows]
        out_ref[0, z, 192:240, :] = down_s[pl.ds(pl.multiple_of(z * 384 + part * 48, 16), 48), :]
        low = pl.multiple_of(z * 96 + part // 4 * 48, 16)
        left = pl.multiple_of(part % 4 * 1152, LANES)
        out_ref[0, z, 240:288, :] = cond_s[pl.ds(low, 48), pl.ds(left, 768)]
        left = pl.multiple_of(part % 4 * 1152 + 768, LANES)
        out_ref[0, z, 288:336, :384] = cond_s[pl.ds(low, 48), pl.ds(left, 384)]
        low = pl.multiple_of(z * 192 + part // 2 * 48, 16)
        left = pl.multiple_of(part % 2 * 384, LANES)
        out_ref[0, z, 288:336, 384:] = outw_s[pl.ds(low, 48), pl.ds(left, 384)]


def weight_grads(pairs, samp, seq):
    flat = [array.reshape(-1, array.shape[-1]) for pair in pairs for array in pair]
    rows = flat[0].shape[0]
    columns = pl.BlockSpec((rows, 384), lambda s: (0, s))
    specs = [whole(array.shape) for array in flat]
    specs[1] = columns
    specs[3] = columns
    return pl.pallas_call(
        weight_grad_kernel,
        out_shape=jax.ShapeDtypeStruct((seq, samp, UNIT, 768), bf16),
        grid=(seq,),
        in_specs=specs,
        out_specs=pl.BlockSpec((1, samp, UNIT, 768), lambda s: (s, 0, 0, 0)),
        scratch_shapes=[
            pltpu.VMEM((1536, 768), bf16),
            pltpu.VMEM((384, 4608), bf16),
            pltpu.VMEM((768, 768), bf16),
        ],
        compiler_params=params(),
        name="weight_grads",
    )(*flat)


def add_into(target, source, lanes=slice(None), rows=48):
    def one(step, carry):
        part = pl.ds(pl.multiple_of(step * rows, 16), rows)
        both = target[part, lanes].astype(f32) + source[part, :].astype(f32)
        target[part, lanes] = both.astype(bf16)
        return carry

    lax.fori_loop(0, target.shape[0] // rows, one, 0)


class GradSum:
    head, tail, full = slice(0, 384), slice(384, 768), slice(0, 768)

    def __init__(self, shapes):
        self.shapes = list(shapes)

    def scratch(self):
        half = (UNIT, 384)
        dma = pltpu.SemaphoreType.DMA
        return [
            pltpu.VMEM((4, 4, UNIT, 768), bf16),
            pltpu.VMEM((4, 4, UNIT, 768), bf16),
            pltpu.VMEM((4, 2) + half, bf16),
            pltpu.VMEM((4, 2) + half, bf16),
            pltpu.VMEM((4,) + half, bf16),
            pltpu.VMEM((4,) + half, bf16),
            pltpu.VMEM((3, UNIT, 768), bf16),
            pltpu.VMEM((8, UNIT, 768), bf16),
            pltpu.VMEM((2, UNIT, 768), f32),
            dma((4, 4)),
            dma((4, 4)),
            dma((4, 4)),
            dma((4, 4)),
            dma((4, 4)),
            dma((4, 2)),
            dma((4, 2)),
            dma((3,)),
            dma((3,)),
            dma((8,)),
            dma((8,)),
            dma((2, 6)),
        ]

    def params(self):
        return pltpu.CompilerParams(
            vmem_limit_bytes=vmem_bytes, collective_id=2, has_side_effects=True
        )

    def bind(self, grads, totals, mine, theirs, from_x, from_y, last_x, last_y, planes, shares, stage, *sems):
        self.grads, self.totals = grads, totals
        self.mine, self.theirs, self.from_x, self.from_y = mine, theirs, from_x, from_y
        self.last_x, self.last_y, self.planes, self.shares = last_x, last_y, planes, shares
        self.stage = stage
        (
            self.s_sib,
            self.r_sib,
            self.s_own,
            self.s_one,
            self.r_one,
            self.s_two,
            self.r_two,
            self.s_z,
            self.r_z,
            self.s_share,
            self.r_share,
            self.s_out,
        ) = sems
        self.z, self.me, self.sib, self.xn, self.yn, self.dg = places()
        self.core, self.chip = self.me % 2, self.me // 2
        self.chip_x, self.chip_y, self.chip_d = self.xn // 2, self.yn // 2, self.dg // 2
        order = [[p ^ hop for hop in (2, 3, 1, 0)] for p in range(4)]
        self.plane = [pick(self.z, [order[p][r] for p in range(4)]) for r in range(4)]

    def there(self, r, j):
        return remote(
            self.grads.at[2 * j + 1 - self.core, self.plane[r]],
            self.theirs.at[r, j],
            self.s_sib.at[r, j],
            self.r_sib.at[r, j],
            (self.z, self.sib),
        )

    def here(self, r, j):
        return pltpu.make_async_copy(
            self.grads.at[2 * j + self.core, self.plane[r]], self.mine.at[r, j], self.s_own.at[r, j]
        )

    def one(self, r, k):
        chip = (self.chip_x, self.chip_d, self.chip_y, self.chip_d)[k]
        lanes = self.head if k < 2 else self.tail
        target = (self.from_x if k < 2 else self.from_y).at[r, k % 2]
        device = (self.z, self.xn if k < 2 else self.yn)
        return remote(
            self.mine.at[r, chip, :, lanes], target, self.s_one.at[r, k], self.r_one.at[r, k], device
        )

    def two(self, r, k):
        chip, lanes, target, device = (
            (self.chip_y, self.head, self.last_y, self.yn),
            (self.chip_x, self.tail, self.last_x, self.xn),
        )[k]
        return remote(
            self.mine.at[r, chip, :, lanes],
            target.at[r],
            self.s_two.at[r, k],
            self.r_two.at[r, k],
            (self.z, device),
        )

    def across(self, r):
        return remote(
            self.mine.at[r, self.chip],
            self.planes.at[r],
            self.s_z.at[r],
            self.r_z.at[r],
            (self.plane[r], self.me),
        )

    def share(self, part, lanes, kind, device):
        ref = self.shares.at[part, :, lanes]
        return remote(ref, ref, self.s_share.at[kind], self.r_share.at[kind], (self.z, device))

    def begin(self, r):
        for j in range(4):
            self.there(r, j).start()
            self.here(r, j).start()

    def pairs(self, r):
        for j in range(4):
            self.there(r, j).wait_recv()
            self.here(r, j).wait()
        for j in range(4):
            add_into(self.mine.at[r, j], self.theirs.at[r, j])
        for k in range(4):
            self.one(r, k).start()

    def middle(self, r):
        self.one(r, 1).wait_recv()
        add_into(self.mine.at[r, self.chip_y], self.from_x.at[r, 1], self.head)
        self.two(r, 0).start()
        self.one(r, 3).wait_recv()
        add_into(self.mine.at[r, self.chip_x], self.from_y.at[r, 1], self.tail)
        self.two(r, 1).start()
        self.one(r, 0).wait_recv()
        add_into(self.mine.at[r, self.chip], self.from_x.at[r, 0], self.head)
        self.one(r, 2).wait_recv()
        add_into(self.mine.at[r, self.chip], self.from_y.at[r, 0], self.tail)

    def finish(self, r):
        self.two(r, 0).wait_recv()
        add_into(self.mine.at[r, self.chip], self.last_y.at[r], self.head)
        self.two(r, 1).wait_recv()
        add_into(self.mine.at[r, self.chip], self.last_x.at[r], self.tail)
        if r < 3:
            self.across(r).start()

    def total(self):
        for r in range(3):
            self.across(r).wait_recv()

        def one(step, carry):
            rows = pl.ds(pl.multiple_of(step * 48, 16), 48)
            both = self.mine[3, self.chip, rows, :].astype(f32)
            for r in range(3):
                both += self.planes[r, rows, :].astype(f32)
            self.shares[self.me, rows, :] = both.astype(bf16)
            return carry

        lax.fori_loop(0, UNIT // 48, one, 0)
        self.share(self.me, self.full, 0, self.xn).start()
        self.share(self.me, self.full, 1, self.yn).start()
        self.share(self.me, self.full, 4, self.sib).start()

    def pieces(self, part):
        proj, upw, down, cond, outw = self.totals
        stage = self.stage.at[part % 2]
        low, left = part // 4 * 48, part % 4 * 1152
        high, right = part // 2 * 48, part % 2 * 384
        return (
            (stage.at[:192, self.head], proj.at[:, part * 384 : (part + 1) * 384]),
            (stage.at[:192, self.tail], upw.at[:, part * 384 : (part + 1) * 384]),
            (stage.at[192:240, :], down.at[part * 48 : (part + 1) * 48, :]),
            (stage.at[240:288, :], cond.at[low : low + 48, left : left + 768]),
            (stage.at[288:336, self.head], cond.at[low : low + 48, left + 768 : left + 1152]),
            (stage.at[288:336, self.tail], outw.at[high : high + 48, right : right + 384]),
        )

    def write(self, part):
        return [
            pltpu.make_async_copy(source, target, self.s_out.at[part % 2, k])
            for k, (source, target) in enumerate(self.pieces(part))
        ]

    def collect(self):
        me, sib, xn, yn, dg = self.me, self.sib, self.xn, self.yn, self.dg
        self.share(xn, self.full, 0, xn).wait_recv()
        self.share(xn, self.head, 2, yn).start()
        self.share(xn, self.full, 5, sib).start()
        self.share(yn, self.full, 1, yn).wait_recv()
        self.share(yn, self.tail, 3, xn).start()
        self.share(yn, self.full, 6, sib).start()
        self.share(dg, self.head, 2, yn).wait_recv()
        self.share(dg, self.tail, 3, xn).wait_recv()
        self.share(dg, self.full, 7, sib).start()
        for kind in range(4, 8):
            self.share(sib, self.full, kind, sib).wait_recv()
        for part in range(8):
            if part >= 2:
                for copy in self.write(part - 2):
                    copy.wait()

            def one(step, carry):
                rows = pl.ds(pl.multiple_of(step * 48, 16), 48)
                self.stage[part % 2, rows, :] = self.shares[part, rows, :].astype(f32)
                return carry

            lax.fori_loop(0, UNIT // 48, one, 0)
            for copy in self.write(part):
                copy.start()
        for part in (6, 7):
            for copy in self.write(part):
                copy.wait()
        for kind, part, lanes, device in (
            (0, me, self.full, xn),
            (1, me, self.full, yn),
            (2, xn, self.head, yn),
            (3, yn, self.tail, xn),
            (4, me, self.full, sib),
            (5, xn, self.full, sib),
            (6, yn, self.full, sib),
            (7, dg, self.full, sib),
        ):
            self.share(part, lanes, kind, device).wait_send()
        for r in range(4):
            for j in range(4):
                self.there(r, j).wait_send()
                self.one(r, j).wait_send()
            for k in range(2):
                self.two(r, k).wait_send()
            if r < 3:
                self.across(r).wait_send()

    def hello(self):
        greet(
            [(self.z, self.sib), (self.z, self.xn), (self.z, self.yn)]
            + [(self.plane[r], self.me) for r in range(3)]
        )
        self.begin(0)
        self.begin(1)

    def slot(self, index, grads, totals, *refs):
        self.bind(grads, totals, *refs)
        plan = {
            0: [self.hello],
            1: [lambda: self.pairs(0), lambda: self.begin(2)],
            2: [lambda: self.pairs(1), lambda: self.begin(3)],
            4: [lambda: self.middle(0)],
            5: [lambda: self.pairs(2)],
            6: [lambda: self.middle(1)],
            7: [lambda: self.finish(0)],
            8: [lambda: self.pairs(3)],
            9: [lambda: self.middle(2), lambda: self.finish(1)],
            11: [lambda: self.finish(2)],
            13: [lambda: self.middle(3)],
            15: [lambda: self.finish(3), self.total],
        }
        for at, actions in plan.items():

            @pl.when(index == at)
            def _():
                for action in actions:
                    action()

    def last(self, grads, totals, *refs):
        self.bind(grads, totals, *refs)
        self.collect()


def small_sum_kernel(
    grads, out_ref, cores, chips, planes, share, total, s_one, r_one, s_two, r_two, s_z, r_z, s_all, r_all
):
    z, me, sib, xn, yn, dg = places()
    core, chip = me % 2, me // 2
    near = (xn, yn, dg)
    others = [lax.rem(z + hop, 4) for hop in (1, 2, 3)]
    greet(
        [(z, sib)]
        + [(z, part) for part in near]
        + [(z, part + 1 - 2 * core) for part in near]
        + [(other, me) for other in others]
    )

    def one(j):
        return remote(
            grads.at[2 * j + 1 - core], cores.at[j], s_one.at[j], r_one.at[j], (z, sib)
        )

    for j in range(4):
        one(j).start()
    for j in range(4):
        one(j).wait()
        both = cores[j].astype(f32) + grads[2 * j + core].astype(f32)
        cores[j] = both.astype(bf16)

    def two(k):
        return remote(cores.at[near[k] // 2], chips.at[k], s_two.at[k], r_two.at[k], (z, near[k]))

    for k in range(3):
        two(k).start()
    both = cores[chip].astype(f32)
    for k in range(3):
        two(k).wait()
        both += chips[k].astype(f32)
    share[...] = both.astype(bf16)

    def three(k):
        return remote(share.at[others[k]], planes.at[k], s_z.at[k], r_z.at[k], (others[k], me))

    for k in range(3):
        three(k).start()
    both = share[z].astype(f32)
    for k in range(3):
        three(k).wait()
        both += planes[k].astype(f32)
    total[me] = both.astype(bf16)

    receivers = [sib] + list(near) + [part + 1 - 2 * core for part in near]

    def four(k, part, device):
        return remote(total.at[part], total.at[part], s_all.at[k], r_all.at[k], (z, device))

    for k, device in enumerate(receivers):
        four(k, me, device).start()
    for k, device in enumerate(receivers):
        four(k, device, device).wait_recv()
    for k, device in enumerate(receivers):
        four(k, me, device).wait_send()
    out_ref[...] = total[...].astype(f32)


def small_sums(grads):
    seq, samp, rows, width = grads.shape
    dma = pltpu.SemaphoreType.DMA
    return pl.pallas_call(
        small_sum_kernel,
        out_shape=jax.ShapeDtypeStruct((seq, rows, width), f32),
        in_specs=[pl.BlockSpec(memory_space=pltpu.VMEM)],
        out_specs=pl.BlockSpec(memory_space=pltpu.VMEM),
        scratch_shapes=[
            pltpu.VMEM((4, samp, rows, width), bf16),
            pltpu.VMEM((3, samp, rows, width), bf16),
            pltpu.VMEM((3, rows, width), bf16),
            pltpu.VMEM((samp, rows, width), bf16),
            pltpu.VMEM((seq, rows, width), bf16),
            dma((4,)),
            dma((4,)),
            dma((3,)),
            dma((3,)),
            dma((3,)),
            dma((3,)),
            dma((7,)),
            dma((7,)),
        ],
        compiler_params=pltpu.CompilerParams(
            vmem_limit_bytes=vmem_bytes, collective_id=3, has_side_effects=True
        ),
        name="small_sums",
    )(grads)


def pair_stats(pairs, fold):
    upper, lower = square_sums(fold, pairs.astype(f32) * pairs.astype(f32))
    features = pairs.shape[0] // WIN_Q
    mean = mm(fold, pairs) * (1.0 / features)
    square = (mm(fold, upper) + mm(fold, lower)) * (1.0 / features)
    var = jnp.maximum(square - mean * mean, 0.0)
    inv_std = lax.rsqrt(var + norm_eps)
    return mean, inv_std


def pair_fold(features):
    shape = (WIN_Q, WIN_Q * features)
    row = lax.broadcasted_iota(jnp.int32, shape, 0)
    column = lax.broadcasted_iota(jnp.int32, shape, 1)
    return jnp.where(column // features == row, 1.0, 0.0).astype(bf16)


def atom_fwd_kernel(
    gather,
    starts,
    ext_ref,
    pairs_ref,
    spread_ref,
    blocked_ref,
    share_ref,
    wide_ref,
    down_ref,
    qbias_ref,
    *refs,
):
    count = len(gather.shapes) if gather is not None else 0
    shards, refs = refs[:count], refs[count:]
    (
        pooled_ref,
        query_ref,
        keyval_ref,
        gate_ref,
        probs_ref,
        attend_ref,
        mid_ref,
    ), refs = refs[:7], refs[7:]
    fulls, refs = refs[:count], refs[count:]
    (bias_s, keys_s, values_s), sems = refs[:3], refs[3:]
    width = ext_ref.shape[-1]
    head_dim = width // ATOM_HEADS
    scale = float(head_dim) ** (-0.5)
    slots = query_ref.shape[1]
    windows = slots // WIN_Q
    hidden_width = down_ref.shape[0]
    model_width = pooled_ref.shape[-1]
    features = pairs_ref.shape[1] // WIN_Q
    sample = pl.program_id(0)
    if gather is not None:
        gather.step(sample, shards, fulls, *sems)

    @pl.when(sample == 0)
    def _():
        fold = pair_fold(features)
        spread = spread_ref[...]
        spread_sum = jnp.sum(spread.astype(f32), -1, keepdims=True)
        first_lane = jnp.where(
            lax.broadcasted_iota(jnp.int32, (ATOM_HEADS * WIN_Q, LANES), 1) == 0, 1.0, 0.0
        ).astype(bf16)

        def one(win, carry):
            pairs = pairs_ref[win]
            mean, inv_std = pair_stats(pairs, fold)
            mean = jnp.concatenate([mean] * ATOM_HEADS, 0)
            inv_std = jnp.concatenate([inv_std] * ATOM_HEADS, 0)
            blocked = blocked_ref[pl.ds(starts[win], WIN_K), :].astype(bf16)
            bias = inv_std * (mm(spread, pairs) - mean * spread_sum)
            bias_s[win] = bias + mm_nt(first_lane, blocked)
            return carry

        lax.fori_loop(0, windows, one, 0)

    rows = ext_ref[0].astype(f32)
    normed_low = norm_stats(rows)[0].astype(bf16)
    key_val = mm(normed_low, wide_ref[:, width : 3 * width]).astype(bf16)
    keyval_ref[0] = key_val
    keys_s[...] = key_val[:, :width].astype(f32)
    values_s[...] = key_val[:, width:].astype(f32)
    own_low = normed_low[RIM : RIM + slots]
    query_ref[0] = (mm(own_low, wide_ref[:, :width]) + qbias_ref[...]).astype(bf16)
    gate_ref[0] = mm(own_low, wide_ref[:, 3 * width : 4 * width])

    def one_window(win):
        first = pl.multiple_of(win * WIN_Q, WIN_Q)
        keys = keys_s[pl.ds(starts[win], WIN_K), :].astype(bf16)
        values = values_s[pl.ds(starts[win], WIN_K), :].astype(bf16)
        stacked = head_stack(query_ref[0, pl.ds(first, WIN_Q), :], ATOM_HEADS, head_dim, 0)
        scores = mm_nt(stacked, keys) * scale + bias_s[win]
        exp_scores = jnp.exp(scores - jnp.max(scores, -1, keepdims=True))
        probs = exp_scores * (1.0 / jnp.sum(exp_scores, -1, keepdims=True))
        probs_low = probs.astype(bf16)
        probs_ref[0, win] = probs_low
        attend = head_fold(mm(probs_low, values), ATOM_HEADS, head_dim, 0)
        attend_ref[0, pl.ds(first, WIN_Q), :] = attend

    def some_windows(step, carry):
        for part in range(4):
            one_window(step * 4 + part)
        return carry

    lax.fori_loop(0, windows // 4, some_windows, 0)

    gated_low = (attend_ref[0] * sigmoid(gate_ref[0])).astype(bf16)
    offset = 4 * width
    upw = wide_ref[:, offset : offset + 2 * hidden_width]
    offset += 2 * hidden_width
    pool_weight = wide_ref[:, offset : offset + model_width]
    outw = wide_ref[:, offset + model_width : offset + model_width + width]
    mid = rows[RIM : RIM + slots] + mm(gated_low, outw)
    mid_ref[0] = mid
    ffn_low = norm_stats(mid)[0].astype(bf16)
    upper = mm(ffn_low, upw)
    first_half, second_half = upper[:, :hidden_width], upper[:, hidden_width:]
    hidden = (first_half * sigmoid(first_half) * second_half).astype(bf16)
    final_low = (mid + mm(hidden, down_ref[...])).astype(bf16)
    pool_pre = mm(final_low, pool_weight)
    share = share_ref[...]
    for lane in range(0, model_width, LANES):
        part = pool_pre[:, lane : lane + LANES]
        part = part * sigmoid(part) * share
        pooled_ref[0, :, lane : lane + LANES] = jnp.sum(
            part.reshape(slots // MAX_ATOMS, MAX_ATOMS, LANES), 1
        )
    if gather is not None:
        gather.last(sample, shards, fulls, *sems)


def atom_forward(ext, starts, pairs, spread, blocked, share, wide, down, qbias, gather, shards):
    samples, ext_slots, width = ext.shape
    slots = ext_slots - 2 * RIM
    tokens = slots // MAX_ATOMS
    windows = slots // WIN_Q
    model_width = wide.shape[1] - 5 * width - 2 * down.shape[0]
    stack = ATOM_HEADS * WIN_Q
    outs = (
        ((tokens, model_width), f32),
        ((slots, width), bf16),
        ((ext_slots, 2 * width), bf16),
        ((slots, width), f32),
        ((windows, stack, WIN_K), bf16),
        ((slots, width), f32),
        ((slots, width), f32),
    )
    place = pl.BlockSpec(memory_space=pl.ANY)
    results = pl.pallas_call(
        functools.partial(atom_fwd_kernel, gather),
        out_shape=[jax.ShapeDtypeStruct((samples,) + shape, kind) for shape, kind in outs]
        + [jax.ShapeDtypeStruct(shape, bf16) for shape in (gather.full_shapes() if gather else [])],
        grid=(samples,),
        in_specs=[
            pl.BlockSpec(memory_space=pltpu.SMEM),
            per_sample((ext_slots, width)),
            whole(pairs.shape),
            whole(spread.shape),
            whole(blocked.shape),
            whole(share.shape),
            whole(wide.shape),
            whole(down.shape),
            whole(qbias.shape),
        ]
        + [place] * len(shards),
        out_specs=[per_sample(shape) for shape, _ in outs] + [place] * len(shards),
        scratch_shapes=[
            pltpu.VMEM((windows, stack, WIN_K), f32),
            pltpu.VMEM((ext_slots, width), f32),
            pltpu.VMEM((ext_slots, width), f32),
        ]
        + (gather.scratch() if gather else []),
        compiler_params=gather.params() if gather else params(),
        name="atom_forward",
    )(starts, ext, pairs, spread, blocked, share, wide, down, qbias, *shards)
    return results[0], results[1:7], results[7:]


def atom_bwd_kernel(
    summing,
    starts,
    grad_ref,
    query_ref,
    keyval_ref,
    gate_ref,
    probs_ref,
    attend_ref,
    mid_ref,
    pairs_ref,
    share_ref,
    wide_ref,
    down_ref,
    *refs,
):
    count = len(summing.shapes) if summing is not None else 0
    grads, refs = refs[: min(count, 1)], refs[min(count, 1) :]
    (
        mix_ref,
        own_ref,
        left_ref,
        right_ref,
        midgrad_ref,
        qbias_ref,
        outw_ref,
        upw_ref,
        downw_ref,
        pool_ref,
        pairw_ref,
        pairm_ref,
    ), refs = refs[:12], refs[12:]
    totals, refs = refs[:count], refs[count:]
    (keys_s, values_s, acck_s, accv_s, bias_s, attlow_s, dq_s), sums = refs[:7], refs[7:]
    width = query_ref.shape[-1]
    head_dim = width // ATOM_HEADS
    scale = float(head_dim) ** (-0.5)
    slots = query_ref.shape[1]
    windows = slots // WIN_Q
    hidden_width = down_ref.shape[0]
    model_width = grad_ref.shape[-1]
    tokens = grad_ref.shape[1]
    sample = pl.program_id(0)
    if summing is not None:
        summing.slot(2 * sample, *grads, totals, *sums)

    @pl.when(sample == 0)
    def _():
        for ref in (qbias_ref, outw_ref, upw_ref, downw_ref, pool_ref, pairw_ref, pairm_ref, bias_s):
            ref[...] = jnp.zeros_like(ref)

    offset = 4 * width
    upw = wide_ref[:, offset : offset + 2 * hidden_width]
    offset += 2 * hidden_width
    pool_weight = wide_ref[:, offset : offset + model_width]
    outw = wide_ref[:, offset + model_width : offset + model_width + width]
    down = down_ref[...]

    mid = mid_ref[0]
    normed_mid, inv_mid = norm_stats(mid)
    ffn_low = normed_mid.astype(bf16)
    upper = mm(ffn_low, upw)
    first_half, second_half = upper[:, :hidden_width], upper[:, hidden_width:]
    sig_first = sigmoid(first_half)
    hidden = (first_half * sig_first * second_half).astype(bf16)
    final_low = (mid + mm(hidden, down)).astype(bf16)
    pool_pre = mm(final_low, pool_weight)
    share = share_ref[...]
    pool_parts = []
    for lane in range(0, model_width, LANES):
        part = pool_pre[:, lane : lane + LANES]
        grad = jnp.broadcast_to(
            grad_ref[0, :, lane : lane + LANES][:, None, :], (tokens, MAX_ATOMS, LANES)
        ).reshape(slots, LANES)
        sig_pool = sigmoid(part)
        pool_parts.append((grad * share * sig_pool * (1.0 + part * (1.0 - sig_pool))).astype(bf16))
    pool_grad = jnp.concatenate(pool_parts, 1)
    final_grad = mm_nt(pool_grad, pool_weight)
    pool_ref[...] += mm_tn(final_low, pool_grad)
    branch_low = final_grad.astype(bf16)
    hidden_grad = mm_nt(branch_low, down)
    first_grad = hidden_grad * second_half * sig_first * (1.0 + first_half * (1.0 - sig_first))
    second_grad = hidden_grad * first_half * sig_first
    upper_grad = jnp.concatenate([first_grad.astype(bf16), second_grad.astype(bf16)], 1)
    downw_ref[...] += mm_tn(hidden, branch_low)
    upw_ref[...] += mm_tn(ffn_low, upper_grad)
    mid_grad = final_grad + norm_back(normed_mid, inv_mid, mm_nt(upper_grad, upw))
    midgrad_ref[0] = mid_grad
    out_low = mid_grad.astype(bf16)
    gated_grad = mm_nt(out_low, outw)
    sig_gate = sigmoid(gate_ref[0])
    attend = attend_ref[0]
    gated_low = (attend * sig_gate).astype(bf16)
    outw_ref[...] += mm_tn(gated_low, out_low)
    attlow_s[...] = (gated_grad * sig_gate).astype(bf16)
    mix_ref[0, :, width:] = (gated_grad * attend * sig_gate * (1.0 - sig_gate)).astype(bf16)

    keys_s[...] = keyval_ref[0, :, :width].astype(f32)
    values_s[...] = keyval_ref[0, :, width:].astype(f32)
    acck_s[...] = jnp.zeros_like(acck_s)
    accv_s[...] = jnp.zeros_like(accv_s)
    if summing is not None:
        summing.slot(2 * sample + 1, *grads, totals, *sums)

    def one_window(win):
        first = pl.multiple_of(win * WIN_Q, WIN_Q)
        start = starts[win]
        keys = keys_s[pl.ds(start, WIN_K), :].astype(bf16)
        values = values_s[pl.ds(start, WIN_K), :].astype(bf16)
        queries = head_stack(query_ref[0, pl.ds(first, WIN_Q), :], ATOM_HEADS, head_dim, 0)
        att = head_stack(attlow_s[pl.ds(first, WIN_Q), :], ATOM_HEADS, head_dim, 0)
        probs_low = probs_ref[0, win]
        probs = probs_low.astype(f32)
        prob_grad = mm_nt(att, values)
        delta = jnp.sum(prob_grad * probs, -1, keepdims=True)
        score_low = (probs * (prob_grad - delta)).astype(bf16)
        bias_s[win] += score_low.astype(f32)
        dq_s[pl.ds(first, WIN_Q), :] = (
            head_fold(mm(score_low, keys), ATOM_HEADS, head_dim, 0) * scale
        )
        shift = start - first
        lane = lax.broadcasted_iota(jnp.int32, probs.shape, 1)

        def placed(values):
            moved = pltpu.roll(values, shift, 1)
            inside = lane >= shift
            return jnp.concatenate(
                [jnp.where(inside, moved, 0.0), jnp.where(inside, 0.0, moved)], 1
            ).astype(bf16)

        rows = pl.ds(first, 2 * WIN_K)
        acck_s[rows, :] += mm_tn(placed(score_low.astype(f32)), queries) * scale
        accv_s[rows, :] += mm_tn(placed(probs), att)

    def some_windows(step, carry):
        for part in range(4):
            one_window(step * 4 + part)
        return carry

    lax.fori_loop(0, windows // 4, some_windows, 0)

    query_grad = dq_s[...]
    qbias_ref[...] += jnp.sum(query_grad, 0, keepdims=True)
    mix_ref[0, :, :width] = query_grad.astype(bf16)
    for ref, low, high in ((own_ref, RIM, RIM + slots), (left_ref, 0, RIM), (right_ref, RIM + slots, slots + 2 * RIM)):
        ref[0, :, :width] = acck_s[low:high, :].astype(ref.dtype)
        ref[0, :, width:] = accv_s[low:high, :].astype(ref.dtype)

    @pl.when(sample == pl.num_programs(0) - 1)
    def _():
        fold = pair_fold(pairs_ref.shape[1] // WIN_Q)

        def one(win, carry):
            pairs = pairs_ref[win]
            mean, inv_std = pair_stats(pairs, fold)
            scaled = bias_s[win] * jnp.concatenate([inv_std] * ATOM_HEADS, 0)
            pairm_ref[...] += scaled * jnp.concatenate([mean] * ATOM_HEADS, 0)
            upper = scaled.astype(bf16)
            lower = (scaled - upper.astype(f32)).astype(bf16)
            pairw_ref[...] += mm_nt(upper, pairs) + mm_nt(lower, pairs)
            return carry

        lax.fori_loop(0, windows, one, 0)
        if summing is not None:
            summing.last(*grads, totals, *sums)


def atom_backward(grad, starts, stored, pairs, share, wide, down, summing, weight_grad_units):
    query, keyval, gate, probs, attend, mid = stored
    samples, slots, width = query.shape
    ext_slots = slots + 2 * RIM
    windows = slots // WIN_Q
    model_width = grad.shape[-1]
    hidden_width = down.shape[0]
    stack = ATOM_HEADS * WIN_Q
    outs = (
        ((slots, 2 * width), bf16),
        ((slots, 2 * width), f32),
        ((RIM, 2 * width), bf16),
        ((RIM, 2 * width), bf16),
        ((slots, width), f32),
    )
    totals = (
        (1, width),
        (width, width),
        (width, 2 * hidden_width),
        (hidden_width, width),
        (width, model_width),
        (stack, pairs.shape[1]),
        (stack, WIN_K),
    )
    place = pl.BlockSpec(memory_space=pl.ANY)
    sums = summing.shapes if summing else []
    results = pl.pallas_call(
        functools.partial(atom_bwd_kernel, summing),
        out_shape=[jax.ShapeDtypeStruct((samples,) + shape, kind) for shape, kind in outs]
        + [jax.ShapeDtypeStruct(shape, f32) for shape in list(totals) + list(sums)],
        grid=(samples,),
        in_specs=[pl.BlockSpec(memory_space=pltpu.SMEM), per_sample(grad.shape[1:])]
        + [per_sample(part.shape[1:]) for part in stored]
        + [whole(part.shape) for part in (pairs, share, wide, down)]
        + [place] * len(weight_grad_units),
        out_specs=[per_sample(shape) for shape, _ in outs]
        + [whole(shape) for shape in totals]
        + [place] * len(sums),
        scratch_shapes=[
            pltpu.VMEM((ext_slots, width), f32),
            pltpu.VMEM((ext_slots, width), f32),
            pltpu.VMEM((slots + 2 * WIN_K, width), f32),
            pltpu.VMEM((slots + 2 * WIN_K, width), f32),
            pltpu.VMEM((windows, stack, WIN_K), f32),
            pltpu.VMEM((slots, width), bf16),
            pltpu.VMEM((slots, width), f32),
        ]
        + (summing.scratch() if summing else []),
        compiler_params=summing.params() if summing else params(),
        name="atom_backward",
    )(starts, grad, *stored, pairs, share, wide, down, *weight_grad_units)
    return results[:12], results[12:]


def atom_input_kernel(
    rows_ref, mix_ref, own_ref, left_ref, right_ref, midgrad_ref, wide_ref, grad_ref, proj_ref
):
    width = rows_ref.shape[-1]

    @pl.when(pl.program_id(0) == 0)
    def _():
        proj_ref[...] = jnp.zeros_like(proj_ref)

    normed, inv_std = norm_stats(rows_ref[0].astype(f32))
    slots = normed.shape[0]
    own = own_ref[0]
    head = own[:RIM] + left_ref[0].astype(f32)
    tail = own[slots - RIM :] + right_ref[0].astype(f32)
    own = jnp.concatenate([head, own[RIM : slots - RIM], tail], 0).astype(bf16)
    mix = jnp.concatenate([mix_ref[0, :, :width], own, mix_ref[0, :, width:]], 1)
    proj_ref[...] += mm_tn(normed.astype(bf16), mix)
    normed_grad = mm_nt(mix, wide_ref[:, : 4 * width])
    grad_ref[0] = midgrad_ref[0] + norm_back(normed, inv_std, normed_grad)


def atom_input_backward(rows, mix, own, left, right, midgrad, wide):
    samples, slots, width = rows.shape
    return pl.pallas_call(
        atom_input_kernel,
        out_shape=[
            jax.ShapeDtypeStruct(rows.shape, f32),
            jax.ShapeDtypeStruct((width, 4 * width), f32),
        ],
        grid=(samples,),
        in_specs=[per_sample(part.shape[1:]) for part in (rows, mix, own, left, right, midgrad)]
        + [whole(wide.shape)],
        out_specs=[per_sample((slots, width)), whole((width, 4 * width))],
        compiler_params=params(),
        name="atom_input_backward",
    )(rows, mix, own, left, right, midgrad, wide)


def row_stats(pairs, ones_op, weights):
    count = weights.shape[0]
    both = mm_nt(jnp.concatenate([weights, ones_op], 0), pairs)
    upper, lower = square_sums(ones_op, pairs.astype(f32) * pairs.astype(f32))
    features = pairs.shape[1]
    mean = both[count : count + 1] * (1.0 / features)
    square = (mm_nt(ones_op, upper) + mm_nt(ones_op, lower))[:1] * (1.0 / features)
    var = jnp.maximum(square - mean * mean, 0.0)
    return both[:count], mean, lax.rsqrt(var + norm_eps)


def pair_bias_kernel(pair_ref, weight_ref, bias_ref):
    weights = weight_ref[...]
    ones_op = jnp.ones((16, weights.shape[1]), bf16)
    weight_sum = jnp.sum(weights.astype(f32), -1, keepdims=True)
    for row in range(pair_ref.shape[0]):
        product, mean, inv_std = row_stats(pair_ref[row], ones_op, weights)
        bias_ref[:, row, :] = inv_std * (product - mean * weight_sum)


def pair_bias(pairs, weights):
    rows, keys, features = pairs.shape
    heads = weights.shape[0]
    return pl.pallas_call(
        pair_bias_kernel,
        out_shape=jax.ShapeDtypeStruct((heads, rows, keys), f32),
        grid=(rows // 8,),
        in_specs=[pl.BlockSpec((8, keys, features), lambda i: (i, 0, 0)), whole(weights.shape)],
        out_specs=pl.BlockSpec((heads, 8, keys), lambda i: (0, i, 0)),
        compiler_params=params(),
        name="pair_bias",
    )(pairs, weights)


def pair_grad_kernel(pair_ref, grad_ref, weight_ref, total_ref, mean_ref):
    @pl.when(pl.program_id(0) == 0)
    def _():
        total_ref[...] = jnp.zeros_like(total_ref)
        mean_ref[...] = jnp.zeros_like(mean_ref)

    heads = grad_ref.shape[0]
    ones_op = jnp.ones((16, pair_ref.shape[2]), bf16)
    total = jnp.zeros(total_ref.shape, f32)
    means = jnp.zeros(mean_ref.shape, f32)
    for row in range(pair_ref.shape[0]):
        pairs = pair_ref[row]
        _, mean, inv_std = row_stats(pairs, ones_op, weight_ref[...])
        scaled = grad_ref[:, row, :] * inv_std
        means += scaled * mean
        upper = scaled.astype(bf16)
        lower = (scaled - upper.astype(f32)).astype(bf16)
        both = mm(jnp.concatenate([upper, lower], 0), pairs)
        total += both[:heads] + both[heads:]
    total_ref[...] += total
    mean_ref[...] += means


def pair_grad(pairs, grads, weights):
    rows, keys, features = pairs.shape
    heads = grads.shape[0]
    total, means = pl.pallas_call(
        pair_grad_kernel,
        out_shape=[
            jax.ShapeDtypeStruct((heads, features), f32),
            jax.ShapeDtypeStruct((heads, keys), f32),
        ],
        grid=(rows // 8,),
        in_specs=[
            pl.BlockSpec((8, keys, features), lambda i: (i, 0, 0)),
            pl.BlockSpec((heads, 8, keys), lambda i: (0, i, 0)),
            whole(weights.shape),
        ],
        out_specs=[whole((heads, features)), whole((heads, keys))],
        compiler_params=params(),
        name="pair_grad",
    )(pairs, grads, weights)
    return total - jnp.sum(means, -1, keepdims=True)


def head_groups(width, heads):
    head_dim = width // heads
    groups = []
    for head in range(0, heads, 4):
        low = head * head_dim
        base = low // LANES * LANES
        groups.append((head, base, low - base))
    return head_dim, groups


def token_fwd_kernel(query_ref, keyval_ref, bias_ref, attend_ref, probs_ref, fold_s):
    tokens, width = query_ref.shape[1:]
    heads = bias_ref.shape[0]
    keys = bias_ref.shape[2]
    head_dim, groups = head_groups(width, heads)
    scale = float(head_dim) ** (-0.5)
    fold_s[...] = jnp.zeros_like(fold_s)
    for head, base, first in groups:
        span = slice(base, base + 256)
        key_rows = keyval_ref[:, 0, :, base : base + 256].reshape(keys, 256)
        value_rows = keyval_ref[:, 0, :, width + base : width + base + 256].reshape(keys, 256)
        stacked = head_stack(query_ref[0, :, span], 4, head_dim, first)
        bias = bias_ref[head : head + 4].reshape(4 * tokens, keys)
        scores = mm_nt(stacked, key_rows) * scale + bias
        exp_scores = jnp.exp(scores - jnp.max(scores, -1, keepdims=True))
        probs = exp_scores * (1.0 / jnp.sum(exp_scores, -1, keepdims=True))
        probs_low = probs.astype(bf16)
        probs_ref[0, head : head + 4] = probs_low.reshape(4, tokens, keys)
        fold_s[:, span] += head_fold(mm(probs_low, value_rows), 4, head_dim, first)
    attend_ref[0] = fold_s[...]


def token_attention(query, keyval, bias):
    samples, tokens, width = query.shape
    heads, _, keys = bias.shape
    devices = keyval.shape[0]
    return pl.pallas_call(
        token_fwd_kernel,
        out_shape=[
            jax.ShapeDtypeStruct(query.shape, f32),
            jax.ShapeDtypeStruct((samples, heads, tokens, keys), bf16),
        ],
        grid=(samples,),
        in_specs=[
            per_sample((tokens, width)),
            pl.BlockSpec((devices, 1, tokens, 2 * width), lambda b: (0, b, 0, 0)),
            whole(bias.shape),
        ],
        out_specs=[per_sample((tokens, width)), per_sample((heads, tokens, keys))],
        scratch_shapes=[pltpu.VMEM((tokens, width), f32)],
        compiler_params=params(),
        name="token_attention",
    )(query, keyval, bias)


def token_bwd_kernel(
    query_ref, keyval_ref, probs_ref, att_ref, dq_ref, dkv_ref, bias_ref, fold_s, grad_s
):
    tokens, width = query_ref.shape[1:]
    heads, _, keys = bias_ref.shape
    devices = keyval_ref.shape[0]
    head_dim, groups = head_groups(width, heads)
    scale = float(head_dim) ** (-0.5)

    @pl.when(pl.program_id(0) == 0)
    def _():
        bias_ref[...] = jnp.zeros_like(bias_ref)

    fold_s[...] = jnp.zeros_like(fold_s)
    grad_s[...] = jnp.zeros_like(grad_s)
    for head, base, first in groups:
        span = slice(base, base + 256)
        key_rows = keyval_ref[:, 0, :, base : base + 256].reshape(keys, 256)
        value_rows = keyval_ref[:, 0, :, width + base : width + base + 256].reshape(keys, 256)
        queries = head_stack(query_ref[0, :, span], 4, head_dim, first)
        att = head_stack(att_ref[0, :, span], 4, head_dim, first)
        probs_low = probs_ref[0, head : head + 4].reshape(4 * tokens, keys)
        probs = probs_low.astype(f32)
        prob_grad = mm_nt(att, value_rows)
        delta = jnp.sum(prob_grad * probs, -1, keepdims=True)
        score_low = (probs * (prob_grad - delta)).astype(bf16)
        bias_ref[head : head + 4] += score_low.astype(f32).reshape(4, tokens, keys)
        fold_s[:, span] += head_fold(mm(score_low, key_rows), 4, head_dim, first) * scale
        grad_s[:, span] += mm_tn(score_low, queries) * scale
        grad_s[:, width + base : width + base + 256] += mm_tn(probs_low, att)
    dq_ref[0] = fold_s[...]
    dkv_ref[:, 0] = grad_s[...].astype(bf16).reshape(devices, tokens, 2 * width)


def token_attention_back(query, keyval, probs, att):
    samples, tokens, width = query.shape
    heads, _, keys = probs.shape[1:]
    devices = keyval.shape[0]
    return pl.pallas_call(
        token_bwd_kernel,
        out_shape=[
            jax.ShapeDtypeStruct(query.shape, f32),
            jax.ShapeDtypeStruct(keyval.shape, bf16),
            jax.ShapeDtypeStruct((heads, tokens, keys), f32),
        ],
        grid=(samples,),
        in_specs=[
            per_sample((tokens, width)),
            pl.BlockSpec((devices, 1, tokens, 2 * width), lambda b: (0, b, 0, 0)),
            per_sample((heads, tokens, keys)),
            per_sample((tokens, width)),
        ],
        out_specs=[
            per_sample((tokens, width)),
            pl.BlockSpec((devices, 1, tokens, 2 * width), lambda b: (0, b, 0, 0)),
            whole((heads, tokens, keys)),
        ],
        scratch_shapes=[
            pltpu.VMEM((tokens, width), f32),
            pltpu.VMEM((keys, 2 * width), f32),
        ],
        compiler_params=params(),
        name="token_attention_back",
    )(query, keyval, probs, att)


def to_blocks(array, width):
    return [array[:, low : low + width] for low in range(0, array.shape[1], width)]


def pack_blocks(arrays, width):
    parts = []
    for array in arrays:
        parts += to_blocks(array, width)
    return jnp.concatenate(parts, 0)


def unpack_blocks(packed, shapes, width):
    arrays, low = [], 0
    for rows, columns in shapes:
        parts = []
        for _ in range(columns // width):
            parts.append(packed[low : low + rows])
            low += rows
        arrays.append(jnp.concatenate(parts, 1) if len(parts) > 1 else parts[0])
    return arrays


def sum_shares(grads, extra):
    samp, seq = lax.axis_size("samp"), lax.axis_size("seq")
    width = grads[2].shape[1]
    shapes = [(grad.shape[0] // samp, grad.shape[1]) for grad in grads]
    packed = jnp.concatenate(
        [
            block.astype(bf16).reshape(samp, -1, width)
            for grad in grads
            for block in to_blocks(grad, width)
        ]
        + [extra.astype(bf16).reshape(samp, -1, width)],
        1,
    )
    rows = packed.shape[1]
    packed = packed.reshape(samp, seq, rows // seq, width).transpose(1, 0, 2, 3)
    part = lax.psum_scatter(packed, "seq", scatter_dimension=0, tiled=False)
    part = lax.psum_scatter(part, "samp", scatter_dimension=0, tiled=False)
    packed = lax.all_gather(part, "seq", axis=0, tiled=True).astype(f32)
    shares = unpack_blocks(packed, shapes, width)
    return shares, packed[sum(r * (c // width) for r, c in shapes) :]


def local(
    atom_input,
    token_input,
    atom_counts,
    key_offsets,
    atom_pairs,
    pair_features,
    single_features,
    noise_levels,
    noise_direction,
    atom_proj,
    atom_qbias,
    atom_pairw,
    atom_outw,
    atom_upw,
    atom_downw,
    pool_weight,
    cond_weight,
    cond_bias,
    token_proj,
    token_qbias,
    token_pairw,
    token_outw,
    token_upw,
    token_downw,
    cotangent,
):
    samp, seq = lax.axis_size("samp"), lax.axis_size("seq")
    seq_pos = lax.axis_index("seq")
    samples, slots, atom_width = atom_input.shape
    tokens, width = token_input.shape[1:]
    features = atom_pairs.shape[-1]

    half = atom_downw.shape[0] // 2
    wide_own = jnp.concatenate(
        [atom_proj, atom_upw, pool_weight, atom_outw, atom_downw[:half], atom_downw[half:]], 1
    )
    tiny_own = jnp.concatenate(
        [
            atom_qbias,
            cond_bias,
            token_qbias,
            atom_pairw.reshape(-1),
            token_pairw.reshape(-1),
        ]
    )
    tiny_own = jnp.pad(tiny_own, (0, -tiny_own.size % (16 * LANES))).reshape(-1, LANES)
    large = (token_proj, token_upw, token_downw, cond_weight, token_outw)
    kernels = samples == 8 and WeightGather.fits([part.shape for part in large], samp, seq)
    up_pairs = [(i, i + 1) for i in range(seq - 1)]
    down_pairs = [(i + 1, i) for i in range(seq - 1)]
    if kernels:
        wide_all, tiny_all, ext = edges(wide_own, tiny_own, atom_input)
    else:
        wide_all = lax.all_gather(wide_own, "samp", axis=0, tiled=True)
        tiny_all = lax.all_gather(tiny_own, "samp", axis=0, tiled=True)
        before = lax.ppermute(atom_input[:, slots - RIM :], "seq", up_pairs)
        after = lax.ppermute(atom_input[:, :RIM], "seq", down_pairs)
        ext = jnp.concatenate([before, atom_input, after], 1)
    tiny_all = tiny_all.reshape(samp, -1)
    wide = wide_all[:, : -2 * atom_width]
    down = (
        wide_all[:, -2 * atom_width :]
        .reshape(samp, half, 2, atom_width)
        .transpose(0, 2, 1, 3)
        .reshape(-1, atom_width)
    )
    sizes = [atom_qbias.size, cond_bias.size, token_qbias.size, atom_pairw.size, token_pairw.size]
    cuts = [sum(sizes[:i]) for i in range(6)]
    tiny = [tiny_all[:, cuts[i] : cuts[i + 1]] for i in range(5)]
    atom_qb = tiny[0].reshape(1, -1).astype(f32)
    cond_b = tiny[1].reshape(-1)
    token_qb = tiny[2].reshape(-1)
    atom_pw = tiny[3].reshape(features, ATOM_HEADS)
    token_pw = tiny[4].reshape(-1, token_pairw.shape[1])

    rim_tokens = RIM // MAX_ATOMS
    counts = lax.dynamic_slice_in_dim(
        jnp.pad(atom_counts, (rim_tokens, rim_tokens)), seq_pos * tokens, tokens + 2 * rim_tokens
    )
    place = jnp.arange(MAX_ATOMS, dtype=jnp.int32)
    used = place[None, :] < counts[:, None]
    blocked = jnp.where(used, 0.0, masked_score).astype(f32).reshape(-1, 1)
    blocked = jnp.broadcast_to(blocked, (blocked.shape[0], LANES))
    own_counts = counts[rim_tokens : rim_tokens + tokens]
    share = used[rim_tokens : rim_tokens + tokens].astype(f32) / own_counts[:, None].astype(f32)
    share = jnp.broadcast_to(share.reshape(-1, 1), (slots, LANES))
    windows = slots // WIN_Q
    starts = jnp.arange(windows, dtype=jnp.int32) * WIN_Q + key_offsets + RIM
    pairs_t = atom_pairs.transpose(0, 1, 3, 2).reshape(windows, WIN_Q * features, WIN_K)
    eye = jnp.eye(WIN_Q, dtype=bool)
    spread = jnp.where(
        eye[None, :, :, None], atom_pw.T[:, None, None, :], jnp.zeros((), bf16)
    ).reshape(ATOM_HEADS * WIN_Q, WIN_Q * features)
    gather = WeightGather([part.shape for part in large], samp, seq) if kernels else None
    pooled, stored, fulls = atom_forward(
        ext,
        starts,
        pairs_t,
        spread,
        blocked,
        share,
        wide,
        down,
        atom_qb,
        gather,
        large if kernels else (),
    )
    if not kernels:
        fulls = [lax.all_gather(part, "samp", axis=0, tiled=True) for part in large]
    proj_w, up_w, down_w, cond_w, out_w = fulls
    block_in = token_input.astype(f32) + pooled

    noise_feature = 0.25 * jnp.log(noise_levels / sigma_data)
    cond_rows = (
        single_features.astype(f32)[None]
        + noise_feature[:, None, None] * noise_direction[None, None, :]
    )
    cond_low = norm_stats(cond_rows)[0].astype(bf16)
    cond_all = dot_last(cond_low, cond_w) + cond_b.astype(f32)
    parts = [cond_all[..., i * width : (i + 1) * width] for i in range(6)]

    pair_w = token_pw.T
    bias = pair_bias(pair_features, pair_w)
    normed_in, inv_in = norm_stats(block_in)
    attn_in = (jax.nn.sigmoid(parts[0]) * normed_in + parts[1]).astype(bf16)
    mix = dot_last(attn_in, proj_w)
    queries = (mix[..., :width] + token_qb.astype(f32)).astype(bf16)
    keyval_own = mix[..., width : 3 * width].astype(bf16)
    gating = mix[..., 3 * width :]
    keyval = lax.all_gather(keyval_own, "seq", axis=0, tiled=False)
    attend, probs = token_attention(queries, keyval, bias)
    sig_gate = jax.nn.sigmoid(gating)
    gated_low = (attend * sig_gate).astype(bf16)
    branch = dot_last(gated_low, out_w)
    gate_one = jax.nn.sigmoid(parts[2])
    mid = block_in + gate_one * branch
    normed_mid, inv_mid = norm_stats(mid)
    scale_two = jax.nn.sigmoid(parts[3])
    ffn_in = (scale_two * normed_mid + parts[4]).astype(bf16)
    upper = dot_last(ffn_in, up_w)
    hidden_width = down_w.shape[0]
    first_half, second_half = upper[..., :hidden_width], upper[..., hidden_width:]
    sig_first = jax.nn.sigmoid(first_half)
    hidden = (first_half * sig_first * second_half).astype(bf16)
    branch_two = dot_last(hidden, down_w)
    gate_two = jax.nn.sigmoid(parts[5])
    block_out = (mid + gate_two * branch_two).astype(bf16)

    out_grad = cotangent.astype(f32)
    branch_two_low = (out_grad * gate_two).astype(bf16)
    gate_two_grad = out_grad * branch_two * gate_two * (1.0 - gate_two)
    hidden_grad = dot_back(branch_two_low, down_w)
    first_grad = hidden_grad * second_half * sig_first * (1.0 + first_half * (1.0 - sig_first))
    second_grad = hidden_grad * first_half * sig_first
    upper_grad = jnp.concatenate([first_grad, second_grad], -1).astype(bf16)
    ffn_grad = dot_back(upper_grad, up_w)
    scale_two_grad = ffn_grad * normed_mid * scale_two * (1.0 - scale_two)
    mid_grad = out_grad + norm_back(normed_mid, inv_mid, ffn_grad * scale_two)
    branch_low = (mid_grad * gate_one).astype(bf16)
    gate_one_grad = mid_grad * branch * gate_one * (1.0 - gate_one)
    gated_grad = dot_back(branch_low, out_w)
    attend_low = (gated_grad * sig_gate).astype(bf16)
    gating_grad = gated_grad * attend * sig_gate * (1.0 - sig_gate)
    query_grad, keyval_part, bias_grad = token_attention_back(queries, keyval, probs, attend_low)
    keyval_grad = lax.psum_scatter(keyval_part, "seq", scatter_dimension=0, tiled=False)
    pairw_grad = pair_grad(pair_features, bias_grad, pair_w).T
    mix_grad = jnp.concatenate(
        [query_grad.astype(bf16), keyval_grad, gating_grad.astype(bf16)], -1
    )
    token_qb_grad = jnp.sum(query_grad, (0, 1))
    attn_in_grad = dot_back(mix_grad, proj_w)
    scale_one = jax.nn.sigmoid(parts[0])
    scale_one_grad = attn_in_grad * normed_in * scale_one * (1.0 - scale_one)
    token_grad = mid_grad + norm_back(normed_in, inv_in, attn_in_grad * scale_one)
    cond_grad = jnp.concatenate(
        [scale_one_grad, attn_in_grad, gate_one_grad, scale_two_grad, ffn_grad, gate_two_grad], -1
    ).astype(bf16)
    cond_b_grad = jnp.sum(cond_grad.astype(f32), (0, 1))

    factors = [
        (attn_in, mix_grad),
        (ffn_in, upper_grad),
        (hidden, branch_two_low),
        (cond_low, cond_grad),
        (gated_low, branch_low),
    ]
    if kernels:
        summing = GradSum([part.shape for part in large])
        units = (weight_grads(factors, samp, seq),)
    else:
        summing, units = None, ()
    atom_results, shares = atom_backward(
        token_grad, starts, stored, pairs_t, share, wide, down, summing, units
    )
    mix_part, own, left, right, atom_mid_grad, *atom_totals = atom_results
    from_right = lax.ppermute(left, "seq", down_pairs)
    from_left = lax.ppermute(right, "seq", up_pairs)
    atom_grad, atom_proj_grad = atom_input_backward(
        atom_input, mix_part, own, from_left, from_right, atom_mid_grad, wide
    )
    qb_grad, outw_grad, upw_grad, downw_grad, pool_grad, pairw_stack, pairw_mean = atom_totals
    diagonal = pairw_stack.reshape(ATOM_HEADS, WIN_Q, WIN_Q, features)
    atom_pw_grad = (
        jnp.sum(jnp.where(eye[None, :, :, None], diagonal, 0.0), (1, 2)).T
        - jnp.sum(pairw_mean.reshape(ATOM_HEADS, -1), 1)[None, :]
    )

    rows = atom_width // samp
    tiny_parts = [qb_grad.reshape(-1), atom_pw_grad, cond_b_grad, token_qb_grad, pairw_grad]
    tiny_flat = jnp.concatenate([part.astype(bf16).reshape(samp, -1) for part in tiny_parts], 1)
    spare = width - upw_grad.shape[1] - atom_width
    tiny_flat = jnp.pad(tiny_flat, ((0, 0), (0, rows * spare - tiny_flat.shape[1])))
    lanes = lambda part: part.astype(bf16).reshape(samp, rows, -1)
    downw_two = downw_grad.astype(bf16).reshape(samp, 2, rows, atom_width)
    small = jnp.stack(
        [
            lanes(pool_grad),
            jnp.concatenate([lanes(atom_proj_grad), downw_two[:, 0], downw_two[:, 1]], -1),
            jnp.concatenate(
                [lanes(upw_grad), lanes(outw_grad), tiny_flat.reshape(samp, rows, spare)], -1
            ),
            jnp.zeros((samp, rows, width), bf16),
        ],
        1,
    ).reshape(samp, -1, width)
    if kernels:
        rest = small_sums(small.reshape(samp, seq, 16, width).transpose(1, 0, 2, 3))
    else:
        shares, rest = sum_shares(
            [weight_grad(*pair) for pair in factors], small.reshape(-1, width)
        )
    rest = rest.reshape(-1, width)
    pool_out, second, third = rest[:rows], rest[rows : 2 * rows], rest[2 * rows : 3 * rows]
    low = atom_proj_grad.shape[1]
    downw_out = jnp.concatenate(
        [second[:, low : low + atom_width], second[:, low + atom_width :]], 0
    )
    high = upw_grad.shape[1]
    tiny_out = third[:, high + atom_width :].reshape(-1)
    tiny_shares, cut = [], 0
    for part in tiny_parts:
        size = part.size // samp
        shape = (part.shape[0] // samp,) + part.shape[1:]
        tiny_shares.append(tiny_out[cut : cut + size].reshape(shape))
        cut += size
    return (
        block_out,
        atom_grad,
        token_grad,
        second[:, :low],
        tiny_shares[0],
        tiny_shares[1],
        third[:, high : high + atom_width],
        third[:, :high],
        downw_out,
        pool_out,
        shares[3],
        tiny_shares[2],
        shares[0],
        tiny_shares[3],
        tiny_shares[4],
        shares[4],
        shares[1],
        shares[2],
    )


def solution(mesh):
    in_specs = (
        P("samp", "seq", None),
        P("samp", "seq", None),
        P(),
        P("seq"),
        P("seq", None, None, None),
        P("seq", None, None),
        P("seq", None),
        P("samp"),
        P(),
        P("samp", None),
        P("samp"),
        P("samp", None),
        P("samp", None),
        P("samp", None),
        P("samp", None),
        P("samp", None),
        P("samp", None),
        P("samp"),
        P("samp", None),
        P("samp"),
        P("samp", None),
        P("samp", None),
        P("samp", None),
        P("samp", None),
        P("samp", "seq", None),
    )
    out_specs = (
        P("samp", "seq", None),
        P("samp", "seq", None),
        P("samp", "seq", None),
        P("samp", None),
        P("samp"),
        P("samp", None),
        P("samp", None),
        P("samp", None),
        P("samp", None),
        P("samp", None),
        P("samp", None),
        P("samp"),
        P("samp", None),
        P("samp"),
        P("samp", None),
        P("samp", None),
        P("samp", None),
        P("samp", None),
    )
    return jax.shard_map(local, mesh=mesh, in_specs=in_specs, out_specs=out_specs, check_vma=False)
```

```python
import functools

import jax
import jax.numpy as jnp
from jax import lax
from jax.experimental import pallas as pl
from jax.experimental.pallas import tpu as pltpu
from jax.sharding import PartitionSpec as P

MAX_ATOMS = 8
WIN_Q = 32
WIN_K = 128
ATOM_HEADS = 4
RIM = 96
LANES = 128

norm_eps = 1e-05
sigma_data = 16.0
masked_score = -1000000000.0
bf16 = jnp.bfloat16
f32 = jnp.float32
vmem_bytes = 56 << 20


def dot_last(left_op, right_op):
    return jnp.einsum("...k,kn->...n", left_op, right_op, preferred_element_type=f32)


def dot_back(grad_op, weight):
    return jnp.einsum("...n,kn->...k", grad_op, weight, preferred_element_type=f32)


def weight_grad(left_op, grad_op):
    flat_left = left_op.reshape(-1, left_op.shape[-1])
    flat_grad = grad_op.reshape(-1, grad_op.shape[-1])
    return jnp.einsum("rk,rn->kn", flat_left, flat_grad, preferred_element_type=f32)


def mm(left_op, right_op):
    return lax.dot_general(left_op, right_op, (((1,), (0,)), ((), ())), preferred_element_type=f32)


def mm_nt(left_op, right_op):
    return lax.dot_general(left_op, right_op, (((1,), (1,)), ((), ())), preferred_element_type=f32)


def mm_tn(left_op, right_op):
    return lax.dot_general(left_op, right_op, (((0,), (0,)), ((), ())), preferred_element_type=f32)


def norm_stats(operand):
    center = operand - jnp.mean(operand, -1, keepdims=True)
    inv_std = lax.rsqrt(jnp.mean(center * center, -1, keepdims=True) + norm_eps)
    return (center * inv_std, inv_std)


def norm_back(normed, inv_std, grad_op):
    return inv_std * (
        grad_op
        - jnp.mean(grad_op, -1, keepdims=True)
        - normed * jnp.mean(grad_op * normed, -1, keepdims=True)
    )


def sigmoid(operand):
    return 1.0 / (1.0 + jnp.exp(-operand))


def whole(shape):
    return pl.BlockSpec(shape, lambda *_: (0,) * len(shape))


def per_sample(shape):
    return pl.BlockSpec((1,) + shape, lambda b, *_: (b,) + (0,) * len(shape))


def params():
    return pltpu.CompilerParams(vmem_limit_bytes=vmem_bytes)


def square_sums(ones_op, squares):
    upper = squares.astype(bf16)
    lower = (squares - upper.astype(f32)).astype(bf16)
    return upper, lower


def head_stack(rows, heads, head_dim, first):
    lane = lax.broadcasted_iota(jnp.int32, rows.shape, 1)
    parts = []
    for head in range(heads):
        low = first + head * head_dim
        parts.append(jnp.where((lane >= low) & (lane < low + head_dim), rows, jnp.zeros_like(rows)))
    return jnp.concatenate(parts, 0)


def head_fold(stacked, heads, head_dim, first):
    count = stacked.shape[0] // heads
    lane = lax.broadcasted_iota(jnp.int32, (count, stacked.shape[1]), 1)
    total = jnp.zeros((count, stacked.shape[1]), f32)
    for head in range(heads):
        low = first + head * head_dim
        part = stacked[head * count : (head + 1) * count]
        total = jnp.where((lane >= low) & (lane < low + head_dim), part, total)
    return total


MESH = pl.DeviceIdType.MESH


def places():
    samp_pos, seq_pos = lax.axis_index("samp"), lax.axis_index("seq")
    core, across, along = seq_pos % 2, seq_pos // 2 % 2, seq_pos // 4

    def index(along, across, core):
        return (along * 2 + across) * 2 + core

    return (
        samp_pos,
        seq_pos,
        index(along, across, 1 - core),
        index(along, 1 - across, core),
        index(1 - along, across, core),
        index(1 - along, 1 - across, core),
    )


def remote(source, target, send_sem, recv_sem, device):
    return pltpu.make_async_remote_copy(
        src_ref=source,
        dst_ref=target,
        send_sem=send_sem,
        recv_sem=recv_sem,
        device_id=device,
        device_id_type=MESH,
    )


def greet(devices):
    barrier = pltpu.get_barrier_semaphore()
    for device in devices:
        pl.semaphore_signal(barrier, inc=1, device_id=device, device_id_type=MESH)
    pl.semaphore_wait(barrier, len(devices))


def pick(position, values):
    chosen = values[0]
    for index, value in enumerate(values[1:], 1):
        chosen = jnp.where(position == index, value, chosen)
    return chosen


class WeightGather:
    def __init__(self, shapes, samp, seq):
        self.shapes, self.samp, self.seq = shapes, samp, seq
        self.splits = [self.split(shape, seq) for shape in shapes]

    @staticmethod
    def split(shape, parts):
        rows, columns = shape
        for down in (1, 2, 4, 8):
            across = parts // down
            if rows % (16 * down) == 0 and columns % (LANES * across) == 0:
                return (down, across)
        return None

    @staticmethod
    def fits(shapes, samp, seq):
        return (
            samp == 4
            and seq == 8
            and len(shapes) == 5
            and all(WeightGather.split(shape, seq) for shape in shapes)
        )

    def full_shapes(self):
        return [(rows * self.samp, columns) for rows, columns in self.shapes]

    def scratch(self):
        count = len(self.shapes)
        return [
            pltpu.SemaphoreType.DMA((9, self.samp, count)),
            pltpu.SemaphoreType.DMA((8, self.samp, count)),
            pltpu.SemaphoreType.DMA((2, count)),
        ] + [pltpu.VMEM(shape, bf16) for shape in self.shapes]

    def params(self):
        return pltpu.CompilerParams(
            vmem_limit_bytes=vmem_bytes, collective_id=1, has_side_effects=True
        )

    def cell(self, ref, weight, origin, part):
        rows, columns = self.shapes[weight]
        down, across = self.splits[weight]
        height, width = rows // down, columns // across
        low = origin * rows + part // across * height
        left = part % across * width
        return ref.at[
            pl.ds(pl.multiple_of(low, 16), height), pl.ds(pl.multiple_of(left, LANES), width)
        ]

    def origin(self, position, turn):
        order = [sorted(range(self.samp), key=lambda o: (abs(o - z), o)) for z in range(self.samp)]
        if isinstance(turn, int):
            return pick(position, [order[z][turn] for z in range(self.samp)])
        return pick(
            position, [pick(turn, [order[z][t] for t in range(self.samp)]) for z in range(self.samp)]
        )

    def own_copies(self, shards, fulls, own, held, stage):
        z = places()[0]
        copies = []
        for w, shard in enumerate(shards):
            rows = self.shapes[w][0]
            target = fulls[w].at[pl.ds(pl.multiple_of(z * rows, 16), rows), :]
            ends = (shard, held[w]) if stage == 0 else (held[w], target)
            copies.append(pltpu.make_async_copy(*ends, own.at[stage, w]))
        return copies

    def start(self, shards, fulls, send, recv, own, held):
        z, me, sib, xn, yn, dg = places()
        above, below = lax.rem(z + 1, self.samp), lax.rem(z + self.samp - 1, self.samp)
        greet([(z, sib), (z, xn), (z, yn), (above, me), (below, me)])
        for w, shard in enumerate(shards):
            source = self.cell(shard, w, 0, me)
            target = self.cell(fulls[w], w, z, me)

            @pl.when(z < self.samp - 1)
            def _():
                remote(source, target, send.at[0, 0, w], recv.at[0, z, w], (z + 1, me)).start()

            @pl.when(z > 0)
            def _():
                remote(source, target, send.at[1, 0, w], recv.at[0, z, w], (z - 1, me)).start()

        for copy in self.own_copies(shards, fulls, own, held, 0):
            copy.start()

    def place_own(self, shards, fulls, own, held):
        for copy in self.own_copies(shards, fulls, own, held, 0):
            copy.wait()
        for copy in self.own_copies(shards, fulls, own, held, 1):
            copy.start()

    def share_own(self, turn, origin, sources, fulls, send, recv):
        z, me, sib, xn, yn, dg = places()
        for kind, part in ((2, xn), (3, yn), (5, sib)):
            for w, source in enumerate(sources):
                target = self.cell(fulls[w], w, origin, me)
                arrival = {2: 1, 3: 2, 5: 4}[kind]
                remote(
                    source, target, send.at[kind, turn, w], recv.at[arrival, origin, w], (z, part)
                ).start()

    def wait_cell(self, fulls, recv, kind, w, origin, part, device):
        target = self.cell(fulls[w], w, origin, part)
        remote(target, target, recv.at[kind, origin, w], recv.at[kind, origin, w], device).wait_recv()

    def issue(self, turn, fulls, send, recv):
        z, me, sib, xn, yn, dg = places()
        origin = self.origin(z, turn)
        count = len(self.shapes)
        for w in range(count):
            self.wait_cell(fulls, recv, 0, w, origin, me, (z, sib))
        for w in range(count):
            cell = self.cell(fulls[w], w, origin, me)

            @pl.when((origin < z) & (z < self.samp - 1))
            def _():
                remote(cell, cell, send.at[0, turn, w], recv.at[0, origin, w], (z + 1, me)).start()

            @pl.when((origin > z) & (z > 0))
            def _():
                remote(cell, cell, send.at[1, turn, w], recv.at[0, origin, w], (z - 1, me)).start()

        cells = [self.cell(fulls[w], w, origin, me) for w in range(count)]
        self.share_own(turn, origin, cells, fulls, send, recv)

    def passed_on(self, w):
        return w in (0, 3)

    def finish(self, turn, fulls, send, recv):
        z, me, sib, xn, yn, dg = places()
        origin = self.origin(z, turn)
        count = len(self.shapes)
        for kind, part, other, by in ((1, xn, yn, True), (2, yn, xn, False)):
            for w in range(count):
                self.wait_cell(fulls, recv, kind, w, origin, part, (z, part))
                cell = self.cell(fulls[w], w, origin, part)
                if self.passed_on(w) == by:
                    remote(
                        cell, cell, send.at[4, turn, w], recv.at[3, origin, w], (z, other)
                    ).start()
                remote(
                    cell, cell, send.at[5 + kind, turn, w], recv.at[4 + kind, origin, w], (z, sib)
                ).start()

    def diagonal(self, turn, fulls, send, recv):
        z, me, sib, xn, yn, dg = places()
        origin = self.origin(z, turn)
        for w in range(len(self.shapes)):
            self.wait_cell(fulls, recv, 3, w, origin, dg, (z, yn))
            cell = self.cell(fulls[w], w, origin, dg)
            remote(cell, cell, send.at[8, turn, w], recv.at[7, origin, w], (z, sib)).start()

    def drain(self, shards, fulls, send, recv, own, held):
        z, me, sib, xn, yn, dg = places()
        count = len(self.shapes)

        def sent(kind, turn, w):
            cell = self.cell(fulls[w], w, 0, me)
            remote(cell, cell, send.at[kind, turn, w], recv.at[0, 0, w], (z, sib)).wait_send()

        def one(turn, carry):
            origin = self.origin(z, turn)
            for w in range(count):
                for kind in range(2, 9):
                    sent(kind, turn, w)

                @pl.when((z < self.samp - 1) & (origin < z))
                def _():
                    sent(0, turn, w)

                @pl.when((z > 0) & (origin > z))
                def _():
                    sent(1, turn, w)

                for kind in range(4, 8):
                    self.wait_cell(fulls, recv, kind, w, origin, sib, (z, sib))
            return carry

        lax.fori_loop(1, self.samp, one, 0)
        for w in range(count):

            @pl.when(z < self.samp - 1)
            def _():
                sent(0, 0, w)

            @pl.when(z > 0)
            def _():
                sent(1, 0, w)

        for copy in self.own_copies(shards, fulls, own, held, 1):
            copy.wait()

    def step(self, sample, shards, fulls, send, recv, own, *held):
        @pl.when(sample == 0)
        def _():
            self.start(shards, fulls, send, recv, own, held)

        @pl.when(sample == 1)
        def _():
            self.place_own(shards, fulls, own, held)

        for at, turn in ((2, 1), (3, 2), (5, 3)):

            @pl.when(sample == at)
            def _():
                self.issue(turn, fulls, send, recv)

        for at, turn in ((4, 1), (5, 2), (7, 3)):

            @pl.when(sample == at)
            def _():
                self.finish(turn, fulls, send, recv)

        for at, turn in ((5, 1), (7, 2)):

            @pl.when(sample == at)
            def _():
                self.diagonal(turn, fulls, send, recv)

    def last(self, sample, shards, fulls, send, recv, own, *held):
        @pl.when(sample == pl.num_programs(0) - 1)
        def _():
            self.diagonal(3, fulls, send, recv)
            self.drain(shards, fulls, send, recv, own, held)


def edge_kernel(samp, seq, wide_ref, tiny_ref, rows_ref, wide_out, tiny_out, ext_out, send, recv):
    z, me = lax.axis_index("samp"), lax.axis_index("seq")
    samples, slots, width = rows_ref.shape
    right, left = lax.rem(me + 1, seq), lax.rem(me + seq - 1, seq)
    others = [(lax.rem(z + hop, samp), me) for hop in range(1, samp)]
    greet(others + [(z, right), (z, left)])
    copies = []
    for hop, device in enumerate(others):
        for kind, (ref, out) in enumerate(((wide_ref, wide_out), (tiny_ref, tiny_out))):
            rows = ref.shape[0]
            target = out.at[pl.ds(pl.multiple_of(z * rows, 16), rows), :]
            copy = remote(ref, target, send.at[kind, hop], recv.at[kind, hop], device)
            copy.start()
            copies.append(copy)
    before, after = ext_out.at[:, :RIM, :], ext_out.at[:, RIM + slots :, :]
    to_right = remote(rows_ref.at[:, slots - RIM :, :], before, send.at[2, 0], recv.at[2, 0], (z, right))
    to_left = remote(rows_ref.at[:, :RIM, :], after, send.at[2, 1], recv.at[2, 1], (z, left))
    first, last = me == 0, me == seq - 1

    @pl.when(~last)
    def _():
        to_right.start()

    @pl.when(~first)
    def _():
        to_left.start()

    @pl.when(first)
    def _():
        ext_out[:, :RIM, :] = jnp.zeros((samples, RIM, width), bf16)

    @pl.when(last)
    def _():
        ext_out[:, RIM + slots :, :] = jnp.zeros((samples, RIM, width), bf16)

    def move(sample, carry):
        ext_out[sample, RIM : RIM + slots, :] = rows_ref[sample]
        return carry

    lax.fori_loop(0, samples, move, 0)
    for ref, out in ((wide_ref, wide_out), (tiny_ref, tiny_out)):
        rows = ref.shape[0]
        out[pl.ds(pl.multiple_of(z * rows, 16), rows), :] = ref[...]
    for copy in copies:
        copy.wait()

    @pl.when(~last)
    def _():
        to_right.wait_send()
        to_left.wait_recv()

    @pl.when(~first)
    def _():
        to_left.wait_send()
        to_right.wait_recv()


def edges(wide_own, tiny_own, rows):
    samp, seq = lax.axis_size("samp"), lax.axis_size("seq")
    samples, slots, width = rows.shape
    place = pl.BlockSpec(memory_space=pltpu.VMEM)
    return pl.pallas_call(
        functools.partial(edge_kernel, samp, seq),
        out_shape=[
            jax.ShapeDtypeStruct((samp * wide_own.shape[0], wide_own.shape[1]), bf16),
            jax.ShapeDtypeStruct((samp * tiny_own.shape[0], tiny_own.shape[1]), bf16),
            jax.ShapeDtypeStruct((samples, slots + 2 * RIM, width), bf16),
        ],
        in_specs=[place] * 3,
        out_specs=[place] * 3,
        scratch_shapes=[
            pltpu.SemaphoreType.DMA((3, samp)),
            pltpu.SemaphoreType.DMA((3, samp)),
        ],
        compiler_params=pltpu.CompilerParams(
            vmem_limit_bytes=vmem_bytes, collective_id=0, has_side_effects=True
        ),
        name="edges",
    )(wide_own, tiny_own, rows)


UNIT = 336


def weight_grad_kernel(
    attn_ref, mix_ref, cond_ref, condgrad_ref, upw_ref, downw_ref, outw_ref, out_ref, cond_s
):
    part = pl.program_id(0)
    samp = out_ref.shape[1]

    @pl.when(part == 0)
    def _():
        for low in range(0, cond_s.shape[1], 768):
            cond_s[:, low : low + 768] = mm_tn(
                cond_ref[...], condgrad_ref[:, low : low + 768]
            ).astype(bf16)

    proj = mm_tn(attn_ref[...], mix_ref[...]).astype(bf16)
    rows = proj.shape[0] // samp
    for z in range(samp):
        out_ref[0, z, :rows, :384] = proj[z * rows : (z + 1) * rows]
        out_ref[0, z, :rows, 384:] = upw_ref[z * rows : (z + 1) * rows, :]
        out_ref[0, z, 192:240, :] = downw_ref[pl.ds(pl.multiple_of(z * 384 + part * 48, 16), 48), :]
        low = pl.multiple_of(z * 96 + part // 4 * 48, 16)
        left = pl.multiple_of(part % 4 * 1152, LANES)
        out_ref[0, z, 240:288, :] = cond_s[pl.ds(low, 48), pl.ds(left, 768)]
        left = pl.multiple_of(part % 4 * 1152 + 768, LANES)
        out_ref[0, z, 288:336, :384] = cond_s[pl.ds(low, 48), pl.ds(left, 384)]
        low = pl.multiple_of(z * 192 + part // 2 * 48, 16)
        left = pl.multiple_of(part % 2 * 384, LANES)
        out_ref[0, z, 288:336, 384:] = outw_ref[pl.ds(low, 48), pl.ds(left, 384)]


def weight_grads(attn_in, mix_grad, cond_low, cond_grad, ready, samp, seq):
    flat = [part.reshape(-1, part.shape[-1]) for part in (attn_in, mix_grad, cond_low, cond_grad)]
    flat += ready
    specs = [whole(array.shape) for array in flat]
    for index in (1, 4):
        specs[index] = pl.BlockSpec((flat[index].shape[0], 384), lambda s: (0, s))
    return pl.pallas_call(
        weight_grad_kernel,
        out_shape=jax.ShapeDtypeStruct((seq, samp, UNIT, 768), bf16),
        grid=(seq,),
        in_specs=specs,
        out_specs=pl.BlockSpec((1, samp, UNIT, 768), lambda s: (s, 0, 0, 0)),
        scratch_shapes=[pltpu.VMEM((384, 4608), bf16)],
        compiler_params=params(),
        name="weight_grads",
    )(*flat)


def add_into(target, source, lanes=slice(None), rows=48):
    def one(step, carry):
        part = pl.ds(pl.multiple_of(step * rows, 16), rows)
        both = target[part, lanes].astype(f32) + source[part, :].astype(f32)
        target[part, lanes] = both.astype(bf16)
        return carry

    lax.fori_loop(0, target.shape[0] // rows, one, 0)


class GradSum:
    head, tail, full = slice(0, 384), slice(384, 768), slice(0, 768)

    def __init__(self, shapes):
        self.shapes = list(shapes)

    def scratch(self):
        half = (UNIT, 384)
        dma = pltpu.SemaphoreType.DMA
        return [
            pltpu.VMEM((4, 4, UNIT, 768), bf16),
            pltpu.VMEM((4, 4, UNIT, 768), bf16),
            pltpu.VMEM((4, 2) + half, bf16),
            pltpu.VMEM((4, 2) + half, bf16),
            pltpu.VMEM((4,) + half, bf16),
            pltpu.VMEM((4,) + half, bf16),
            pltpu.VMEM((3, UNIT, 768), bf16),
            pltpu.VMEM((8, UNIT, 768), bf16),
            pltpu.VMEM((2, UNIT, 768), f32),
            dma((4, 4)),
            dma((4, 4)),
            dma((4, 4)),
            dma((4, 4)),
            dma((4, 4)),
            dma((4, 2)),
            dma((4, 2)),
            dma((3,)),
            dma((3,)),
            dma((8,)),
            dma((8,)),
            dma((2, 6)),
        ]

    def params(self):
        return pltpu.CompilerParams(
            vmem_limit_bytes=vmem_bytes, collective_id=2, has_side_effects=True
        )

    def bind(self, grads, totals, mine, theirs, from_x, from_y, last_x, last_y, planes, shares, stage, *sems):
        self.grads, self.totals = grads, totals
        self.mine, self.theirs, self.from_x, self.from_y = mine, theirs, from_x, from_y
        self.last_x, self.last_y, self.planes, self.shares = last_x, last_y, planes, shares
        self.stage = stage
        (
            self.s_sib,
            self.r_sib,
            self.s_own,
            self.s_one,
            self.r_one,
            self.s_two,
            self.r_two,
            self.s_z,
            self.r_z,
            self.s_share,
            self.r_share,
            self.s_out,
        ) = sems
        self.z, self.me, self.sib, self.xn, self.yn, self.dg = places()
        self.core, self.chip = self.me % 2, self.me // 2
        self.chip_x, self.chip_y, self.chip_d = self.xn // 2, self.yn // 2, self.dg // 2
        order = [[p ^ hop for hop in (2, 3, 1, 0)] for p in range(4)]
        self.plane = [pick(self.z, [order[p][r] for p in range(4)]) for r in range(4)]

    def there(self, r, j):
        return remote(
            self.grads.at[2 * j + 1 - self.core, self.plane[r]],
            self.theirs.at[r, j],
            self.s_sib.at[r, j],
            self.r_sib.at[r, j],
            (self.z, self.sib),
        )

    def here(self, r, j):
        return pltpu.make_async_copy(
            self.grads.at[2 * j + self.core, self.plane[r]], self.mine.at[r, j], self.s_own.at[r, j]
        )

    def one(self, r, k):
        chip = (self.chip_x, self.chip_d, self.chip_y, self.chip_d)[k]
        lanes = self.head if k < 2 else self.tail
        target = (self.from_x if k < 2 else self.from_y).at[r, k % 2]
        device = (self.z, self.xn if k < 2 else self.yn)
        return remote(
            self.mine.at[r, chip, :, lanes], target, self.s_one.at[r, k], self.r_one.at[r, k], device
        )

    def two(self, r, k):
        chip, lanes, target, device = (
            (self.chip_y, self.head, self.last_y, self.yn),
            (self.chip_x, self.tail, self.last_x, self.xn),
        )[k]
        return remote(
            self.mine.at[r, chip, :, lanes],
            target.at[r],
            self.s_two.at[r, k],
            self.r_two.at[r, k],
            (self.z, device),
        )

    def across(self, r):
        return remote(
            self.mine.at[r, self.chip],
            self.planes.at[r],
            self.s_z.at[r],
            self.r_z.at[r],
            (self.plane[r], self.me),
        )

    def share(self, part, lanes, kind, device):
        ref = self.shares.at[part, :, lanes]
        return remote(ref, ref, self.s_share.at[kind], self.r_share.at[kind], (self.z, device))

    def begin(self, r):
        for j in range(4):
            self.there(r, j).start()
            self.here(r, j).start()

    def pairs(self, r):
        for j in range(4):
            self.there(r, j).wait_recv()
            self.here(r, j).wait()
        for j in range(4):
            add_into(self.mine.at[r, j], self.theirs.at[r, j])
        for k in range(4):
            self.one(r, k).start()

    def middle(self, r):
        self.one(r, 1).wait_recv()
        add_into(self.mine.at[r, self.chip_y], self.from_x.at[r, 1], self.head)
        self.two(r, 0).start()
        self.one(r, 3).wait_recv()
        add_into(self.mine.at[r, self.chip_x], self.from_y.at[r, 1], self.tail)
        self.two(r, 1).start()
        self.one(r, 0).wait_recv()
        add_into(self.mine.at[r, self.chip], self.from_x.at[r, 0], self.head)
        self.one(r, 2).wait_recv()
        add_into(self.mine.at[r, self.chip], self.from_y.at[r, 0], self.tail)

    def finish(self, r):
        self.two(r, 0).wait_recv()
        add_into(self.mine.at[r, self.chip], self.last_y.at[r], self.head)
        self.two(r, 1).wait_recv()
        add_into(self.mine.at[r, self.chip], self.last_x.at[r], self.tail)
        if r < 3:
            self.across(r).start()

    def total(self):
        for r in range(3):
            self.across(r).wait_recv()

        def one(step, carry):
            rows = pl.ds(pl.multiple_of(step * 48, 16), 48)
            both = self.mine[3, self.chip, rows, :].astype(f32)
            for r in range(3):
                both += self.planes[r, rows, :].astype(f32)
            self.shares[self.me, rows, :] = both.astype(bf16)
            return carry

        lax.fori_loop(0, UNIT // 48, one, 0)
        self.share(self.me, self.full, 0, self.xn).start()
        self.share(self.me, self.full, 1, self.yn).start()
        self.share(self.me, self.full, 4, self.sib).start()

    def pieces(self, part):
        proj, upw, down, cond, outw = self.totals
        stage = self.stage.at[part % 2]
        low, left = part // 4 * 48, part % 4 * 1152
        high, right = part // 2 * 48, part % 2 * 384
        return (
            (stage.at[:192, self.head], proj.at[:, part * 384 : (part + 1) * 384]),
            (stage.at[:192, self.tail], upw.at[:, part * 384 : (part + 1) * 384]),
            (stage.at[192:240, :], down.at[part * 48 : (part + 1) * 48, :]),
            (stage.at[240:288, :], cond.at[low : low + 48, left : left + 768]),
            (stage.at[288:336, self.head], cond.at[low : low + 48, left + 768 : left + 1152]),
            (stage.at[288:336, self.tail], outw.at[high : high + 48, right : right + 384]),
        )

    def write(self, part):
        return [
            pltpu.make_async_copy(source, target, self.s_out.at[part % 2, k])
            for k, (source, target) in enumerate(self.pieces(part))
        ]

    def collect(self):
        me, sib, xn, yn, dg = self.me, self.sib, self.xn, self.yn, self.dg
        self.share(xn, self.full, 0, xn).wait_recv()
        self.share(xn, self.head, 2, yn).start()
        self.share(xn, self.full, 5, sib).start()
        self.share(yn, self.full, 1, yn).wait_recv()
        self.share(yn, self.tail, 3, xn).start()
        self.share(yn, self.full, 6, sib).start()
        self.share(dg, self.head, 2, yn).wait_recv()
        self.share(dg, self.tail, 3, xn).wait_recv()
        self.share(dg, self.full, 7, sib).start()
        for kind in range(4, 8):
            self.share(sib, self.full, kind, sib).wait_recv()
        for part in range(8):
            if part >= 2:
                for copy in self.write(part - 2):
                    copy.wait()

            def one(step, carry):
                rows = pl.ds(pl.multiple_of(step * 48, 16), 48)
                self.stage[part % 2, rows, :] = self.shares[part, rows, :].astype(f32)
                return carry

            lax.fori_loop(0, UNIT // 48, one, 0)
            for copy in self.write(part):
                copy.start()
        for part in (6, 7):
            for copy in self.write(part):
                copy.wait()
        for kind, part, lanes, device in (
            (0, me, self.full, xn),
            (1, me, self.full, yn),
            (2, xn, self.head, yn),
            (3, yn, self.tail, xn),
            (4, me, self.full, sib),
            (5, xn, self.full, sib),
            (6, yn, self.full, sib),
            (7, dg, self.full, sib),
        ):
            self.share(part, lanes, kind, device).wait_send()
        for r in range(4):
            for j in range(4):
                self.there(r, j).wait_send()
                self.one(r, j).wait_send()
            for k in range(2):
                self.two(r, k).wait_send()
            if r < 3:
                self.across(r).wait_send()

    def hello(self):
        greet(
            [(self.z, self.sib), (self.z, self.xn), (self.z, self.yn)]
            + [(self.plane[r], self.me) for r in range(3)]
        )
        self.begin(0)
        self.begin(1)

    def slot(self, index, grads, totals, *refs):
        self.bind(grads, totals, *refs)
        plan = {
            0: [self.hello],
            1: [lambda: self.pairs(0), lambda: self.begin(2)],
            2: [lambda: self.pairs(1), lambda: self.begin(3)],
            4: [lambda: self.middle(0)],
            5: [lambda: self.pairs(2)],
            6: [lambda: self.middle(1)],
            7: [lambda: self.finish(0)],
            8: [lambda: self.pairs(3)],
            9: [lambda: self.middle(2), lambda: self.finish(1)],
            11: [lambda: self.finish(2)],
            13: [lambda: self.middle(3)],
            15: [lambda: self.finish(3), self.total],
        }
        for at, actions in plan.items():

            @pl.when(index == at)
            def _():
                for action in actions:
                    action()

    def last(self, grads, totals, *refs):
        self.bind(grads, totals, *refs)
        self.collect()


def small_sum_kernel(
    grads, out_ref, cores, chips, planes, share, total, s_one, r_one, s_two, r_two, s_z, r_z, s_all, r_all
):
    z, me, sib, xn, yn, dg = places()
    core, chip = me % 2, me // 2
    near = (xn, yn, dg)
    others = [lax.rem(z + hop, 4) for hop in (1, 2, 3)]
    greet(
        [(z, sib)]
        + [(z, part) for part in near]
        + [(z, part + 1 - 2 * core) for part in near]
        + [(other, me) for other in others]
    )

    def one(j):
        return remote(
            grads.at[2 * j + 1 - core], cores.at[j], s_one.at[j], r_one.at[j], (z, sib)
        )

    for j in range(4):
        one(j).start()
    for j in range(4):
        one(j).wait()
        both = cores[j].astype(f32) + grads[2 * j + core].astype(f32)
        cores[j] = both.astype(bf16)

    def two(k):
        return remote(cores.at[near[k] // 2], chips.at[k], s_two.at[k], r_two.at[k], (z, near[k]))

    for k in range(3):
        two(k).start()
    both = cores[chip].astype(f32)
    for k in range(3):
        two(k).wait()
        both += chips[k].astype(f32)
    share[...] = both.astype(bf16)

    def three(k):
        return remote(share.at[others[k]], planes.at[k], s_z.at[k], r_z.at[k], (others[k], me))

    for k in range(3):
        three(k).start()
    both = share[z].astype(f32)
    for k in range(3):
        three(k).wait()
        both += planes[k].astype(f32)
    total[me] = both.astype(bf16)

    receivers = [sib] + list(near) + [part + 1 - 2 * core for part in near]

    def four(k, part, device):
        return remote(total.at[part], total.at[part], s_all.at[k], r_all.at[k], (z, device))

    for k, device in enumerate(receivers):
        four(k, me, device).start()
    for k, device in enumerate(receivers):
        four(k, device, device).wait_recv()
    for k, device in enumerate(receivers):
        four(k, me, device).wait_send()
    out_ref[...] = total[...].astype(f32)


def small_sums(grads):
    seq, samp, rows, width = grads.shape
    dma = pltpu.SemaphoreType.DMA
    return pl.pallas_call(
        small_sum_kernel,
        out_shape=jax.ShapeDtypeStruct((seq, rows, width), f32),
        in_specs=[pl.BlockSpec(memory_space=pltpu.VMEM)],
        out_specs=pl.BlockSpec(memory_space=pltpu.VMEM),
        scratch_shapes=[
            pltpu.VMEM((4, samp, rows, width), bf16),
            pltpu.VMEM((3, samp, rows, width), bf16),
            pltpu.VMEM((3, rows, width), bf16),
            pltpu.VMEM((samp, rows, width), bf16),
            pltpu.VMEM((seq, rows, width), bf16),
            dma((4,)),
            dma((4,)),
            dma((3,)),
            dma((3,)),
            dma((3,)),
            dma((3,)),
            dma((7,)),
            dma((7,)),
        ],
        compiler_params=pltpu.CompilerParams(
            vmem_limit_bytes=vmem_bytes, collective_id=3, has_side_effects=True
        ),
        name="small_sums",
    )(grads)


def pair_stats(pairs, fold):
    upper, lower = square_sums(fold, pairs.astype(f32) * pairs.astype(f32))
    features = pairs.shape[0] // WIN_Q
    mean = mm(fold, pairs) * (1.0 / features)
    square = (mm(fold, upper) + mm(fold, lower)) * (1.0 / features)
    var = jnp.maximum(square - mean * mean, 0.0)
    inv_std = lax.rsqrt(var + norm_eps)
    return mean, inv_std


def pair_fold(features):
    shape = (WIN_Q, WIN_Q * features)
    row = lax.broadcasted_iota(jnp.int32, shape, 0)
    column = lax.broadcasted_iota(jnp.int32, shape, 1)
    return jnp.where(column // features == row, 1.0, 0.0).astype(bf16)


def atom_fwd_kernel(
    gather,
    starts,
    ext_ref,
    pairs_ref,
    spread_ref,
    blocked_ref,
    share_ref,
    wide_ref,
    down_ref,
    qbias_ref,
    *refs,
):
    count = len(gather.shapes) if gather is not None else 0
    shards, refs = refs[:count], refs[count:]
    (
        pooled_ref,
        query_ref,
        keyval_ref,
        gate_ref,
        probs_ref,
        attend_ref,
        mid_ref,
    ), refs = refs[:7], refs[7:]
    fulls, refs = refs[:count], refs[count:]
    (bias_s, keys_s, values_s), sems = refs[:3], refs[3:]
    width = ext_ref.shape[-1]
    head_dim = width // ATOM_HEADS
    scale = float(head_dim) ** (-0.5)
    slots = query_ref.shape[1]
    windows = slots // WIN_Q
    hidden_width = down_ref.shape[0]
    model_width = pooled_ref.shape[-1]
    features = pairs_ref.shape[1] // WIN_Q
    sample = pl.program_id(0)
    if gather is not None:
        gather.step(sample, shards, fulls, *sems)

    @pl.when(sample == 0)
    def _():
        fold = pair_fold(features)
        spread = spread_ref[...]
        spread_sum = jnp.sum(spread.astype(f32), -1, keepdims=True)
        first_lane = jnp.where(
            lax.broadcasted_iota(jnp.int32, (ATOM_HEADS * WIN_Q, LANES), 1) == 0, 1.0, 0.0
        ).astype(bf16)

        def one(win, carry):
            pairs = pairs_ref[win]
            mean, inv_std = pair_stats(pairs, fold)
            mean = jnp.concatenate([mean] * ATOM_HEADS, 0)
            inv_std = jnp.concatenate([inv_std] * ATOM_HEADS, 0)
            blocked = blocked_ref[pl.ds(starts[win], WIN_K), :].astype(bf16)
            bias = inv_std * (mm(spread, pairs) - mean * spread_sum)
            bias_s[win] = bias + mm_nt(first_lane, blocked)
            return carry

        lax.fori_loop(0, windows, one, 0)

    rows = ext_ref[0].astype(f32)
    normed_low = norm_stats(rows)[0].astype(bf16)
    key_val = mm(normed_low, wide_ref[:, width : 3 * width]).astype(bf16)
    keyval_ref[0] = key_val
    keys_s[...] = key_val[:, :width].astype(f32)
    values_s[...] = key_val[:, width:].astype(f32)
    own_low = normed_low[RIM : RIM + slots]
    query_ref[0] = (mm(own_low, wide_ref[:, :width]) + qbias_ref[...]).astype(bf16)
    gate_ref[0] = mm(own_low, wide_ref[:, 3 * width : 4 * width])

    def one_window(win):
        first = pl.multiple_of(win * WIN_Q, WIN_Q)
        keys = keys_s[pl.ds(starts[win], WIN_K), :].astype(bf16)
        values = values_s[pl.ds(starts[win], WIN_K), :].astype(bf16)
        stacked = head_stack(query_ref[0, pl.ds(first, WIN_Q), :], ATOM_HEADS, head_dim, 0)
        scores = mm_nt(stacked, keys) * scale + bias_s[win]
        exp_scores = jnp.exp(scores - jnp.max(scores, -1, keepdims=True))
        probs = exp_scores * (1.0 / jnp.sum(exp_scores, -1, keepdims=True))
        probs_low = probs.astype(bf16)
        probs_ref[0, win] = probs_low
        attend = head_fold(mm(probs_low, values), ATOM_HEADS, head_dim, 0)
        attend_ref[0, pl.ds(first, WIN_Q), :] = attend

    def some_windows(step, carry):
        for part in range(4):
            one_window(step * 4 + part)
        return carry

    lax.fori_loop(0, windows // 4, some_windows, 0)

    gated_low = (attend_ref[0] * sigmoid(gate_ref[0])).astype(bf16)
    offset = 4 * width
    upw = wide_ref[:, offset : offset + 2 * hidden_width]
    offset += 2 * hidden_width
    pool_weight = wide_ref[:, offset : offset + model_width]
    outw = wide_ref[:, offset + model_width : offset + model_width + width]
    mid = rows[RIM : RIM + slots] + mm(gated_low, outw)
    mid_ref[0] = mid
    ffn_low = norm_stats(mid)[0].astype(bf16)
    upper = mm(ffn_low, upw)
    first_half, second_half = upper[:, :hidden_width], upper[:, hidden_width:]
    hidden = (first_half * sigmoid(first_half) * second_half).astype(bf16)
    final_low = (mid + mm(hidden, down_ref[...])).astype(bf16)
    pool_pre = mm(final_low, pool_weight)
    share = share_ref[...]
    for lane in range(0, model_width, LANES):
        part = pool_pre[:, lane : lane + LANES]
        part = part * sigmoid(part) * share
        pooled_ref[0, :, lane : lane + LANES] = jnp.sum(
            part.reshape(slots // MAX_ATOMS, MAX_ATOMS, LANES), 1
        )
    if gather is not None:
        gather.last(sample, shards, fulls, *sems)


def atom_forward(ext, starts, pairs, spread, blocked, share, wide, down, qbias, gather, shards):
    samples, ext_slots, width = ext.shape
    slots = ext_slots - 2 * RIM
    tokens = slots // MAX_ATOMS
    windows = slots // WIN_Q
    model_width = wide.shape[1] - 5 * width - 2 * down.shape[0]
    stack = ATOM_HEADS * WIN_Q
    outs = (
        ((tokens, model_width), f32),
        ((slots, width), bf16),
        ((ext_slots, 2 * width), bf16),
        ((slots, width), f32),
        ((windows, stack, WIN_K), bf16),
        ((slots, width), f32),
        ((slots, width), f32),
    )
    place = pl.BlockSpec(memory_space=pl.ANY)
    results = pl.pallas_call(
        functools.partial(atom_fwd_kernel, gather),
        out_shape=[jax.ShapeDtypeStruct((samples,) + shape, kind) for shape, kind in outs]
        + [jax.ShapeDtypeStruct(shape, bf16) for shape in (gather.full_shapes() if gather else [])],
        grid=(samples,),
        in_specs=[
            pl.BlockSpec(memory_space=pltpu.SMEM),
            per_sample((ext_slots, width)),
            whole(pairs.shape),
            whole(spread.shape),
            whole(blocked.shape),
            whole(share.shape),
            whole(wide.shape),
            whole(down.shape),
            whole(qbias.shape),
        ]
        + [place] * len(shards),
        out_specs=[per_sample(shape) for shape, _ in outs] + [place] * len(shards),
        scratch_shapes=[
            pltpu.VMEM((windows, stack, WIN_K), f32),
            pltpu.VMEM((ext_slots, width), f32),
            pltpu.VMEM((ext_slots, width), f32),
        ]
        + (gather.scratch() if gather else []),
        compiler_params=gather.params() if gather else params(),
        name="atom_forward",
    )(starts, ext, pairs, spread, blocked, share, wide, down, qbias, *shards)
    return results[0], results[1:7], results[7:]


def atom_bwd_kernel(
    summing,
    starts,
    grad_ref,
    query_ref,
    keyval_ref,
    gate_ref,
    probs_ref,
    attend_ref,
    mid_ref,
    pairs_ref,
    share_ref,
    wide_ref,
    down_ref,
    *refs,
):
    count = len(summing.shapes) if summing is not None else 0
    grads, refs = refs[: min(count, 1)], refs[min(count, 1) :]
    (
        mix_ref,
        own_ref,
        left_ref,
        right_ref,
        midgrad_ref,
        qbias_ref,
        outw_ref,
        upw_ref,
        downw_ref,
        pool_ref,
        pairw_ref,
        pairm_ref,
    ), refs = refs[:12], refs[12:]
    totals, refs = refs[:count], refs[count:]
    (keys_s, values_s, acck_s, accv_s, bias_s, attlow_s, dq_s), sums = refs[:7], refs[7:]
    width = query_ref.shape[-1]
    head_dim = width // ATOM_HEADS
    scale = float(head_dim) ** (-0.5)
    slots = query_ref.shape[1]
    windows = slots // WIN_Q
    hidden_width = down_ref.shape[0]
    model_width = grad_ref.shape[-1]
    tokens = grad_ref.shape[1]
    sample = pl.program_id(0)
    if summing is not None:
        summing.slot(2 * sample, *grads, totals, *sums)

    @pl.when(sample == 0)
    def _():
        for ref in (qbias_ref, outw_ref, upw_ref, downw_ref, pool_ref, pairw_ref, pairm_ref, bias_s):
            ref[...] = jnp.zeros_like(ref)

    offset = 4 * width
    upw = wide_ref[:, offset : offset + 2 * hidden_width]
    offset += 2 * hidden_width
    pool_weight = wide_ref[:, offset : offset + model_width]
    outw = wide_ref[:, offset + model_width : offset + model_width + width]
    down = down_ref[...]

    mid = mid_ref[0]
    normed_mid, inv_mid = norm_stats(mid)
    ffn_low = normed_mid.astype(bf16)
    upper = mm(ffn_low, upw)
    first_half, second_half = upper[:, :hidden_width], upper[:, hidden_width:]
    sig_first = sigmoid(first_half)
    hidden = (first_half * sig_first * second_half).astype(bf16)
    final_low = (mid + mm(hidden, down)).astype(bf16)
    pool_pre = mm(final_low, pool_weight)
    share = share_ref[...]
    pool_parts = []
    for lane in range(0, model_width, LANES):
        part = pool_pre[:, lane : lane + LANES]
        grad = jnp.broadcast_to(
            grad_ref[0, :, lane : lane + LANES][:, None, :], (tokens, MAX_ATOMS, LANES)
        ).reshape(slots, LANES)
        sig_pool = sigmoid(part)
        pool_parts.append((grad * share * sig_pool * (1.0 + part * (1.0 - sig_pool))).astype(bf16))
    pool_grad = jnp.concatenate(pool_parts, 1)
    final_grad = mm_nt(pool_grad, pool_weight)
    pool_ref[...] += mm_tn(final_low, pool_grad)
    branch_low = final_grad.astype(bf16)
    hidden_grad = mm_nt(branch_low, down)
    first_grad = hidden_grad * second_half * sig_first * (1.0 + first_half * (1.0 - sig_first))
    second_grad = hidden_grad * first_half * sig_first
    upper_grad = jnp.concatenate([first_grad.astype(bf16), second_grad.astype(bf16)], 1)
    downw_ref[...] += mm_tn(hidden, branch_low)
    upw_ref[...] += mm_tn(ffn_low, upper_grad)
    mid_grad = final_grad + norm_back(normed_mid, inv_mid, mm_nt(upper_grad, upw))
    midgrad_ref[0] = mid_grad
    out_low = mid_grad.astype(bf16)
    gated_grad = mm_nt(out_low, outw)
    sig_gate = sigmoid(gate_ref[0])
    attend = attend_ref[0]
    gated_low = (attend * sig_gate).astype(bf16)
    outw_ref[...] += mm_tn(gated_low, out_low)
    attlow_s[...] = (gated_grad * sig_gate).astype(bf16)
    mix_ref[0, :, width:] = (gated_grad * attend * sig_gate * (1.0 - sig_gate)).astype(bf16)

    keys_s[...] = keyval_ref[0, :, :width].astype(f32)
    values_s[...] = keyval_ref[0, :, width:].astype(f32)
    acck_s[...] = jnp.zeros_like(acck_s)
    accv_s[...] = jnp.zeros_like(accv_s)
    if summing is not None:
        summing.slot(2 * sample + 1, *grads, totals, *sums)

    def one_window(win):
        first = pl.multiple_of(win * WIN_Q, WIN_Q)
        start = starts[win]
        keys = keys_s[pl.ds(start, WIN_K), :].astype(bf16)
        values = values_s[pl.ds(start, WIN_K), :].astype(bf16)
        queries = head_stack(query_ref[0, pl.ds(first, WIN_Q), :], ATOM_HEADS, head_dim, 0)
        att = head_stack(attlow_s[pl.ds(first, WIN_Q), :], ATOM_HEADS, head_dim, 0)
        probs_low = probs_ref[0, win]
        probs = probs_low.astype(f32)
        prob_grad = mm_nt(att, values)
        delta = jnp.sum(prob_grad * probs, -1, keepdims=True)
        score_low = (probs * (prob_grad - delta)).astype(bf16)
        bias_s[win] += score_low.astype(f32)
        dq_s[pl.ds(first, WIN_Q), :] = (
            head_fold(mm(score_low, keys), ATOM_HEADS, head_dim, 0) * scale
        )
        shift = start - first
        lane = lax.broadcasted_iota(jnp.int32, probs.shape, 1)

        def placed(values):
            moved = pltpu.roll(values, shift, 1)
            inside = lane >= shift
            return jnp.concatenate(
                [jnp.where(inside, moved, 0.0), jnp.where(inside, 0.0, moved)], 1
            ).astype(bf16)

        rows = pl.ds(first, 2 * WIN_K)
        acck_s[rows, :] += mm_tn(placed(score_low.astype(f32)), queries) * scale
        accv_s[rows, :] += mm_tn(placed(probs), att)

    def some_windows(step, carry):
        for part in range(4):
            one_window(step * 4 + part)
        return carry

    lax.fori_loop(0, windows // 4, some_windows, 0)

    query_grad = dq_s[...]
    qbias_ref[...] += jnp.sum(query_grad, 0, keepdims=True)
    mix_ref[0, :, :width] = query_grad.astype(bf16)
    for ref, low, high in ((own_ref, RIM, RIM + slots), (left_ref, 0, RIM), (right_ref, RIM + slots, slots + 2 * RIM)):
        ref[0, :, :width] = acck_s[low:high, :].astype(ref.dtype)
        ref[0, :, width:] = accv_s[low:high, :].astype(ref.dtype)

    @pl.when(sample == pl.num_programs(0) - 1)
    def _():
        fold = pair_fold(pairs_ref.shape[1] // WIN_Q)

        def one(win, carry):
            pairs = pairs_ref[win]
            mean, inv_std = pair_stats(pairs, fold)
            scaled = bias_s[win] * jnp.concatenate([inv_std] * ATOM_HEADS, 0)
            pairm_ref[...] += scaled * jnp.concatenate([mean] * ATOM_HEADS, 0)
            upper = scaled.astype(bf16)
            lower = (scaled - upper.astype(f32)).astype(bf16)
            pairw_ref[...] += mm_nt(upper, pairs) + mm_nt(lower, pairs)
            return carry

        lax.fori_loop(0, windows, one, 0)
        if summing is not None:
            summing.last(*grads, totals, *sums)


def atom_backward(grad, starts, stored, pairs, share, wide, down, summing, weight_grad_units):
    query, keyval, gate, probs, attend, mid = stored
    samples, slots, width = query.shape
    ext_slots = slots + 2 * RIM
    windows = slots // WIN_Q
    model_width = grad.shape[-1]
    hidden_width = down.shape[0]
    stack = ATOM_HEADS * WIN_Q
    outs = (
        ((slots, 2 * width), bf16),
        ((slots, 2 * width), f32),
        ((RIM, 2 * width), bf16),
        ((RIM, 2 * width), bf16),
        ((slots, width), f32),
    )
    totals = (
        (1, width),
        (width, width),
        (width, 2 * hidden_width),
        (hidden_width, width),
        (width, model_width),
        (stack, pairs.shape[1]),
        (stack, WIN_K),
    )
    place = pl.BlockSpec(memory_space=pl.ANY)
    sums = summing.shapes if summing else []
    results = pl.pallas_call(
        functools.partial(atom_bwd_kernel, summing),
        out_shape=[jax.ShapeDtypeStruct((samples,) + shape, kind) for shape, kind in outs]
        + [jax.ShapeDtypeStruct(shape, f32) for shape in list(totals) + list(sums)],
        grid=(samples,),
        in_specs=[pl.BlockSpec(memory_space=pltpu.SMEM), per_sample(grad.shape[1:])]
        + [per_sample(part.shape[1:]) for part in stored]
        + [whole(part.shape) for part in (pairs, share, wide, down)]
        + [place] * len(weight_grad_units),
        out_specs=[per_sample(shape) for shape, _ in outs]
        + [whole(shape) for shape in totals]
        + [place] * len(sums),
        scratch_shapes=[
            pltpu.VMEM((ext_slots, width), f32),
            pltpu.VMEM((ext_slots, width), f32),
            pltpu.VMEM((slots + 2 * WIN_K, width), f32),
            pltpu.VMEM((slots + 2 * WIN_K, width), f32),
            pltpu.VMEM((windows, stack, WIN_K), f32),
            pltpu.VMEM((slots, width), bf16),
            pltpu.VMEM((slots, width), f32),
        ]
        + (summing.scratch() if summing else []),
        compiler_params=summing.params() if summing else params(),
        name="atom_backward",
    )(starts, grad, *stored, pairs, share, wide, down, *weight_grad_units)
    return results[:12], results[12:]


def atom_input_kernel(
    rows_ref, mix_ref, own_ref, left_ref, right_ref, midgrad_ref, wide_ref, grad_ref, proj_ref
):
    width = rows_ref.shape[-1]

    @pl.when(pl.program_id(0) == 0)
    def _():
        proj_ref[...] = jnp.zeros_like(proj_ref)

    normed, inv_std = norm_stats(rows_ref[0].astype(f32))
    slots = normed.shape[0]
    own = own_ref[0]
    head = own[:RIM] + left_ref[0].astype(f32)
    tail = own[slots - RIM :] + right_ref[0].astype(f32)
    own = jnp.concatenate([head, own[RIM : slots - RIM], tail], 0).astype(bf16)
    mix = jnp.concatenate([mix_ref[0, :, :width], own, mix_ref[0, :, width:]], 1)
    proj_ref[...] += mm_tn(normed.astype(bf16), mix)
    normed_grad = mm_nt(mix, wide_ref[:, : 4 * width])
    grad_ref[0] = midgrad_ref[0] + norm_back(normed, inv_std, normed_grad)


def atom_input_backward(rows, mix, own, left, right, midgrad, wide):
    samples, slots, width = rows.shape
    return pl.pallas_call(
        atom_input_kernel,
        out_shape=[
            jax.ShapeDtypeStruct(rows.shape, f32),
            jax.ShapeDtypeStruct((width, 4 * width), f32),
        ],
        grid=(samples,),
        in_specs=[per_sample(part.shape[1:]) for part in (rows, mix, own, left, right, midgrad)]
        + [whole(wide.shape)],
        out_specs=[per_sample((slots, width)), whole((width, 4 * width))],
        compiler_params=params(),
        name="atom_input_backward",
    )(rows, mix, own, left, right, midgrad, wide)


def row_stats(pairs, ones_op, weights):
    count = weights.shape[0]
    both = mm_nt(jnp.concatenate([weights, ones_op], 0), pairs)
    upper, lower = square_sums(ones_op, pairs.astype(f32) * pairs.astype(f32))
    features = pairs.shape[1]
    mean = both[count : count + 1] * (1.0 / features)
    square = (mm_nt(ones_op, upper) + mm_nt(ones_op, lower))[:1] * (1.0 / features)
    var = jnp.maximum(square - mean * mean, 0.0)
    return both[:count], mean, lax.rsqrt(var + norm_eps)


def pair_bias_kernel(pair_ref, weight_ref, bias_ref):
    weights = weight_ref[...]
    ones_op = jnp.ones((16, weights.shape[1]), bf16)
    weight_sum = jnp.sum(weights.astype(f32), -1, keepdims=True)
    for row in range(pair_ref.shape[0]):
        product, mean, inv_std = row_stats(pair_ref[row], ones_op, weights)
        bias_ref[:, row, :] = inv_std * (product - mean * weight_sum)


def pair_bias(pairs, weights):
    rows, keys, features = pairs.shape
    heads = weights.shape[0]
    return pl.pallas_call(
        pair_bias_kernel,
        out_shape=jax.ShapeDtypeStruct((heads, rows, keys), f32),
        grid=(rows // 8,),
        in_specs=[pl.BlockSpec((8, keys, features), lambda i: (i, 0, 0)), whole(weights.shape)],
        out_specs=pl.BlockSpec((heads, 8, keys), lambda i: (0, i, 0)),
        compiler_params=params(),
        name="pair_bias",
    )(pairs, weights)


def pair_grad_kernel(pair_ref, grad_ref, weight_ref, total_ref, mean_ref):
    @pl.when(pl.program_id(0) == 0)
    def _():
        total_ref[...] = jnp.zeros_like(total_ref)
        mean_ref[...] = jnp.zeros_like(mean_ref)

    heads = grad_ref.shape[0]
    ones_op = jnp.ones((16, pair_ref.shape[2]), bf16)
    total = jnp.zeros(total_ref.shape, f32)
    means = jnp.zeros(mean_ref.shape, f32)
    for row in range(pair_ref.shape[0]):
        pairs = pair_ref[row]
        _, mean, inv_std = row_stats(pairs, ones_op, weight_ref[...])
        scaled = grad_ref[:, row, :] * inv_std
        means += scaled * mean
        upper = scaled.astype(bf16)
        lower = (scaled - upper.astype(f32)).astype(bf16)
        both = mm(jnp.concatenate([upper, lower], 0), pairs)
        total += both[:heads] + both[heads:]
    total_ref[...] += total
    mean_ref[...] += means


def pair_grad(pairs, grads, weights):
    rows, keys, features = pairs.shape
    heads = grads.shape[0]
    total, means = pl.pallas_call(
        pair_grad_kernel,
        out_shape=[
            jax.ShapeDtypeStruct((heads, features), f32),
            jax.ShapeDtypeStruct((heads, keys), f32),
        ],
        grid=(rows // 8,),
        in_specs=[
            pl.BlockSpec((8, keys, features), lambda i: (i, 0, 0)),
            pl.BlockSpec((heads, 8, keys), lambda i: (0, i, 0)),
            whole(weights.shape),
        ],
        out_specs=[whole((heads, features)), whole((heads, keys))],
        compiler_params=params(),
        name="pair_grad",
    )(pairs, grads, weights)
    return total - jnp.sum(means, -1, keepdims=True)


def head_groups(width, heads):
    head_dim = width // heads
    groups = []
    for head in range(0, heads, 4):
        low = head * head_dim
        base = low // LANES * LANES
        groups.append((head, base, low - base))
    return head_dim, groups


def token_fwd_kernel(query_ref, keyval_ref, bias_ref, attend_ref, probs_ref, fold_s):
    tokens, width = query_ref.shape[1:]
    heads = bias_ref.shape[0]
    keys = bias_ref.shape[2]
    head_dim, groups = head_groups(width, heads)
    scale = float(head_dim) ** (-0.5)
    fold_s[...] = jnp.zeros_like(fold_s)
    for head, base, first in groups:
        span = slice(base, base + 256)
        key_rows = keyval_ref[:, 0, :, base : base + 256].reshape(keys, 256)
        value_rows = keyval_ref[:, 0, :, width + base : width + base + 256].reshape(keys, 256)
        stacked = head_stack(query_ref[0, :, span], 4, head_dim, first)
        bias = bias_ref[head : head + 4].reshape(4 * tokens, keys)
        scores = mm_nt(stacked, key_rows) * scale + bias
        exp_scores = jnp.exp(scores - jnp.max(scores, -1, keepdims=True))
        probs = exp_scores * (1.0 / jnp.sum(exp_scores, -1, keepdims=True))
        probs_low = probs.astype(bf16)
        probs_ref[0, head : head + 4] = probs_low.reshape(4, tokens, keys)
        fold_s[:, span] += head_fold(mm(probs_low, value_rows), 4, head_dim, first)
    attend_ref[0] = fold_s[...]


def token_attention(query, keyval, bias):
    samples, tokens, width = query.shape
    heads, _, keys = bias.shape
    devices = keyval.shape[0]
    return pl.pallas_call(
        token_fwd_kernel,
        out_shape=[
            jax.ShapeDtypeStruct(query.shape, f32),
            jax.ShapeDtypeStruct((samples, heads, tokens, keys), bf16),
        ],
        grid=(samples,),
        in_specs=[
            per_sample((tokens, width)),
            pl.BlockSpec((devices, 1, tokens, 2 * width), lambda b: (0, b, 0, 0)),
            whole(bias.shape),
        ],
        out_specs=[per_sample((tokens, width)), per_sample((heads, tokens, keys))],
        scratch_shapes=[pltpu.VMEM((tokens, width), f32)],
        compiler_params=params(),
        name="token_attention",
    )(query, keyval, bias)


def token_bwd_kernel(
    query_ref, keyval_ref, probs_ref, att_ref, dq_ref, dkv_ref, bias_ref, fold_s, grad_s
):
    tokens, width = query_ref.shape[1:]
    heads, _, keys = bias_ref.shape
    devices = keyval_ref.shape[0]
    head_dim, groups = head_groups(width, heads)
    scale = float(head_dim) ** (-0.5)

    @pl.when(pl.program_id(0) == 0)
    def _():
        bias_ref[...] = jnp.zeros_like(bias_ref)

    fold_s[...] = jnp.zeros_like(fold_s)
    grad_s[...] = jnp.zeros_like(grad_s)
    for head, base, first in groups:
        span = slice(base, base + 256)
        key_rows = keyval_ref[:, 0, :, base : base + 256].reshape(keys, 256)
        value_rows = keyval_ref[:, 0, :, width + base : width + base + 256].reshape(keys, 256)
        queries = head_stack(query_ref[0, :, span], 4, head_dim, first)
        att = head_stack(att_ref[0, :, span], 4, head_dim, first)
        probs_low = probs_ref[0, head : head + 4].reshape(4 * tokens, keys)
        probs = probs_low.astype(f32)
        prob_grad = mm_nt(att, value_rows)
        delta = jnp.sum(prob_grad * probs, -1, keepdims=True)
        score_low = (probs * (prob_grad - delta)).astype(bf16)
        bias_ref[head : head + 4] += score_low.astype(f32).reshape(4, tokens, keys)
        fold_s[:, span] += head_fold(mm(score_low, key_rows), 4, head_dim, first) * scale
        grad_s[:, span] += mm_tn(score_low, queries) * scale
        grad_s[:, width + base : width + base + 256] += mm_tn(probs_low, att)
    dq_ref[0] = fold_s[...]
    dkv_ref[:, 0] = grad_s[...].astype(bf16).reshape(devices, tokens, 2 * width)


def token_attention_back(query, keyval, probs, att):
    samples, tokens, width = query.shape
    heads, _, keys = probs.shape[1:]
    devices = keyval.shape[0]
    return pl.pallas_call(
        token_bwd_kernel,
        out_shape=[
            jax.ShapeDtypeStruct(query.shape, f32),
            jax.ShapeDtypeStruct(keyval.shape, bf16),
            jax.ShapeDtypeStruct((heads, tokens, keys), f32),
        ],
        grid=(samples,),
        in_specs=[
            per_sample((tokens, width)),
            pl.BlockSpec((devices, 1, tokens, 2 * width), lambda b: (0, b, 0, 0)),
            per_sample((heads, tokens, keys)),
            per_sample((tokens, width)),
        ],
        out_specs=[
            per_sample((tokens, width)),
            pl.BlockSpec((devices, 1, tokens, 2 * width), lambda b: (0, b, 0, 0)),
            whole((heads, tokens, keys)),
        ],
        scratch_shapes=[
            pltpu.VMEM((tokens, width), f32),
            pltpu.VMEM((keys, 2 * width), f32),
        ],
        compiler_params=params(),
        name="token_attention_back",
    )(query, keyval, probs, att)


def attend_groups(heads, width, tokens, query, keyval, bias, probs_ref, fold_s):
    head_dim, groups = head_groups(width, heads)
    scale = float(head_dim) ** (-0.5)
    fold_s[...] = jnp.zeros_like(fold_s)
    for head, base, first in groups:
        span = slice(base, base + 256)
        stacked = head_stack(query[:, span], 4, head_dim, first)
        scores = mm_nt(stacked, keyval(base)) * scale + bias(head)
        exp_scores = jnp.exp(scores - jnp.max(scores, -1, keepdims=True))
        probs = exp_scores * (1.0 / jnp.sum(exp_scores, -1, keepdims=True))
        probs_low = probs.astype(bf16)
        probs_ref[0, head : head + 4] = probs_low.reshape(4, tokens, -1)
        fold_s[:, span] += head_fold(mm(probs_low, keyval(width + base)), 4, head_dim, first)


def gather_attend_kernel(
    query_ref,
    own_ref,
    pair_ref,
    weight_ref,
    attend_ref,
    probs_ref,
    keyval_ref,
    stats_ref,
    all_s,
    bias_s,
    fold_s,
    send,
    recv,
    load,
):
    z, me, sib, xn, yn, dg = places()
    step = pl.program_id(0)
    tokens, width = query_ref.shape[1:]
    heads = weight_ref.shape[0]
    devices, samples = all_s.shape[:2]
    keys = devices * tokens
    head, tail, full = slice(0, width), slice(width, 2 * width), slice(0, 2 * width)

    def unit(part, sample, lanes, kind, device):
        ref = all_s.at[part, sample, :, lanes]
        return remote(ref, ref, send.at[kind, sample], recv.at[kind, sample], (z, device))

    def issue(sample):
        unit(me, sample, full, 0, xn).start()
        unit(me, sample, full, 1, yn).start()
        unit(me, sample, full, 4, sib).start()

    def relay(sample):
        unit(xn, sample, full, 0, xn).wait_recv()
        unit(xn, sample, head, 2, yn).start()
        unit(xn, sample, full, 5, sib).start()
        unit(yn, sample, full, 1, yn).wait_recv()
        unit(yn, sample, tail, 3, xn).start()
        unit(yn, sample, full, 6, sib).start()

    def collect(sample):
        unit(dg, sample, head, 2, yn).wait_recv()
        unit(dg, sample, tail, 3, xn).wait_recv()
        unit(dg, sample, full, 7, sib).start()

    @pl.when(step == 0)
    def _():
        copy = pltpu.make_async_copy(own_ref, all_s.at[me], load)
        copy.start()
        greet([(z, sib), (z, xn), (z, yn)])
        copy.wait()
        issue(0)
        issue(1)

    @pl.when((step >= 1) & (step + 1 < samples))
    def _():
        issue(step + 1)

    @pl.when((step >= 1) & (step - 1 < samples))
    def _():
        relay(step - 1)

    @pl.when(step < 2)
    def _():
        weights = weight_ref[...]
        ones_op = jnp.ones((16, weights.shape[1]), bf16)
        weight_sum = jnp.sum(weights.astype(f32), -1, keepdims=True)
        groups = pair_ref.shape[0] // 8

        def one(group, carry):
            for row in range(8):
                product, mean, inv_std = row_stats(pair_ref[group * 8 + row], ones_op, weights)
                place = step * groups + group
                bias_s[:, place, row, :] = inv_std * (product - mean * weight_sum)
                stats_ref[0, place, row : row + 1, :] = mean
                stats_ref[1, place, row : row + 1, :] = inv_std
            return carry

        lax.fori_loop(0, groups, one, 0)

    @pl.when(step >= 2)
    def _():
        sample = step - 2
        collect(sample)
        for kind, part in ((4, sib), (5, sib), (6, sib), (7, sib)):
            unit(part, sample, full, kind, sib).wait_recv()
        for part in range(devices):
            keyval_ref[part, 0] = all_s[part, sample]
        attend_groups(
            heads,
            width,
            tokens,
            query_ref[0],
            lambda base: keyval_ref[:, 0, :, base : base + 256].reshape(keys, 256),
            lambda head: bias_s[head : head + 4].reshape(4 * tokens, keys),
            probs_ref,
            fold_s,
        )
        attend_ref[0] = fold_s[...]

    @pl.when(step == pl.num_programs(0) - 1)
    def _():
        def sent(sample, carry):
            for kind in (0, 1, 4, 5, 6, 7):
                unit(me, sample, full, kind, sib).wait_send()
            unit(me, sample, head, 2, sib).wait_send()
            unit(me, sample, tail, 3, sib).wait_send()
            return carry

        lax.fori_loop(0, samples, sent, 0)


def gather_attend(query, own, pairs, weights, seq):
    samples, tokens, width = query.shape
    heads, features = weights.shape
    keys = seq * tokens
    late = lambda g: jnp.maximum(g - 2, 0)
    sample_block = lambda shape: pl.BlockSpec((1,) + shape, lambda g: (late(g),) + (0,) * len(shape))
    dma = pltpu.SemaphoreType.DMA
    return pl.pallas_call(
        gather_attend_kernel,
        out_shape=[
            jax.ShapeDtypeStruct(query.shape, f32),
            jax.ShapeDtypeStruct((samples, heads, tokens, keys), bf16),
            jax.ShapeDtypeStruct((seq, samples, tokens, 2 * width), bf16),
            jax.ShapeDtypeStruct((2, tokens // 8, 8, keys), f32),
        ],
        grid=(samples + 2,),
        in_specs=[
            sample_block((tokens, width)),
            pl.BlockSpec(memory_space=pl.ANY),
            pl.BlockSpec((tokens // 2, keys, features), lambda g: (jnp.minimum(g, 1), 0, 0)),
            whole(weights.shape),
        ],
        out_specs=[
            sample_block((tokens, width)),
            sample_block((heads, tokens, keys)),
            pl.BlockSpec((seq, 1, tokens, 2 * width), lambda g: (0, late(g), 0, 0)),
            whole((2, tokens // 8, 8, keys)),
        ],
        scratch_shapes=[
            pltpu.VMEM((seq, samples, tokens, 2 * width), bf16),
            pltpu.VMEM((heads, tokens // 8, 8, keys), f32),
            pltpu.VMEM((tokens, width), f32),
            dma((8, samples)),
            dma((8, samples)),
            dma,
        ],
        compiler_params=pltpu.CompilerParams(
            vmem_limit_bytes=vmem_bytes, collective_id=4, has_side_effects=True
        ),
        name="gather_attend",
    )(query, own, pairs, weights)


def attend_back_scatter_kernel(
    query_ref,
    keyval_ref,
    probs_ref,
    att_ref,
    pair_ref,
    stats_ref,
    ffn_ref,
    upper_ref,
    hidden_ref,
    two_ref,
    gated_ref,
    branch_ref,
    dq_ref,
    dkv_ref,
    pairw_ref,
    pairm_ref,
    upw_ref,
    downw_ref,
    outw_ref,
    fold_s,
    grad_s,
    bias_s,
    mine,
    theirs,
    from_x,
    from_y,
    last_x,
    last_y,
    s_sib,
    r_sib,
    s_one,
    r_one,
    s_two,
    r_two,
):
    z, me, sib, xn, yn, dg = places()
    core, chip = me % 2, me // 2
    chip_x, chip_y, chip_d = xn // 2, yn // 2, dg // 2
    step = pl.program_id(0)
    tokens, width = query_ref.shape[1:]
    samples = mine.shape[0]
    heads, keys = probs_ref.shape[1], probs_ref.shape[3]
    head_dim, groups = head_groups(width, heads)
    scale = float(head_dim) ** (-0.5)
    head, tail = slice(0, width), slice(width, 2 * width)

    def there(b):
        return remote(
            mine.at[b, :, 1 - core], theirs.at[b], s_sib.at[b], r_sib.at[b], (z, sib)
        )

    def one(b, k):
        part = (chip_x, chip_d, chip_y, chip_d)[k]
        lanes = head if k < 2 else tail
        target = (from_x if k < 2 else from_y).at[b, k % 2]
        device = xn if k < 2 else yn
        source = mine.at[b, part, core, :, lanes]
        return remote(source, target, s_one.at[b, k], r_one.at[b, k], (z, device))

    def two(b, k):
        part, lanes, target, device = ((chip_y, head, last_y, yn), (chip_x, tail, last_x, xn))[k]
        source = mine.at[b, part, core, :, lanes]
        return remote(source, target.at[b], s_two.at[b, k], r_two.at[b, k], (z, device))

    def add(b, part, lanes, source):
        both = mine[b, part, core, :, lanes].astype(f32) + source.astype(f32)
        mine[b, part, core, :, lanes] = both.astype(bf16)

    @pl.when(step == 0)
    def _():
        greet([(z, sib), (z, xn), (z, yn)])
        bias_s[...] = jnp.zeros_like(bias_s)
        pairw_ref[...] = jnp.zeros_like(pairw_ref)
        pairm_ref[...] = jnp.zeros_like(pairm_ref)

    @pl.when((step >= 1) & (step - 1 < samples))
    def _():
        b = step - 1
        there(b).wait_recv()

        def chips(j, carry):
            add(b, j, slice(0, 2 * width), theirs[b, j])
            return carry

        lax.fori_loop(0, 4, chips, 0)
        for k in range(4):
            one(b, k).start()

    @pl.when((step >= 2) & (step - 2 < samples))
    def _():
        b = step - 2
        one(b, 1).wait_recv()
        add(b, chip_y, head, from_x[b, 1])
        two(b, 0).start()
        one(b, 3).wait_recv()
        add(b, chip_x, tail, from_y[b, 1])
        two(b, 1).start()
        one(b, 0).wait_recv()
        add(b, chip, head, from_x[b, 0])
        one(b, 2).wait_recv()
        add(b, chip, tail, from_y[b, 0])

    @pl.when((step >= 3) & (step - 3 < samples))
    def _():
        b = step - 3
        two(b, 0).wait_recv()
        add(b, chip, head, last_y[b])
        two(b, 1).wait_recv()
        add(b, chip, tail, last_x[b])
        dkv_ref[0] = mine[b, chip, core]

    @pl.when(step < samples)
    def _():
        fold_s[...] = jnp.zeros_like(fold_s)
        grad_s[...] = jnp.zeros_like(grad_s)
        for first_head, base, first in groups:
            span = slice(base, base + 256)
            key_rows = keyval_ref[:, 0, :, base : base + 256].reshape(keys, 256)
            value_rows = keyval_ref[:, 0, :, width + base : width + base + 256].reshape(keys, 256)
            queries = head_stack(query_ref[0, :, span], 4, head_dim, first)
            att = head_stack(att_ref[0, :, span], 4, head_dim, first)
            probs_low = probs_ref[0, first_head : first_head + 4].reshape(4 * tokens, keys)
            probs = probs_low.astype(f32)
            prob_grad = mm_nt(att, value_rows)
            delta = jnp.sum(prob_grad * probs, -1, keepdims=True)
            score_low = (probs * (prob_grad - delta)).astype(bf16)
            bias_s[first_head : first_head + 4] += score_low.astype(f32).reshape(
                4, tokens // 8, 8, keys
            )
            fold_s[:, span] += head_fold(mm(score_low, key_rows), 4, head_dim, first) * scale
            grad_s[:, span] += mm_tn(score_low, queries) * scale
            grad_s[:, width + base : width + base + 256] += mm_tn(probs_low, att)
        dq_ref[0] = fold_s[...]
        mine[step] = grad_s[...].astype(bf16).reshape(mine.shape[1:])
        there(step).start()
        upw_ref[...] = mm_tn(ffn_ref[...], upper_ref[...]).astype(bf16)

    @pl.when(step < 6)
    def _():
        downw_ref[...] = mm_tn(hidden_ref[...], two_ref[...]).astype(bf16)

    @pl.when((step >= 6) & (step < 8))
    def _():
        outw_ref[...] = mm_tn(gated_ref[...], branch_ref[...]).astype(bf16)

    @pl.when((step >= samples) & (step < samples + 2))
    def _():
        rows = pair_ref.shape[0] // 8

        def some(group, carry):
            total, means = carry
            place = (step - samples) * rows + group
            for row in range(8):
                inv_std = stats_ref[1, place, row : row + 1, :]
                scaled = bias_s[:, place, row, :] * inv_std
                means += scaled * stats_ref[0, place, row : row + 1, :]
                upper = scaled.astype(bf16)
                lower = (scaled - upper.astype(f32)).astype(bf16)
                both = mm(jnp.concatenate([upper, lower], 0), pair_ref[group * 8 + row])
                total += both[:heads] + both[heads:]
            return total, means

        zeros = (jnp.zeros(pairw_ref.shape, f32), jnp.zeros(pairm_ref.shape, f32))
        total, means = lax.fori_loop(0, rows, some, zeros)
        pairw_ref[...] += total
        pairm_ref[...] += means

    @pl.when(step == pl.num_programs(0) - 1)
    def _():
        def sent(b, carry):
            there(b).wait_send()
            for k in range(4):
                one(b, k).wait_send()
            for k in range(2):
                two(b, k).wait_send()
            return carry

        lax.fori_loop(0, samples, sent, 0)


def attend_back_scatter(query, keyval, probs, att, pairs, stats, ffn, upper, hidden, two, gated, branch):
    samples, tokens, width = query.shape
    heads, _, keys = probs.shape[1:]
    seq = keyval.shape[0]
    features = pairs.shape[-1]
    flat = [part.reshape(-1, part.shape[-1]) for part in (ffn, upper, hidden, two, gated, branch)]
    rows = flat[0].shape[0]
    held = lambda g: jnp.minimum(g, samples - 1)
    late = lambda g: jnp.clip(g - 3, 0, samples - 1)
    pair_step = lambda g: jnp.clip(g - samples, 0, 1)
    up_step = lambda g: jnp.minimum(g, seq - 1)
    down_step = lambda g: jnp.minimum(g, 5)
    out_step = lambda g: jnp.clip(g - 6, 0, 1)
    sample_block = lambda shape, at: pl.BlockSpec((1,) + shape, lambda g: (at(g),) + (0,) * len(shape))
    keyval_block = pl.BlockSpec((seq, 1, tokens, 2 * width), lambda g: (0, held(g), 0, 0))
    up_width = flat[1].shape[1] // seq
    hidden_width = flat[2].shape[1]
    dma = pltpu.SemaphoreType.DMA
    results = pl.pallas_call(
        attend_back_scatter_kernel,
        out_shape=[
            jax.ShapeDtypeStruct(query.shape, f32),
            jax.ShapeDtypeStruct((samples, tokens, 2 * width), bf16),
            jax.ShapeDtypeStruct((heads, features), f32),
            jax.ShapeDtypeStruct((heads, keys), f32),
            jax.ShapeDtypeStruct((width, flat[1].shape[1]), bf16),
            jax.ShapeDtypeStruct((hidden_width, width), bf16),
            jax.ShapeDtypeStruct((width, width), bf16),
        ],
        grid=(samples + 3,),
        in_specs=[
            sample_block((tokens, width), held),
            keyval_block,
            sample_block((heads, tokens, keys), held),
            sample_block((tokens, width), held),
            pl.BlockSpec((tokens // 2, keys, features), lambda g: (pair_step(g), 0, 0)),
            whole(stats.shape),
            whole(flat[0].shape),
            pl.BlockSpec((rows, up_width), lambda g: (0, up_step(g))),
            pl.BlockSpec((rows, 256), lambda g: (0, down_step(g))),
            whole(flat[3].shape),
            pl.BlockSpec((rows, width // 2), lambda g: (0, out_step(g))),
            whole(flat[5].shape),
        ],
        out_specs=[
            sample_block((tokens, width), held),
            sample_block((tokens, 2 * width), late),
            whole((heads, features)),
            whole((heads, keys)),
            pl.BlockSpec((width, up_width), lambda g: (0, up_step(g))),
            pl.BlockSpec((256, width), lambda g: (down_step(g), 0)),
            pl.BlockSpec((width // 2, width), lambda g: (out_step(g), 0)),
        ],
        scratch_shapes=[
            pltpu.VMEM((tokens, width), f32),
            pltpu.VMEM((keys, 2 * width), f32),
            pltpu.VMEM((heads, tokens // 8, 8, keys), f32),
            pltpu.VMEM((samples, seq // 2, 2, tokens, 2 * width), bf16),
            pltpu.VMEM((samples, seq // 2, tokens, 2 * width), bf16),
            pltpu.VMEM((samples, 2, tokens, width), bf16),
            pltpu.VMEM((samples, 2, tokens, width), bf16),
            pltpu.VMEM((samples, tokens, width), bf16),
            pltpu.VMEM((samples, tokens, width), bf16),
            dma((samples,)),
            dma((samples,)),
            dma((samples, 4)),
            dma((samples, 4)),
            dma((samples, 2)),
            dma((samples, 2)),
        ],
        compiler_params=pltpu.CompilerParams(
            vmem_limit_bytes=60 << 20, collective_id=5, has_side_effects=True
        ),
        name="attend_back_scatter",
    )(query, keyval, probs, att, pairs, stats, *flat)
    dq, dkv, total, means, upw, downw, outw = results
    return dq, dkv, total - jnp.sum(means, -1, keepdims=True), (upw, downw, outw)


def to_blocks(array, width):
    return [array[:, low : low + width] for low in range(0, array.shape[1], width)]


def pack_blocks(arrays, width):
    parts = []
    for array in arrays:
        parts += to_blocks(array, width)
    return jnp.concatenate(parts, 0)


def unpack_blocks(packed, shapes, width):
    arrays, low = [], 0
    for rows, columns in shapes:
        parts = []
        for _ in range(columns // width):
            parts.append(packed[low : low + rows])
            low += rows
        arrays.append(jnp.concatenate(parts, 1) if len(parts) > 1 else parts[0])
    return arrays


def sum_shares(grads, extra):
    samp, seq = lax.axis_size("samp"), lax.axis_size("seq")
    width = grads[2].shape[1]
    shapes = [(grad.shape[0] // samp, grad.shape[1]) for grad in grads]
    packed = jnp.concatenate(
        [
            block.astype(bf16).reshape(samp, -1, width)
            for grad in grads
            for block in to_blocks(grad, width)
        ]
        + [extra.astype(bf16).reshape(samp, -1, width)],
        1,
    )
    rows = packed.shape[1]
    packed = packed.reshape(samp, seq, rows // seq, width).transpose(1, 0, 2, 3)
    part = lax.psum_scatter(packed, "seq", scatter_dimension=0, tiled=False)
    part = lax.psum_scatter(part, "samp", scatter_dimension=0, tiled=False)
    packed = lax.all_gather(part, "seq", axis=0, tiled=True).astype(f32)
    shares = unpack_blocks(packed, shapes, width)
    return shares, packed[sum(r * (c // width) for r, c in shapes) :]


def local(
    atom_input,
    token_input,
    atom_counts,
    key_offsets,
    atom_pairs,
    pair_features,
    single_features,
    noise_levels,
    noise_direction,
    atom_proj,
    atom_qbias,
    atom_pairw,
    atom_outw,
    atom_upw,
    atom_downw,
    pool_weight,
    cond_weight,
    cond_bias,
    token_proj,
    token_qbias,
    token_pairw,
    token_outw,
    token_upw,
    token_downw,
    cotangent,
):
    samp, seq = lax.axis_size("samp"), lax.axis_size("seq")
    seq_pos = lax.axis_index("seq")
    samples, slots, atom_width = atom_input.shape
    tokens, width = token_input.shape[1:]
    features = atom_pairs.shape[-1]

    half = atom_downw.shape[0] // 2
    wide_own = jnp.concatenate(
        [atom_proj, atom_upw, pool_weight, atom_outw, atom_downw[:half], atom_downw[half:]], 1
    )
    tiny_own = jnp.concatenate(
        [
            atom_qbias,
            cond_bias,
            token_qbias,
            atom_pairw.reshape(-1),
            token_pairw.reshape(-1),
        ]
    )
    tiny_own = jnp.pad(tiny_own, (0, -tiny_own.size % (16 * LANES))).reshape(-1, LANES)
    large = (token_proj, token_upw, token_downw, cond_weight, token_outw)
    kernels = samples == 8 and WeightGather.fits([part.shape for part in large], samp, seq)
    up_pairs = [(i, i + 1) for i in range(seq - 1)]
    down_pairs = [(i + 1, i) for i in range(seq - 1)]
    if kernels:
        wide_all, tiny_all, ext = edges(wide_own, tiny_own, atom_input)
    else:
        wide_all = lax.all_gather(wide_own, "samp", axis=0, tiled=True)
        tiny_all = lax.all_gather(tiny_own, "samp", axis=0, tiled=True)
        before = lax.ppermute(atom_input[:, slots - RIM :], "seq", up_pairs)
        after = lax.ppermute(atom_input[:, :RIM], "seq", down_pairs)
        ext = jnp.concatenate([before, atom_input, after], 1)
    tiny_all = tiny_all.reshape(samp, -1)
    wide = wide_all[:, : -2 * atom_width]
    down = (
        wide_all[:, -2 * atom_width :]
        .reshape(samp, half, 2, atom_width)
        .transpose(0, 2, 1, 3)
        .reshape(-1, atom_width)
    )
    sizes = [atom_qbias.size, cond_bias.size, token_qbias.size, atom_pairw.size, token_pairw.size]
    cuts = [sum(sizes[:i]) for i in range(6)]
    tiny = [tiny_all[:, cuts[i] : cuts[i + 1]] for i in range(5)]
    atom_qb = tiny[0].reshape(1, -1).astype(f32)
    cond_b = tiny[1].reshape(-1)
    token_qb = tiny[2].reshape(-1)
    atom_pw = tiny[3].reshape(features, ATOM_HEADS)
    token_pw = tiny[4].reshape(-1, token_pairw.shape[1])

    rim_tokens = RIM // MAX_ATOMS
    counts = lax.dynamic_slice_in_dim(
        jnp.pad(atom_counts, (rim_tokens, rim_tokens)), seq_pos * tokens, tokens + 2 * rim_tokens
    )
    place = jnp.arange(MAX_ATOMS, dtype=jnp.int32)
    used = place[None, :] < counts[:, None]
    blocked = jnp.where(used, 0.0, masked_score).astype(f32).reshape(-1, 1)
    blocked = jnp.broadcast_to(blocked, (blocked.shape[0], LANES))
    own_counts = counts[rim_tokens : rim_tokens + tokens]
    share = used[rim_tokens : rim_tokens + tokens].astype(f32) / own_counts[:, None].astype(f32)
    share = jnp.broadcast_to(share.reshape(-1, 1), (slots, LANES))
    windows = slots // WIN_Q
    starts = jnp.arange(windows, dtype=jnp.int32) * WIN_Q + key_offsets + RIM
    pairs_t = atom_pairs.transpose(0, 1, 3, 2).reshape(windows, WIN_Q * features, WIN_K)
    eye = jnp.eye(WIN_Q, dtype=bool)
    spread = jnp.where(
        eye[None, :, :, None], atom_pw.T[:, None, None, :], jnp.zeros((), bf16)
    ).reshape(ATOM_HEADS * WIN_Q, WIN_Q * features)
    gather = WeightGather([part.shape for part in large], samp, seq) if kernels else None
    pooled, stored, fulls = atom_forward(
        ext,
        starts,
        pairs_t,
        spread,
        blocked,
        share,
        wide,
        down,
        atom_qb,
        gather,
        large if kernels else (),
    )
    if not kernels:
        fulls = [lax.all_gather(part, "samp", axis=0, tiled=True) for part in large]
    proj_w, up_w, down_w, cond_w, out_w = fulls
    block_in = token_input.astype(f32) + pooled

    noise_feature = 0.25 * jnp.log(noise_levels / sigma_data)
    cond_rows = (
        single_features.astype(f32)[None]
        + noise_feature[:, None, None] * noise_direction[None, None, :]
    )
    cond_low = norm_stats(cond_rows)[0].astype(bf16)
    cond_all = dot_last(cond_low, cond_w) + cond_b.astype(f32)
    parts = [cond_all[..., i * width : (i + 1) * width] for i in range(6)]

    pair_w = token_pw.T
    normed_in, inv_in = norm_stats(block_in)
    attn_in = (jax.nn.sigmoid(parts[0]) * normed_in + parts[1]).astype(bf16)
    mix = dot_last(attn_in, proj_w)
    queries = (mix[..., :width] + token_qb.astype(f32)).astype(bf16)
    keyval_own = mix[..., width : 3 * width].astype(bf16)
    gating = mix[..., 3 * width :]
    if kernels:
        attend, probs, keyval, stats = gather_attend(
            queries, keyval_own, pair_features, pair_w, seq
        )
    else:
        bias = pair_bias(pair_features, pair_w)
        keyval = lax.all_gather(keyval_own, "seq", axis=0, tiled=False)
        attend, probs = token_attention(queries, keyval, bias)
    sig_gate = jax.nn.sigmoid(gating)
    gated_low = (attend * sig_gate).astype(bf16)
    branch = dot_last(gated_low, out_w)
    gate_one = jax.nn.sigmoid(parts[2])
    mid = block_in + gate_one * branch
    normed_mid, inv_mid = norm_stats(mid)
    scale_two = jax.nn.sigmoid(parts[3])
    ffn_in = (scale_two * normed_mid + parts[4]).astype(bf16)
    upper = dot_last(ffn_in, up_w)
    hidden_width = down_w.shape[0]
    first_half, second_half = upper[..., :hidden_width], upper[..., hidden_width:]
    sig_first = jax.nn.sigmoid(first_half)
    hidden = (first_half * sig_first * second_half).astype(bf16)
    branch_two = dot_last(hidden, down_w)
    gate_two = jax.nn.sigmoid(parts[5])
    block_out = (mid + gate_two * branch_two).astype(bf16)

    out_grad = cotangent.astype(f32)
    branch_two_low = (out_grad * gate_two).astype(bf16)
    gate_two_grad = out_grad * branch_two * gate_two * (1.0 - gate_two)
    hidden_grad = dot_back(branch_two_low, down_w)
    first_grad = hidden_grad * second_half * sig_first * (1.0 + first_half * (1.0 - sig_first))
    second_grad = hidden_grad * first_half * sig_first
    upper_grad = jnp.concatenate([first_grad, second_grad], -1).astype(bf16)
    ffn_grad = dot_back(upper_grad, up_w)
    scale_two_grad = ffn_grad * normed_mid * scale_two * (1.0 - scale_two)
    mid_grad = out_grad + norm_back(normed_mid, inv_mid, ffn_grad * scale_two)
    branch_low = (mid_grad * gate_one).astype(bf16)
    gate_one_grad = mid_grad * branch * gate_one * (1.0 - gate_one)
    gated_grad = dot_back(branch_low, out_w)
    attend_low = (gated_grad * sig_gate).astype(bf16)
    gating_grad = gated_grad * attend * sig_gate * (1.0 - sig_gate)
    if kernels:
        query_grad, keyval_grad, pairw_grad, ready = attend_back_scatter(
            queries,
            keyval,
            probs,
            attend_low,
            pair_features,
            stats,
            ffn_in,
            upper_grad,
            hidden,
            branch_two_low,
            gated_low,
            branch_low,
        )
    else:
        query_grad, keyval_part, bias_grad = token_attention_back(
            queries, keyval, probs, attend_low
        )
        keyval_grad = lax.psum_scatter(keyval_part, "seq", scatter_dimension=0, tiled=False)
        pairw_grad = pair_grad(pair_features, bias_grad, pair_w)
    pairw_grad = pairw_grad.T
    mix_grad = jnp.concatenate(
        [query_grad.astype(bf16), keyval_grad, gating_grad.astype(bf16)], -1
    )
    token_qb_grad = jnp.sum(query_grad, (0, 1))
    attn_in_grad = dot_back(mix_grad, proj_w)
    scale_one = jax.nn.sigmoid(parts[0])
    scale_one_grad = attn_in_grad * normed_in * scale_one * (1.0 - scale_one)
    token_grad = mid_grad + norm_back(normed_in, inv_in, attn_in_grad * scale_one)
    cond_grad = jnp.concatenate(
        [scale_one_grad, attn_in_grad, gate_one_grad, scale_two_grad, ffn_grad, gate_two_grad], -1
    ).astype(bf16)
    cond_b_grad = jnp.sum(cond_grad.astype(f32), (0, 1))

    if kernels:
        summing = GradSum([part.shape for part in large])
        units = (weight_grads(attn_in, mix_grad, cond_low, cond_grad, ready, samp, seq),)
    else:
        summing, units = None, ()
    atom_results, shares = atom_backward(
        token_grad, starts, stored, pairs_t, share, wide, down, summing, units
    )
    mix_part, own, left, right, atom_mid_grad, *atom_totals = atom_results
    from_right = lax.ppermute(left, "seq", down_pairs)
    from_left = lax.ppermute(right, "seq", up_pairs)
    atom_grad, atom_proj_grad = atom_input_backward(
        atom_input, mix_part, own, from_left, from_right, atom_mid_grad, wide
    )
    qb_grad, outw_grad, upw_grad, downw_grad, pool_grad, pairw_stack, pairw_mean = atom_totals
    diagonal = pairw_stack.reshape(ATOM_HEADS, WIN_Q, WIN_Q, features)
    atom_pw_grad = (
        jnp.sum(jnp.where(eye[None, :, :, None], diagonal, 0.0), (1, 2)).T
        - jnp.sum(pairw_mean.reshape(ATOM_HEADS, -1), 1)[None, :]
    )

    rows = atom_width // samp
    tiny_parts = [qb_grad.reshape(-1), atom_pw_grad, cond_b_grad, token_qb_grad, pairw_grad]
    tiny_flat = jnp.concatenate([part.astype(bf16).reshape(samp, -1) for part in tiny_parts], 1)
    spare = width - upw_grad.shape[1] - atom_width
    tiny_flat = jnp.pad(tiny_flat, ((0, 0), (0, rows * spare - tiny_flat.shape[1])))
    lanes = lambda part: part.astype(bf16).reshape(samp, rows, -1)
    downw_two = downw_grad.astype(bf16).reshape(samp, 2, rows, atom_width)
    small = jnp.stack(
        [
            lanes(pool_grad),
            jnp.concatenate([lanes(atom_proj_grad), downw_two[:, 0], downw_two[:, 1]], -1),
            jnp.concatenate(
                [lanes(upw_grad), lanes(outw_grad), tiny_flat.reshape(samp, rows, spare)], -1
            ),
            jnp.zeros((samp, rows, width), bf16),
        ],
        1,
    ).reshape(samp, -1, width)
    if kernels:
        rest = small_sums(small.reshape(samp, seq, 16, width).transpose(1, 0, 2, 3))
    else:
        factors = [
            (attn_in, mix_grad),
            (ffn_in, upper_grad),
            (hidden, branch_two_low),
            (cond_low, cond_grad),
            (gated_low, branch_low),
        ]
        shares, rest = sum_shares(
            [weight_grad(*pair) for pair in factors], small.reshape(-1, width)
        )
    rest = rest.reshape(-1, width)
    pool_out, second, third = rest[:rows], rest[rows : 2 * rows], rest[2 * rows : 3 * rows]
    low = atom_proj_grad.shape[1]
    downw_out = jnp.concatenate(
        [second[:, low : low + atom_width], second[:, low + atom_width :]], 0
    )
    high = upw_grad.shape[1]
    tiny_out = third[:, high + atom_width :].reshape(-1)
    tiny_shares, cut = [], 0
    for part in tiny_parts:
        size = part.size // samp
        shape = (part.shape[0] // samp,) + part.shape[1:]
        tiny_shares.append(tiny_out[cut : cut + size].reshape(shape))
        cut += size
    return (
        block_out,
        atom_grad,
        token_grad,
        second[:, :low],
        tiny_shares[0],
        tiny_shares[1],
        third[:, high : high + atom_width],
        third[:, :high],
        downw_out,
        pool_out,
        shares[3],
        tiny_shares[2],
        shares[0],
        tiny_shares[3],
        tiny_shares[4],
        shares[4],
        shares[1],
        shares[2],
    )


def solution(mesh):
    in_specs = (
        P("samp", "seq", None),
        P("samp", "seq", None),
        P(),
        P("seq"),
        P("seq", None, None, None),
        P("seq", None, None),
        P("seq", None),
        P("samp"),
        P(),
        P("samp", None),
        P("samp"),
        P("samp", None),
        P("samp", None),
        P("samp", None),
        P("samp", None),
        P("samp", None),
        P("samp", None),
        P("samp"),
        P("samp", None),
        P("samp"),
        P("samp", None),
        P("samp", None),
        P("samp", None),
        P("samp", None),
        P("samp", "seq", None),
    )
    out_specs = (
        P("samp", "seq", None),
        P("samp", "seq", None),
        P("samp", "seq", None),
        P("samp", None),
        P("samp"),
        P("samp", None),
        P("samp", None),
        P("samp", None),
        P("samp", None),
        P("samp", None),
        P("samp", None),
        P("samp"),
        P("samp", None),
        P("samp"),
        P("samp", None),
        P("samp", None),
        P("samp", None),
        P("samp", None),
    )
    return jax.shard_map(local, mesh=mesh, in_specs=in_specs, out_specs=out_specs, check_vma=False)
```

```python
import functools

import jax
import jax.numpy as jnp
from jax import lax
from jax.experimental import pallas as pl
from jax.experimental.pallas import tpu as pltpu
from jax.sharding import PartitionSpec as P

MAX_ATOMS = 8
WIN_Q = 32
WIN_K = 128
ATOM_HEADS = 4
RIM = 96
LANES = 128

norm_eps = 1e-05
sigma_data = 16.0
masked_score = -1000000000.0
bf16 = jnp.bfloat16
f32 = jnp.float32
vmem_bytes = 56 << 20


def dot_last(left_op, right_op):
    return jnp.einsum("...k,kn->...n", left_op, right_op, preferred_element_type=f32)


def dot_back(grad_op, weight):
    return jnp.einsum("...n,kn->...k", grad_op, weight, preferred_element_type=f32)


def weight_grad(left_op, grad_op):
    flat_left = left_op.reshape(-1, left_op.shape[-1])
    flat_grad = grad_op.reshape(-1, grad_op.shape[-1])
    return jnp.einsum("rk,rn->kn", flat_left, flat_grad, preferred_element_type=f32)


def mm(left_op, right_op):
    return lax.dot_general(left_op, right_op, (((1,), (0,)), ((), ())), preferred_element_type=f32)


def mm_nt(left_op, right_op):
    return lax.dot_general(left_op, right_op, (((1,), (1,)), ((), ())), preferred_element_type=f32)


def mm_tn(left_op, right_op):
    return lax.dot_general(left_op, right_op, (((0,), (0,)), ((), ())), preferred_element_type=f32)


def norm_stats(operand):
    center = operand - jnp.mean(operand, -1, keepdims=True)
    inv_std = lax.rsqrt(jnp.mean(center * center, -1, keepdims=True) + norm_eps)
    return (center * inv_std, inv_std)


def norm_back(normed, inv_std, grad_op):
    return inv_std * (
        grad_op
        - jnp.mean(grad_op, -1, keepdims=True)
        - normed * jnp.mean(grad_op * normed, -1, keepdims=True)
    )


def sigmoid(operand):
    return 1.0 / (1.0 + jnp.exp(-operand))


def whole(shape):
    return pl.BlockSpec(shape, lambda *_: (0,) * len(shape))


def per_sample(shape):
    return pl.BlockSpec((1,) + shape, lambda b, *_: (b,) + (0,) * len(shape))


def params():
    return pltpu.CompilerParams(vmem_limit_bytes=vmem_bytes)


def square_sums(ones_op, squares):
    upper = squares.astype(bf16)
    lower = (squares - upper.astype(f32)).astype(bf16)
    return upper, lower


def head_masks(count, width, heads, head_dim, first):
    row = lax.broadcasted_iota(jnp.int32, (heads * count, width), 0)
    lane = lax.broadcasted_iota(jnp.int32, (heads * count, width), 1)
    inside = (lane - first) // head_dim == row // count
    return jnp.where(inside & (lane >= first), 1.0, 0.0).astype(bf16)


def head_stack(rows, heads, head_dim, first, masks=None):
    if masks is None:
        masks = head_masks(rows.shape[0], rows.shape[1], heads, head_dim, first)
    return jnp.concatenate([rows] * heads, 0) * masks


def head_fold(stacked, heads, head_dim, first):
    count = stacked.shape[0] // heads
    lane = lax.broadcasted_iota(jnp.int32, (count, stacked.shape[1]), 1)
    total = jnp.zeros((count, stacked.shape[1]), f32)
    for head in range(heads):
        low = first + head * head_dim
        part = stacked[head * count : (head + 1) * count]
        total = jnp.where((lane >= low) & (lane < low + head_dim), part, total)
    return total


MESH = pl.DeviceIdType.MESH


def places():
    samp_pos, seq_pos = lax.axis_index("samp"), lax.axis_index("seq")
    core, across, along = seq_pos % 2, seq_pos // 2 % 2, seq_pos // 4

    def index(along, across, core):
        return (along * 2 + across) * 2 + core

    return (
        samp_pos,
        seq_pos,
        index(along, across, 1 - core),
        index(along, 1 - across, core),
        index(1 - along, across, core),
        index(1 - along, 1 - across, core),
    )


def remote(source, target, send_sem, recv_sem, device):
    return pltpu.make_async_remote_copy(
        src_ref=source,
        dst_ref=target,
        send_sem=send_sem,
        recv_sem=recv_sem,
        device_id=device,
        device_id_type=MESH,
    )


def greet(devices):
    barrier = pltpu.get_barrier_semaphore()
    for device in devices:
        pl.semaphore_signal(barrier, inc=1, device_id=device, device_id_type=MESH)
    pl.semaphore_wait(barrier, len(devices))


def pick(position, values):
    chosen = values[0]
    for index, value in enumerate(values[1:], 1):
        chosen = jnp.where(position == index, value, chosen)
    return chosen


class WeightGather:
    def __init__(self, shapes, samp, seq):
        self.shapes, self.samp, self.seq = shapes, samp, seq
        self.splits = [self.split(shape, seq) for shape in shapes]

    @staticmethod
    def split(shape, parts):
        rows, columns = shape
        for down in (1, 2, 4, 8):
            across = parts // down
            if rows % (16 * down) == 0 and columns % (LANES * across) == 0:
                return (down, across)
        return None

    @staticmethod
    def fits(shapes, samp, seq):
        return (
            samp == 4
            and seq == 8
            and len(shapes) == 5
            and all(WeightGather.split(shape, seq) for shape in shapes)
        )

    def full_shapes(self):
        return [(rows * self.samp, columns) for rows, columns in self.shapes]

    def scratch(self):
        count = len(self.shapes)
        return [
            pltpu.SemaphoreType.DMA((9, self.samp, count)),
            pltpu.SemaphoreType.DMA((8, self.samp, count)),
            pltpu.SemaphoreType.DMA((2, count)),
        ] + [pltpu.VMEM(shape, bf16) for shape in self.shapes]

    def params(self):
        return pltpu.CompilerParams(
            vmem_limit_bytes=vmem_bytes, collective_id=1, has_side_effects=True
        )

    def cell(self, ref, weight, origin, part):
        rows, columns = self.shapes[weight]
        down, across = self.splits[weight]
        height, width = rows // down, columns // across
        low = origin * rows + part // across * height
        left = part % across * width
        return ref.at[
            pl.ds(pl.multiple_of(low, 16), height), pl.ds(pl.multiple_of(left, LANES), width)
        ]

    def origin(self, position, turn):
        order = [sorted(range(self.samp), key=lambda o: (abs(o - z), o)) for z in range(self.samp)]
        if isinstance(turn, int):
            return pick(position, [order[z][turn] for z in range(self.samp)])
        return pick(
            position, [pick(turn, [order[z][t] for t in range(self.samp)]) for z in range(self.samp)]
        )

    def own_copies(self, shards, fulls, own, held, stage):
        z = places()[0]
        copies = []
        for w, shard in enumerate(shards):
            rows = self.shapes[w][0]
            target = fulls[w].at[pl.ds(pl.multiple_of(z * rows, 16), rows), :]
            ends = (shard, held[w]) if stage == 0 else (held[w], target)
            copies.append(pltpu.make_async_copy(*ends, own.at[stage, w]))
        return copies

    def start(self, shards, fulls, send, recv, own, held):
        z, me, sib, xn, yn, dg = places()
        above, below = lax.rem(z + 1, self.samp), lax.rem(z + self.samp - 1, self.samp)
        greet([(z, sib), (z, xn), (z, yn), (above, me), (below, me)])
        for w, shard in enumerate(shards):
            source = self.cell(shard, w, 0, me)
            target = self.cell(fulls[w], w, z, me)

            @pl.when(z < self.samp - 1)
            def _():
                remote(source, target, send.at[0, 0, w], recv.at[0, z, w], (z + 1, me)).start()

            @pl.when(z > 0)
            def _():
                remote(source, target, send.at[1, 0, w], recv.at[0, z, w], (z - 1, me)).start()

        for copy in self.own_copies(shards, fulls, own, held, 0):
            copy.start()

    def place_own(self, shards, fulls, own, held):
        for copy in self.own_copies(shards, fulls, own, held, 0):
            copy.wait()
        for copy in self.own_copies(shards, fulls, own, held, 1):
            copy.start()

    def share_own(self, turn, origin, sources, fulls, send, recv):
        z, me, sib, xn, yn, dg = places()
        for kind, part in ((2, xn), (3, yn), (5, sib)):
            for w, source in enumerate(sources):
                target = self.cell(fulls[w], w, origin, me)
                arrival = {2: 1, 3: 2, 5: 4}[kind]
                remote(
                    source, target, send.at[kind, turn, w], recv.at[arrival, origin, w], (z, part)
                ).start()

    def wait_cell(self, fulls, recv, kind, w, origin, part, device):
        target = self.cell(fulls[w], w, origin, part)
        remote(target, target, recv.at[kind, origin, w], recv.at[kind, origin, w], device).wait_recv()

    def issue(self, turn, fulls, send, recv):
        z, me, sib, xn, yn, dg = places()
        origin = self.origin(z, turn)
        count = len(self.shapes)
        for w in range(count):
            self.wait_cell(fulls, recv, 0, w, origin, me, (z, sib))
        for w in range(count):
            cell = self.cell(fulls[w], w, origin, me)

            @pl.when((origin < z) & (z < self.samp - 1))
            def _():
                remote(cell, cell, send.at[0, turn, w], recv.at[0, origin, w], (z + 1, me)).start()

            @pl.when((origin > z) & (z > 0))
            def _():
                remote(cell, cell, send.at[1, turn, w], recv.at[0, origin, w], (z - 1, me)).start()

        cells = [self.cell(fulls[w], w, origin, me) for w in range(count)]
        self.share_own(turn, origin, cells, fulls, send, recv)

    def passed_on(self, w):
        return w in (0, 3)

    def finish(self, turn, fulls, send, recv):
        z, me, sib, xn, yn, dg = places()
        origin = self.origin(z, turn)
        count = len(self.shapes)
        for kind, part, other, by in ((1, xn, yn, True), (2, yn, xn, False)):
            for w in range(count):
                self.wait_cell(fulls, recv, kind, w, origin, part, (z, part))
                cell = self.cell(fulls[w], w, origin, part)
                if self.passed_on(w) == by:
                    remote(
                        cell, cell, send.at[4, turn, w], recv.at[3, origin, w], (z, other)
                    ).start()
                remote(
                    cell, cell, send.at[5 + kind, turn, w], recv.at[4 + kind, origin, w], (z, sib)
                ).start()

    def diagonal(self, turn, fulls, send, recv):
        z, me, sib, xn, yn, dg = places()
        origin = self.origin(z, turn)
        for w in range(len(self.shapes)):
            self.wait_cell(fulls, recv, 3, w, origin, dg, (z, yn))
            cell = self.cell(fulls[w], w, origin, dg)
            remote(cell, cell, send.at[8, turn, w], recv.at[7, origin, w], (z, sib)).start()

    def drain(self, shards, fulls, send, recv, own, held):
        z, me, sib, xn, yn, dg = places()
        count = len(self.shapes)

        def sent(kind, turn, w):
            cell = self.cell(fulls[w], w, 0, me)
            remote(cell, cell, send.at[kind, turn, w], recv.at[0, 0, w], (z, sib)).wait_send()

        def one(turn, carry):
            origin = self.origin(z, turn)
            for w in range(count):
                for kind in range(2, 9):
                    sent(kind, turn, w)

                @pl.when((z < self.samp - 1) & (origin < z))
                def _():
                    sent(0, turn, w)

                @pl.when((z > 0) & (origin > z))
                def _():
                    sent(1, turn, w)

                for kind in range(4, 8):
                    self.wait_cell(fulls, recv, kind, w, origin, sib, (z, sib))
            return carry

        lax.fori_loop(1, self.samp, one, 0)
        for w in range(count):

            @pl.when(z < self.samp - 1)
            def _():
                sent(0, 0, w)

            @pl.when(z > 0)
            def _():
                sent(1, 0, w)

        for copy in self.own_copies(shards, fulls, own, held, 1):
            copy.wait()

    def step(self, sample, shards, fulls, send, recv, own, *held):
        @pl.when(sample == 0)
        def _():
            self.start(shards, fulls, send, recv, own, held)

        @pl.when(sample == 1)
        def _():
            self.place_own(shards, fulls, own, held)

        for at, turn in ((2, 1), (3, 2), (5, 3)):

            @pl.when(sample == at)
            def _():
                self.issue(turn, fulls, send, recv)

        for at, turn in ((4, 1), (5, 2), (7, 3)):

            @pl.when(sample == at)
            def _():
                self.finish(turn, fulls, send, recv)

        for at, turn in ((5, 1), (7, 2)):

            @pl.when(sample == at)
            def _():
                self.diagonal(turn, fulls, send, recv)

    def last(self, sample, shards, fulls, send, recv, own, *held):
        @pl.when(sample == pl.num_programs(0) - 1)
        def _():
            self.diagonal(3, fulls, send, recv)
            self.drain(shards, fulls, send, recv, own, held)


def edge_kernel(samp, seq, wide_ref, tiny_ref, rows_ref, wide_out, tiny_out, ext_out, send, recv):
    z, me = lax.axis_index("samp"), lax.axis_index("seq")
    samples, slots, width = rows_ref.shape
    right, left = lax.rem(me + 1, seq), lax.rem(me + seq - 1, seq)
    others = [(lax.rem(z + hop, samp), me) for hop in range(1, samp)]
    greet(others + [(z, right), (z, left)])
    copies = []
    for hop, device in enumerate(others):
        for kind, (ref, out) in enumerate(((wide_ref, wide_out), (tiny_ref, tiny_out))):
            rows = ref.shape[0]
            target = out.at[pl.ds(pl.multiple_of(z * rows, 16), rows), :]
            copy = remote(ref, target, send.at[kind, hop], recv.at[kind, hop], device)
            copy.start()
            copies.append(copy)
    before, after = ext_out.at[:, :RIM, :], ext_out.at[:, RIM + slots :, :]
    to_right = remote(rows_ref.at[:, slots - RIM :, :], before, send.at[2, 0], recv.at[2, 0], (z, right))
    to_left = remote(rows_ref.at[:, :RIM, :], after, send.at[2, 1], recv.at[2, 1], (z, left))
    first, last = me == 0, me == seq - 1

    @pl.when(~last)
    def _():
        to_right.start()

    @pl.when(~first)
    def _():
        to_left.start()

    @pl.when(first)
    def _():
        ext_out[:, :RIM, :] = jnp.zeros((samples, RIM, width), bf16)

    @pl.when(last)
    def _():
        ext_out[:, RIM + slots :, :] = jnp.zeros((samples, RIM, width), bf16)

    def move(sample, carry):
        ext_out[sample, RIM : RIM + slots, :] = rows_ref[sample]
        return carry

    lax.fori_loop(0, samples, move, 0)
    for ref, out in ((wide_ref, wide_out), (tiny_ref, tiny_out)):
        rows = ref.shape[0]
        out[pl.ds(pl.multiple_of(z * rows, 16), rows), :] = ref[...]
    for copy in copies:
        copy.wait()

    @pl.when(~last)
    def _():
        to_right.wait_send()
        to_left.wait_recv()

    @pl.when(~first)
    def _():
        to_left.wait_send()
        to_right.wait_recv()


def edges(wide_own, tiny_own, rows):
    samp, seq = lax.axis_size("samp"), lax.axis_size("seq")
    samples, slots, width = rows.shape
    place = pl.BlockSpec(memory_space=pltpu.VMEM)
    return pl.pallas_call(
        functools.partial(edge_kernel, samp, seq),
        out_shape=[
            jax.ShapeDtypeStruct((samp * wide_own.shape[0], wide_own.shape[1]), bf16),
            jax.ShapeDtypeStruct((samp * tiny_own.shape[0], tiny_own.shape[1]), bf16),
            jax.ShapeDtypeStruct((samples, slots + 2 * RIM, width), bf16),
        ],
        in_specs=[place] * 3,
        out_specs=[place] * 3,
        scratch_shapes=[
            pltpu.SemaphoreType.DMA((3, samp)),
            pltpu.SemaphoreType.DMA((3, samp)),
        ],
        compiler_params=pltpu.CompilerParams(
            vmem_limit_bytes=vmem_bytes, collective_id=0, has_side_effects=True
        ),
        name="edges",
    )(wide_own, tiny_own, rows)


UNIT = 336


def add_into(target, source, lanes=slice(None), rows=48):
    def one(step, carry):
        part = pl.ds(pl.multiple_of(step * rows, 16), rows)
        target[part, lanes] = target[part, lanes] + source[part, :]
        return carry

    lax.fori_loop(0, target.shape[0] // rows, one, 0)


class GradSum:
    head, tail, full = slice(0, 384), slice(384, 768), slice(0, 768)

    def __init__(self, shapes):
        self.shapes = list(shapes)

    def scratch(self):
        half = (UNIT, 384)
        dma = pltpu.SemaphoreType.DMA
        return [
            pltpu.VMEM((4, 4, UNIT, 768), bf16),
            pltpu.VMEM((4, 4, UNIT, 768), bf16),
            pltpu.VMEM((4, 2) + half, bf16),
            pltpu.VMEM((4, 2) + half, bf16),
            pltpu.VMEM((4,) + half, bf16),
            pltpu.VMEM((4,) + half, bf16),
            pltpu.VMEM((3, UNIT, 768), bf16),
            pltpu.VMEM((UNIT, 768), bf16),
            dma((4, 4)),
            dma((4, 4)),
            dma((4, 4)),
            dma((4, 4)),
            dma((4, 4)),
            dma((4, 2)),
            dma((4, 2)),
            dma((3,)),
            dma((3,)),
            dma,
        ]

    def params(self):
        return pltpu.CompilerParams(
            vmem_limit_bytes=vmem_bytes, collective_id=2, has_side_effects=True
        )

    def bind(
        self, grads, shares, mine, theirs, from_x, from_y, last_x, last_y, planes, own_share, *sems
    ):
        self.grads, self.shares, self.own_share = grads, shares, own_share
        self.mine, self.theirs, self.from_x, self.from_y = mine, theirs, from_x, from_y
        self.last_x, self.last_y, self.planes = last_x, last_y, planes
        (
            self.s_sib,
            self.r_sib,
            self.s_own,
            self.s_one,
            self.r_one,
            self.s_two,
            self.r_two,
            self.s_z,
            self.r_z,
            self.s_out,
        ) = sems
        self.z, self.me, self.sib, self.xn, self.yn, self.dg = places()
        self.core, self.chip = self.me % 2, self.me // 2
        self.chip_x, self.chip_y, self.chip_d = self.xn // 2, self.yn // 2, self.dg // 2
        order = [[p ^ hop for hop in (2, 3, 1, 0)] for p in range(4)]
        self.plane = [pick(self.z, [order[p][r] for p in range(4)]) for r in range(4)]

    def there(self, r, j):
        return remote(
            self.grads.at[2 * j + 1 - self.core, self.plane[r]],
            self.theirs.at[r, j],
            self.s_sib.at[r, j],
            self.r_sib.at[r, j],
            (self.z, self.sib),
        )

    def here(self, r, j):
        return pltpu.make_async_copy(
            self.grads.at[2 * j + self.core, self.plane[r]], self.mine.at[r, j], self.s_own.at[r, j]
        )

    def one(self, r, k):
        chip = (self.chip_x, self.chip_d, self.chip_y, self.chip_d)[k]
        lanes = self.head if k < 2 else self.tail
        target = (self.from_x if k < 2 else self.from_y).at[r, k % 2]
        device = (self.z, self.xn if k < 2 else self.yn)
        return remote(
            self.mine.at[r, chip, :, lanes], target, self.s_one.at[r, k], self.r_one.at[r, k], device
        )

    def two(self, r, k):
        chip, lanes, target, device = (
            (self.chip_y, self.head, self.last_y, self.yn),
            (self.chip_x, self.tail, self.last_x, self.xn),
        )[k]
        return remote(
            self.mine.at[r, chip, :, lanes],
            target.at[r],
            self.s_two.at[r, k],
            self.r_two.at[r, k],
            (self.z, device),
        )

    def across(self, r):
        return remote(
            self.mine.at[r, self.chip],
            self.planes.at[r],
            self.s_z.at[r],
            self.r_z.at[r],
            (self.plane[r], self.me),
        )

    def keep(self):
        return pltpu.make_async_copy(self.own_share, self.shares, self.s_out)

    def begin(self, r):
        for j in range(4):
            self.there(r, j).start()
            self.here(r, j).start()

    def pairs(self, r):
        for j in range(4):
            self.there(r, j).wait_recv()
            self.here(r, j).wait()
        for j in range(4):
            add_into(self.mine.at[r, j], self.theirs.at[r, j])
        for k in range(4):
            self.one(r, k).start()

    def middle(self, r):
        self.one(r, 1).wait_recv()
        add_into(self.mine.at[r, self.chip_y], self.from_x.at[r, 1], self.head)
        self.two(r, 0).start()
        self.one(r, 3).wait_recv()
        add_into(self.mine.at[r, self.chip_x], self.from_y.at[r, 1], self.tail)
        self.two(r, 1).start()
        self.one(r, 0).wait_recv()
        add_into(self.mine.at[r, self.chip], self.from_x.at[r, 0], self.head)
        self.one(r, 2).wait_recv()
        add_into(self.mine.at[r, self.chip], self.from_y.at[r, 0], self.tail)

    def finish(self, r):
        self.two(r, 0).wait_recv()
        add_into(self.mine.at[r, self.chip], self.last_y.at[r], self.head)
        self.two(r, 1).wait_recv()
        add_into(self.mine.at[r, self.chip], self.last_x.at[r], self.tail)
        if r < 3:
            self.across(r).start()

    def total(self):
        for r in range(3):
            self.across(r).wait_recv()

        def one(step, carry):
            rows = pl.ds(pl.multiple_of(step * 48, 16), 48)
            both = self.mine[3, self.chip, rows, :].astype(f32)
            for r in range(3):
                both += self.planes[r, rows, :].astype(f32)
            self.own_share[rows, :] = both.astype(bf16)
            return carry

        lax.fori_loop(0, UNIT // 48, one, 0)
        self.keep().start()

    def collect(self):
        self.keep().wait()
        for r in range(4):
            for j in range(4):
                self.there(r, j).wait_send()
                self.one(r, j).wait_send()
            for k in range(2):
                self.two(r, k).wait_send()
            if r < 3:
                self.across(r).wait_send()

    def hello(self):
        greet(
            [(self.z, self.sib), (self.z, self.xn), (self.z, self.yn)]
            + [(self.plane[r], self.me) for r in range(3)]
            + [(self.z, lax.rem(self.me + 1, 8)), (self.z, lax.rem(self.me + 7, 8))]
        )
        self.begin(0)
        self.begin(1)

    def slot(self, index):
        plan = {
            0: [self.hello],
            1: [lambda: self.pairs(0), lambda: self.begin(2)],
            3: [lambda: self.pairs(1), lambda: self.begin(3)],
            4: [lambda: self.middle(0)],
            6: [lambda: self.pairs(2), lambda: self.finish(0)],
            7: [lambda: self.middle(1)],
            9: [lambda: self.pairs(3), lambda: self.finish(1)],
            10: [lambda: self.middle(2)],
            12: [lambda: self.finish(2)],
            13: [lambda: self.middle(3)],
            14: [lambda: self.finish(3)],
            15: [self.total],
        }
        for at, actions in plan.items():

            @pl.when(index == at)
            def _():
                for action in actions:
                    action()


def small_sum_kernel(
    main,
    tiny,
    own,
    out_ref,
    shares,
    grads,
    cores,
    chips,
    planes,
    share,
    total,
    s_one,
    r_one,
    s_two,
    r_two,
    s_z,
    r_z,
    s_all,
    r_all,
    s_share,
    r_share,
    s_own,
):
    z, me, sib, xn, yn, dg = places()
    core, chip = me % 2, me // 2
    near = (xn, yn, dg)
    parts, samp, rows = grads.shape[:3]
    for part in range(parts):
        for p in range(samp):
            grads[part, p] = main[p, part * rows : (part + 1) * rows, :]
    low, width = 2 * tiny.shape[1], tiny.shape[2]
    for part in range(tiny.shape[1] // rows):
        for p in range(samp):
            grads[low // rows + part, p, :, -width:] = tiny[p, part * rows : (part + 1) * rows, :]
    others = [lax.rem(z + hop, 4) for hop in (1, 2, 3)]
    greet(
        [(z, sib)]
        + [(z, part) for part in near]
        + [(z, part + 1 - 2 * core) for part in near]
        + [(other, me) for other in others]
    )

    def one(j):
        return remote(
            grads.at[2 * j + 1 - core], cores.at[j], s_one.at[j], r_one.at[j], (z, sib)
        )

    width = own.shape[1]
    head, tail, full = slice(0, width // 2), slice(width // 2, width), slice(0, width)

    def give(part, lanes, kind, device):
        target = shares.at[part, :, lanes]
        source = own if kind in (0, 1, 4) else target
        return remote(source, target, s_share.at[kind], r_share.at[kind], (z, device))

    keep = pltpu.make_async_copy(own, shares.at[me], s_own)
    gifts = [give(me, full, 0, xn), give(me, full, 1, yn), give(me, full, 4, sib)]

    for j in range(4):
        one(j).start()
    for j in range(4):
        one(j).wait()
        both = cores[j].astype(f32) + grads[2 * j + core].astype(f32)
        cores[j] = both.astype(bf16)

    def two(k):
        return remote(cores.at[near[k] // 2], chips.at[k], s_two.at[k], r_two.at[k], (z, near[k]))

    for k in range(3):
        two(k).start()
    keep.start()
    for gift in gifts:
        gift.start()
    both = cores[chip].astype(f32)
    for k in range(3):
        two(k).wait()
        both += chips[k].astype(f32)
    share[...] = both.astype(bf16)

    def three(k):
        return remote(share.at[others[k]], planes.at[k], s_z.at[k], r_z.at[k], (others[k], me))

    for k in range(3):
        three(k).start()
    both = share[z].astype(f32)
    for k in range(3):
        three(k).wait()
        both += planes[k].astype(f32)
    total[me] = both.astype(bf16)

    receivers = [sib] + list(near) + [part + 1 - 2 * core for part in near]

    def four(k, part, device):
        return remote(total.at[part], total.at[part], s_all.at[k], r_all.at[k], (z, device))

    for k, device in enumerate(receivers):
        four(k, me, device).start()
    give(xn, full, 0, xn).wait_recv()
    gifts += [give(xn, head, 2, yn), give(xn, full, 5, sib)]
    give(yn, full, 1, yn).wait_recv()
    gifts += [give(yn, tail, 3, xn), give(yn, full, 6, sib)]
    for gift in gifts[3:]:
        gift.start()
    for k, device in enumerate(receivers):
        four(k, device, device).wait_recv()
    for k, device in enumerate(receivers):
        four(k, me, device).wait_send()
    for part in range(parts):
        out_ref[part * rows : (part + 1) * rows, :] = total[part]
    give(dg, head, 2, yn).wait_recv()
    give(dg, tail, 3, xn).wait_recv()
    gifts.append(give(dg, full, 7, sib))
    gifts[-1].start()
    for kind in range(4, 8):
        give(sib, full, kind, sib).wait_recv()
    keep.wait()
    for gift in gifts:
        gift.wait_send()


def small_sums(main, tiny, own):
    seq = lax.axis_size("seq")
    samp, rows, width = main.shape
    rows //= seq
    dma = pltpu.SemaphoreType.DMA
    return pl.pallas_call(
        small_sum_kernel,
        out_shape=[
            jax.ShapeDtypeStruct((seq * rows, width), bf16),
            jax.ShapeDtypeStruct((seq,) + own.shape, bf16),
        ],
        in_specs=[pl.BlockSpec(memory_space=pltpu.VMEM)] * 3,
        out_specs=[
            pl.BlockSpec(memory_space=pltpu.VMEM),
            pl.BlockSpec(memory_space=pl.ANY),
        ],
        scratch_shapes=[
            pltpu.VMEM((seq, samp, rows, width), bf16),
            pltpu.VMEM((4, samp, rows, width), bf16),
            pltpu.VMEM((3, samp, rows, width), bf16),
            pltpu.VMEM((3, rows, width), bf16),
            pltpu.VMEM((samp, rows, width), bf16),
            pltpu.VMEM((seq, rows, width), bf16),
            dma((4,)),
            dma((4,)),
            dma((3,)),
            dma((3,)),
            dma((3,)),
            dma((3,)),
            dma((7,)),
            dma((7,)),
            dma((8,)),
            dma((8,)),
            dma,
        ],
        compiler_params=pltpu.CompilerParams(
            vmem_limit_bytes=vmem_bytes, collective_id=3, has_side_effects=True
        ),
        name="small_sums",
    )(main, tiny, own)


def pair_stats(pairs, fold):
    upper, lower = square_sums(fold, pairs.astype(f32) * pairs.astype(f32))
    features = pairs.shape[0] // WIN_Q
    mean = mm(fold, pairs) * (1.0 / features)
    square = (mm(fold, upper) + mm(fold, lower)) * (1.0 / features)
    var = jnp.maximum(square - mean * mean, 0.0)
    inv_std = lax.rsqrt(var + norm_eps)
    return mean, inv_std


def pair_fold(features):
    shape = (WIN_Q, WIN_Q * features)
    row = lax.broadcasted_iota(jnp.int32, shape, 0)
    column = lax.broadcasted_iota(jnp.int32, shape, 1)
    return jnp.where(column // features == row, 1.0, 0.0).astype(bf16)


def atom_fwd_kernel(
    gather,
    starts,
    ext_ref,
    pairs_ref,
    spread_ref,
    blocked_ref,
    share_ref,
    wide_ref,
    down_ref,
    qbias_ref,
    *refs,
):
    count = len(gather.shapes) if gather is not None else 0
    shards, refs = refs[:count], refs[count:]
    (
        pooled_ref,
        query_ref,
        keyval_ref,
        gate_ref,
        probs_ref,
        attend_ref,
        mid_ref,
    ), refs = refs[:7], refs[7:]
    fulls, refs = refs[:count], refs[count:]
    bias_s, sems = refs[0], refs[1:]
    width = ext_ref.shape[-1]
    head_dim = width // ATOM_HEADS
    scale = float(head_dim) ** (-0.5)
    slots = query_ref.shape[1]
    windows = slots // WIN_Q
    hidden_width = down_ref.shape[0]
    model_width = pooled_ref.shape[-1]
    features = pairs_ref.shape[1] // WIN_Q
    sample = pl.program_id(0)
    if gather is not None:
        gather.step(sample, shards, fulls, *sems)

    @pl.when(sample == 0)
    def _():
        fold = pair_fold(features)
        spread = spread_ref[...]
        spread_sum = jnp.sum(spread.astype(f32), -1, keepdims=True)
        first_lane = jnp.where(
            lax.broadcasted_iota(jnp.int32, (ATOM_HEADS * WIN_Q, LANES), 1) == 0, 1.0, 0.0
        ).astype(bf16)

        fill = jnp.full((ATOM_HEADS * WIN_Q, WIN_K), masked_score, f32)

        def one(duo, carry):
            base = pl.multiple_of(duo * 2 * WIN_Q, 2 * WIN_Q)
            blocked = mm_nt(first_lane, blocked_ref[pl.ds(base, 2 * WIN_K), :].astype(bf16))
            for part in range(2):
                win = duo * 2 + part
                pairs = pairs_ref[win]
                mean, inv_std = pair_stats(pairs, fold)
                mean = jnp.concatenate([mean] * ATOM_HEADS, 0)
                inv_std = jnp.concatenate([inv_std] * ATOM_HEADS, 0)
                bias = inv_std * (mm(spread, pairs) - mean * spread_sum)
                bias = pltpu.roll(jnp.concatenate([bias, fill], 1), starts[win] - base, 1) + blocked
                for head in range(ATOM_HEADS):
                    low = (head * 2 + part) * WIN_Q
                    bias_s[duo, low : low + WIN_Q, :] = bias[head * WIN_Q : (head + 1) * WIN_Q]
            return carry

        lax.fori_loop(0, windows // 2, one, 0)

    rows = ext_ref[0].astype(f32)
    normed_low = norm_stats(rows)[0].astype(bf16)
    key_val = mm(normed_low, wide_ref[:, width : 3 * width]).astype(bf16)
    keyval_ref[0] = key_val
    own_low = normed_low[RIM : RIM + slots]
    query_ref[0] = (mm(own_low, wide_ref[:, :width]) + qbias_ref[...]).astype(bf16)
    gate_ref[0] = mm(own_low, wide_ref[:, 3 * width : 4 * width])

    masks = head_masks(2 * WIN_Q, width, ATOM_HEADS, head_dim, 0)

    def two_windows(duo):
        first = pl.multiple_of(duo * 2 * WIN_Q, 2 * WIN_Q)
        span = pl.ds(first, 2 * WIN_K)
        own = pl.ds(first, 2 * WIN_Q)
        stacked = head_stack(query_ref[0, own, :], ATOM_HEADS, head_dim, 0, masks)
        scores = mm_nt(stacked, keyval_ref[0, span, :width]) * scale + bias_s[duo]
        exp_scores = jnp.exp(scores - jnp.max(scores, -1, keepdims=True))
        probs = exp_scores * (1.0 / jnp.sum(exp_scores, -1, keepdims=True))
        probs_low = probs.astype(bf16)
        probs_ref[0, duo] = probs_low
        attend_ref[0, own, :] = head_fold(
            mm(probs_low, keyval_ref[0, span, width:]), ATOM_HEADS, head_dim, 0
        )

    def some_windows(step, carry):
        for part in range(2):
            two_windows(step * 2 + part)
        return carry

    lax.fori_loop(0, windows // 4, some_windows, 0)

    gated_low = (attend_ref[0] * sigmoid(gate_ref[0])).astype(bf16)
    offset = 4 * width
    upw = wide_ref[:, offset : offset + 2 * hidden_width]
    offset += 2 * hidden_width
    pool_weight = wide_ref[:, offset : offset + model_width]
    outw = wide_ref[:, offset + model_width : offset + model_width + width]
    mid = rows[RIM : RIM + slots] + mm(gated_low, outw)
    mid_ref[0] = mid
    ffn_low = norm_stats(mid)[0].astype(bf16)
    upper = mm(ffn_low, upw)
    first_half, second_half = upper[:, :hidden_width], upper[:, hidden_width:]
    hidden = (first_half * sigmoid(first_half) * second_half).astype(bf16)
    final_low = (mid + mm(hidden, down_ref[...])).astype(bf16)
    pool_pre = mm(final_low, pool_weight)
    share = share_ref[...]
    for lane in range(0, model_width, LANES):
        part = pool_pre[:, lane : lane + LANES]
        part = part * sigmoid(part) * share
        pooled_ref[0, :, lane : lane + LANES] = jnp.sum(
            part.reshape(slots // MAX_ATOMS, MAX_ATOMS, LANES), 1
        )
    if gather is not None:
        gather.last(sample, shards, fulls, *sems)


def atom_forward(ext, starts, pairs, spread, blocked, share, wide, down, qbias, gather, shards):
    samples, ext_slots, width = ext.shape
    slots = ext_slots - 2 * RIM
    tokens = slots // MAX_ATOMS
    windows = slots // WIN_Q
    model_width = wide.shape[1] - 5 * width - 2 * down.shape[0]
    stack = ATOM_HEADS * WIN_Q
    outs = (
        ((tokens, model_width), f32),
        ((slots, width), bf16),
        ((ext_slots, 2 * width), bf16),
        ((slots, width), f32),
        ((windows // 2, 2 * stack, 2 * WIN_K), bf16),
        ((slots, width), f32),
        ((slots, width), f32),
    )
    place = pl.BlockSpec(memory_space=pl.ANY)
    results = pl.pallas_call(
        functools.partial(atom_fwd_kernel, gather),
        out_shape=[jax.ShapeDtypeStruct((samples,) + shape, kind) for shape, kind in outs]
        + [jax.ShapeDtypeStruct(shape, bf16) for shape in (gather.full_shapes() if gather else [])],
        grid=(samples,),
        in_specs=[
            pl.BlockSpec(memory_space=pltpu.SMEM),
            per_sample((ext_slots, width)),
            whole(pairs.shape),
            whole(spread.shape),
            whole(blocked.shape),
            whole(share.shape),
            whole(wide.shape),
            whole(down.shape),
            whole(qbias.shape),
        ]
        + [place] * len(shards),
        out_specs=[per_sample(shape) for shape, _ in outs] + [place] * len(shards),
        scratch_shapes=[pltpu.VMEM((windows // 2, 2 * stack, 2 * WIN_K), f32)]
        + (gather.scratch() if gather else []),
        compiler_params=gather.params() if gather else params(),
        name="atom_forward",
    )(starts, ext, pairs, spread, blocked, share, wide, down, qbias, *shards)
    return results[0], results[1:7], results[7:]


def atom_bwd_dense(sample_refs, consts, accs, attlow_s, gate_grad_at, mid_grad_at):
    grad_ref, query_ref, gate_ref, attend_ref, mid_ref = sample_refs
    share_ref, wide_ref, down_ref = consts
    outw_ref, upw_ref, downw_ref, pool_ref = accs
    width = query_ref.shape[-1]
    slots = query_ref.shape[1]
    hidden_width = down_ref.shape[0]
    model_width = grad_ref.shape[-1]
    tokens = grad_ref.shape[1]
    offset = 4 * width
    upw = wide_ref[:, offset : offset + 2 * hidden_width]
    offset += 2 * hidden_width
    pool_weight = wide_ref[:, offset : offset + model_width]
    outw = wide_ref[:, offset + model_width : offset + model_width + width]
    down = down_ref[...]

    mid = mid_ref[0]
    normed_mid, inv_mid = norm_stats(mid)
    ffn_low = normed_mid.astype(bf16)
    upper = mm(ffn_low, upw)
    first_half, second_half = upper[:, :hidden_width], upper[:, hidden_width:]
    sig_first = sigmoid(first_half)
    hidden = (first_half * sig_first * second_half).astype(bf16)
    final_low = (mid + mm(hidden, down)).astype(bf16)
    pool_pre = mm(final_low, pool_weight)
    share = share_ref[...]
    pool_parts = []
    for lane in range(0, model_width, LANES):
        part = pool_pre[:, lane : lane + LANES]
        grad = jnp.broadcast_to(
            grad_ref[0, :, lane : lane + LANES][:, None, :], (tokens, MAX_ATOMS, LANES)
        ).reshape(slots, LANES)
        sig_pool = sigmoid(part)
        pool_parts.append((grad * share * sig_pool * (1.0 + part * (1.0 - sig_pool))).astype(bf16))
    pool_grad = jnp.concatenate(pool_parts, 1)
    final_grad = mm_nt(pool_grad, pool_weight)
    pool_ref[...] += mm_tn(final_low, pool_grad)
    branch_low = final_grad.astype(bf16)
    hidden_grad = mm_nt(branch_low, down)
    first_grad = hidden_grad * second_half * sig_first * (1.0 + first_half * (1.0 - sig_first))
    second_grad = hidden_grad * first_half * sig_first
    upper_grad = jnp.concatenate([first_grad.astype(bf16), second_grad.astype(bf16)], 1)
    downw_ref[...] += mm_tn(hidden, branch_low)
    upw_ref[...] += mm_tn(ffn_low, upper_grad)
    mid_grad = final_grad + norm_back(normed_mid, inv_mid, mm_nt(upper_grad, upw))
    mid_grad_at[...] = mid_grad
    out_low = mid_grad.astype(bf16)
    gated_grad = mm_nt(out_low, outw)
    sig_gate = sigmoid(gate_ref[0])
    attend = attend_ref[0]
    gated_low = (attend * sig_gate).astype(bf16)
    outw_ref[...] += mm_tn(gated_low, out_low)
    attlow_s[...] = (gated_grad * sig_gate).astype(bf16)
    gate_grad_at[...] = (gated_grad * attend * sig_gate * (1.0 - sig_gate)).astype(bf16)


def atom_bwd_windows(sample_refs, scratch):
    query_ref, keyval_ref, probs_ref = sample_refs
    acck_s, accv_s, bias_s, attlow_s, dq_s = scratch
    width = query_ref.shape[-1]
    head_dim = width // ATOM_HEADS
    scale = float(head_dim) ** (-0.5)
    windows = query_ref.shape[1] // WIN_Q
    acck_s[...] = jnp.zeros_like(acck_s)
    accv_s[...] = jnp.zeros_like(accv_s)
    masks = head_masks(2 * WIN_Q, width, ATOM_HEADS, head_dim, 0)

    def two_windows(duo):
        first = pl.multiple_of(duo * 2 * WIN_Q, 2 * WIN_Q)
        span = pl.ds(first, 2 * WIN_K)
        own = pl.ds(first, 2 * WIN_Q)
        queries = head_stack(query_ref[0, own, :], ATOM_HEADS, head_dim, 0, masks)
        att = head_stack(attlow_s[own, :], ATOM_HEADS, head_dim, 0, masks)
        probs_low = probs_ref[0, duo]
        probs = probs_low.astype(f32)
        prob_grad = mm_nt(att, keyval_ref[0, span, width:])
        delta = jnp.sum(prob_grad * probs, -1, keepdims=True)
        score_low = (probs * (prob_grad - delta)).astype(bf16)
        bias_s[duo] += score_low.astype(f32)
        dq_s[own, :] = (
            head_fold(mm(score_low, keyval_ref[0, span, :width]), ATOM_HEADS, head_dim, 0) * scale
        )
        acck_s[span, :] += mm_tn(score_low, queries) * scale
        accv_s[span, :] += mm_tn(probs_low, att)

    def some_windows(step, carry):
        for part in range(2):
            two_windows(step * 2 + part)
        return carry

    lax.fori_loop(0, windows // 4, some_windows, 0)


def atom_bwd_pairs(starts, pairs_ref, bias_s, pairw_ref, pairm_ref):
    fold = pair_fold(pairs_ref.shape[1] // WIN_Q)

    def one(duo, carry):
        for part in range(2):
            win = duo * 2 + part
            pairs = pairs_ref[win]
            mean, inv_std = pair_stats(pairs, fold)
            lows = [(head * 2 + part) * WIN_Q for head in range(ATOM_HEADS)]
            placed = jnp.concatenate([bias_s[duo, low : low + WIN_Q, :] for low in lows], 0)
            shift = starts[win] - duo * 2 * WIN_Q
            grad = pltpu.roll(placed, lax.rem(2 * WIN_K - shift, 2 * WIN_K), 1)[:, :WIN_K]
            scaled = grad * jnp.concatenate([inv_std] * ATOM_HEADS, 0)
            pairm_ref[...] += scaled * jnp.concatenate([mean] * ATOM_HEADS, 0)
            upper = scaled.astype(bf16)
            lower = (scaled - upper.astype(f32)).astype(bf16)
            pairw_ref[...] += mm_nt(upper, pairs) + mm_nt(lower, pairs)
        return carry

    lax.fori_loop(0, pairs_ref.shape[0] // 2, one, 0)


def atom_bwd_kernel(
    starts,
    grad_ref,
    query_ref,
    keyval_ref,
    gate_ref,
    probs_ref,
    attend_ref,
    mid_ref,
    pairs_ref,
    share_ref,
    wide_ref,
    down_ref,
    mix_ref,
    own_ref,
    left_ref,
    right_ref,
    midgrad_ref,
    qbias_ref,
    outw_ref,
    upw_ref,
    downw_ref,
    pool_ref,
    pairw_ref,
    pairm_ref,
    *scratch,
):
    acck_s, accv_s, bias_s, attlow_s, dq_s = scratch
    width = query_ref.shape[-1]
    slots = query_ref.shape[1]
    sample = pl.program_id(0)

    @pl.when(sample == 0)
    def _():
        for ref in (qbias_ref, outw_ref, upw_ref, downw_ref, pool_ref, pairw_ref, pairm_ref, bias_s):
            ref[...] = jnp.zeros_like(ref)

    atom_bwd_dense(
        (grad_ref, query_ref, gate_ref, attend_ref, mid_ref),
        (share_ref, wide_ref, down_ref),
        (outw_ref, upw_ref, downw_ref, pool_ref),
        attlow_s,
        mix_ref.at[0, :, width:],
        midgrad_ref.at[0],
    )
    atom_bwd_windows((query_ref, keyval_ref, probs_ref), scratch)
    query_grad = dq_s[...]
    qbias_ref[...] += jnp.sum(query_grad, 0, keepdims=True)
    mix_ref[0, :, :width] = query_grad.astype(bf16)
    for ref, low, high in (
        (own_ref, RIM, RIM + slots),
        (left_ref, 0, RIM),
        (right_ref, RIM + slots, slots + 2 * RIM),
    ):
        ref[0, :, :width] = acck_s[low:high, :].astype(ref.dtype)
        ref[0, :, width:] = accv_s[low:high, :].astype(ref.dtype)

    @pl.when(sample == pl.num_programs(0) - 1)
    def _():
        atom_bwd_pairs(starts, pairs_ref, bias_s, pairw_ref, pairm_ref)


def atom_bwd_sum_kernel(
    summing,
    starts,
    grad_ref,
    query_ref,
    keyval_ref,
    gate_ref,
    probs_ref,
    attend_ref,
    mid_ref,
    rows_ref,
    pairs_ref,
    share_ref,
    wide_ref,
    down_ref,
    units_ref,
    atomgrad_ref,
    qbias_ref,
    pairw_ref,
    pairm_ref,
    small_ref,
    shares_ref,
    acck_s,
    accv_s,
    bias_s,
    attlow_s,
    dq_s,
    mix_s,
    midgrad_s,
    outw_s,
    upw_s,
    downw_s,
    pool_s,
    proj_s,
    to_left,
    to_right,
    from_left,
    from_right,
    s_rim,
    r_rim,
    *sums,
):
    summing.bind(units_ref, shares_ref, *sums)
    z, me = lax.axis_index("samp"), lax.axis_index("seq")
    seq = lax.axis_size("seq")
    first_place, last_place = me == 0, me == seq - 1
    width = query_ref.shape[-1]
    slots = query_ref.shape[1]
    step = pl.program_id(0)
    samples = pl.num_programs(0) - 1
    summing.slot(2 * step)

    def rim(b, side):
        ends = ((to_left, from_right, me - 1), (to_right, from_left, me + 1))[side]
        source, target, device = ends
        return remote(source.at[b], target.at[b], s_rim.at[side, b], r_rim.at[side, b], (z, device))

    def arrived(b, side):
        target = (from_right, from_left)[side]
        return remote(
            target.at[b], target.at[b], s_rim.at[side, b], r_rim.at[side, b], (z, lax.rem(me + 1, seq))
        )

    @pl.when(step == 0)
    def _():
        for ref in (qbias_ref, outw_s, upw_s, downw_s, pool_s, proj_s, pairw_ref, pairm_ref, bias_s):
            ref[...] = jnp.zeros_like(ref)

        @pl.when(first_place)
        def _():
            from_left[...] = jnp.zeros_like(from_left)

        @pl.when(last_place)
        def _():
            from_right[...] = jnp.zeros_like(from_right)

    slot_now = step % 2

    @pl.when(step < samples)
    def _():
        atom_bwd_dense(
            (grad_ref, query_ref, gate_ref, attend_ref, mid_ref),
            (share_ref, wide_ref, down_ref),
            (outw_s, upw_s, downw_s, pool_s),
            attlow_s,
            mix_s.at[slot_now, :, width:],
            midgrad_s.at[slot_now],
        )

    summing.slot(2 * step + 1)

    @pl.when(step > 0)
    def _():
        b = step - 1

        @pl.when(~first_place)
        def _():
            arrived(b, 1).wait_recv()

        @pl.when(~last_place)
        def _():
            arrived(b, 0).wait_recv()

        normed, inv_std = norm_stats(rows_ref[0].astype(f32))
        parts = []
        for acc, lanes in ((acck_s, slice(0, width)), (accv_s, slice(width, 2 * width))):
            own = acc[RIM : RIM + slots, :]
            begin = own[:RIM] + from_left[b, :, lanes].astype(f32)
            end = own[slots - RIM :] + from_right[b, :, lanes].astype(f32)
            parts.append(jnp.concatenate([begin, own[RIM : slots - RIM], end], 0).astype(bf16))
        before = mix_s.at[1 - slot_now]
        mix = jnp.concatenate([before[:, :width], parts[0], parts[1], before[:, width:]], 1)
        proj_s[...] += mm_tn(normed.astype(bf16), mix)
        normed_grad = mm_nt(mix, wide_ref[:, : 4 * width])
        atomgrad_ref[0] = midgrad_s[1 - slot_now] + norm_back(normed, inv_std, normed_grad)

    @pl.when(step < samples)
    def _():
        atom_bwd_windows(
            (query_ref, keyval_ref, probs_ref), (acck_s, accv_s, bias_s, attlow_s, dq_s)
        )
        query_grad = dq_s[...]
        qbias_ref[...] += jnp.sum(query_grad, 0, keepdims=True)
        mix_s[slot_now, :, :width] = query_grad.astype(bf16)
        for ref, low in ((to_left, 0), (to_right, RIM + slots)):
            ref[step, :, :width] = acck_s[low : low + RIM, :].astype(bf16)
            ref[step, :, width:] = accv_s[low : low + RIM, :].astype(bf16)

        @pl.when(~first_place)
        def _():
            rim(step, 0).start()

        @pl.when(~last_place)
        def _():
            rim(step, 1).start()

    @pl.when(step == samples)
    def _():
        atom_bwd_pairs(starts, pairs_ref, bias_s, pairw_ref, pairm_ref)
        samp = small_ref.shape[0]
        rows = width // samp
        for p in range(samp):
            span = slice(p * rows, (p + 1) * rows)
            small_ref[p, :rows, :] = pool_s[span, :].astype(bf16)
            small_ref[p, rows : 2 * rows, : 4 * width] = proj_s[span, :].astype(bf16)
            for part in range(2):
                low = (2 * p + part) * rows
                small_ref[p, rows : 2 * rows, (4 + part) * width : (5 + part) * width] = downw_s[
                    low : low + rows, :
                ].astype(bf16)
            small_ref[p, 2 * rows : 3 * rows, : 4 * width] = upw_s[span, :].astype(bf16)
            small_ref[p, 2 * rows : 3 * rows, 4 * width : 5 * width] = outw_s[span, :].astype(bf16)
            small_ref[p, 2 * rows : 3 * rows, 5 * width :] = jnp.zeros((rows, width), bf16)
            small_ref[p, 3 * rows :, :] = jnp.zeros((rows, 6 * width), bf16)
        summing.collect()

        def sent(b, carry):
            @pl.when(~first_place)
            def _():
                rim(b, 0).wait_send()

            @pl.when(~last_place)
            def _():
                rim(b, 1).wait_send()

            return carry

        lax.fori_loop(0, samples, sent, 0)


def atom_backward_sum(grad, starts, stored, rows, pairs, share, wide, down, summing, units):
    query = stored[0]
    samples, slots, width = query.shape
    samp = lax.axis_size("samp")
    ext_slots = slots + 2 * RIM
    windows = slots // WIN_Q
    model_width = grad.shape[-1]
    hidden_width = down.shape[0]
    stack = ATOM_HEADS * WIN_Q
    place = pl.BlockSpec(memory_space=pl.ANY)

    def now(shape):
        return pl.BlockSpec(
            (1,) + shape, lambda g: (jnp.minimum(g, samples - 1),) + (0,) * len(shape)
        )

    def late(shape):
        return pl.BlockSpec((1,) + shape, lambda g: (jnp.maximum(g - 1, 0),) + (0,) * len(shape))

    dma = pltpu.SemaphoreType.DMA
    rim_shape = (samples, RIM, 2 * width)
    small_shape = (samp, 4 * width // samp, model_width)
    return pl.pallas_call(
        functools.partial(atom_bwd_sum_kernel, summing),
        out_shape=[
            jax.ShapeDtypeStruct(rows.shape, f32),
            jax.ShapeDtypeStruct((1, width), f32),
            jax.ShapeDtypeStruct((stack, pairs.shape[1]), f32),
            jax.ShapeDtypeStruct((stack, WIN_K), f32),
            jax.ShapeDtypeStruct(small_shape, bf16),
            jax.ShapeDtypeStruct((UNIT, 768), bf16),
        ],
        grid=(samples + 1,),
        in_specs=[pl.BlockSpec(memory_space=pltpu.SMEM), now(grad.shape[1:])]
        + [now(part.shape[1:]) for part in stored]
        + [late(rows.shape[1:])]
        + [whole(part.shape) for part in (pairs, share, wide, down)]
        + [place],
        out_specs=[
            late(rows.shape[1:]),
            whole((1, width)),
            whole((stack, pairs.shape[1])),
            whole((stack, WIN_K)),
            whole(small_shape),
            place,
        ],
        scratch_shapes=[
            pltpu.VMEM((ext_slots, width), f32),
            pltpu.VMEM((ext_slots, width), f32),
            pltpu.VMEM((windows // 2, 2 * stack, 2 * WIN_K), f32),
            pltpu.VMEM((slots, width), bf16),
            pltpu.VMEM((slots, width), f32),
            pltpu.VMEM((2, slots, 2 * width), bf16),
            pltpu.VMEM((2, slots, width), f32),
            pltpu.VMEM((width, width), f32),
            pltpu.VMEM((width, 2 * hidden_width), f32),
            pltpu.VMEM((hidden_width, width), f32),
            pltpu.VMEM((width, model_width), f32),
            pltpu.VMEM((width, 4 * width), f32),
            pltpu.VMEM(rim_shape, bf16),
            pltpu.VMEM(rim_shape, bf16),
            pltpu.VMEM(rim_shape, bf16),
            pltpu.VMEM(rim_shape, bf16),
            dma((2, samples)),
            dma((2, samples)),
        ]
        + summing.scratch(),
        compiler_params=summing.params(),
        name="atom_backward",
    )(starts, grad, *stored, rows, pairs, share, wide, down, units)


def unpack_kernel(units_ref, small_ref, proj_ref, up_ref, down_ref, cond_ref, outw_ref, *atoms):
    proj_ref[...] = units_ref[0, :192, :384].astype(f32)
    up_ref[...] = units_ref[0, :192, 384:].astype(f32)
    down_ref[...] = units_ref[0, 192:240, :].astype(f32)
    cond_ref[:, :768] = units_ref[0, 240:288, :].astype(f32)
    cond_ref[:, 768:] = units_ref[0, 288:336, :384].astype(f32)
    outw_ref[...] = units_ref[0, 288:336, 384:].astype(f32)

    @pl.when(pl.program_id(0) == 0)
    def _():
        pool_ref, atomproj_ref, atomdown_ref, atomup_ref, atomout_ref, tiny_ref = atoms
        rows, width = atomout_ref.shape
        pool_ref[...] = small_ref[:rows, :].astype(f32)
        atomproj_ref[...] = small_ref[rows : 2 * rows, : 4 * width].astype(f32)
        for part in range(2):
            atomdown_ref[part * rows : (part + 1) * rows, :] = small_ref[
                rows : 2 * rows, (4 + part) * width : (5 + part) * width
            ].astype(f32)
        atomup_ref[...] = small_ref[2 * rows : 3 * rows, : 4 * width].astype(f32)
        atomout_ref[...] = small_ref[2 * rows : 3 * rows, 4 * width : 5 * width].astype(f32)
        tiny_ref[...] = small_ref[2 * rows : 3 * rows, 5 * width :].astype(f32)


def unpack(units, small, shapes, rows, width):
    outs = list(shapes) + [
        (rows, 6 * width),
        (rows, 4 * width),
        (2 * rows, width),
        (rows, 4 * width),
        (rows, width),
        (rows, width),
    ]
    specs = [
        pl.BlockSpec((192, 384), lambda s: (0, s)),
        pl.BlockSpec((192, 384), lambda s: (0, s)),
        pl.BlockSpec((48, 768), lambda s: (s, 0)),
        pl.BlockSpec((48, 1152), lambda s: (s // 4, s % 4)),
        pl.BlockSpec((48, 384), lambda s: (s // 2, s % 2)),
    ]
    return pl.pallas_call(
        unpack_kernel,
        out_shape=[jax.ShapeDtypeStruct(shape, f32) for shape in outs],
        grid=(8,),
        in_specs=[pl.BlockSpec((1, UNIT, 768), lambda s: (s, 0, 0)), whole(small.shape)],
        out_specs=specs + [whole(shape) for shape in outs[5:]],
        compiler_params=params(),
        name="unpack",
    )(units, small)


def atom_backward(grad, starts, stored, pairs, share, wide, down):
    query = stored[0]
    samples, slots, width = query.shape
    ext_slots = slots + 2 * RIM
    windows = slots // WIN_Q
    model_width = grad.shape[-1]
    hidden_width = down.shape[0]
    stack = ATOM_HEADS * WIN_Q
    outs = (
        ((slots, 2 * width), bf16),
        ((slots, 2 * width), f32),
        ((RIM, 2 * width), bf16),
        ((RIM, 2 * width), bf16),
        ((slots, width), f32),
    )
    totals = (
        (1, width),
        (width, width),
        (width, 2 * hidden_width),
        (hidden_width, width),
        (width, model_width),
        (stack, pairs.shape[1]),
        (stack, WIN_K),
    )
    return pl.pallas_call(
        atom_bwd_kernel,
        out_shape=[jax.ShapeDtypeStruct((samples,) + shape, kind) for shape, kind in outs]
        + [jax.ShapeDtypeStruct(shape, f32) for shape in totals],
        grid=(samples,),
        in_specs=[pl.BlockSpec(memory_space=pltpu.SMEM), per_sample(grad.shape[1:])]
        + [per_sample(part.shape[1:]) for part in stored]
        + [whole(part.shape) for part in (pairs, share, wide, down)],
        out_specs=[per_sample(shape) for shape, _ in outs] + [whole(shape) for shape in totals],
        scratch_shapes=[
            pltpu.VMEM((ext_slots, width), f32),
            pltpu.VMEM((ext_slots, width), f32),
            pltpu.VMEM((windows // 2, 2 * stack, 2 * WIN_K), f32),
            pltpu.VMEM((slots, width), bf16),
            pltpu.VMEM((slots, width), f32),
        ],
        compiler_params=params(),
        name="atom_backward",
    )(starts, grad, *stored, pairs, share, wide, down)


def atom_input_kernel(
    rows_ref, mix_ref, own_ref, left_ref, right_ref, midgrad_ref, wide_ref, grad_ref, proj_ref
):
    width = rows_ref.shape[-1]

    @pl.when(pl.program_id(0) == 0)
    def _():
        proj_ref[...] = jnp.zeros_like(proj_ref)

    normed, inv_std = norm_stats(rows_ref[0].astype(f32))
    slots = normed.shape[0]
    own = own_ref[0]
    head = own[:RIM] + left_ref[0].astype(f32)
    tail = own[slots - RIM :] + right_ref[0].astype(f32)
    own = jnp.concatenate([head, own[RIM : slots - RIM], tail], 0).astype(bf16)
    mix = jnp.concatenate([mix_ref[0, :, :width], own, mix_ref[0, :, width:]], 1)
    proj_ref[...] += mm_tn(normed.astype(bf16), mix)
    normed_grad = mm_nt(mix, wide_ref[:, : 4 * width])
    grad_ref[0] = midgrad_ref[0] + norm_back(normed, inv_std, normed_grad)


def atom_input_backward(rows, mix, own, left, right, midgrad, wide):
    samples, slots, width = rows.shape
    return pl.pallas_call(
        atom_input_kernel,
        out_shape=[
            jax.ShapeDtypeStruct(rows.shape, f32),
            jax.ShapeDtypeStruct((width, 4 * width), f32),
        ],
        grid=(samples,),
        in_specs=[per_sample(part.shape[1:]) for part in (rows, mix, own, left, right, midgrad)]
        + [whole(wide.shape)],
        out_specs=[per_sample((slots, width)), whole((width, 4 * width))],
        compiler_params=params(),
        name="atom_input_backward",
    )(rows, mix, own, left, right, midgrad, wide)


def row_stats(pairs, ones_op, weights):
    count = weights.shape[0]
    both = mm_nt(jnp.concatenate([weights, ones_op], 0), pairs)
    upper, lower = square_sums(ones_op, pairs.astype(f32) * pairs.astype(f32))
    features = pairs.shape[1]
    mean = both[count : count + 1] * (1.0 / features)
    square = (mm_nt(ones_op, upper) + mm_nt(ones_op, lower))[:1] * (1.0 / features)
    var = jnp.maximum(square - mean * mean, 0.0)
    return both[:count], mean, lax.rsqrt(var + norm_eps)


def pair_bias_kernel(pair_ref, weight_ref, bias_ref):
    weights = weight_ref[...]
    ones_op = jnp.ones((16, weights.shape[1]), bf16)
    weight_sum = jnp.sum(weights.astype(f32), -1, keepdims=True)
    for row in range(pair_ref.shape[0]):
        product, mean, inv_std = row_stats(pair_ref[row], ones_op, weights)
        bias_ref[:, row, :] = inv_std * (product - mean * weight_sum)


def pair_bias(pairs, weights):
    rows, keys, features = pairs.shape
    heads = weights.shape[0]
    return pl.pallas_call(
        pair_bias_kernel,
        out_shape=jax.ShapeDtypeStruct((heads, rows, keys), f32),
        grid=(rows // 8,),
        in_specs=[pl.BlockSpec((8, keys, features), lambda i: (i, 0, 0)), whole(weights.shape)],
        out_specs=pl.BlockSpec((heads, 8, keys), lambda i: (0, i, 0)),
        compiler_params=params(),
        name="pair_bias",
    )(pairs, weights)


def pair_grad_kernel(pair_ref, grad_ref, weight_ref, total_ref, mean_ref):
    @pl.when(pl.program_id(0) == 0)
    def _():
        total_ref[...] = jnp.zeros_like(total_ref)
        mean_ref[...] = jnp.zeros_like(mean_ref)

    heads = grad_ref.shape[0]
    ones_op = jnp.ones((16, pair_ref.shape[2]), bf16)
    total = jnp.zeros(total_ref.shape, f32)
    means = jnp.zeros(mean_ref.shape, f32)
    for row in range(pair_ref.shape[0]):
        pairs = pair_ref[row]
        _, mean, inv_std = row_stats(pairs, ones_op, weight_ref[...])
        scaled = grad_ref[:, row, :] * inv_std
        means += scaled * mean
        upper = scaled.astype(bf16)
        lower = (scaled - upper.astype(f32)).astype(bf16)
        both = mm(jnp.concatenate([upper, lower], 0), pairs)
        total += both[:heads] + both[heads:]
    total_ref[...] += total
    mean_ref[...] += means


def pair_grad(pairs, grads, weights):
    rows, keys, features = pairs.shape
    heads = grads.shape[0]
    total, means = pl.pallas_call(
        pair_grad_kernel,
        out_shape=[
            jax.ShapeDtypeStruct((heads, features), f32),
            jax.ShapeDtypeStruct((heads, keys), f32),
        ],
        grid=(rows // 8,),
        in_specs=[
            pl.BlockSpec((8, keys, features), lambda i: (i, 0, 0)),
            pl.BlockSpec((heads, 8, keys), lambda i: (0, i, 0)),
            whole(weights.shape),
        ],
        out_specs=[whole((heads, features)), whole((heads, keys))],
        compiler_params=params(),
        name="pair_grad",
    )(pairs, grads, weights)
    return total - jnp.sum(means, -1, keepdims=True)


def head_groups(width, heads):
    head_dim = width // heads
    groups = []
    for head in range(0, heads, 4):
        low = head * head_dim
        base = low // LANES * LANES
        groups.append((head, base, low - base))
    return head_dim, groups


def token_fwd_kernel(query_ref, keyval_ref, bias_ref, attend_ref, probs_ref, fold_s):
    tokens, width = query_ref.shape[1:]
    heads = bias_ref.shape[0]
    keys = bias_ref.shape[2]
    head_dim, groups = head_groups(width, heads)
    scale = float(head_dim) ** (-0.5)
    fold_s[...] = jnp.zeros_like(fold_s)
    for head, base, first in groups:
        span = slice(base, base + 256)
        key_rows = keyval_ref[:, 0, :, base : base + 256].reshape(keys, 256)
        value_rows = keyval_ref[:, 0, :, width + base : width + base + 256].reshape(keys, 256)
        stacked = head_stack(query_ref[0, :, span], 4, head_dim, first)
        bias = bias_ref[head : head + 4].reshape(4 * tokens, keys)
        scores = mm_nt(stacked, key_rows) * scale + bias
        exp_scores = jnp.exp(scores - jnp.max(scores, -1, keepdims=True))
        probs = exp_scores * (1.0 / jnp.sum(exp_scores, -1, keepdims=True))
        probs_low = probs.astype(bf16)
        probs_ref[0, head : head + 4] = probs_low.reshape(4, tokens, keys)
        fold_s[:, span] += head_fold(mm(probs_low, value_rows), 4, head_dim, first)
    attend_ref[0] = fold_s[...]


def token_attention(query, keyval, bias):
    samples, tokens, width = query.shape
    heads, _, keys = bias.shape
    devices = keyval.shape[0]
    return pl.pallas_call(
        token_fwd_kernel,
        out_shape=[
            jax.ShapeDtypeStruct(query.shape, f32),
            jax.ShapeDtypeStruct((samples, heads, tokens, keys), bf16),
        ],
        grid=(samples,),
        in_specs=[
            per_sample((tokens, width)),
            pl.BlockSpec((devices, 1, tokens, 2 * width), lambda b: (0, b, 0, 0)),
            whole(bias.shape),
        ],
        out_specs=[per_sample((tokens, width)), per_sample((heads, tokens, keys))],
        scratch_shapes=[pltpu.VMEM((tokens, width), f32)],
        compiler_params=params(),
        name="token_attention",
    )(query, keyval, bias)


def token_bwd_kernel(
    query_ref, keyval_ref, probs_ref, att_ref, dq_ref, dkv_ref, bias_ref, fold_s, grad_s
):
    tokens, width = query_ref.shape[1:]
    heads, _, keys = bias_ref.shape
    devices = keyval_ref.shape[0]
    head_dim, groups = head_groups(width, heads)
    scale = float(head_dim) ** (-0.5)

    @pl.when(pl.program_id(0) == 0)
    def _():
        bias_ref[...] = jnp.zeros_like(bias_ref)

    fold_s[...] = jnp.zeros_like(fold_s)
    grad_s[...] = jnp.zeros_like(grad_s)
    for head, base, first in groups:
        span = slice(base, base + 256)
        key_rows = keyval_ref[:, 0, :, base : base + 256].reshape(keys, 256)
        value_rows = keyval_ref[:, 0, :, width + base : width + base + 256].reshape(keys, 256)
        queries = head_stack(query_ref[0, :, span], 4, head_dim, first)
        att = head_stack(att_ref[0, :, span], 4, head_dim, first)
        probs_low = probs_ref[0, head : head + 4].reshape(4 * tokens, keys)
        probs = probs_low.astype(f32)
        prob_grad = mm_nt(att, value_rows)
        delta = jnp.sum(prob_grad * probs, -1, keepdims=True)
        score_low = (probs * (prob_grad - delta)).astype(bf16)
        bias_ref[head : head + 4] += score_low.astype(f32).reshape(4, tokens, keys)
        fold_s[:, span] += head_fold(mm(score_low, key_rows), 4, head_dim, first) * scale
        grad_s[:, span] += mm_tn(score_low, queries) * scale
        grad_s[:, width + base : width + base + 256] += mm_tn(probs_low, att)
    dq_ref[0] = fold_s[...]
    dkv_ref[:, 0] = grad_s[...].astype(bf16).reshape(devices, tokens, 2 * width)


def token_attention_back(query, keyval, probs, att):
    samples, tokens, width = query.shape
    heads, _, keys = probs.shape[1:]
    devices = keyval.shape[0]
    return pl.pallas_call(
        token_bwd_kernel,
        out_shape=[
            jax.ShapeDtypeStruct(query.shape, f32),
            jax.ShapeDtypeStruct(keyval.shape, bf16),
            jax.ShapeDtypeStruct((heads, tokens, keys), f32),
        ],
        grid=(samples,),
        in_specs=[
            per_sample((tokens, width)),
            pl.BlockSpec((devices, 1, tokens, 2 * width), lambda b: (0, b, 0, 0)),
            per_sample((heads, tokens, keys)),
            per_sample((tokens, width)),
        ],
        out_specs=[
            per_sample((tokens, width)),
            pl.BlockSpec((devices, 1, tokens, 2 * width), lambda b: (0, b, 0, 0)),
            whole((heads, tokens, keys)),
        ],
        scratch_shapes=[
            pltpu.VMEM((tokens, width), f32),
            pltpu.VMEM((keys, 2 * width), f32),
        ],
        compiler_params=params(),
        name="token_attention_back",
    )(query, keyval, probs, att)


def attend_groups(heads, width, tokens, query, keyval, bias, probs_ref, fold_s):
    head_dim, groups = head_groups(width, heads)
    scale = float(head_dim) ** (-0.5)
    fold_s[...] = jnp.zeros_like(fold_s)
    for head, base, first in groups:
        span = slice(base, base + 256)
        stacked = head_stack(query[:, span], 4, head_dim, first)
        scores = mm_nt(stacked, keyval(base)) * scale + bias(head)
        exp_scores = jnp.exp(scores - jnp.max(scores, -1, keepdims=True))
        probs = exp_scores * (1.0 / jnp.sum(exp_scores, -1, keepdims=True))
        probs_low = probs.astype(bf16)
        probs_ref[0, head : head + 4] = probs_low.reshape(4, tokens, -1)
        fold_s[:, span] += head_fold(mm(probs_low, keyval(width + base)), 4, head_dim, first)


def gather_attend_kernel(
    query_ref,
    own_ref,
    pair_ref,
    weight_ref,
    attend_ref,
    probs_ref,
    keyval_ref,
    stats_ref,
    all_s,
    bias_s,
    fold_s,
    send,
    recv,
    load,
):
    z, me, sib, xn, yn, dg = places()
    step = pl.program_id(0)
    tokens, width = query_ref.shape[1:]
    heads = weight_ref.shape[0]
    devices, samples = all_s.shape[:2]
    keys = devices * tokens
    head, tail, full = slice(0, width), slice(width, 2 * width), slice(0, 2 * width)

    def unit(part, sample, lanes, kind, device):
        ref = all_s.at[part, sample, :, lanes]
        return remote(ref, ref, send.at[kind, sample], recv.at[kind, sample], (z, device))

    def issue(sample):
        unit(me, sample, full, 0, xn).start()
        unit(me, sample, full, 1, yn).start()
        unit(me, sample, full, 4, sib).start()

    def relay(sample):
        unit(xn, sample, full, 0, xn).wait_recv()
        unit(xn, sample, head, 2, yn).start()
        unit(xn, sample, full, 5, sib).start()
        unit(yn, sample, full, 1, yn).wait_recv()
        unit(yn, sample, tail, 3, xn).start()
        unit(yn, sample, full, 6, sib).start()

    def collect(sample):
        unit(dg, sample, head, 2, yn).wait_recv()
        unit(dg, sample, tail, 3, xn).wait_recv()
        unit(dg, sample, full, 7, sib).start()

    @pl.when(step == 0)
    def _():
        copy = pltpu.make_async_copy(own_ref, all_s.at[me], load)
        copy.start()
        greet([(z, sib), (z, xn), (z, yn)])
        copy.wait()
        issue(0)
        issue(1)

    @pl.when((step >= 1) & (step + 1 < samples))
    def _():
        issue(step + 1)

    @pl.when((step >= 1) & (step - 1 < samples))
    def _():
        relay(step - 1)

    @pl.when(step < 2)
    def _():
        weights = weight_ref[...]
        ones_op = jnp.ones((16, weights.shape[1]), bf16)
        weight_sum = jnp.sum(weights.astype(f32), -1, keepdims=True)
        groups = pair_ref.shape[0] // 8

        def one(group, carry):
            for row in range(8):
                product, mean, inv_std = row_stats(pair_ref[group * 8 + row], ones_op, weights)
                place = step * groups + group
                bias_s[:, place, row, :] = inv_std * (product - mean * weight_sum)
                stats_ref[0, place, row : row + 1, :] = mean
                stats_ref[1, place, row : row + 1, :] = inv_std
            return carry

        lax.fori_loop(0, groups, one, 0)

    @pl.when(step >= 2)
    def _():
        sample = step - 2
        collect(sample)
        for kind, part in ((4, sib), (5, sib), (6, sib), (7, sib)):
            unit(part, sample, full, kind, sib).wait_recv()
        for part in range(devices):
            keyval_ref[part, 0] = all_s[part, sample]
        attend_groups(
            heads,
            width,
            tokens,
            query_ref[0],
            lambda base: keyval_ref[:, 0, :, base : base + 256].reshape(keys, 256),
            lambda head: bias_s[head : head + 4].reshape(4 * tokens, keys),
            probs_ref,
            fold_s,
        )
        attend_ref[0] = fold_s[...]

    @pl.when(step == pl.num_programs(0) - 1)
    def _():
        def sent(sample, carry):
            for kind in (0, 1, 4, 5, 6, 7):
                unit(me, sample, full, kind, sib).wait_send()
            unit(me, sample, head, 2, sib).wait_send()
            unit(me, sample, tail, 3, sib).wait_send()
            return carry

        lax.fori_loop(0, samples, sent, 0)


def gather_attend(query, own, pairs, weights, seq):
    samples, tokens, width = query.shape
    heads, features = weights.shape
    keys = seq * tokens
    late = lambda g: jnp.maximum(g - 2, 0)
    sample_block = lambda shape: pl.BlockSpec((1,) + shape, lambda g: (late(g),) + (0,) * len(shape))
    dma = pltpu.SemaphoreType.DMA
    return pl.pallas_call(
        gather_attend_kernel,
        out_shape=[
            jax.ShapeDtypeStruct(query.shape, f32),
            jax.ShapeDtypeStruct((samples, heads, tokens, keys), bf16),
            jax.ShapeDtypeStruct((seq, samples, tokens, 2 * width), bf16),
            jax.ShapeDtypeStruct((2, tokens // 8, 8, keys), f32),
        ],
        grid=(samples + 2,),
        in_specs=[
            sample_block((tokens, width)),
            pl.BlockSpec(memory_space=pl.ANY),
            pl.BlockSpec((tokens // 2, keys, features), lambda g: (jnp.minimum(g, 1), 0, 0)),
            whole(weights.shape),
        ],
        out_specs=[
            sample_block((tokens, width)),
            sample_block((heads, tokens, keys)),
            pl.BlockSpec((seq, 1, tokens, 2 * width), lambda g: (0, late(g), 0, 0)),
            whole((2, tokens // 8, 8, keys)),
        ],
        scratch_shapes=[
            pltpu.VMEM((seq, samples, tokens, 2 * width), bf16),
            pltpu.VMEM((heads, tokens // 8, 8, keys), f32),
            pltpu.VMEM((tokens, width), f32),
            dma((8, samples)),
            dma((8, samples)),
            dma,
        ],
        compiler_params=pltpu.CompilerParams(
            vmem_limit_bytes=vmem_bytes, collective_id=4, has_side_effects=True
        ),
        name="gather_attend",
    )(query, own, pairs, weights)


def attend_back_scatter_kernel(
    query_ref,
    keyval_ref,
    probs_ref,
    att_ref,
    pair_ref,
    stats_ref,
    ffn_ref,
    upper_ref,
    hidden_ref,
    two_ref,
    gated_ref,
    branch_ref,
    dq_ref,
    dkv_ref,
    pairw_ref,
    pairm_ref,
    upw_ref,
    downw_ref,
    outw_ref,
    fold_s,
    grad_s,
    bias_s,
    mine,
    theirs,
    from_x,
    from_y,
    last_x,
    last_y,
    s_sib,
    r_sib,
    s_one,
    r_one,
    s_two,
    r_two,
):
    z, me, sib, xn, yn, dg = places()
    core, chip = me % 2, me // 2
    chip_x, chip_y, chip_d = xn // 2, yn // 2, dg // 2
    step = pl.program_id(0)
    tokens, width = query_ref.shape[1:]
    samples = mine.shape[0]
    heads, keys = probs_ref.shape[1], probs_ref.shape[3]
    head_dim, groups = head_groups(width, heads)
    scale = float(head_dim) ** (-0.5)
    head, tail = slice(0, width), slice(width, 2 * width)

    def there(b):
        return remote(
            mine.at[b, :, 1 - core], theirs.at[b], s_sib.at[b], r_sib.at[b], (z, sib)
        )

    def one(b, k):
        part = (chip_x, chip_d, chip_y, chip_d)[k]
        lanes = head if k < 2 else tail
        target = (from_x if k < 2 else from_y).at[b, k % 2]
        device = xn if k < 2 else yn
        source = mine.at[b, part, core, :, lanes]
        return remote(source, target, s_one.at[b, k], r_one.at[b, k], (z, device))

    def two(b, k):
        part, lanes, target, device = ((chip_y, head, last_y, yn), (chip_x, tail, last_x, xn))[k]
        source = mine.at[b, part, core, :, lanes]
        return remote(source, target.at[b], s_two.at[b, k], r_two.at[b, k], (z, device))

    def add(b, part, lanes, source):
        both = mine[b, part, core, :, lanes].astype(f32) + source.astype(f32)
        mine[b, part, core, :, lanes] = both.astype(bf16)

    @pl.when(step == 0)
    def _():
        greet([(z, sib), (z, xn), (z, yn)])
        bias_s[...] = jnp.zeros_like(bias_s)
        pairw_ref[...] = jnp.zeros_like(pairw_ref)
        pairm_ref[...] = jnp.zeros_like(pairm_ref)

    @pl.when((step >= 1) & (step - 1 < samples))
    def _():
        b = step - 1
        there(b).wait_recv()

        def chips(j, carry):
            add(b, j, slice(0, 2 * width), theirs[b, j])
            return carry

        lax.fori_loop(0, 4, chips, 0)
        for k in range(4):
            one(b, k).start()

    @pl.when((step >= 2) & (step - 2 < samples))
    def _():
        b = step - 2
        one(b, 1).wait_recv()
        add(b, chip_y, head, from_x[b, 1])
        two(b, 0).start()
        one(b, 3).wait_recv()
        add(b, chip_x, tail, from_y[b, 1])
        two(b, 1).start()
        one(b, 0).wait_recv()
        add(b, chip, head, from_x[b, 0])
        one(b, 2).wait_recv()
        add(b, chip, tail, from_y[b, 0])

    @pl.when((step >= 3) & (step - 3 < samples))
    def _():
        b = step - 3
        two(b, 0).wait_recv()
        add(b, chip, head, last_y[b])
        two(b, 1).wait_recv()
        add(b, chip, tail, last_x[b])
        dkv_ref[0] = mine[b, chip, core]

    @pl.when(step < samples)
    def _():
        fold_s[...] = jnp.zeros_like(fold_s)
        grad_s[...] = jnp.zeros_like(grad_s)
        for first_head, base, first in groups:
            span = slice(base, base + 256)
            key_rows = keyval_ref[:, 0, :, base : base + 256].reshape(keys, 256)
            value_rows = keyval_ref[:, 0, :, width + base : width + base + 256].reshape(keys, 256)
            queries = head_stack(query_ref[0, :, span], 4, head_dim, first)
            att = head_stack(att_ref[0, :, span], 4, head_dim, first)
            probs_low = probs_ref[0, first_head : first_head + 4].reshape(4 * tokens, keys)
            probs = probs_low.astype(f32)
            prob_grad = mm_nt(att, value_rows)
            delta = jnp.sum(prob_grad * probs, -1, keepdims=True)
            score_low = (probs * (prob_grad - delta)).astype(bf16)
            bias_s[first_head : first_head + 4] += score_low.astype(f32).reshape(
                4, tokens // 8, 8, keys
            )
            fold_s[:, span] += head_fold(mm(score_low, key_rows), 4, head_dim, first) * scale
            grad_s[:, span] += mm_tn(score_low, queries) * scale
            grad_s[:, width + base : width + base + 256] += mm_tn(probs_low, att)
        dq_ref[0] = fold_s[...]
        mine[step] = grad_s[...].astype(bf16).reshape(mine.shape[1:])
        there(step).start()
        upw_ref[...] = mm_tn(ffn_ref[...], upper_ref[...]).astype(bf16)

    @pl.when(step < 6)
    def _():
        downw_ref[...] = mm_tn(hidden_ref[...], two_ref[...]).astype(bf16)

    @pl.when((step >= 6) & (step < 8))
    def _():
        outw_ref[...] = mm_tn(gated_ref[...], branch_ref[...]).astype(bf16)

    @pl.when((step >= samples) & (step < samples + 2))
    def _():
        rows = pair_ref.shape[0] // 8

        def some(group, carry):
            total, means = carry
            place = (step - samples) * rows + group
            for row in range(8):
                inv_std = stats_ref[1, place, row : row + 1, :]
                scaled = bias_s[:, place, row, :] * inv_std
                means += scaled * stats_ref[0, place, row : row + 1, :]
                upper = scaled.astype(bf16)
                lower = (scaled - upper.astype(f32)).astype(bf16)
                both = mm(jnp.concatenate([upper, lower], 0), pair_ref[group * 8 + row])
                total += both[:heads] + both[heads:]
            return total, means

        zeros = (jnp.zeros(pairw_ref.shape, f32), jnp.zeros(pairm_ref.shape, f32))
        total, means = lax.fori_loop(0, rows, some, zeros)
        pairw_ref[...] += total
        pairm_ref[...] += means

    @pl.when(step == pl.num_programs(0) - 1)
    def _():
        def sent(b, carry):
            there(b).wait_send()
            for k in range(4):
                one(b, k).wait_send()
            for k in range(2):
                two(b, k).wait_send()
            return carry

        lax.fori_loop(0, samples, sent, 0)


def attend_back_scatter(query, keyval, probs, att, pairs, stats, ffn, upper, hidden, two, gated, branch):
    samples, tokens, width = query.shape
    heads, _, keys = probs.shape[1:]
    seq = keyval.shape[0]
    features = pairs.shape[-1]
    flat = [part.reshape(-1, part.shape[-1]) for part in (ffn, upper, hidden, two, gated, branch)]
    rows = flat[0].shape[0]
    held = lambda g: jnp.minimum(g, samples - 1)
    late = lambda g: jnp.clip(g - 3, 0, samples - 1)
    pair_step = lambda g: jnp.clip(g - samples, 0, 1)
    up_step = lambda g: jnp.minimum(g, seq - 1)
    down_step = lambda g: jnp.minimum(g, 5)
    out_step = lambda g: jnp.clip(g - 6, 0, 1)
    sample_block = lambda shape, at: pl.BlockSpec((1,) + shape, lambda g: (at(g),) + (0,) * len(shape))
    keyval_block = pl.BlockSpec((seq, 1, tokens, 2 * width), lambda g: (0, held(g), 0, 0))
    up_width = flat[1].shape[1] // seq
    hidden_width = flat[2].shape[1]
    dma = pltpu.SemaphoreType.DMA
    results = pl.pallas_call(
        attend_back_scatter_kernel,
        out_shape=[
            jax.ShapeDtypeStruct(query.shape, f32),
            jax.ShapeDtypeStruct((samples, tokens, 2 * width), bf16),
            jax.ShapeDtypeStruct((heads, features), f32),
            jax.ShapeDtypeStruct((heads, keys), f32),
            jax.ShapeDtypeStruct((width, flat[1].shape[1]), bf16),
            jax.ShapeDtypeStruct((hidden_width, width), bf16),
            jax.ShapeDtypeStruct((width, width), bf16),
        ],
        grid=(samples + 3,),
        in_specs=[
            sample_block((tokens, width), held),
            keyval_block,
            sample_block((heads, tokens, keys), held),
            sample_block((tokens, width), held),
            pl.BlockSpec((tokens // 2, keys, features), lambda g: (pair_step(g), 0, 0)),
            whole(stats.shape),
            whole(flat[0].shape),
            pl.BlockSpec((rows, up_width), lambda g: (0, up_step(g))),
            pl.BlockSpec((rows, 256), lambda g: (0, down_step(g))),
            whole(flat[3].shape),
            pl.BlockSpec((rows, width // 2), lambda g: (0, out_step(g))),
            whole(flat[5].shape),
        ],
        out_specs=[
            sample_block((tokens, width), held),
            sample_block((tokens, 2 * width), late),
            whole((heads, features)),
            whole((heads, keys)),
            pl.BlockSpec((width, up_width), lambda g: (0, up_step(g))),
            pl.BlockSpec((256, width), lambda g: (down_step(g), 0)),
            pl.BlockSpec((width // 2, width), lambda g: (out_step(g), 0)),
        ],
        scratch_shapes=[
            pltpu.VMEM((tokens, width), f32),
            pltpu.VMEM((keys, 2 * width), f32),
            pltpu.VMEM((heads, tokens // 8, 8, keys), f32),
            pltpu.VMEM((samples, seq // 2, 2, tokens, 2 * width), bf16),
            pltpu.VMEM((samples, seq // 2, tokens, 2 * width), bf16),
            pltpu.VMEM((samples, 2, tokens, width), bf16),
            pltpu.VMEM((samples, 2, tokens, width), bf16),
            pltpu.VMEM((samples, tokens, width), bf16),
            pltpu.VMEM((samples, tokens, width), bf16),
            dma((samples,)),
            dma((samples,)),
            dma((samples, 4)),
            dma((samples, 4)),
            dma((samples, 2)),
            dma((samples, 2)),
        ],
        compiler_params=pltpu.CompilerParams(
            vmem_limit_bytes=60 << 20, collective_id=5, has_side_effects=True
        ),
        name="attend_back_scatter",
    )(query, keyval, probs, att, pairs, stats, *flat)
    dq, dkv, total, means, upw, downw, outw = results
    return dq, dkv, total - jnp.sum(means, -1, keepdims=True), (upw, downw, outw)


def token_middle_kernel(
    attend_ref,
    gating_ref,
    block_ref,
    gate1_ref,
    scale2_ref,
    shift2_ref,
    gate2_ref,
    cotangent_ref,
    outw_ref,
    upw_ref,
    downw_ref,
    result_ref,
    ffn_ref,
    upper_ref,
    hidden_ref,
    two_ref,
    gated_ref,
    branch_ref,
    att_ref,
    gategrad_ref,
    midgrad_ref,
    condgrad_ref,
):
    width = attend_ref.shape[1]
    hidden_width = downw_ref.shape[0]
    outw, upw, downw = outw_ref[...], upw_ref[...], downw_ref[...]
    attend = attend_ref[...]
    sig_gate = sigmoid(gating_ref[...])
    gated_low = (attend * sig_gate).astype(bf16)
    gated_ref[...] = gated_low
    branch = mm(gated_low, outw)
    gate_one = sigmoid(gate1_ref[...])
    mid = block_ref[...] + gate_one * branch
    normed, inv_std = norm_stats(mid)
    scale_two = sigmoid(scale2_ref[...])
    ffn_in = (scale_two * normed + shift2_ref[...]).astype(bf16)
    ffn_ref[...] = ffn_in
    first_half = mm(ffn_in, upw[:, :hidden_width])
    second_half = mm(ffn_in, upw[:, hidden_width:])
    sig_first = sigmoid(first_half)
    hidden = (first_half * sig_first * second_half).astype(bf16)
    hidden_ref[...] = hidden
    branch_two = mm(hidden, downw)
    gate_two = sigmoid(gate2_ref[...])
    result_ref[...] = (mid + gate_two * branch_two).astype(bf16)

    out_grad = cotangent_ref[...].astype(f32)
    two_low = (out_grad * gate_two).astype(bf16)
    two_ref[...] = two_low
    condgrad_ref[:, 3 * width :] = (
        out_grad * branch_two * gate_two * (1.0 - gate_two)
    ).astype(bf16)
    hidden_grad = mm_nt(two_low, downw)
    first_grad = (
        hidden_grad * second_half * sig_first * (1.0 + first_half * (1.0 - sig_first))
    ).astype(bf16)
    second_grad = (hidden_grad * first_half * sig_first).astype(bf16)
    upper_ref[:, :hidden_width] = first_grad
    upper_ref[:, hidden_width:] = second_grad
    ffn_grad = mm_nt(first_grad, upw[:, :hidden_width]) + mm_nt(second_grad, upw[:, hidden_width:])
    condgrad_ref[:, 2 * width : 3 * width] = ffn_grad.astype(bf16)
    condgrad_ref[:, width : 2 * width] = (
        ffn_grad * normed * scale_two * (1.0 - scale_two)
    ).astype(bf16)
    mid_grad = out_grad + norm_back(normed, inv_std, ffn_grad * scale_two)
    midgrad_ref[...] = mid_grad
    branch_low = (mid_grad * gate_one).astype(bf16)
    branch_ref[...] = branch_low
    condgrad_ref[:, :width] = (mid_grad * branch * gate_one * (1.0 - gate_one)).astype(bf16)
    gated_grad = mm_nt(branch_low, outw)
    att_ref[...] = (gated_grad * sig_gate).astype(bf16)
    gategrad_ref[...] = (gated_grad * attend * sig_gate * (1.0 - sig_gate)).astype(bf16)


def row_block(block, width, column=0):
    return pl.BlockSpec((block, width), lambda i, *_: (i, column))


def token_middle(attend, mix, block_in, cond_all, cotangent, outw, upw, downw):
    samples, tokens, width = attend.shape
    rows = samples * tokens
    block = rows // 4
    hidden_width = downw.shape[0]
    flat = lambda part: part.reshape(rows, part.shape[-1])
    cond = flat(cond_all)
    outs = (
        (width, bf16),
        (width, bf16),
        (2 * hidden_width, bf16),
        (hidden_width, bf16),
        (width, bf16),
        (width, bf16),
        (width, bf16),
        (width, bf16),
        (width, bf16),
        (width, f32),
        (4 * width, bf16),
    )
    return pl.pallas_call(
        token_middle_kernel,
        out_shape=[jax.ShapeDtypeStruct((rows, lanes), kind) for lanes, kind in outs],
        grid=(rows // block,),
        in_specs=[
            row_block(block, width),
            row_block(block, width, 3),
            row_block(block, width),
            row_block(block, width, 2),
            row_block(block, width, 3),
            row_block(block, width, 4),
            row_block(block, width, 5),
            row_block(block, width),
        ]
        + [whole(part.shape) for part in (outw, upw, downw)],
        out_specs=[row_block(block, lanes) for lanes, _ in outs],
        compiler_params=params(),
        name="token_middle",
    )(flat(attend), flat(mix), flat(block_in), cond, cond, cond, cond, flat(cotangent), outw, upw, downw)


def token_close_kernel(
    dq_ref,
    dkv_ref,
    gategrad_ref,
    midgrad_ref,
    block_ref,
    scale1_ref,
    tail_ref,
    proj_ref,
    attn_ref,
    cond_ref,
    upw_ref,
    downw_ref,
    outw_ref,
    tokengrad_ref,
    qbias_ref,
    cbias_ref,
    units_ref,
    mix_s,
    condgrad_s,
    cond_s,
):
    step = pl.program_id(0)
    block, width = dq_ref.shape
    blocks = mix_s.shape[0] // block
    samp = units_ref.shape[1]

    @pl.when(step == 0)
    def _():
        qbias_ref[...] = jnp.zeros_like(qbias_ref)
        cbias_ref[...] = jnp.zeros_like(cbias_ref)

    @pl.when(step < blocks)
    def _():
        rows = pl.ds(pl.multiple_of(step * block, block), block)
        dq = dq_ref[...]
        qbias_ref[...] += jnp.sum(dq, 0, keepdims=True)
        mix = jnp.concatenate([dq.astype(bf16), dkv_ref[...], gategrad_ref[...]], 1)
        mix_s[rows, :] = mix
        attn_grad = mm_nt(mix, proj_ref[...])
        normed, inv_std = norm_stats(block_ref[...])
        scale_one = sigmoid(scale1_ref[...])
        scale_grad = (attn_grad * normed * scale_one * (1.0 - scale_one)).astype(bf16)
        tokengrad_ref[...] = midgrad_ref[...] + norm_back(normed, inv_std, attn_grad * scale_one)
        shift_grad = attn_grad.astype(bf16)
        tail = tail_ref[...]
        condgrad_s[rows, :width] = scale_grad
        condgrad_s[rows, width : 2 * width] = shift_grad
        condgrad_s[rows, 2 * width :] = tail
        for part, low in ((scale_grad, 0), (shift_grad, width), (tail, 2 * width)):
            cbias_ref[:, low : low + part.shape[1]] += jnp.sum(
                part.astype(f32), 0, keepdims=True
            )

    @pl.when(step == blocks)
    def _():
        for low in range(0, cond_s.shape[1], 768):
            cond_s[:, low : low + 768] = mm_tn(
                cond_ref[...], condgrad_s[:, low : low + 768]
            ).astype(bf16)

    @pl.when(step >= blocks)
    def _():
        part = step - blocks
        left = pl.multiple_of(part * 384, LANES)
        proj = mm_tn(attn_ref[...], mix_s[:, pl.ds(left, 384)]).astype(bf16)
        rows = proj.shape[0] // samp
        for z in range(samp):
            units_ref[0, z, :rows, :384] = proj[z * rows : (z + 1) * rows]
            units_ref[0, z, :rows, 384:] = upw_ref[z * rows : (z + 1) * rows, :]
            units_ref[0, z, 192:240, :] = downw_ref[
                pl.ds(pl.multiple_of(z * 384 + part * 48, 16), 48), :
            ]
            low = pl.multiple_of(z * 96 + part // 4 * 48, 16)
            left = pl.multiple_of(part % 4 * 1152, LANES)
            units_ref[0, z, 240:288, :] = cond_s[pl.ds(low, 48), pl.ds(left, 768)]
            left = pl.multiple_of(part % 4 * 1152 + 768, LANES)
            units_ref[0, z, 288:336, :384] = cond_s[pl.ds(low, 48), pl.ds(left, 384)]
            low = pl.multiple_of(z * 192 + part // 2 * 48, 16)
            left = pl.multiple_of(part % 2 * 384, LANES)
            units_ref[0, z, 288:336, 384:] = outw_ref[pl.ds(low, 48), pl.ds(left, 384)]


def token_close(dq, dkv, gategrad, midgrad, block_in, cond_all, tail, proj, attn_in, cond_low, ready, samp, seq):
    samples, tokens, width = dq.shape
    rows = samples * tokens
    blocks = 4
    block = rows // blocks
    flat = lambda part: part.reshape(rows, part.shape[-1])
    upw, downw, outw = ready
    attn, cond = flat(attn_in), flat(cond_low)

    def early(lanes, column=0):
        return pl.BlockSpec((block, lanes), lambda g: (jnp.minimum(g, blocks - 1), column))

    late = lambda g: jnp.maximum(g - blocks, 0)
    return pl.pallas_call(
        token_close_kernel,
        out_shape=[
            jax.ShapeDtypeStruct((rows, width), f32),
            jax.ShapeDtypeStruct((1, width), f32),
            jax.ShapeDtypeStruct((1, 6 * width), f32),
            jax.ShapeDtypeStruct((seq, samp, UNIT, 768), bf16),
        ],
        grid=(blocks + seq,),
        in_specs=[
            early(width),
            early(2 * width),
            early(width),
            early(width),
            early(width),
            early(width),
            early(4 * width),
            whole(proj.shape),
            whole(attn.shape),
            whole(cond.shape),
            pl.BlockSpec((width, 384), lambda g: (0, late(g))),
            whole(downw.shape),
            whole(outw.shape),
        ],
        out_specs=[
            early(width),
            whole((1, width)),
            whole((1, 6 * width)),
            pl.BlockSpec((1, samp, UNIT, 768), lambda g: (late(g), 0, 0, 0)),
        ],
        scratch_shapes=[
            pltpu.VMEM((rows, 4 * width), bf16),
            pltpu.VMEM((rows, 6 * width), bf16),
            pltpu.VMEM((cond.shape[1], 6 * width), bf16),
        ],
        compiler_params=params(),
        name="token_close",
    )(
        flat(dq),
        flat(dkv),
        gategrad,
        midgrad,
        flat(block_in),
        flat(cond_all),
        tail,
        proj,
        attn,
        cond,
        upw,
        downw,
        outw,
    )


def to_blocks(array, width):
    return [array[:, low : low + width] for low in range(0, array.shape[1], width)]


def pack_blocks(arrays, width):
    parts = []
    for array in arrays:
        parts += to_blocks(array, width)
    return jnp.concatenate(parts, 0)


def unpack_blocks(packed, shapes, width):
    arrays, low = [], 0
    for rows, columns in shapes:
        parts = []
        for _ in range(columns // width):
            parts.append(packed[low : low + rows])
            low += rows
        arrays.append(jnp.concatenate(parts, 1) if len(parts) > 1 else parts[0])
    return arrays


def sum_shares(grads, extra):
    samp, seq = lax.axis_size("samp"), lax.axis_size("seq")
    width = grads[2].shape[1]
    shapes = [(grad.shape[0] // samp, grad.shape[1]) for grad in grads]
    packed = jnp.concatenate(
        [
            block.astype(bf16).reshape(samp, -1, width)
            for grad in grads
            for block in to_blocks(grad, width)
        ]
        + [extra.astype(bf16).reshape(samp, -1, width)],
        1,
    )
    rows = packed.shape[1]
    packed = packed.reshape(samp, seq, rows // seq, width).transpose(1, 0, 2, 3)
    part = lax.psum_scatter(packed, "seq", scatter_dimension=0, tiled=False)
    part = lax.psum_scatter(part, "samp", scatter_dimension=0, tiled=False)
    packed = lax.all_gather(part, "seq", axis=0, tiled=True).astype(f32)
    shares = unpack_blocks(packed, shapes, width)
    return shares, packed[sum(r * (c // width) for r, c in shapes) :]


def local(
    atom_input,
    token_input,
    atom_counts,
    key_offsets,
    atom_pairs,
    pair_features,
    single_features,
    noise_levels,
    noise_direction,
    atom_proj,
    atom_qbias,
    atom_pairw,
    atom_outw,
    atom_upw,
    atom_downw,
    pool_weight,
    cond_weight,
    cond_bias,
    token_proj,
    token_qbias,
    token_pairw,
    token_outw,
    token_upw,
    token_downw,
    cotangent,
):
    samp, seq = lax.axis_size("samp"), lax.axis_size("seq")
    seq_pos = lax.axis_index("seq")
    samples, slots, atom_width = atom_input.shape
    tokens, width = token_input.shape[1:]
    features = atom_pairs.shape[-1]

    half = atom_downw.shape[0] // 2
    wide_own = jnp.concatenate(
        [atom_proj, atom_upw, pool_weight, atom_outw, atom_downw[:half], atom_downw[half:]], 1
    )
    tiny_own = jnp.concatenate(
        [
            atom_qbias,
            cond_bias,
            token_qbias,
            atom_pairw.reshape(-1),
            token_pairw.reshape(-1),
        ]
    )
    tiny_own = jnp.pad(tiny_own, (0, -tiny_own.size % (16 * LANES))).reshape(-1, LANES)
    large = (token_proj, token_upw, token_downw, cond_weight, token_outw)
    kernels = samples == 8 and WeightGather.fits([part.shape for part in large], samp, seq)
    up_pairs = [(i, i + 1) for i in range(seq - 1)]
    down_pairs = [(i + 1, i) for i in range(seq - 1)]
    if kernels:
        wide_all, tiny_all, ext = edges(wide_own, tiny_own, atom_input)
    else:
        wide_all = lax.all_gather(wide_own, "samp", axis=0, tiled=True)
        tiny_all = lax.all_gather(tiny_own, "samp", axis=0, tiled=True)
        before = lax.ppermute(atom_input[:, slots - RIM :], "seq", up_pairs)
        after = lax.ppermute(atom_input[:, :RIM], "seq", down_pairs)
        ext = jnp.concatenate([before, atom_input, after], 1)
    tiny_all = tiny_all.reshape(samp, -1)
    wide = wide_all[:, : -2 * atom_width]
    down = (
        wide_all[:, -2 * atom_width :]
        .reshape(samp, half, 2, atom_width)
        .transpose(0, 2, 1, 3)
        .reshape(-1, atom_width)
    )
    sizes = [atom_qbias.size, cond_bias.size, token_qbias.size, atom_pairw.size, token_pairw.size]
    cuts = [sum(sizes[:i]) for i in range(6)]
    tiny = [tiny_all[:, cuts[i] : cuts[i + 1]] for i in range(5)]
    atom_qb = tiny[0].reshape(1, -1).astype(f32)
    cond_b = tiny[1].reshape(-1)
    token_qb = tiny[2].reshape(-1)
    atom_pw = tiny[3].reshape(features, ATOM_HEADS)
    token_pw = tiny[4].reshape(-1, token_pairw.shape[1])

    rim_tokens = RIM // MAX_ATOMS
    counts = lax.dynamic_slice_in_dim(
        jnp.pad(atom_counts, (rim_tokens, rim_tokens)), seq_pos * tokens, tokens + 2 * rim_tokens
    )
    place = jnp.arange(MAX_ATOMS, dtype=jnp.int32)
    used = place[None, :] < counts[:, None]
    blocked = jnp.where(used, 0.0, masked_score).astype(f32).reshape(-1, 1)
    blocked = jnp.broadcast_to(blocked, (blocked.shape[0], LANES))
    own_counts = counts[rim_tokens : rim_tokens + tokens]
    share = used[rim_tokens : rim_tokens + tokens].astype(f32) / own_counts[:, None].astype(f32)
    share = jnp.broadcast_to(share.reshape(-1, 1), (slots, LANES))
    windows = slots // WIN_Q
    starts = jnp.arange(windows, dtype=jnp.int32) * WIN_Q + key_offsets + RIM
    pairs_t = atom_pairs.transpose(0, 1, 3, 2).reshape(windows, WIN_Q * features, WIN_K)
    eye = jnp.eye(WIN_Q, dtype=bool)
    spread = jnp.where(
        eye[None, :, :, None], atom_pw.T[:, None, None, :], jnp.zeros((), bf16)
    ).reshape(ATOM_HEADS * WIN_Q, WIN_Q * features)
    gather = WeightGather([part.shape for part in large], samp, seq) if kernels else None
    pooled, stored, fulls = atom_forward(
        ext,
        starts,
        pairs_t,
        spread,
        blocked,
        share,
        wide,
        down,
        atom_qb,
        gather,
        large if kernels else (),
    )
    if not kernels:
        fulls = [lax.all_gather(part, "samp", axis=0, tiled=True) for part in large]
    proj_w, up_w, down_w, cond_w, out_w = fulls
    block_in = token_input.astype(f32) + pooled

    noise_feature = 0.25 * jnp.log(noise_levels / sigma_data)
    cond_rows = (
        single_features.astype(f32)[None]
        + noise_feature[:, None, None] * noise_direction[None, None, :]
    )
    cond_low = norm_stats(cond_rows)[0].astype(bf16)
    cond_all = dot_last(cond_low, cond_w) + cond_b.astype(f32)
    parts = [cond_all[..., i * width : (i + 1) * width] for i in range(6)]

    pair_w = token_pw.T
    normed_in, inv_in = norm_stats(block_in)
    attn_in = (jax.nn.sigmoid(parts[0]) * normed_in + parts[1]).astype(bf16)
    mix = dot_last(attn_in, proj_w)
    queries = (mix[..., :width] + token_qb.astype(f32)).astype(bf16)
    keyval_own = mix[..., width : 3 * width].astype(bf16)
    gating = mix[..., 3 * width :]
    if kernels:
        attend, probs, keyval, stats = gather_attend(
            queries, keyval_own, pair_features, pair_w, seq
        )
    else:
        bias = pair_bias(pair_features, pair_w)
        keyval = lax.all_gather(keyval_own, "seq", axis=0, tiled=False)
        attend, probs = token_attention(queries, keyval, bias)
    if kernels:
        (
            block_out,
            ffn_in,
            upper_grad,
            hidden,
            branch_two_low,
            gated_low,
            branch_low,
            attend_low,
            gating_grad,
            mid_grad,
            cond_tail,
        ) = token_middle(attend, mix, block_in, cond_all, cotangent, out_w, up_w, down_w)
        query_grad, keyval_grad, pairw_grad, ready = attend_back_scatter(
            queries,
            keyval,
            probs,
            attend_low.reshape(queries.shape),
            pair_features,
            stats,
            ffn_in,
            upper_grad,
            hidden,
            branch_two_low,
            gated_low,
            branch_low,
        )
        token_grad, token_qb_grad, cond_b_grad, grad_units = token_close(
            query_grad,
            keyval_grad,
            gating_grad,
            mid_grad,
            block_in,
            cond_all,
            cond_tail,
            proj_w,
            attn_in,
            cond_low,
            ready,
            samp,
            seq,
        )
        block_out = block_out.reshape(token_input.shape)
        token_grad = token_grad.reshape(token_input.shape)
        token_qb_grad, cond_b_grad = token_qb_grad.reshape(-1), cond_b_grad.reshape(-1)
    else:
        sig_gate = jax.nn.sigmoid(gating)
        gated_low = (attend * sig_gate).astype(bf16)
        branch = dot_last(gated_low, out_w)
        gate_one = jax.nn.sigmoid(parts[2])
        mid = block_in + gate_one * branch
        normed_mid, inv_mid = norm_stats(mid)
        scale_two = jax.nn.sigmoid(parts[3])
        ffn_in = (scale_two * normed_mid + parts[4]).astype(bf16)
        upper = dot_last(ffn_in, up_w)
        hidden_width = down_w.shape[0]
        first_half, second_half = upper[..., :hidden_width], upper[..., hidden_width:]
        sig_first = jax.nn.sigmoid(first_half)
        hidden = (first_half * sig_first * second_half).astype(bf16)
        branch_two = dot_last(hidden, down_w)
        gate_two = jax.nn.sigmoid(parts[5])
        block_out = (mid + gate_two * branch_two).astype(bf16)

        out_grad = cotangent.astype(f32)
        branch_two_low = (out_grad * gate_two).astype(bf16)
        gate_two_grad = out_grad * branch_two * gate_two * (1.0 - gate_two)
        hidden_grad = dot_back(branch_two_low, down_w)
        first_grad = hidden_grad * second_half * sig_first * (1.0 + first_half * (1.0 - sig_first))
        second_grad = hidden_grad * first_half * sig_first
        upper_grad = jnp.concatenate([first_grad, second_grad], -1).astype(bf16)
        ffn_grad = dot_back(upper_grad, up_w)
        scale_two_grad = ffn_grad * normed_mid * scale_two * (1.0 - scale_two)
        mid_grad = out_grad + norm_back(normed_mid, inv_mid, ffn_grad * scale_two)
        branch_low = (mid_grad * gate_one).astype(bf16)
        gate_one_grad = mid_grad * branch * gate_one * (1.0 - gate_one)
        gated_grad = dot_back(branch_low, out_w)
        attend_low = (gated_grad * sig_gate).astype(bf16)
        gating_grad = gated_grad * attend * sig_gate * (1.0 - sig_gate)
        query_grad, keyval_part, bias_grad = token_attention_back(queries, keyval, probs, attend_low)
        keyval_grad = lax.psum_scatter(keyval_part, "seq", scatter_dimension=0, tiled=False)
        pairw_grad = pair_grad(pair_features, bias_grad, pair_w)
        mix_grad = jnp.concatenate(
            [query_grad.astype(bf16), keyval_grad, gating_grad.astype(bf16)], -1
        )
        token_qb_grad = jnp.sum(query_grad, (0, 1))
        attn_in_grad = dot_back(mix_grad, proj_w)
        scale_one = jax.nn.sigmoid(parts[0])
        scale_one_grad = attn_in_grad * normed_in * scale_one * (1.0 - scale_one)
        token_grad = mid_grad + norm_back(normed_in, inv_in, attn_in_grad * scale_one)
        cond_grad = jnp.concatenate(
            [scale_one_grad, attn_in_grad, gate_one_grad, scale_two_grad, ffn_grad, gate_two_grad], -1
        ).astype(bf16)
        cond_b_grad = jnp.sum(cond_grad.astype(f32), (0, 1))
    pairw_grad = pairw_grad.T

    if kernels:
        atom_grad, qb_grad, pairw_stack, pairw_mean, small, units = atom_backward_sum(
            token_grad,
            starts,
            stored,
            atom_input,
            pairs_t,
            share,
            wide,
            down,
            GradSum([part.shape for part in large]),
            grad_units,
        )
    else:
        mix_part, own, left, right, atom_mid_grad, *atom_totals = atom_backward(
            token_grad, starts, stored, pairs_t, share, wide, down
        )
        from_right = lax.ppermute(left, "seq", down_pairs)
        from_left = lax.ppermute(right, "seq", up_pairs)
        atom_grad, atom_proj_grad = atom_input_backward(
            atom_input, mix_part, own, from_left, from_right, atom_mid_grad, wide
        )
        qb_grad, outw_grad, upw_grad, downw_grad, pool_grad, pairw_stack, pairw_mean = atom_totals
    diagonal = pairw_stack.reshape(ATOM_HEADS, WIN_Q, WIN_Q, features)
    atom_pw_grad = (
        jnp.sum(jnp.where(eye[None, :, :, None], diagonal, 0.0), (1, 2)).T
        - jnp.sum(pairw_mean.reshape(ATOM_HEADS, -1), 1)[None, :]
    )

    rows = atom_width // samp
    tiny_parts = [qb_grad.reshape(-1), atom_pw_grad, cond_b_grad, token_qb_grad, pairw_grad]
    tiny_flat = jnp.concatenate([part.astype(bf16).reshape(samp, -1) for part in tiny_parts], 1)
    spare = atom_width
    tiny_flat = jnp.pad(tiny_flat, ((0, 0), (0, rows * spare - tiny_flat.shape[1])))
    tiny_rows = tiny_flat.reshape(samp, rows, spare)
    if kernels:
        total, units = small_sums(small, tiny_rows, units)
        *shares, pool_out, proj_out, downw_out, upw_out, outw_out, tiny_out = unpack(
            units, total, [part.shape for part in large], rows, atom_width
        )
    else:
        lanes = lambda part: part.astype(bf16).reshape(samp, rows, -1)
        downw_two = downw_grad.astype(bf16).reshape(samp, 2, rows, atom_width)
        small = jnp.stack(
            [
                lanes(pool_grad),
                jnp.concatenate([lanes(atom_proj_grad), downw_two[:, 0], downw_two[:, 1]], -1),
                jnp.concatenate([lanes(upw_grad), lanes(outw_grad), tiny_rows], -1),
                jnp.zeros((samp, rows, width), bf16),
            ],
            1,
        )
        factors = [
            (attn_in, mix_grad),
            (ffn_in, upper_grad),
            (hidden, branch_two_low),
            (cond_low, cond_grad),
            (gated_low, branch_low),
        ]
        shares, rest = sum_shares(
            [weight_grad(*pair) for pair in factors], small.reshape(-1, width)
        )
        rest = rest.reshape(-1, width)
        pool_out, second, third = rest[:rows], rest[rows : 2 * rows], rest[2 * rows : 3 * rows]
        low = 4 * atom_width
        proj_out = second[:, :low]
        downw_out = jnp.concatenate(
            [second[:, low : low + atom_width], second[:, low + atom_width :]], 0
        )
        upw_out, outw_out = third[:, :low], third[:, low : low + atom_width]
        tiny_out = third[:, low + atom_width :]
    tiny_out = tiny_out.reshape(-1)
    tiny_shares, cut = [], 0
    for part in tiny_parts:
        size = part.size // samp
        shape = (part.shape[0] // samp,) + part.shape[1:]
        tiny_shares.append(tiny_out[cut : cut + size].reshape(shape))
        cut += size
    return (
        block_out,
        atom_grad,
        token_grad,
        proj_out,
        tiny_shares[0],
        tiny_shares[1],
        outw_out,
        upw_out,
        downw_out,
        pool_out,
        shares[3],
        tiny_shares[2],
        shares[0],
        tiny_shares[3],
        tiny_shares[4],
        shares[4],
        shares[1],
        shares[2],
    )


def solution(mesh):
    in_specs = (
        P("samp", "seq", None),
        P("samp", "seq", None),
        P(),
        P("seq"),
        P("seq", None, None, None),
        P("seq", None, None),
        P("seq", None),
        P("samp"),
        P(),
        P("samp", None),
        P("samp"),
        P("samp", None),
        P("samp", None),
        P("samp", None),
        P("samp", None),
        P("samp", None),
        P("samp", None),
        P("samp"),
        P("samp", None),
        P("samp"),
        P("samp", None),
        P("samp", None),
        P("samp", None),
        P("samp", None),
        P("samp", "seq", None),
    )
    out_specs = (
        P("samp", "seq", None),
        P("samp", "seq", None),
        P("samp", "seq", None),
        P("samp", None),
        P("samp"),
        P("samp", None),
        P("samp", None),
        P("samp", None),
        P("samp", None),
        P("samp", None),
        P("samp", None),
        P("samp"),
        P("samp", None),
        P("samp"),
        P("samp", None),
        P("samp", None),
        P("samp", None),
        P("samp", None),
    )
    return jax.shard_map(local, mesh=mesh, in_specs=in_specs, out_specs=out_specs, check_vma=False)
```

```python
import functools

import jax
import jax.numpy as jnp
from jax import lax
from jax.experimental import pallas as pl
from jax.experimental.pallas import tpu as pltpu
from jax.sharding import PartitionSpec as P

MAX_ATOMS = 8
WIN_Q = 32
WIN_K = 128
ATOM_HEADS = 4
RIM = 96
LANES = 128

norm_eps = 1e-05
sigma_data = 16.0
masked_score = -1000000000.0
bf16 = jnp.bfloat16
f32 = jnp.float32
vmem_bytes = 56 << 20


def dot_last(left_op, right_op):
    return jnp.einsum("...k,kn->...n", left_op, right_op, preferred_element_type=f32)


def dot_back(grad_op, weight):
    return jnp.einsum("...n,kn->...k", grad_op, weight, preferred_element_type=f32)


def weight_grad(left_op, grad_op):
    flat_left = left_op.reshape(-1, left_op.shape[-1])
    flat_grad = grad_op.reshape(-1, grad_op.shape[-1])
    return jnp.einsum("rk,rn->kn", flat_left, flat_grad, preferred_element_type=f32)


def mm(left_op, right_op):
    return lax.dot_general(left_op, right_op, (((1,), (0,)), ((), ())), preferred_element_type=f32)


def mm_nt(left_op, right_op):
    return lax.dot_general(left_op, right_op, (((1,), (1,)), ((), ())), preferred_element_type=f32)


def mm_tn(left_op, right_op):
    return lax.dot_general(left_op, right_op, (((0,), (0,)), ((), ())), preferred_element_type=f32)


def norm_stats(operand):
    center = operand - jnp.mean(operand, -1, keepdims=True)
    inv_std = lax.rsqrt(jnp.mean(center * center, -1, keepdims=True) + norm_eps)
    return (center * inv_std, inv_std)


def norm_back(normed, inv_std, grad_op):
    return inv_std * (
        grad_op
        - jnp.mean(grad_op, -1, keepdims=True)
        - normed * jnp.mean(grad_op * normed, -1, keepdims=True)
    )


def sigmoid(operand):
    return 1.0 / (1.0 + jnp.exp(-operand))


def whole(shape):
    return pl.BlockSpec(shape, lambda *_: (0,) * len(shape))


def per_sample(shape):
    return pl.BlockSpec((1,) + shape, lambda b, *_: (b,) + (0,) * len(shape))


def params():
    return pltpu.CompilerParams(vmem_limit_bytes=vmem_bytes)


def square_sums(ones_op, squares):
    upper = squares.astype(bf16)
    lower = (squares - upper.astype(f32)).astype(bf16)
    return upper, lower


def head_masks(count, width, heads, head_dim, first):
    row = lax.broadcasted_iota(jnp.int32, (heads * count, width), 0)
    lane = lax.broadcasted_iota(jnp.int32, (heads * count, width), 1)
    inside = (lane - first) // head_dim == row // count
    return jnp.where(inside & (lane >= first), 1.0, 0.0).astype(bf16)


def head_stack(rows, heads, head_dim, first, masks=None):
    if masks is None:
        masks = head_masks(rows.shape[0], rows.shape[1], heads, head_dim, first)
    return jnp.concatenate([rows] * heads, 0) * masks


def head_fold(stacked, heads, head_dim, first):
    count = stacked.shape[0] // heads
    lane = lax.broadcasted_iota(jnp.int32, (count, stacked.shape[1]), 1)
    total = jnp.zeros((count, stacked.shape[1]), f32)
    for head in range(heads):
        low = first + head * head_dim
        part = stacked[head * count : (head + 1) * count]
        total = jnp.where((lane >= low) & (lane < low + head_dim), part, total)
    return total


MESH = pl.DeviceIdType.MESH


def places():
    samp_pos, seq_pos = lax.axis_index("samp"), lax.axis_index("seq")
    core, across, along = seq_pos % 2, seq_pos // 2 % 2, seq_pos // 4

    def index(along, across, core):
        return (along * 2 + across) * 2 + core

    return (
        samp_pos,
        seq_pos,
        index(along, across, 1 - core),
        index(along, 1 - across, core),
        index(1 - along, across, core),
        index(1 - along, 1 - across, core),
    )


def remote(source, target, send_sem, recv_sem, device):
    return pltpu.make_async_remote_copy(
        src_ref=source,
        dst_ref=target,
        send_sem=send_sem,
        recv_sem=recv_sem,
        device_id=device,
        device_id_type=MESH,
    )


def greet(devices):
    barrier = pltpu.get_barrier_semaphore()
    for device in devices:
        pl.semaphore_signal(barrier, inc=1, device_id=device, device_id_type=MESH)
    pl.semaphore_wait(barrier, len(devices))


def pick(position, values):
    chosen = values[0]
    for index, value in enumerate(values[1:], 1):
        chosen = jnp.where(position == index, value, chosen)
    return chosen


class WeightGather:
    def __init__(self, shapes, samp, seq):
        self.shapes, self.samp, self.seq = shapes, samp, seq
        self.splits = [self.split(shape, seq) for shape in shapes]

    @staticmethod
    def split(shape, parts):
        rows, columns = shape
        for down in (1, 2, 4, 8):
            across = parts // down
            if rows % (16 * down) == 0 and columns % (LANES * across) == 0:
                return (down, across)
        return None

    @staticmethod
    def fits(shapes, samp, seq):
        return (
            samp == 4
            and seq == 8
            and len(shapes) == 5
            and all(WeightGather.split(shape, seq) for shape in shapes)
        )

    def full_shapes(self):
        return [(rows * self.samp, columns) for rows, columns in self.shapes]

    def scratch(self):
        count = len(self.shapes)
        return [
            pltpu.SemaphoreType.DMA((9, self.samp, count)),
            pltpu.SemaphoreType.DMA((8, self.samp, count)),
            pltpu.SemaphoreType.DMA((2, count)),
        ] + [pltpu.VMEM(shape, bf16) for shape in self.shapes]

    def params(self):
        return pltpu.CompilerParams(
            vmem_limit_bytes=vmem_bytes, collective_id=1, has_side_effects=True
        )

    def cell(self, ref, weight, origin, part):
        rows, columns = self.shapes[weight]
        down, across = self.splits[weight]
        height, width = rows // down, columns // across
        low = origin * rows + part // across * height
        left = part % across * width
        return ref.at[
            pl.ds(pl.multiple_of(low, 16), height), pl.ds(pl.multiple_of(left, LANES), width)
        ]

    def origin(self, position, turn):
        order = [sorted(range(self.samp), key=lambda o: (abs(o - z), o)) for z in range(self.samp)]
        if isinstance(turn, int):
            return pick(position, [order[z][turn] for z in range(self.samp)])
        return pick(
            position, [pick(turn, [order[z][t] for t in range(self.samp)]) for z in range(self.samp)]
        )

    def own_copies(self, shards, fulls, own, held, stage):
        z = places()[0]
        copies = []
        for w, shard in enumerate(shards):
            rows = self.shapes[w][0]
            target = fulls[w].at[pl.ds(pl.multiple_of(z * rows, 16), rows), :]
            ends = (shard, held[w]) if stage == 0 else (held[w], target)
            copies.append(pltpu.make_async_copy(*ends, own.at[stage, w]))
        return copies

    def start(self, shards, fulls, send, recv, own, held):
        z, me, sib, xn, yn, dg = places()
        above, below = lax.rem(z + 1, self.samp), lax.rem(z + self.samp - 1, self.samp)
        greet([(z, sib), (z, xn), (z, yn), (above, me), (below, me)])
        for w, shard in enumerate(shards):
            source = self.cell(shard, w, 0, me)
            target = self.cell(fulls[w], w, z, me)

            @pl.when(z < self.samp - 1)
            def _():
                remote(source, target, send.at[0, 0, w], recv.at[0, z, w], (z + 1, me)).start()

            @pl.when(z > 0)
            def _():
                remote(source, target, send.at[1, 0, w], recv.at[0, z, w], (z - 1, me)).start()

        for copy in self.own_copies(shards, fulls, own, held, 0):
            copy.start()

    def place_own(self, shards, fulls, own, held):
        for copy in self.own_copies(shards, fulls, own, held, 0):
            copy.wait()
        for copy in self.own_copies(shards, fulls, own, held, 1):
            copy.start()

    def share_own(self, turn, origin, sources, fulls, send, recv):
        z, me, sib, xn, yn, dg = places()
        for kind, part in ((2, xn), (3, yn), (5, sib)):
            for w, source in enumerate(sources):
                target = self.cell(fulls[w], w, origin, me)
                arrival = {2: 1, 3: 2, 5: 4}[kind]
                remote(
                    source, target, send.at[kind, turn, w], recv.at[arrival, origin, w], (z, part)
                ).start()

    def wait_cell(self, fulls, recv, kind, w, origin, part, device):
        target = self.cell(fulls[w], w, origin, part)
        remote(target, target, recv.at[kind, origin, w], recv.at[kind, origin, w], device).wait_recv()

    def issue(self, turn, fulls, send, recv):
        z, me, sib, xn, yn, dg = places()
        origin = self.origin(z, turn)
        count = len(self.shapes)
        for w in range(count):
            self.wait_cell(fulls, recv, 0, w, origin, me, (z, sib))
        for w in range(count):
            cell = self.cell(fulls[w], w, origin, me)

            @pl.when((origin < z) & (z < self.samp - 1))
            def _():
                remote(cell, cell, send.at[0, turn, w], recv.at[0, origin, w], (z + 1, me)).start()

            @pl.when((origin > z) & (z > 0))
            def _():
                remote(cell, cell, send.at[1, turn, w], recv.at[0, origin, w], (z - 1, me)).start()

        cells = [self.cell(fulls[w], w, origin, me) for w in range(count)]
        self.share_own(turn, origin, cells, fulls, send, recv)

    def passed_on(self, w):
        return w in (0, 3)

    def finish(self, turn, fulls, send, recv):
        z, me, sib, xn, yn, dg = places()
        origin = self.origin(z, turn)
        count = len(self.shapes)
        for kind, part, other, by in ((1, xn, yn, True), (2, yn, xn, False)):
            for w in range(count):
                self.wait_cell(fulls, recv, kind, w, origin, part, (z, part))
                cell = self.cell(fulls[w], w, origin, part)
                if self.passed_on(w) == by:
                    remote(
                        cell, cell, send.at[4, turn, w], recv.at[3, origin, w], (z, other)
                    ).start()
                remote(
                    cell, cell, send.at[5 + kind, turn, w], recv.at[4 + kind, origin, w], (z, sib)
                ).start()

    def diagonal(self, turn, fulls, send, recv):
        z, me, sib, xn, yn, dg = places()
        origin = self.origin(z, turn)
        for w in range(len(self.shapes)):
            self.wait_cell(fulls, recv, 3, w, origin, dg, (z, yn))
            cell = self.cell(fulls[w], w, origin, dg)
            remote(cell, cell, send.at[8, turn, w], recv.at[7, origin, w], (z, sib)).start()

    def drain(self, shards, fulls, send, recv, own, held):
        z, me, sib, xn, yn, dg = places()
        count = len(self.shapes)

        def sent(kind, turn, w):
            cell = self.cell(fulls[w], w, 0, me)
            remote(cell, cell, send.at[kind, turn, w], recv.at[0, 0, w], (z, sib)).wait_send()

        def one(turn, carry):
            origin = self.origin(z, turn)
            for w in range(count):
                for kind in range(2, 9):
                    sent(kind, turn, w)

                @pl.when((z < self.samp - 1) & (origin < z))
                def _():
                    sent(0, turn, w)

                @pl.when((z > 0) & (origin > z))
                def _():
                    sent(1, turn, w)

                for kind in range(4, 8):
                    self.wait_cell(fulls, recv, kind, w, origin, sib, (z, sib))
            return carry

        lax.fori_loop(1, self.samp, one, 0)
        for w in range(count):

            @pl.when(z < self.samp - 1)
            def _():
                sent(0, 0, w)

            @pl.when(z > 0)
            def _():
                sent(1, 0, w)

        for copy in self.own_copies(shards, fulls, own, held, 1):
            copy.wait()

    def step(self, sample, shards, fulls, send, recv, own, *held):
        @pl.when(sample == 0)
        def _():
            self.start(shards, fulls, send, recv, own, held)

        @pl.when(sample == 1)
        def _():
            self.place_own(shards, fulls, own, held)

        for at, turn in ((2, 1), (3, 2), (5, 3)):

            @pl.when(sample == at)
            def _():
                self.issue(turn, fulls, send, recv)

        for at, turn in ((4, 1), (5, 2), (7, 3)):

            @pl.when(sample == at)
            def _():
                self.finish(turn, fulls, send, recv)

        for at, turn in ((5, 1), (7, 2)):

            @pl.when(sample == at)
            def _():
                self.diagonal(turn, fulls, send, recv)

    def last(self, sample, shards, fulls, send, recv, own, *held):
        @pl.when(sample == pl.num_programs(0) - 1)
        def _():
            self.diagonal(3, fulls, send, recv)
            self.drain(shards, fulls, send, recv, own, held)


def edge_kernel(
    samp,
    seq,
    proj_ref,
    upw_ref,
    pool_ref,
    outw_ref,
    down_ref,
    tiny_ref,
    rows_ref,
    wide_out,
    down_out,
    tiny_out,
    ext_out,
    held,
    send,
    recv,
):
    z, me = lax.axis_index("samp"), lax.axis_index("seq")
    sib = places()[2]
    core = me % 2
    samples, slots, width = rows_ref.shape
    right, left = lax.rem(me + 1, seq), lax.rem(me + seq - 1, seq)
    others = [lax.rem(z + hop, samp) for hop in range(1, samp)]
    greet([(other, me) for other in others] + [(z, sib), (z, right), (z, left)])
    low = 0
    for ref in (proj_ref, upw_ref, pool_ref, outw_ref):
        held[:, low : low + ref.shape[1]] = ref[...]
        low += ref.shape[1]

    def half(out, origin, part):
        rows = out.shape[0] // samp
        first = origin * rows + part * (rows // 2)
        return out.at[pl.ds(pl.multiple_of(first, 16), rows // 2), :]

    def own_half(ref):
        rows = ref.shape[0]
        return ref.at[pl.ds(pl.multiple_of(core * (rows // 2), 16), rows // 2), :]

    def tiny_place(origin):
        rows = tiny_ref.shape[0]
        return tiny_out.at[pl.ds(pl.multiple_of(origin * rows, 16), rows), :]

    copies = []
    for hop, other in enumerate(others):
        device = (other, me)
        copies.append(
            [
                remote(own_half(held), half(wide_out, z, core), send.at[0, hop], recv.at[0, hop], device),
                remote(own_half(down_ref), half(down_out, z, core), send.at[1, hop], recv.at[1, hop], device),
                remote(tiny_ref, tiny_place(z), send.at[2, hop], recv.at[2, hop], device),
            ]
        )
    for group in copies:
        for copy in group:
            copy.start()
    before, after = ext_out.at[:, :RIM, :], ext_out.at[:, RIM + slots :, :]
    to_right = remote(rows_ref.at[:, slots - RIM :, :], before, send.at[5, 0], recv.at[5, 0], (z, right))
    to_left = remote(rows_ref.at[:, :RIM, :], after, send.at[5, 1], recv.at[5, 1], (z, left))
    first, last = me == 0, me == seq - 1

    @pl.when(~last)
    def _():
        to_right.start()

    @pl.when(~first)
    def _():
        to_left.start()

    @pl.when(first)
    def _():
        ext_out[:, :RIM, :] = jnp.zeros((samples, RIM, width), bf16)

    @pl.when(last)
    def _():
        ext_out[:, RIM + slots :, :] = jnp.zeros((samples, RIM, width), bf16)

    def move(sample, carry):
        ext_out[sample, RIM : RIM + slots, :] = rows_ref[sample]
        return carry

    lax.fori_loop(0, samples, move, 0)
    for ref, out in ((held, wide_out), (down_ref, down_out), (tiny_ref, tiny_out)):
        rows = ref.shape[0]
        out[pl.ds(pl.multiple_of(z * rows, 16), rows), :] = ref[...]
    passed = []
    for hop in range(samp - 1):
        origin = lax.rem(z + samp - 1 - hop, samp)
        for kind, out in ((0, wide_out), (1, down_out)):
            copies[hop][kind].wait_recv()
            cell = half(out, origin, core)
            copy = remote(cell, cell, send.at[3 + kind, hop], recv.at[3 + kind, hop], (z, sib))
            copy.start()
            passed.append(copy)
    for hop in range(samp - 1):
        copies[hop][2].wait_recv()
        for copy in copies[hop]:
            copy.wait_send()
    for copy in passed:
        copy.wait()

    @pl.when(~last)
    def _():
        to_right.wait_send()
        to_left.wait_recv()

    @pl.when(~first)
    def _():
        to_left.wait_send()
        to_right.wait_recv()


def edges(weights, tiny_own, rows):
    samp, seq = lax.axis_size("samp"), lax.axis_size("seq")
    samples, slots, width = rows.shape
    place = pl.BlockSpec(memory_space=pltpu.VMEM)
    lanes = sum(part.shape[1] for part in weights[:4])
    return pl.pallas_call(
        functools.partial(edge_kernel, samp, seq),
        out_shape=[
            jax.ShapeDtypeStruct((samp * weights[0].shape[0], lanes), bf16),
            jax.ShapeDtypeStruct((samp * weights[4].shape[0], weights[4].shape[1]), bf16),
            jax.ShapeDtypeStruct((samp * tiny_own.shape[0], tiny_own.shape[1]), bf16),
            jax.ShapeDtypeStruct((samples, slots + 2 * RIM, width), bf16),
        ],
        in_specs=[place] * 7,
        out_specs=[place] * 4,
        scratch_shapes=[
            pltpu.VMEM((weights[0].shape[0], lanes), bf16),
            pltpu.SemaphoreType.DMA((6, samp)),
            pltpu.SemaphoreType.DMA((6, samp)),
        ],
        compiler_params=pltpu.CompilerParams(
            vmem_limit_bytes=vmem_bytes, collective_id=0, has_side_effects=True
        ),
        name="edges",
    )(*weights, tiny_own, rows)


UNIT = 336


def add_into(target, source, lanes=slice(None), rows=48):
    def one(step, carry):
        part = pl.ds(pl.multiple_of(step * rows, 16), rows)
        target[part, lanes] = target[part, lanes] + source[part, :]
        return carry

    lax.fori_loop(0, target.shape[0] // rows, one, 0)


class GradSum:
    head, tail, full = slice(0, 384), slice(384, 768), slice(0, 768)

    def __init__(self, shapes):
        self.shapes = list(shapes)

    def scratch(self):
        half = (UNIT, 384)
        dma = pltpu.SemaphoreType.DMA
        return [
            pltpu.VMEM((4, 4, UNIT, 768), bf16),
            pltpu.VMEM((4, 4, UNIT, 768), bf16),
            pltpu.VMEM((4, 2) + half, bf16),
            pltpu.VMEM((4, 2) + half, bf16),
            pltpu.VMEM((4,) + half, bf16),
            pltpu.VMEM((4,) + half, bf16),
            pltpu.VMEM((3, UNIT, 768), bf16),
            pltpu.VMEM((UNIT, 768), bf16),
            dma((4, 4)),
            dma((4, 4)),
            dma((4, 4)),
            dma((4, 4)),
            dma((4, 4)),
            dma((4, 2)),
            dma((4, 2)),
            dma((3,)),
            dma((3,)),
            dma,
        ]

    def params(self):
        return pltpu.CompilerParams(
            vmem_limit_bytes=vmem_bytes, collective_id=2, has_side_effects=True
        )

    def bind(
        self, grads, shares, mine, theirs, from_x, from_y, last_x, last_y, planes, own_share, *sems
    ):
        self.grads, self.shares, self.own_share = grads, shares, own_share
        self.mine, self.theirs, self.from_x, self.from_y = mine, theirs, from_x, from_y
        self.last_x, self.last_y, self.planes = last_x, last_y, planes
        (
            self.s_sib,
            self.r_sib,
            self.s_own,
            self.s_one,
            self.r_one,
            self.s_two,
            self.r_two,
            self.s_z,
            self.r_z,
            self.s_out,
        ) = sems
        self.z, self.me, self.sib, self.xn, self.yn, self.dg = places()
        self.core, self.chip = self.me % 2, self.me // 2
        self.chip_x, self.chip_y, self.chip_d = self.xn // 2, self.yn // 2, self.dg // 2
        order = [[p ^ hop for hop in (2, 3, 1, 0)] for p in range(4)]
        self.plane = [pick(self.z, [order[p][r] for p in range(4)]) for r in range(4)]

    def there(self, r, j):
        return remote(
            self.grads.at[2 * j + 1 - self.core, self.plane[r]],
            self.theirs.at[r, j],
            self.s_sib.at[r, j],
            self.r_sib.at[r, j],
            (self.z, self.sib),
        )

    def here(self, r, j):
        return pltpu.make_async_copy(
            self.grads.at[2 * j + self.core, self.plane[r]], self.mine.at[r, j], self.s_own.at[r, j]
        )

    def one(self, r, k):
        chip = (self.chip_x, self.chip_d, self.chip_y, self.chip_d)[k]
        lanes = self.head if k < 2 else self.tail
        target = (self.from_x if k < 2 else self.from_y).at[r, k % 2]
        device = (self.z, self.xn if k < 2 else self.yn)
        return remote(
            self.mine.at[r, chip, :, lanes], target, self.s_one.at[r, k], self.r_one.at[r, k], device
        )

    def two(self, r, k):
        chip, lanes, target, device = (
            (self.chip_y, self.head, self.last_y, self.yn),
            (self.chip_x, self.tail, self.last_x, self.xn),
        )[k]
        return remote(
            self.mine.at[r, chip, :, lanes],
            target.at[r],
            self.s_two.at[r, k],
            self.r_two.at[r, k],
            (self.z, device),
        )

    def across(self, r):
        return remote(
            self.mine.at[r, self.chip],
            self.planes.at[r],
            self.s_z.at[r],
            self.r_z.at[r],
            (self.plane[r], self.me),
        )

    def keep(self):
        return pltpu.make_async_copy(self.own_share, self.shares, self.s_out)

    def begin(self, r):
        for j in range(4):
            self.there(r, j).start()
            self.here(r, j).start()

    def pairs(self, r):
        for j in range(4):
            self.there(r, j).wait_recv()
            self.here(r, j).wait()
        for j in range(4):
            add_into(self.mine.at[r, j], self.theirs.at[r, j])
        for k in range(4):
            self.one(r, k).start()

    def middle(self, r):
        self.one(r, 1).wait_recv()
        add_into(self.mine.at[r, self.chip_y], self.from_x.at[r, 1], self.head)
        self.two(r, 0).start()
        self.one(r, 3).wait_recv()
        add_into(self.mine.at[r, self.chip_x], self.from_y.at[r, 1], self.tail)
        self.two(r, 1).start()
        self.one(r, 0).wait_recv()
        add_into(self.mine.at[r, self.chip], self.from_x.at[r, 0], self.head)
        self.one(r, 2).wait_recv()
        add_into(self.mine.at[r, self.chip], self.from_y.at[r, 0], self.tail)

    def finish(self, r):
        self.two(r, 0).wait_recv()
        add_into(self.mine.at[r, self.chip], self.last_y.at[r], self.head)
        self.two(r, 1).wait_recv()
        add_into(self.mine.at[r, self.chip], self.last_x.at[r], self.tail)
        if r < 3:
            self.across(r).start()

    def total(self):
        for r in range(3):
            self.across(r).wait_recv()

        def one(step, carry):
            rows = pl.ds(pl.multiple_of(step * 48, 16), 48)
            both = self.mine[3, self.chip, rows, :].astype(f32)
            for r in range(3):
                both += self.planes[r, rows, :].astype(f32)
            self.own_share[rows, :] = both.astype(bf16)
            return carry

        lax.fori_loop(0, UNIT // 48, one, 0)
        self.keep().start()

    def collect(self):
        self.keep().wait()
        for r in range(4):
            for j in range(4):
                self.there(r, j).wait_send()
                self.one(r, j).wait_send()
            for k in range(2):
                self.two(r, k).wait_send()
            if r < 3:
                self.across(r).wait_send()

    def hello(self):
        greet(
            [(self.z, self.sib), (self.z, self.xn), (self.z, self.yn)]
            + [(self.plane[r], self.me) for r in range(3)]
            + [(self.z, lax.rem(self.me + 1, 8)), (self.z, lax.rem(self.me + 7, 8))]
        )
        self.begin(0)
        self.begin(1)

    def slot(self, index):
        plan = {
            0: [self.hello],
            1: [lambda: self.pairs(0), lambda: self.begin(2)],
            3: [lambda: self.pairs(1), lambda: self.begin(3)],
            4: [lambda: self.middle(0)],
            6: [lambda: self.pairs(2), lambda: self.finish(0)],
            7: [lambda: self.middle(1)],
            9: [lambda: self.pairs(3), lambda: self.finish(1)],
            10: [lambda: self.middle(2)],
            12: [lambda: self.finish(2)],
            13: [lambda: self.middle(3)],
            14: [lambda: self.finish(3)],
            15: [self.total],
        }
        for at, actions in plan.items():

            @pl.when(index == at)
            def _():
                for action in actions:
                    action()


def small_sum_kernel(
    main,
    tiny,
    own,
    out_ref,
    shares,
    grads,
    cores,
    chips,
    planes,
    share,
    total,
    s_one,
    r_one,
    s_two,
    r_two,
    s_z,
    r_z,
    s_all,
    r_all,
    s_share,
    r_share,
    s_own,
):
    z, me, sib, xn, yn, dg = places()
    core, chip = me % 2, me // 2
    near = (xn, yn, dg)
    parts, samp, rows = grads.shape[:3]
    for part in range(parts):
        for p in range(samp):
            grads[part, p] = main[p, part * rows : (part + 1) * rows, :]
    low, width = 2 * tiny.shape[1], tiny.shape[2]
    for part in range(tiny.shape[1] // rows):
        for p in range(samp):
            grads[low // rows + part, p, :, -width:] = tiny[p, part * rows : (part + 1) * rows, :]
    others = [lax.rem(z + hop, 4) for hop in (1, 2, 3)]
    greet(
        [(z, sib)]
        + [(z, part) for part in near]
        + [(z, part + 1 - 2 * core) for part in near]
        + [(other, me) for other in others]
    )

    def one(j):
        return remote(
            grads.at[2 * j + 1 - core], cores.at[j], s_one.at[j], r_one.at[j], (z, sib)
        )

    width = own.shape[1]
    head, tail, full = slice(0, width // 2), slice(width // 2, width), slice(0, width)

    def give(part, lanes, kind, device):
        target = shares.at[part, :, lanes]
        source = own if kind in (0, 1, 4) else target
        return remote(source, target, s_share.at[kind], r_share.at[kind], (z, device))

    keep = pltpu.make_async_copy(own, shares.at[me], s_own)
    gifts = [give(me, full, 0, xn), give(me, full, 1, yn), give(me, full, 4, sib)]

    for gift in gifts:
        gift.start()
    for j in range(4):
        one(j).start()
    for j in range(4):
        one(j).wait()
        both = cores[j].astype(f32) + grads[2 * j + core].astype(f32)
        cores[j] = both.astype(bf16)

    def two(k):
        return remote(cores.at[near[k] // 2], chips.at[k], s_two.at[k], r_two.at[k], (z, near[k]))

    for k in range(3):
        two(k).start()
    keep.start()
    give(xn, full, 0, xn).wait_recv()
    gifts += [give(xn, head, 2, yn), give(xn, full, 5, sib)]
    give(yn, full, 1, yn).wait_recv()
    gifts += [give(yn, tail, 3, xn), give(yn, full, 6, sib)]
    for gift in gifts[3:]:
        gift.start()
    both = cores[chip].astype(f32)
    for k in range(3):
        two(k).wait()
        both += chips[k].astype(f32)
    share[...] = both.astype(bf16)

    def three(k):
        return remote(share.at[others[k]], planes.at[k], s_z.at[k], r_z.at[k], (others[k], me))

    for k in range(3):
        three(k).start()
    both = share[z].astype(f32)
    for k in range(3):
        three(k).wait()
        both += planes[k].astype(f32)
    total[me] = both.astype(bf16)

    receivers = [sib] + list(near) + [part + 1 - 2 * core for part in near]

    def four(k, part, device):
        return remote(total.at[part], total.at[part], s_all.at[k], r_all.at[k], (z, device))

    for k, device in enumerate(receivers):
        four(k, me, device).start()
    for k, device in enumerate(receivers):
        four(k, device, device).wait_recv()
    for k, device in enumerate(receivers):
        four(k, me, device).wait_send()
    for part in range(parts):
        out_ref[part * rows : (part + 1) * rows, :] = total[part]
    give(dg, head, 2, yn).wait_recv()
    give(dg, tail, 3, xn).wait_recv()
    gifts.append(give(dg, full, 7, sib))
    gifts[-1].start()
    for kind in range(4, 8):
        give(sib, full, kind, sib).wait_recv()
    keep.wait()
    for gift in gifts:
        gift.wait_send()


def small_sums(main, tiny, own):
    seq = lax.axis_size("seq")
    samp, rows, width = main.shape
    rows //= seq
    dma = pltpu.SemaphoreType.DMA
    return pl.pallas_call(
        small_sum_kernel,
        out_shape=[
            jax.ShapeDtypeStruct((seq * rows, width), bf16),
            jax.ShapeDtypeStruct((seq,) + own.shape, bf16),
        ],
        in_specs=[pl.BlockSpec(memory_space=pltpu.VMEM)] * 3,
        out_specs=[
            pl.BlockSpec(memory_space=pltpu.VMEM),
            pl.BlockSpec(memory_space=pl.ANY),
        ],
        scratch_shapes=[
            pltpu.VMEM((seq, samp, rows, width), bf16),
            pltpu.VMEM((4, samp, rows, width), bf16),
            pltpu.VMEM((3, samp, rows, width), bf16),
            pltpu.VMEM((3, rows, width), bf16),
            pltpu.VMEM((samp, rows, width), bf16),
            pltpu.VMEM((seq, rows, width), bf16),
            dma((4,)),
            dma((4,)),
            dma((3,)),
            dma((3,)),
            dma((3,)),
            dma((3,)),
            dma((7,)),
            dma((7,)),
            dma((8,)),
            dma((8,)),
            dma,
        ],
        compiler_params=pltpu.CompilerParams(
            vmem_limit_bytes=vmem_bytes, collective_id=3, has_side_effects=True
        ),
        name="small_sums",
    )(main, tiny, own)


def pair_stats(pairs, fold):
    upper, lower = square_sums(fold, pairs.astype(f32) * pairs.astype(f32))
    features = pairs.shape[0] // WIN_Q
    mean = mm(fold, pairs) * (1.0 / features)
    square = (mm(fold, upper) + mm(fold, lower)) * (1.0 / features)
    var = jnp.maximum(square - mean * mean, 0.0)
    inv_std = lax.rsqrt(var + norm_eps)
    return mean, inv_std


def pair_fold(features):
    shape = (WIN_Q, WIN_Q * features)
    row = lax.broadcasted_iota(jnp.int32, shape, 0)
    column = lax.broadcasted_iota(jnp.int32, shape, 1)
    return jnp.where(column // features == row, 1.0, 0.0).astype(bf16)


def atom_fwd_kernel(
    gather,
    starts,
    ext_ref,
    pairs_ref,
    spread_ref,
    blocked_ref,
    share_ref,
    wide_ref,
    down_ref,
    qbias_ref,
    *refs,
):
    count = len(gather.shapes) if gather is not None else 0
    shards, refs = refs[:count], refs[count:]
    (
        pooled_ref,
        query_ref,
        keyval_ref,
        gate_ref,
        probs_ref,
        attend_ref,
        mid_ref,
    ), refs = refs[:7], refs[7:]
    fulls, refs = refs[:count], refs[count:]
    bias_s, sems = refs[0], refs[1:]
    width = ext_ref.shape[-1]
    head_dim = width // ATOM_HEADS
    scale = float(head_dim) ** (-0.5)
    slots = query_ref.shape[1]
    windows = slots // WIN_Q
    hidden_width = down_ref.shape[0]
    model_width = pooled_ref.shape[-1]
    features = pairs_ref.shape[1] // WIN_Q
    sample = pl.program_id(0)
    if gather is not None:
        gather.step(sample, shards, fulls, *sems)

    @pl.when(sample == 0)
    def _():
        fold = pair_fold(features)
        spread = spread_ref[...]
        spread_sum = jnp.sum(spread.astype(f32), -1, keepdims=True)
        first_lane = jnp.where(
            lax.broadcasted_iota(jnp.int32, (ATOM_HEADS * WIN_Q, LANES), 1) == 0, 1.0, 0.0
        ).astype(bf16)

        fill = jnp.full((ATOM_HEADS * WIN_Q, WIN_K), masked_score, f32)

        def one(duo, carry):
            base = pl.multiple_of(duo * 2 * WIN_Q, 2 * WIN_Q)
            blocked = mm_nt(first_lane, blocked_ref[pl.ds(base, 2 * WIN_K), :].astype(bf16))
            for part in range(2):
                win = duo * 2 + part
                pairs = pairs_ref[win]
                mean, inv_std = pair_stats(pairs, fold)
                mean = jnp.concatenate([mean] * ATOM_HEADS, 0)
                inv_std = jnp.concatenate([inv_std] * ATOM_HEADS, 0)
                bias = inv_std * (mm(spread, pairs) - mean * spread_sum)
                bias = pltpu.roll(jnp.concatenate([bias, fill], 1), starts[win] - base, 1) + blocked
                for head in range(ATOM_HEADS):
                    low = (head * 2 + part) * WIN_Q
                    bias_s[duo, low : low + WIN_Q, :] = bias[head * WIN_Q : (head + 1) * WIN_Q]
            return carry

        lax.fori_loop(0, windows // 2, one, 0)

    rows = ext_ref[0].astype(f32)
    normed_low = norm_stats(rows)[0].astype(bf16)
    key_val = mm(normed_low, wide_ref[:, width : 3 * width]).astype(bf16)
    keyval_ref[0] = key_val
    own_low = normed_low[RIM : RIM + slots]
    query_ref[0] = (mm(own_low, wide_ref[:, :width]) + qbias_ref[...]).astype(bf16)
    gate_ref[0] = mm(own_low, wide_ref[:, 3 * width : 4 * width])

    masks = head_masks(2 * WIN_Q, width, ATOM_HEADS, head_dim, 0)

    def two_windows(duo):
        first = pl.multiple_of(duo * 2 * WIN_Q, 2 * WIN_Q)
        span = pl.ds(first, 2 * WIN_K)
        own = pl.ds(first, 2 * WIN_Q)
        stacked = head_stack(query_ref[0, own, :], ATOM_HEADS, head_dim, 0, masks)
        scores = mm_nt(stacked, keyval_ref[0, span, :width]) * scale + bias_s[duo]
        exp_scores = jnp.exp(scores - jnp.max(scores, -1, keepdims=True))
        probs = exp_scores * (1.0 / jnp.sum(exp_scores, -1, keepdims=True))
        probs_low = probs.astype(bf16)
        probs_ref[0, duo] = probs_low
        attend_ref[0, own, :] = head_fold(
            mm(probs_low, keyval_ref[0, span, width:]), ATOM_HEADS, head_dim, 0
        )

    def some_windows(step, carry):
        for part in range(2):
            two_windows(step * 2 + part)
        return carry

    lax.fori_loop(0, windows // 4, some_windows, 0)

    gated_low = (attend_ref[0] * sigmoid(gate_ref[0])).astype(bf16)
    offset = 4 * width
    upw = wide_ref[:, offset : offset + 2 * hidden_width]
    offset += 2 * hidden_width
    pool_weight = wide_ref[:, offset : offset + model_width]
    outw = wide_ref[:, offset + model_width : offset + model_width + width]
    mid = rows[RIM : RIM + slots] + mm(gated_low, outw)
    mid_ref[0] = mid
    ffn_low = norm_stats(mid)[0].astype(bf16)
    upper = mm(ffn_low, upw)
    first_half, second_half = upper[:, :hidden_width], upper[:, hidden_width:]
    hidden = (first_half * sigmoid(first_half) * second_half).astype(bf16)
    final_low = (mid + mm(hidden, down_ref[...])).astype(bf16)
    pool_pre = mm(final_low, pool_weight)
    share = share_ref[...]
    for lane in range(0, model_width, LANES):
        part = pool_pre[:, lane : lane + LANES]
        part = part * sigmoid(part) * share
        pooled_ref[0, :, lane : lane + LANES] = jnp.sum(
            part.reshape(slots // MAX_ATOMS, MAX_ATOMS, LANES), 1
        )
    if gather is not None:
        gather.last(sample, shards, fulls, *sems)


def atom_forward(ext, starts, pairs, spread, blocked, share, wide, down, qbias, gather, shards):
    samples, ext_slots, width = ext.shape
    slots = ext_slots - 2 * RIM
    tokens = slots // MAX_ATOMS
    windows = slots // WIN_Q
    model_width = wide.shape[1] - 5 * width - 2 * down.shape[0]
    stack = ATOM_HEADS * WIN_Q
    outs = (
        ((tokens, model_width), f32),
        ((slots, width), bf16),
        ((ext_slots, 2 * width), bf16),
        ((slots, width), f32),
        ((windows // 2, 2 * stack, 2 * WIN_K), bf16),
        ((slots, width), f32),
        ((slots, width), f32),
    )
    place = pl.BlockSpec(memory_space=pl.ANY)
    results = pl.pallas_call(
        functools.partial(atom_fwd_kernel, gather),
        out_shape=[jax.ShapeDtypeStruct((samples,) + shape, kind) for shape, kind in outs]
        + [jax.ShapeDtypeStruct(shape, bf16) for shape in (gather.full_shapes() if gather else [])],
        grid=(samples,),
        in_specs=[
            pl.BlockSpec(memory_space=pltpu.SMEM),
            per_sample((ext_slots, width)),
            whole(pairs.shape),
            whole(spread.shape),
            whole(blocked.shape),
            whole(share.shape),
            whole(wide.shape),
            whole(down.shape),
            whole(qbias.shape),
        ]
        + [place] * len(shards),
        out_specs=[per_sample(shape) for shape, _ in outs] + [place] * len(shards),
        scratch_shapes=[pltpu.VMEM((windows // 2, 2 * stack, 2 * WIN_K), f32)]
        + (gather.scratch() if gather else []),
        compiler_params=gather.params() if gather else params(),
        name="atom_forward",
    )(starts, ext, pairs, spread, blocked, share, wide, down, qbias, *shards)
    return results[0], results[1:7], results[7:]


def atom_bwd_dense(sample_refs, consts, accs, attlow_s, gate_grad_at, mid_grad_at):
    grad_ref, query_ref, gate_ref, attend_ref, mid_ref = sample_refs
    share_ref, wide_ref, down_ref = consts
    outw_ref, upw_ref, downw_ref, pool_ref = accs
    width = query_ref.shape[-1]
    slots = query_ref.shape[1]
    hidden_width = down_ref.shape[0]
    model_width = grad_ref.shape[-1]
    tokens = grad_ref.shape[1]
    offset = 4 * width
    upw = wide_ref[:, offset : offset + 2 * hidden_width]
    offset += 2 * hidden_width
    pool_weight = wide_ref[:, offset : offset + model_width]
    outw = wide_ref[:, offset + model_width : offset + model_width + width]
    down = down_ref[...]

    mid = mid_ref[0]
    normed_mid, inv_mid = norm_stats(mid)
    ffn_low = normed_mid.astype(bf16)
    upper = mm(ffn_low, upw)
    first_half, second_half = upper[:, :hidden_width], upper[:, hidden_width:]
    sig_first = sigmoid(first_half)
    hidden = (first_half * sig_first * second_half).astype(bf16)
    final_low = (mid + mm(hidden, down)).astype(bf16)
    pool_pre = mm(final_low, pool_weight)
    share = share_ref[...]
    pool_parts = []
    for lane in range(0, model_width, LANES):
        part = pool_pre[:, lane : lane + LANES]
        grad = jnp.broadcast_to(
            grad_ref[0, :, lane : lane + LANES][:, None, :], (tokens, MAX_ATOMS, LANES)
        ).reshape(slots, LANES)
        sig_pool = sigmoid(part)
        pool_parts.append((grad * share * sig_pool * (1.0 + part * (1.0 - sig_pool))).astype(bf16))
    pool_grad = jnp.concatenate(pool_parts, 1)
    final_grad = mm_nt(pool_grad, pool_weight)
    pool_ref[...] += mm_tn(final_low, pool_grad)
    branch_low = final_grad.astype(bf16)
    hidden_grad = mm_nt(branch_low, down)
    first_grad = hidden_grad * second_half * sig_first * (1.0 + first_half * (1.0 - sig_first))
    second_grad = hidden_grad * first_half * sig_first
    upper_grad = jnp.concatenate([first_grad.astype(bf16), second_grad.astype(bf16)], 1)
    downw_ref[...] += mm_tn(hidden, branch_low)
    upw_ref[...] += mm_tn(ffn_low, upper_grad)
    mid_grad = final_grad + norm_back(normed_mid, inv_mid, mm_nt(upper_grad, upw))
    mid_grad_at[...] = mid_grad
    out_low = mid_grad.astype(bf16)
    gated_grad = mm_nt(out_low, outw)
    sig_gate = sigmoid(gate_ref[0])
    attend = attend_ref[0]
    gated_low = (attend * sig_gate).astype(bf16)
    outw_ref[...] += mm_tn(gated_low, out_low)
    attlow_s[...] = (gated_grad * sig_gate).astype(bf16)
    gate_grad_at[...] = (gated_grad * attend * sig_gate * (1.0 - sig_gate)).astype(bf16)


def atom_bwd_windows(sample_refs, scratch):
    query_ref, keyval_ref, probs_ref = sample_refs
    acck_s, accv_s, bias_s, attlow_s, dq_s = scratch
    width = query_ref.shape[-1]
    head_dim = width // ATOM_HEADS
    scale = float(head_dim) ** (-0.5)
    windows = query_ref.shape[1] // WIN_Q
    acck_s[...] = jnp.zeros_like(acck_s)
    accv_s[...] = jnp.zeros_like(accv_s)
    masks = head_masks(2 * WIN_Q, width, ATOM_HEADS, head_dim, 0)

    def two_windows(duo):
        first = pl.multiple_of(duo * 2 * WIN_Q, 2 * WIN_Q)
        span = pl.ds(first, 2 * WIN_K)
        own = pl.ds(first, 2 * WIN_Q)
        queries = head_stack(query_ref[0, own, :], ATOM_HEADS, head_dim, 0, masks)
        att = head_stack(attlow_s[own, :], ATOM_HEADS, head_dim, 0, masks)
        probs_low = probs_ref[0, duo]
        probs = probs_low.astype(f32)
        prob_grad = mm_nt(att, keyval_ref[0, span, width:])
        delta = jnp.sum(prob_grad * probs, -1, keepdims=True)
        score_low = (probs * (prob_grad - delta)).astype(bf16)
        bias_s[duo] += score_low.astype(f32)
        dq_s[own, :] = (
            head_fold(mm(score_low, keyval_ref[0, span, :width]), ATOM_HEADS, head_dim, 0) * scale
        )
        acck_s[span, :] += mm_tn(score_low, queries) * scale
        accv_s[span, :] += mm_tn(probs_low, att)

    def some_windows(step, carry):
        for part in range(2):
            two_windows(step * 2 + part)
        return carry

    lax.fori_loop(0, windows // 4, some_windows, 0)


def atom_bwd_pairs(starts, pairs_ref, bias_s, pairw_ref, pairm_ref):
    fold = pair_fold(pairs_ref.shape[1] // WIN_Q)

    def one(duo, carry):
        for part in range(2):
            win = duo * 2 + part
            pairs = pairs_ref[win]
            mean, inv_std = pair_stats(pairs, fold)
            lows = [(head * 2 + part) * WIN_Q for head in range(ATOM_HEADS)]
            placed = jnp.concatenate([bias_s[duo, low : low + WIN_Q, :] for low in lows], 0)
            shift = starts[win] - duo * 2 * WIN_Q
            grad = pltpu.roll(placed, lax.rem(2 * WIN_K - shift, 2 * WIN_K), 1)[:, :WIN_K]
            scaled = grad * jnp.concatenate([inv_std] * ATOM_HEADS, 0)
            pairm_ref[...] += scaled * jnp.concatenate([mean] * ATOM_HEADS, 0)
            upper = scaled.astype(bf16)
            lower = (scaled - upper.astype(f32)).astype(bf16)
            pairw_ref[...] += mm_nt(upper, pairs) + mm_nt(lower, pairs)
        return carry

    lax.fori_loop(0, pairs_ref.shape[0] // 2, one, 0)


def atom_bwd_kernel(
    starts,
    grad_ref,
    query_ref,
    keyval_ref,
    gate_ref,
    probs_ref,
    attend_ref,
    mid_ref,
    pairs_ref,
    share_ref,
    wide_ref,
    down_ref,
    mix_ref,
    own_ref,
    left_ref,
    right_ref,
    midgrad_ref,
    qbias_ref,
    outw_ref,
    upw_ref,
    downw_ref,
    pool_ref,
    pairw_ref,
    pairm_ref,
    *scratch,
):
    acck_s, accv_s, bias_s, attlow_s, dq_s = scratch
    width = query_ref.shape[-1]
    slots = query_ref.shape[1]
    sample = pl.program_id(0)

    @pl.when(sample == 0)
    def _():
        for ref in (qbias_ref, outw_ref, upw_ref, downw_ref, pool_ref, pairw_ref, pairm_ref, bias_s):
            ref[...] = jnp.zeros_like(ref)

    atom_bwd_dense(
        (grad_ref, query_ref, gate_ref, attend_ref, mid_ref),
        (share_ref, wide_ref, down_ref),
        (outw_ref, upw_ref, downw_ref, pool_ref),
        attlow_s,
        mix_ref.at[0, :, width:],
        midgrad_ref.at[0],
    )
    atom_bwd_windows((query_ref, keyval_ref, probs_ref), scratch)
    query_grad = dq_s[...]
    qbias_ref[...] += jnp.sum(query_grad, 0, keepdims=True)
    mix_ref[0, :, :width] = query_grad.astype(bf16)
    for ref, low, high in (
        (own_ref, RIM, RIM + slots),
        (left_ref, 0, RIM),
        (right_ref, RIM + slots, slots + 2 * RIM),
    ):
        ref[0, :, :width] = acck_s[low:high, :].astype(ref.dtype)
        ref[0, :, width:] = accv_s[low:high, :].astype(ref.dtype)

    @pl.when(sample == pl.num_programs(0) - 1)
    def _():
        atom_bwd_pairs(starts, pairs_ref, bias_s, pairw_ref, pairm_ref)


def atom_bwd_sum_kernel(
    summing,
    starts,
    grad_ref,
    query_ref,
    keyval_ref,
    gate_ref,
    probs_ref,
    attend_ref,
    mid_ref,
    rows_ref,
    pairs_ref,
    share_ref,
    wide_ref,
    down_ref,
    units_ref,
    atomgrad_ref,
    qbias_ref,
    pairw_ref,
    pairm_ref,
    small_ref,
    shares_ref,
    acck_s,
    accv_s,
    bias_s,
    attlow_s,
    dq_s,
    mix_s,
    midgrad_s,
    outw_s,
    upw_s,
    downw_s,
    pool_s,
    proj_s,
    to_left,
    to_right,
    from_left,
    from_right,
    s_rim,
    r_rim,
    *sums,
):
    summing.bind(units_ref, shares_ref, *sums)
    z, me = lax.axis_index("samp"), lax.axis_index("seq")
    seq = lax.axis_size("seq")
    first_place, last_place = me == 0, me == seq - 1
    width = query_ref.shape[-1]
    slots = query_ref.shape[1]
    step = pl.program_id(0)
    samples = pl.num_programs(0) - 1
    summing.slot(2 * step)

    def rim(b, side):
        ends = ((to_left, from_right, me - 1), (to_right, from_left, me + 1))[side]
        source, target, device = ends
        return remote(source.at[b], target.at[b], s_rim.at[side, b], r_rim.at[side, b], (z, device))

    def arrived(b, side):
        target = (from_right, from_left)[side]
        return remote(
            target.at[b], target.at[b], s_rim.at[side, b], r_rim.at[side, b], (z, lax.rem(me + 1, seq))
        )

    @pl.when(step == 0)
    def _():
        for ref in (qbias_ref, outw_s, upw_s, downw_s, pool_s, proj_s, pairw_ref, pairm_ref, bias_s):
            ref[...] = jnp.zeros_like(ref)

        @pl.when(first_place)
        def _():
            from_left[...] = jnp.zeros_like(from_left)

        @pl.when(last_place)
        def _():
            from_right[...] = jnp.zeros_like(from_right)

    slot_now = step % 2

    @pl.when(step < samples)
    def _():
        atom_bwd_dense(
            (grad_ref, query_ref, gate_ref, attend_ref, mid_ref),
            (share_ref, wide_ref, down_ref),
            (outw_s, upw_s, downw_s, pool_s),
            attlow_s,
            mix_s.at[slot_now, :, width:],
            midgrad_s.at[slot_now],
        )

    summing.slot(2 * step + 1)

    @pl.when(step > 0)
    def _():
        b = step - 1

        @pl.when(~first_place)
        def _():
            arrived(b, 1).wait_recv()

        @pl.when(~last_place)
        def _():
            arrived(b, 0).wait_recv()

        normed, inv_std = norm_stats(rows_ref[0].astype(f32))
        parts = []
        for acc, lanes in ((acck_s, slice(0, width)), (accv_s, slice(width, 2 * width))):
            own = acc[RIM : RIM + slots, :]
            begin = own[:RIM] + from_left[b, :, lanes].astype(f32)
            end = own[slots - RIM :] + from_right[b, :, lanes].astype(f32)
            parts.append(jnp.concatenate([begin, own[RIM : slots - RIM], end], 0).astype(bf16))
        before = mix_s.at[1 - slot_now]
        mix = jnp.concatenate([before[:, :width], parts[0], parts[1], before[:, width:]], 1)
        proj_s[...] += mm_tn(normed.astype(bf16), mix)
        normed_grad = mm_nt(mix, wide_ref[:, : 4 * width])
        atomgrad_ref[0] = midgrad_s[1 - slot_now] + norm_back(normed, inv_std, normed_grad)

    @pl.when(step < samples)
    def _():
        atom_bwd_windows(
            (query_ref, keyval_ref, probs_ref), (acck_s, accv_s, bias_s, attlow_s, dq_s)
        )
        query_grad = dq_s[...]
        qbias_ref[...] += jnp.sum(query_grad, 0, keepdims=True)
        mix_s[slot_now, :, :width] = query_grad.astype(bf16)
        for ref, low in ((to_left, 0), (to_right, RIM + slots)):
            ref[step, :, :width] = acck_s[low : low + RIM, :].astype(bf16)
            ref[step, :, width:] = accv_s[low : low + RIM, :].astype(bf16)

        @pl.when(~first_place)
        def _():
            rim(step, 0).start()

        @pl.when(~last_place)
        def _():
            rim(step, 1).start()

    @pl.when(step == samples)
    def _():
        atom_bwd_pairs(starts, pairs_ref, bias_s, pairw_ref, pairm_ref)
        samp = small_ref.shape[0]
        rows = width // samp
        for p in range(samp):
            span = slice(p * rows, (p + 1) * rows)
            small_ref[p, :rows, :] = pool_s[span, :].astype(bf16)
            small_ref[p, rows : 2 * rows, : 4 * width] = proj_s[span, :].astype(bf16)
            for part in range(2):
                low = (2 * p + part) * rows
                small_ref[p, rows : 2 * rows, (4 + part) * width : (5 + part) * width] = downw_s[
                    low : low + rows, :
                ].astype(bf16)
            small_ref[p, 2 * rows : 3 * rows, : 4 * width] = upw_s[span, :].astype(bf16)
            small_ref[p, 2 * rows : 3 * rows, 4 * width : 5 * width] = outw_s[span, :].astype(bf16)
            small_ref[p, 2 * rows : 3 * rows, 5 * width :] = jnp.zeros((rows, width), bf16)
            small_ref[p, 3 * rows :, :] = jnp.zeros((rows, 6 * width), bf16)
        summing.collect()

        def sent(b, carry):
            @pl.when(~first_place)
            def _():
                rim(b, 0).wait_send()

            @pl.when(~last_place)
            def _():
                rim(b, 1).wait_send()

            return carry

        lax.fori_loop(0, samples, sent, 0)


def atom_backward_sum(grad, starts, stored, rows, pairs, share, wide, down, summing, units):
    query = stored[0]
    samples, slots, width = query.shape
    samp = lax.axis_size("samp")
    ext_slots = slots + 2 * RIM
    windows = slots // WIN_Q
    model_width = grad.shape[-1]
    hidden_width = down.shape[0]
    stack = ATOM_HEADS * WIN_Q
    place = pl.BlockSpec(memory_space=pl.ANY)

    def now(shape):
        return pl.BlockSpec(
            (1,) + shape, lambda g: (jnp.minimum(g, samples - 1),) + (0,) * len(shape)
        )

    def late(shape):
        return pl.BlockSpec((1,) + shape, lambda g: (jnp.maximum(g - 1, 0),) + (0,) * len(shape))

    dma = pltpu.SemaphoreType.DMA
    rim_shape = (samples, RIM, 2 * width)
    small_shape = (samp, 4 * width // samp, model_width)
    return pl.pallas_call(
        functools.partial(atom_bwd_sum_kernel, summing),
        out_shape=[
            jax.ShapeDtypeStruct(rows.shape, f32),
            jax.ShapeDtypeStruct((1, width), f32),
            jax.ShapeDtypeStruct((stack, pairs.shape[1]), f32),
            jax.ShapeDtypeStruct((stack, WIN_K), f32),
            jax.ShapeDtypeStruct(small_shape, bf16),
            jax.ShapeDtypeStruct((UNIT, 768), bf16),
        ],
        grid=(samples + 1,),
        in_specs=[pl.BlockSpec(memory_space=pltpu.SMEM), now(grad.shape[1:])]
        + [now(part.shape[1:]) for part in stored]
        + [late(rows.shape[1:])]
        + [whole(part.shape) for part in (pairs, share, wide, down)]
        + [place],
        out_specs=[
            late(rows.shape[1:]),
            whole((1, width)),
            whole((stack, pairs.shape[1])),
            whole((stack, WIN_K)),
            whole(small_shape),
            place,
        ],
        scratch_shapes=[
            pltpu.VMEM((ext_slots, width), f32),
            pltpu.VMEM((ext_slots, width), f32),
            pltpu.VMEM((windows // 2, 2 * stack, 2 * WIN_K), f32),
            pltpu.VMEM((slots, width), bf16),
            pltpu.VMEM((slots, width), f32),
            pltpu.VMEM((2, slots, 2 * width), bf16),
            pltpu.VMEM((2, slots, width), f32),
            pltpu.VMEM((width, width), f32),
            pltpu.VMEM((width, 2 * hidden_width), f32),
            pltpu.VMEM((hidden_width, width), f32),
            pltpu.VMEM((width, model_width), f32),
            pltpu.VMEM((width, 4 * width), f32),
            pltpu.VMEM(rim_shape, bf16),
            pltpu.VMEM(rim_shape, bf16),
            pltpu.VMEM(rim_shape, bf16),
            pltpu.VMEM(rim_shape, bf16),
            dma((2, samples)),
            dma((2, samples)),
        ]
        + summing.scratch(),
        compiler_params=summing.params(),
        name="atom_backward",
    )(starts, grad, *stored, rows, pairs, share, wide, down, units)


def unpack_kernel(units_ref, small_ref, proj_ref, up_ref, down_ref, cond_ref, outw_ref, *atoms):
    proj_ref[...] = units_ref[0, :192, :384].astype(f32)
    up_ref[...] = units_ref[0, :192, 384:].astype(f32)
    down_ref[...] = units_ref[0, 192:240, :].astype(f32)
    cond_ref[:, :768] = units_ref[0, 240:288, :].astype(f32)
    cond_ref[:, 768:] = units_ref[0, 288:336, :384].astype(f32)
    outw_ref[...] = units_ref[0, 288:336, 384:].astype(f32)

    @pl.when(pl.program_id(0) == 0)
    def _():
        pool_ref, atomproj_ref, atomdown_ref, atomup_ref, atomout_ref, tiny_ref = atoms
        rows, width = atomout_ref.shape
        pool_ref[...] = small_ref[:rows, :].astype(f32)
        atomproj_ref[...] = small_ref[rows : 2 * rows, : 4 * width].astype(f32)
        for part in range(2):
            atomdown_ref[part * rows : (part + 1) * rows, :] = small_ref[
                rows : 2 * rows, (4 + part) * width : (5 + part) * width
            ].astype(f32)
        atomup_ref[...] = small_ref[2 * rows : 3 * rows, : 4 * width].astype(f32)
        atomout_ref[...] = small_ref[2 * rows : 3 * rows, 4 * width : 5 * width].astype(f32)
        tiny_ref[...] = small_ref[2 * rows : 3 * rows, 5 * width :].astype(f32)


def unpack(units, small, shapes, rows, width):
    outs = list(shapes) + [
        (rows, 6 * width),
        (rows, 4 * width),
        (2 * rows, width),
        (rows, 4 * width),
        (rows, width),
        (rows, width),
    ]
    specs = [
        pl.BlockSpec((192, 384), lambda s: (0, s)),
        pl.BlockSpec((192, 384), lambda s: (0, s)),
        pl.BlockSpec((48, 768), lambda s: (s, 0)),
        pl.BlockSpec((48, 1152), lambda s: (s // 4, s % 4)),
        pl.BlockSpec((48, 384), lambda s: (s // 2, s % 2)),
    ]
    return pl.pallas_call(
        unpack_kernel,
        out_shape=[jax.ShapeDtypeStruct(shape, f32) for shape in outs],
        grid=(8,),
        in_specs=[pl.BlockSpec((1, UNIT, 768), lambda s: (s, 0, 0)), whole(small.shape)],
        out_specs=specs + [whole(shape) for shape in outs[5:]],
        compiler_params=params(),
        name="unpack",
    )(units, small)


def atom_backward(grad, starts, stored, pairs, share, wide, down):
    query = stored[0]
    samples, slots, width = query.shape
    ext_slots = slots + 2 * RIM
    windows = slots // WIN_Q
    model_width = grad.shape[-1]
    hidden_width = down.shape[0]
    stack = ATOM_HEADS * WIN_Q
    outs = (
        ((slots, 2 * width), bf16),
        ((slots, 2 * width), f32),
        ((RIM, 2 * width), bf16),
        ((RIM, 2 * width), bf16),
        ((slots, width), f32),
    )
    totals = (
        (1, width),
        (width, width),
        (width, 2 * hidden_width),
        (hidden_width, width),
        (width, model_width),
        (stack, pairs.shape[1]),
        (stack, WIN_K),
    )
    return pl.pallas_call(
        atom_bwd_kernel,
        out_shape=[jax.ShapeDtypeStruct((samples,) + shape, kind) for shape, kind in outs]
        + [jax.ShapeDtypeStruct(shape, f32) for shape in totals],
        grid=(samples,),
        in_specs=[pl.BlockSpec(memory_space=pltpu.SMEM), per_sample(grad.shape[1:])]
        + [per_sample(part.shape[1:]) for part in stored]
        + [whole(part.shape) for part in (pairs, share, wide, down)],
        out_specs=[per_sample(shape) for shape, _ in outs] + [whole(shape) for shape in totals],
        scratch_shapes=[
            pltpu.VMEM((ext_slots, width), f32),
            pltpu.VMEM((ext_slots, width), f32),
            pltpu.VMEM((windows // 2, 2 * stack, 2 * WIN_K), f32),
            pltpu.VMEM((slots, width), bf16),
            pltpu.VMEM((slots, width), f32),
        ],
        compiler_params=params(),
        name="atom_backward",
    )(starts, grad, *stored, pairs, share, wide, down)


def atom_input_kernel(
    rows_ref, mix_ref, own_ref, left_ref, right_ref, midgrad_ref, wide_ref, grad_ref, proj_ref
):
    width = rows_ref.shape[-1]

    @pl.when(pl.program_id(0) == 0)
    def _():
        proj_ref[...] = jnp.zeros_like(proj_ref)

    normed, inv_std = norm_stats(rows_ref[0].astype(f32))
    slots = normed.shape[0]
    own = own_ref[0]
    head = own[:RIM] + left_ref[0].astype(f32)
    tail = own[slots - RIM :] + right_ref[0].astype(f32)
    own = jnp.concatenate([head, own[RIM : slots - RIM], tail], 0).astype(bf16)
    mix = jnp.concatenate([mix_ref[0, :, :width], own, mix_ref[0, :, width:]], 1)
    proj_ref[...] += mm_tn(normed.astype(bf16), mix)
    normed_grad = mm_nt(mix, wide_ref[:, : 4 * width])
    grad_ref[0] = midgrad_ref[0] + norm_back(normed, inv_std, normed_grad)


def atom_input_backward(rows, mix, own, left, right, midgrad, wide):
    samples, slots, width = rows.shape
    return pl.pallas_call(
        atom_input_kernel,
        out_shape=[
            jax.ShapeDtypeStruct(rows.shape, f32),
            jax.ShapeDtypeStruct((width, 4 * width), f32),
        ],
        grid=(samples,),
        in_specs=[per_sample(part.shape[1:]) for part in (rows, mix, own, left, right, midgrad)]
        + [whole(wide.shape)],
        out_specs=[per_sample((slots, width)), whole((width, 4 * width))],
        compiler_params=params(),
        name="atom_input_backward",
    )(rows, mix, own, left, right, midgrad, wide)


def row_stats(pairs, ones_op, weights):
    count = weights.shape[0]
    both = mm_nt(jnp.concatenate([weights, ones_op], 0), pairs)
    upper, lower = square_sums(ones_op, pairs.astype(f32) * pairs.astype(f32))
    features = pairs.shape[1]
    mean = both[count : count + 1] * (1.0 / features)
    square = (mm_nt(ones_op, upper) + mm_nt(ones_op, lower))[:1] * (1.0 / features)
    var = jnp.maximum(square - mean * mean, 0.0)
    return both[:count], mean, lax.rsqrt(var + norm_eps)


def pair_bias_kernel(pair_ref, weight_ref, bias_ref):
    weights = weight_ref[...]
    ones_op = jnp.ones((16, weights.shape[1]), bf16)
    weight_sum = jnp.sum(weights.astype(f32), -1, keepdims=True)
    for row in range(pair_ref.shape[0]):
        product, mean, inv_std = row_stats(pair_ref[row], ones_op, weights)
        bias_ref[:, row, :] = inv_std * (product - mean * weight_sum)


def pair_bias(pairs, weights):
    rows, keys, features = pairs.shape
    heads = weights.shape[0]
    return pl.pallas_call(
        pair_bias_kernel,
        out_shape=jax.ShapeDtypeStruct((heads, rows, keys), f32),
        grid=(rows // 8,),
        in_specs=[pl.BlockSpec((8, keys, features), lambda i: (i, 0, 0)), whole(weights.shape)],
        out_specs=pl.BlockSpec((heads, 8, keys), lambda i: (0, i, 0)),
        compiler_params=params(),
        name="pair_bias",
    )(pairs, weights)


def pair_grad_kernel(pair_ref, grad_ref, weight_ref, total_ref, mean_ref):
    @pl.when(pl.program_id(0) == 0)
    def _():
        total_ref[...] = jnp.zeros_like(total_ref)
        mean_ref[...] = jnp.zeros_like(mean_ref)

    heads = grad_ref.shape[0]
    ones_op = jnp.ones((16, pair_ref.shape[2]), bf16)
    total = jnp.zeros(total_ref.shape, f32)
    means = jnp.zeros(mean_ref.shape, f32)
    for row in range(pair_ref.shape[0]):
        pairs = pair_ref[row]
        _, mean, inv_std = row_stats(pairs, ones_op, weight_ref[...])
        scaled = grad_ref[:, row, :] * inv_std
        means += scaled * mean
        upper = scaled.astype(bf16)
        lower = (scaled - upper.astype(f32)).astype(bf16)
        both = mm(jnp.concatenate([upper, lower], 0), pairs)
        total += both[:heads] + both[heads:]
    total_ref[...] += total
    mean_ref[...] += means


def pair_grad(pairs, grads, weights):
    rows, keys, features = pairs.shape
    heads = grads.shape[0]
    total, means = pl.pallas_call(
        pair_grad_kernel,
        out_shape=[
            jax.ShapeDtypeStruct((heads, features), f32),
            jax.ShapeDtypeStruct((heads, keys), f32),
        ],
        grid=(rows // 8,),
        in_specs=[
            pl.BlockSpec((8, keys, features), lambda i: (i, 0, 0)),
            pl.BlockSpec((heads, 8, keys), lambda i: (0, i, 0)),
            whole(weights.shape),
        ],
        out_specs=[whole((heads, features)), whole((heads, keys))],
        compiler_params=params(),
        name="pair_grad",
    )(pairs, grads, weights)
    return total - jnp.sum(means, -1, keepdims=True)


def head_groups(width, heads):
    head_dim = width // heads
    groups = []
    for head in range(0, heads, 4):
        low = head * head_dim
        base = low // LANES * LANES
        groups.append((head, base, low - base))
    return head_dim, groups


def token_fwd_kernel(query_ref, keyval_ref, bias_ref, attend_ref, probs_ref, fold_s):
    tokens, width = query_ref.shape[1:]
    heads = bias_ref.shape[0]
    keys = bias_ref.shape[2]
    head_dim, groups = head_groups(width, heads)
    scale = float(head_dim) ** (-0.5)
    fold_s[...] = jnp.zeros_like(fold_s)
    for head, base, first in groups:
        span = slice(base, base + 256)
        key_rows = keyval_ref[:, 0, :, base : base + 256].reshape(keys, 256)
        value_rows = keyval_ref[:, 0, :, width + base : width + base + 256].reshape(keys, 256)
        stacked = head_stack(query_ref[0, :, span], 4, head_dim, first)
        bias = bias_ref[head : head + 4].reshape(4 * tokens, keys)
        scores = mm_nt(stacked, key_rows) * scale + bias
        exp_scores = jnp.exp(scores - jnp.max(scores, -1, keepdims=True))
        probs = exp_scores * (1.0 / jnp.sum(exp_scores, -1, keepdims=True))
        probs_low = probs.astype(bf16)
        probs_ref[0, head : head + 4] = probs_low.reshape(4, tokens, keys)
        fold_s[:, span] += head_fold(mm(probs_low, value_rows), 4, head_dim, first)
    attend_ref[0] = fold_s[...]


def token_attention(query, keyval, bias):
    samples, tokens, width = query.shape
    heads, _, keys = bias.shape
    devices = keyval.shape[0]
    return pl.pallas_call(
        token_fwd_kernel,
        out_shape=[
            jax.ShapeDtypeStruct(query.shape, f32),
            jax.ShapeDtypeStruct((samples, heads, tokens, keys), bf16),
        ],
        grid=(samples,),
        in_specs=[
            per_sample((tokens, width)),
            pl.BlockSpec((devices, 1, tokens, 2 * width), lambda b: (0, b, 0, 0)),
            whole(bias.shape),
        ],
        out_specs=[per_sample((tokens, width)), per_sample((heads, tokens, keys))],
        scratch_shapes=[pltpu.VMEM((tokens, width), f32)],
        compiler_params=params(),
        name="token_attention",
    )(query, keyval, bias)


def token_bwd_kernel(
    query_ref, keyval_ref, probs_ref, att_ref, dq_ref, dkv_ref, bias_ref, fold_s, grad_s
):
    tokens, width = query_ref.shape[1:]
    heads, _, keys = bias_ref.shape
    devices = keyval_ref.shape[0]
    head_dim, groups = head_groups(width, heads)
    scale = float(head_dim) ** (-0.5)

    @pl.when(pl.program_id(0) == 0)
    def _():
        bias_ref[...] = jnp.zeros_like(bias_ref)

    fold_s[...] = jnp.zeros_like(fold_s)
    grad_s[...] = jnp.zeros_like(grad_s)
    for head, base, first in groups:
        span = slice(base, base + 256)
        key_rows = keyval_ref[:, 0, :, base : base + 256].reshape(keys, 256)
        value_rows = keyval_ref[:, 0, :, width + base : width + base + 256].reshape(keys, 256)
        queries = head_stack(query_ref[0, :, span], 4, head_dim, first)
        att = head_stack(att_ref[0, :, span], 4, head_dim, first)
        probs_low = probs_ref[0, head : head + 4].reshape(4 * tokens, keys)
        probs = probs_low.astype(f32)
        prob_grad = mm_nt(att, value_rows)
        delta = jnp.sum(prob_grad * probs, -1, keepdims=True)
        score_low = (probs * (prob_grad - delta)).astype(bf16)
        bias_ref[head : head + 4] += score_low.astype(f32).reshape(4, tokens, keys)
        fold_s[:, span] += head_fold(mm(score_low, key_rows), 4, head_dim, first) * scale
        grad_s[:, span] += mm_tn(score_low, queries) * scale
        grad_s[:, width + base : width + base + 256] += mm_tn(probs_low, att)
    dq_ref[0] = fold_s[...]
    dkv_ref[:, 0] = grad_s[...].astype(bf16).reshape(devices, tokens, 2 * width)


def token_attention_back(query, keyval, probs, att):
    samples, tokens, width = query.shape
    heads, _, keys = probs.shape[1:]
    devices = keyval.shape[0]
    return pl.pallas_call(
        token_bwd_kernel,
        out_shape=[
            jax.ShapeDtypeStruct(query.shape, f32),
            jax.ShapeDtypeStruct(keyval.shape, bf16),
            jax.ShapeDtypeStruct((heads, tokens, keys), f32),
        ],
        grid=(samples,),
        in_specs=[
            per_sample((tokens, width)),
            pl.BlockSpec((devices, 1, tokens, 2 * width), lambda b: (0, b, 0, 0)),
            per_sample((heads, tokens, keys)),
            per_sample((tokens, width)),
        ],
        out_specs=[
            per_sample((tokens, width)),
            pl.BlockSpec((devices, 1, tokens, 2 * width), lambda b: (0, b, 0, 0)),
            whole((heads, tokens, keys)),
        ],
        scratch_shapes=[
            pltpu.VMEM((tokens, width), f32),
            pltpu.VMEM((keys, 2 * width), f32),
        ],
        compiler_params=params(),
        name="token_attention_back",
    )(query, keyval, probs, att)


def token_middle_rows(
    attend,
    gating_ref,
    block_ref,
    gate1_ref,
    scale2_ref,
    shift2_ref,
    gate2_ref,
    cotangent_ref,
    outw_ref,
    upw_ref,
    downw_ref,
    result_ref,
    ffn_ref,
    upper_ref,
    hidden_ref,
    two_ref,
    gated_ref,
    branch_ref,
    att_ref,
    gategrad_ref,
    midgrad_ref,
    condgrad_ref,
):
    width = attend.shape[1]
    hidden_width = downw_ref.shape[0]
    outw, upw, downw = outw_ref[...], upw_ref[...], downw_ref[...]
    sig_gate = sigmoid(gating_ref[...])
    gated_low = (attend * sig_gate).astype(bf16)
    gated_ref[...] = gated_low
    branch = mm(gated_low, outw)
    gate_one = sigmoid(gate1_ref[...])
    mid = block_ref[...] + gate_one * branch
    normed, inv_std = norm_stats(mid)
    scale_two = sigmoid(scale2_ref[...])
    ffn_in = (scale_two * normed + shift2_ref[...]).astype(bf16)
    ffn_ref[...] = ffn_in
    first_half = mm(ffn_in, upw[:, :hidden_width])
    second_half = mm(ffn_in, upw[:, hidden_width:])
    sig_first = sigmoid(first_half)
    hidden = (first_half * sig_first * second_half).astype(bf16)
    hidden_ref[...] = hidden
    branch_two = mm(hidden, downw)
    gate_two = sigmoid(gate2_ref[...])
    result_ref[...] = (mid + gate_two * branch_two).astype(bf16)

    out_grad = cotangent_ref[...].astype(f32)
    two_low = (out_grad * gate_two).astype(bf16)
    two_ref[...] = two_low
    condgrad_ref[:, 3 * width :] = (
        out_grad * branch_two * gate_two * (1.0 - gate_two)
    ).astype(bf16)
    hidden_grad = mm_nt(two_low, downw)
    first_grad = (
        hidden_grad * second_half * sig_first * (1.0 + first_half * (1.0 - sig_first))
    ).astype(bf16)
    second_grad = (hidden_grad * first_half * sig_first).astype(bf16)
    upper_ref[:, :hidden_width] = first_grad
    upper_ref[:, hidden_width:] = second_grad
    ffn_grad = mm_nt(first_grad, upw[:, :hidden_width]) + mm_nt(second_grad, upw[:, hidden_width:])
    condgrad_ref[:, 2 * width : 3 * width] = ffn_grad.astype(bf16)
    condgrad_ref[:, width : 2 * width] = (
        ffn_grad * normed * scale_two * (1.0 - scale_two)
    ).astype(bf16)
    mid_grad = out_grad + norm_back(normed, inv_std, ffn_grad * scale_two)
    midgrad_ref[...] = mid_grad
    branch_low = (mid_grad * gate_one).astype(bf16)
    branch_ref[...] = branch_low
    condgrad_ref[:, :width] = (mid_grad * branch * gate_one * (1.0 - gate_one)).astype(bf16)
    gated_grad = mm_nt(branch_low, outw)
    att_ref[...] = (gated_grad * sig_gate).astype(bf16)
    gategrad_ref[...] = (gated_grad * attend * sig_gate * (1.0 - sig_gate)).astype(bf16)


def attend_groups(heads, width, tokens, query, keyval, bias, probs_ref, fold_s):
    head_dim, groups = head_groups(width, heads)
    scale = float(head_dim) ** (-0.5)
    fold_s[...] = jnp.zeros_like(fold_s)
    for head, base, first in groups:
        span = slice(base, base + 256)
        stacked = head_stack(query[:, span], 4, head_dim, first)
        scores = mm_nt(stacked, keyval(base)) * scale + bias(head)
        exp_scores = jnp.exp(scores - jnp.max(scores, -1, keepdims=True))
        probs = exp_scores * (1.0 / jnp.sum(exp_scores, -1, keepdims=True))
        probs_low = probs.astype(bf16)
        probs_ref[0, head : head + 4] = probs_low.reshape(4, tokens, -1)
        fold_s[:, span] += head_fold(mm(probs_low, keyval(width + base)), 4, head_dim, first)


def gather_attend_kernel(
    query_ref,
    own_ref,
    pair_ref,
    weight_ref,
    gating_ref,
    block_ref,
    gate1_ref,
    scale2_ref,
    shift2_ref,
    gate2_ref,
    cotangent_ref,
    outw_ref,
    upw_ref,
    downw_ref,
    probs_ref,
    keyval_ref,
    stats_ref,
    *refs,
):
    middle, (all_s, bias_s, fold_s, attend_s, send, recv, load) = refs[:11], refs[11:]
    z, me, sib, xn, yn, dg = places()
    step = pl.program_id(0)
    tokens, width = query_ref.shape[1:]
    heads = weight_ref.shape[0]
    devices, samples = all_s.shape[:2]
    keys = devices * tokens
    head, tail, full = slice(0, width), slice(width, 2 * width), slice(0, 2 * width)

    def unit(part, sample, lanes, kind, device):
        ref = all_s.at[part, sample, :, lanes]
        return remote(ref, ref, send.at[kind, sample], recv.at[kind, sample], (z, device))

    def issue(sample):
        unit(me, sample, full, 0, xn).start()
        unit(me, sample, full, 1, yn).start()
        unit(me, sample, full, 4, sib).start()

    def relay(sample):
        unit(xn, sample, full, 0, xn).wait_recv()
        unit(xn, sample, head, 2, yn).start()
        unit(xn, sample, full, 5, sib).start()
        unit(yn, sample, full, 1, yn).wait_recv()
        unit(yn, sample, tail, 3, xn).start()
        unit(yn, sample, full, 6, sib).start()

    def collect(sample):
        unit(dg, sample, head, 2, yn).wait_recv()
        unit(dg, sample, tail, 3, xn).wait_recv()
        unit(dg, sample, full, 7, sib).start()

    @pl.when(step == 0)
    def _():
        copy = pltpu.make_async_copy(own_ref, all_s.at[me], load)
        copy.start()
        greet([(z, sib), (z, xn), (z, yn)])
        copy.wait()
        issue(0)
        issue(1)

    @pl.when((step >= 1) & (step - 1 < samples))
    def _():
        relay(step - 1)

    @pl.when((step >= 1) & (step + 1 < samples))
    def _():
        issue(step + 1)

    @pl.when((step >= 2) & (step - 2 < samples))
    def _():
        collect(step - 2)

    @pl.when(step < 2)
    def _():
        weights = weight_ref[...]
        ones_op = jnp.ones((16, weights.shape[1]), bf16)
        weight_sum = jnp.sum(weights.astype(f32), -1, keepdims=True)
        groups = pair_ref.shape[0] // 8

        def one(group, carry):
            for row in range(8):
                product, mean, inv_std = row_stats(pair_ref[group * 8 + row], ones_op, weights)
                place = step * groups + group
                bias_s[:, place, row, :] = inv_std * (product - mean * weight_sum)
                stats_ref[0, place, row : row + 1, :] = mean
                stats_ref[1, place, row : row + 1, :] = inv_std
            return carry

        lax.fori_loop(0, groups, one, 0)

    @pl.when(step >= 3)
    def _():
        sample = step - 3
        for kind, part in ((4, sib), (5, sib), (6, sib), (7, sib)):
            unit(part, sample, full, kind, sib).wait_recv()
        for part in range(devices):
            keyval_ref[part, 0] = all_s[part, sample]
        attend_groups(
            heads,
            width,
            tokens,
            query_ref[0],
            lambda base: keyval_ref[:, 0, :, base : base + 256].reshape(keys, 256),
            lambda head: bias_s[head : head + 4].reshape(4 * tokens, keys),
            probs_ref,
            fold_s,
        )
        attend_s[pl.ds(pl.multiple_of(sample % 2 * tokens, 16), tokens), :] = fold_s[...]

    @pl.when((step >= 3) & (step % 2 == 0))
    def _():
        token_middle_rows(
            attend_s[...],
            gating_ref,
            block_ref,
            gate1_ref,
            scale2_ref,
            shift2_ref,
            gate2_ref,
            cotangent_ref,
            outw_ref,
            upw_ref,
            downw_ref,
            *middle,
        )

    @pl.when(step == pl.num_programs(0) - 1)
    def _():
        def sent(sample, carry):
            for kind in (0, 1, 4, 5, 6, 7):
                unit(me, sample, full, kind, sib).wait_send()
            unit(me, sample, head, 2, sib).wait_send()
            unit(me, sample, tail, 3, sib).wait_send()
            return carry

        lax.fori_loop(0, samples, sent, 0)


def held_once(shape):
    return pl.BlockSpec(shape, lambda *_: (0,) * len(shape), pipeline_mode=pl.Buffered(1))


def gather_attend(query, own, pairs, weights, mix, block_in, cond_all, cotangent, outw, upw, downw):
    samples, tokens, width = query.shape
    heads, features = weights.shape
    seq = lax.axis_size("seq")
    keys = seq * tokens
    hidden_width = downw.shape[0]
    rows, block = samples * tokens, 2 * tokens
    late = lambda g: jnp.maximum(g - 3, 0)
    sample_block = lambda shape: pl.BlockSpec((1,) + shape, lambda g: (late(g),) + (0,) * len(shape))
    duo_block = lambda lanes, column=0: pl.BlockSpec((block, lanes), lambda g: (late(g) // 2, column))
    flat = lambda part: part.reshape(rows, part.shape[-1])
    cond = flat(cond_all)
    dma = pltpu.SemaphoreType.DMA
    outs = (
        (width, bf16),
        (width, bf16),
        (2 * hidden_width, bf16),
        (hidden_width, bf16),
        (width, bf16),
        (width, bf16),
        (width, bf16),
        (width, bf16),
        (width, bf16),
        (width, f32),
        (4 * width, bf16),
    )
    results = pl.pallas_call(
        gather_attend_kernel,
        out_shape=[
            jax.ShapeDtypeStruct((samples, heads, tokens, keys), bf16),
            jax.ShapeDtypeStruct((seq, samples, tokens, 2 * width), bf16),
            jax.ShapeDtypeStruct((2, tokens // 8, 8, keys), f32),
        ]
        + [jax.ShapeDtypeStruct((rows, lanes), kind) for lanes, kind in outs],
        grid=(samples + 3,),
        in_specs=[
            sample_block((tokens, width)),
            pl.BlockSpec(memory_space=pl.ANY),
            pl.BlockSpec((tokens // 2, keys, features), lambda g: (jnp.minimum(g, 1), 0, 0)),
            whole(weights.shape),
            duo_block(width, 3),
            duo_block(width),
            duo_block(width, 2),
            duo_block(width, 3),
            duo_block(width, 4),
            duo_block(width, 5),
            duo_block(width),
        ]
        + [held_once(part.shape) for part in (outw, upw, downw)],
        out_specs=[
            sample_block((heads, tokens, keys)),
            pl.BlockSpec((seq, 1, tokens, 2 * width), lambda g: (0, late(g), 0, 0)),
            whole((2, tokens // 8, 8, keys)),
        ]
        + [duo_block(lanes) for lanes, _ in outs],
        scratch_shapes=[
            pltpu.VMEM((seq, samples, tokens, 2 * width), bf16),
            pltpu.VMEM((heads, tokens // 8, 8, keys), f32),
            pltpu.VMEM((tokens, width), f32),
            pltpu.VMEM((block, width), f32),
            dma((8, samples)),
            dma((8, samples)),
            dma,
        ],
        compiler_params=pltpu.CompilerParams(
            vmem_limit_bytes=60 << 20, collective_id=4, has_side_effects=True
        ),
        name="gather_attend",
    )(
        query,
        own,
        pairs,
        weights,
        flat(mix),
        flat(block_in),
        cond,
        cond,
        cond,
        cond,
        flat(cotangent),
        outw,
        upw,
        downw,
    )
    return results[:3], results[3:]


def attend_back_scatter_kernel(
    query_ref,
    keyval_ref,
    probs_ref,
    att_ref,
    pair_ref,
    stats_ref,
    ffn_ref,
    upper_ref,
    hidden_ref,
    two_ref,
    gated_ref,
    branch_ref,
    dq_ref,
    dkv_ref,
    pairw_ref,
    pairm_ref,
    upw_ref,
    downw_ref,
    outw_ref,
    fold_s,
    grad_s,
    bias_s,
    mine,
    theirs,
    from_x,
    from_y,
    last_x,
    last_y,
    s_sib,
    r_sib,
    s_one,
    r_one,
    s_two,
    r_two,
):
    z, me, sib, xn, yn, dg = places()
    core, chip = me % 2, me // 2
    chip_x, chip_y, chip_d = xn // 2, yn // 2, dg // 2
    step = pl.program_id(0)
    tokens, width = query_ref.shape[1:]
    samples = mine.shape[0]
    heads, keys = probs_ref.shape[1], probs_ref.shape[3]
    head_dim, groups = head_groups(width, heads)
    scale = float(head_dim) ** (-0.5)
    head, tail = slice(0, width), slice(width, 2 * width)

    def there(b):
        return remote(
            mine.at[b, :, 1 - core], theirs.at[b], s_sib.at[b], r_sib.at[b], (z, sib)
        )

    def one(b, k):
        part = (chip_x, chip_d, chip_y, chip_d)[k]
        lanes = head if k < 2 else tail
        target = (from_x if k < 2 else from_y).at[b, k % 2]
        device = xn if k < 2 else yn
        source = mine.at[b, part, core, :, lanes]
        return remote(source, target, s_one.at[b, k], r_one.at[b, k], (z, device))

    def two(b, k):
        part, lanes, target, device = ((chip_y, head, last_y, yn), (chip_x, tail, last_x, xn))[k]
        source = mine.at[b, part, core, :, lanes]
        return remote(source, target.at[b], s_two.at[b, k], r_two.at[b, k], (z, device))

    def add(b, part, lanes, source):
        both = mine[b, part, core, :, lanes].astype(f32) + source.astype(f32)
        mine[b, part, core, :, lanes] = both.astype(bf16)

    @pl.when(step == 0)
    def _():
        greet([(z, sib), (z, xn), (z, yn)])
        bias_s[...] = jnp.zeros_like(bias_s)
        pairw_ref[...] = jnp.zeros_like(pairw_ref)
        pairm_ref[...] = jnp.zeros_like(pairm_ref)

    @pl.when((step >= 1) & (step - 1 < samples))
    def _():
        b = step - 1
        there(b).wait_recv()

        def chips(j, carry):
            add(b, j, slice(0, 2 * width), theirs[b, j])
            return carry

        lax.fori_loop(0, 4, chips, 0)
        for k in range(4):
            one(b, k).start()

    @pl.when((step >= 2) & (step - 2 < samples))
    def _():
        b = step - 2
        one(b, 1).wait_recv()
        add(b, chip_y, head, from_x[b, 1])
        two(b, 0).start()
        one(b, 3).wait_recv()
        add(b, chip_x, tail, from_y[b, 1])
        two(b, 1).start()
        one(b, 0).wait_recv()
        add(b, chip, head, from_x[b, 0])
        one(b, 2).wait_recv()
        add(b, chip, tail, from_y[b, 0])

    @pl.when((step >= 3) & (step - 3 < samples))
    def _():
        b = step - 3
        two(b, 0).wait_recv()
        add(b, chip, head, last_y[b])
        two(b, 1).wait_recv()
        add(b, chip, tail, last_x[b])
        dkv_ref[0] = mine[b, chip, core]

    @pl.when(step < samples)
    def _():
        fold_s[...] = jnp.zeros_like(fold_s)
        grad_s[...] = jnp.zeros_like(grad_s)
        for first_head, base, first in groups:
            span = slice(base, base + 256)
            key_rows = keyval_ref[:, 0, :, base : base + 256].reshape(keys, 256)
            value_rows = keyval_ref[:, 0, :, width + base : width + base + 256].reshape(keys, 256)
            queries = head_stack(query_ref[0, :, span], 4, head_dim, first)
            att = head_stack(att_ref[0, :, span], 4, head_dim, first)
            probs_low = probs_ref[0, first_head : first_head + 4].reshape(4 * tokens, keys)
            probs = probs_low.astype(f32)
            prob_grad = mm_nt(att, value_rows)
            delta = jnp.sum(prob_grad * probs, -1, keepdims=True)
            score_low = (probs * (prob_grad - delta)).astype(bf16)
            bias_s[first_head : first_head + 4] += score_low.astype(f32).reshape(
                4, tokens // 8, 8, keys
            )
            fold_s[:, span] += head_fold(mm(score_low, key_rows), 4, head_dim, first) * scale
            grad_s[:, span] += mm_tn(score_low, queries) * scale
            grad_s[:, width + base : width + base + 256] += mm_tn(probs_low, att)
        dq_ref[0] = fold_s[...]
        mine[step] = grad_s[...].astype(bf16).reshape(mine.shape[1:])
        there(step).start()
        upw_ref[...] = mm_tn(ffn_ref[...], upper_ref[...]).astype(bf16)

    @pl.when(step < 6)
    def _():
        downw_ref[...] = mm_tn(hidden_ref[...], two_ref[...]).astype(bf16)

    @pl.when((step >= 6) & (step < 8))
    def _():
        outw_ref[...] = mm_tn(gated_ref[...], branch_ref[...]).astype(bf16)

    @pl.when((step >= samples) & (step < samples + 2))
    def _():
        rows = pair_ref.shape[0] // 8

        def some(group, carry):
            total, means = carry
            place = (step - samples) * rows + group
            for row in range(8):
                inv_std = stats_ref[1, place, row : row + 1, :]
                scaled = bias_s[:, place, row, :] * inv_std
                means += scaled * stats_ref[0, place, row : row + 1, :]
                upper = scaled.astype(bf16)
                lower = (scaled - upper.astype(f32)).astype(bf16)
                both = mm(jnp.concatenate([upper, lower], 0), pair_ref[group * 8 + row])
                total += both[:heads] + both[heads:]
            return total, means

        zeros = (jnp.zeros(pairw_ref.shape, f32), jnp.zeros(pairm_ref.shape, f32))
        total, means = lax.fori_loop(0, rows, some, zeros)
        pairw_ref[...] += total
        pairm_ref[...] += means

    @pl.when(step == pl.num_programs(0) - 1)
    def _():
        def sent(b, carry):
            there(b).wait_send()
            for k in range(4):
                one(b, k).wait_send()
            for k in range(2):
                two(b, k).wait_send()
            return carry

        lax.fori_loop(0, samples, sent, 0)


def attend_back_scatter(query, keyval, probs, att, pairs, stats, ffn, upper, hidden, two, gated, branch):
    samples, tokens, width = query.shape
    heads, _, keys = probs.shape[1:]
    seq = keyval.shape[0]
    features = pairs.shape[-1]
    flat = [part.reshape(-1, part.shape[-1]) for part in (ffn, upper, hidden, two, gated, branch)]
    rows = flat[0].shape[0]
    held = lambda g: jnp.minimum(g, samples - 1)
    late = lambda g: jnp.clip(g - 3, 0, samples - 1)
    pair_step = lambda g: jnp.clip(g - samples, 0, 1)
    up_step = lambda g: jnp.minimum(g, seq - 1)
    down_step = lambda g: jnp.minimum(g, 5)
    out_step = lambda g: jnp.clip(g - 6, 0, 1)
    sample_block = lambda shape, at: pl.BlockSpec((1,) + shape, lambda g: (at(g),) + (0,) * len(shape))
    keyval_block = pl.BlockSpec((seq, 1, tokens, 2 * width), lambda g: (0, held(g), 0, 0))
    up_width = flat[1].shape[1] // seq
    hidden_width = flat[2].shape[1]
    dma = pltpu.SemaphoreType.DMA
    results = pl.pallas_call(
        attend_back_scatter_kernel,
        out_shape=[
            jax.ShapeDtypeStruct(query.shape, f32),
            jax.ShapeDtypeStruct((samples, tokens, 2 * width), bf16),
            jax.ShapeDtypeStruct((heads, features), f32),
            jax.ShapeDtypeStruct((heads, keys), f32),
            jax.ShapeDtypeStruct((width, flat[1].shape[1]), bf16),
            jax.ShapeDtypeStruct((hidden_width, width), bf16),
            jax.ShapeDtypeStruct((width, width), bf16),
        ],
        grid=(samples + 3,),
        in_specs=[
            sample_block((tokens, width), held),
            keyval_block,
            sample_block((heads, tokens, keys), held),
            sample_block((tokens, width), held),
            pl.BlockSpec((tokens // 2, keys, features), lambda g: (pair_step(g), 0, 0)),
            whole(stats.shape),
            whole(flat[0].shape),
            pl.BlockSpec((rows, up_width), lambda g: (0, up_step(g))),
            pl.BlockSpec((rows, 256), lambda g: (0, down_step(g))),
            whole(flat[3].shape),
            pl.BlockSpec((rows, width // 2), lambda g: (0, out_step(g))),
            whole(flat[5].shape),
        ],
        out_specs=[
            sample_block((tokens, width), held),
            sample_block((tokens, 2 * width), late),
            whole((heads, features)),
            whole((heads, keys)),
            pl.BlockSpec((width, up_width), lambda g: (0, up_step(g))),
            pl.BlockSpec((256, width), lambda g: (down_step(g), 0)),
            pl.BlockSpec((width // 2, width), lambda g: (out_step(g), 0)),
        ],
        scratch_shapes=[
            pltpu.VMEM((tokens, width), f32),
            pltpu.VMEM((keys, 2 * width), f32),
            pltpu.VMEM((heads, tokens // 8, 8, keys), f32),
            pltpu.VMEM((samples, seq // 2, 2, tokens, 2 * width), bf16),
            pltpu.VMEM((samples, seq // 2, tokens, 2 * width), bf16),
            pltpu.VMEM((samples, 2, tokens, width), bf16),
            pltpu.VMEM((samples, 2, tokens, width), bf16),
            pltpu.VMEM((samples, tokens, width), bf16),
            pltpu.VMEM((samples, tokens, width), bf16),
            dma((samples,)),
            dma((samples,)),
            dma((samples, 4)),
            dma((samples, 4)),
            dma((samples, 2)),
            dma((samples, 2)),
        ],
        compiler_params=pltpu.CompilerParams(
            vmem_limit_bytes=60 << 20, collective_id=5, has_side_effects=True
        ),
        name="attend_back_scatter",
    )(query, keyval, probs, att, pairs, stats, *flat)
    dq, dkv, total, means, upw, downw, outw = results
    return dq, dkv, total - jnp.sum(means, -1, keepdims=True), (upw, downw, outw)


def token_close_kernel(
    dq_ref,
    dkv_ref,
    gategrad_ref,
    midgrad_ref,
    block_ref,
    scale1_ref,
    tail_ref,
    proj_ref,
    attn_ref,
    cond_ref,
    upw_ref,
    downw_ref,
    outw_ref,
    tokengrad_ref,
    qbias_ref,
    cbias_ref,
    units_ref,
    mix_s,
    condgrad_s,
    cond_s,
):
    step = pl.program_id(0)
    block, width = dq_ref.shape
    blocks = mix_s.shape[0] // block
    samp = units_ref.shape[1]

    @pl.when(step == 0)
    def _():
        qbias_ref[...] = jnp.zeros_like(qbias_ref)
        cbias_ref[...] = jnp.zeros_like(cbias_ref)

    @pl.when(step < blocks)
    def _():
        rows = pl.ds(pl.multiple_of(step * block, block), block)
        dq = dq_ref[...]
        qbias_ref[...] += jnp.sum(dq, 0, keepdims=True)
        mix = jnp.concatenate([dq.astype(bf16), dkv_ref[...], gategrad_ref[...]], 1)
        mix_s[rows, :] = mix
        attn_grad = mm_nt(mix, proj_ref[...])
        normed, inv_std = norm_stats(block_ref[...])
        scale_one = sigmoid(scale1_ref[...])
        scale_grad = (attn_grad * normed * scale_one * (1.0 - scale_one)).astype(bf16)
        tokengrad_ref[...] = midgrad_ref[...] + norm_back(normed, inv_std, attn_grad * scale_one)
        shift_grad = attn_grad.astype(bf16)
        tail = tail_ref[...]
        condgrad_s[rows, :width] = scale_grad
        condgrad_s[rows, width : 2 * width] = shift_grad
        condgrad_s[rows, 2 * width :] = tail
        for part, low in ((scale_grad, 0), (shift_grad, width), (tail, 2 * width)):
            cbias_ref[:, low : low + part.shape[1]] += jnp.sum(
                part.astype(f32), 0, keepdims=True
            )

    @pl.when(step == blocks)
    def _():
        for low in range(0, cond_s.shape[1], 768):
            cond_s[:, low : low + 768] = mm_tn(
                cond_ref[...], condgrad_s[:, low : low + 768]
            ).astype(bf16)

    @pl.when(step >= blocks)
    def _():
        part = step - blocks
        left = pl.multiple_of(part * 384, LANES)
        proj = mm_tn(attn_ref[...], mix_s[:, pl.ds(left, 384)]).astype(bf16)
        rows = proj.shape[0] // samp
        for z in range(samp):
            units_ref[0, z, :rows, :384] = proj[z * rows : (z + 1) * rows]
            units_ref[0, z, :rows, 384:] = upw_ref[z * rows : (z + 1) * rows, :]
            units_ref[0, z, 192:240, :] = downw_ref[
                pl.ds(pl.multiple_of(z * 384 + part * 48, 16), 48), :
            ]
            low = pl.multiple_of(z * 96 + part // 4 * 48, 16)
            left = pl.multiple_of(part % 4 * 1152, LANES)
            units_ref[0, z, 240:288, :] = cond_s[pl.ds(low, 48), pl.ds(left, 768)]
            left = pl.multiple_of(part % 4 * 1152 + 768, LANES)
            units_ref[0, z, 288:336, :384] = cond_s[pl.ds(low, 48), pl.ds(left, 384)]
            low = pl.multiple_of(z * 192 + part // 2 * 48, 16)
            left = pl.multiple_of(part % 2 * 384, LANES)
            units_ref[0, z, 288:336, 384:] = outw_ref[pl.ds(low, 48), pl.ds(left, 384)]


def token_close(dq, dkv, gategrad, midgrad, block_in, cond_all, tail, proj, attn_in, cond_low, ready, samp, seq):
    samples, tokens, width = dq.shape
    rows = samples * tokens
    blocks = 4
    block = rows // blocks
    flat = lambda part: part.reshape(rows, part.shape[-1])
    upw, downw, outw = ready
    attn, cond = flat(attn_in), flat(cond_low)

    def early(lanes, column=0):
        return pl.BlockSpec((block, lanes), lambda g: (jnp.minimum(g, blocks - 1), column))

    late = lambda g: jnp.maximum(g - blocks, 0)
    return pl.pallas_call(
        token_close_kernel,
        out_shape=[
            jax.ShapeDtypeStruct((rows, width), f32),
            jax.ShapeDtypeStruct((1, width), f32),
            jax.ShapeDtypeStruct((1, 6 * width), f32),
            jax.ShapeDtypeStruct((seq, samp, UNIT, 768), bf16),
        ],
        grid=(blocks + seq,),
        in_specs=[
            early(width),
            early(2 * width),
            early(width),
            early(width),
            early(width),
            early(width),
            early(4 * width),
            whole(proj.shape),
            whole(attn.shape),
            whole(cond.shape),
            pl.BlockSpec((width, 384), lambda g: (0, late(g))),
            whole(downw.shape),
            whole(outw.shape),
        ],
        out_specs=[
            early(width),
            whole((1, width)),
            whole((1, 6 * width)),
            pl.BlockSpec((1, samp, UNIT, 768), lambda g: (late(g), 0, 0, 0)),
        ],
        scratch_shapes=[
            pltpu.VMEM((rows, 4 * width), bf16),
            pltpu.VMEM((rows, 6 * width), bf16),
            pltpu.VMEM((cond.shape[1], 6 * width), bf16),
        ],
        compiler_params=params(),
        name="token_close",
    )(
        flat(dq),
        flat(dkv),
        gategrad,
        midgrad,
        flat(block_in),
        flat(cond_all),
        tail,
        proj,
        attn,
        cond,
        upw,
        downw,
        outw,
    )


def to_blocks(array, width):
    return [array[:, low : low + width] for low in range(0, array.shape[1], width)]


def pack_blocks(arrays, width):
    parts = []
    for array in arrays:
        parts += to_blocks(array, width)
    return jnp.concatenate(parts, 0)


def unpack_blocks(packed, shapes, width):
    arrays, low = [], 0
    for rows, columns in shapes:
        parts = []
        for _ in range(columns // width):
            parts.append(packed[low : low + rows])
            low += rows
        arrays.append(jnp.concatenate(parts, 1) if len(parts) > 1 else parts[0])
    return arrays


def sum_shares(grads, extra):
    samp, seq = lax.axis_size("samp"), lax.axis_size("seq")
    width = grads[2].shape[1]
    shapes = [(grad.shape[0] // samp, grad.shape[1]) for grad in grads]
    packed = jnp.concatenate(
        [
            block.astype(bf16).reshape(samp, -1, width)
            for grad in grads
            for block in to_blocks(grad, width)
        ]
        + [extra.astype(bf16).reshape(samp, -1, width)],
        1,
    )
    rows = packed.shape[1]
    packed = packed.reshape(samp, seq, rows // seq, width).transpose(1, 0, 2, 3)
    part = lax.psum_scatter(packed, "seq", scatter_dimension=0, tiled=False)
    part = lax.psum_scatter(part, "samp", scatter_dimension=0, tiled=False)
    packed = lax.all_gather(part, "seq", axis=0, tiled=True).astype(f32)
    shares = unpack_blocks(packed, shapes, width)
    return shares, packed[sum(r * (c // width) for r, c in shapes) :]


def local(
    atom_input,
    token_input,
    atom_counts,
    key_offsets,
    atom_pairs,
    pair_features,
    single_features,
    noise_levels,
    noise_direction,
    atom_proj,
    atom_qbias,
    atom_pairw,
    atom_outw,
    atom_upw,
    atom_downw,
    pool_weight,
    cond_weight,
    cond_bias,
    token_proj,
    token_qbias,
    token_pairw,
    token_outw,
    token_upw,
    token_downw,
    cotangent,
):
    samp, seq = lax.axis_size("samp"), lax.axis_size("seq")
    seq_pos = lax.axis_index("seq")
    samples, slots, atom_width = atom_input.shape
    tokens, width = token_input.shape[1:]
    features = atom_pairs.shape[-1]

    tiny_own = jnp.concatenate(
        [
            atom_qbias,
            cond_bias,
            token_qbias,
            atom_pairw.reshape(-1),
            token_pairw.reshape(-1),
        ]
    )
    tiny_own = jnp.pad(tiny_own, (0, -tiny_own.size % (16 * LANES))).reshape(-1, LANES)
    large = (token_proj, token_upw, token_downw, cond_weight, token_outw)
    kernels = samples == 8 and WeightGather.fits([part.shape for part in large], samp, seq)
    up_pairs = [(i, i + 1) for i in range(seq - 1)]
    down_pairs = [(i + 1, i) for i in range(seq - 1)]
    if kernels:
        wide, down, tiny_all, ext = edges(
            (atom_proj, atom_upw, pool_weight, atom_outw, atom_downw), tiny_own, atom_input
        )
    else:
        wide_own = jnp.concatenate([atom_proj, atom_upw, pool_weight, atom_outw], 1)
        wide = lax.all_gather(wide_own, "samp", axis=0, tiled=True)
        down = lax.all_gather(atom_downw, "samp", axis=0, tiled=True)
        tiny_all = lax.all_gather(tiny_own, "samp", axis=0, tiled=True)
        before = lax.ppermute(atom_input[:, slots - RIM :], "seq", up_pairs)
        after = lax.ppermute(atom_input[:, :RIM], "seq", down_pairs)
        ext = jnp.concatenate([before, atom_input, after], 1)
    tiny_all = tiny_all.reshape(samp, -1)
    sizes = [atom_qbias.size, cond_bias.size, token_qbias.size, atom_pairw.size, token_pairw.size]
    cuts = [sum(sizes[:i]) for i in range(6)]
    tiny = [tiny_all[:, cuts[i] : cuts[i + 1]] for i in range(5)]
    atom_qb = tiny[0].reshape(1, -1).astype(f32)
    cond_b = tiny[1].reshape(-1)
    token_qb = tiny[2].reshape(-1)
    atom_pw = tiny[3].reshape(features, ATOM_HEADS)
    token_pw = tiny[4].reshape(-1, token_pairw.shape[1])

    rim_tokens = RIM // MAX_ATOMS
    counts = lax.dynamic_slice_in_dim(
        jnp.pad(atom_counts, (rim_tokens, rim_tokens)), seq_pos * tokens, tokens + 2 * rim_tokens
    )
    place = jnp.arange(MAX_ATOMS, dtype=jnp.int32)
    used = place[None, :] < counts[:, None]
    blocked = jnp.where(used, 0.0, masked_score).astype(f32).reshape(-1, 1)
    blocked = jnp.broadcast_to(blocked, (blocked.shape[0], LANES))
    own_counts = counts[rim_tokens : rim_tokens + tokens]
    share = used[rim_tokens : rim_tokens + tokens].astype(f32) / own_counts[:, None].astype(f32)
    share = jnp.broadcast_to(share.reshape(-1, 1), (slots, LANES))
    windows = slots // WIN_Q
    starts = jnp.arange(windows, dtype=jnp.int32) * WIN_Q + key_offsets + RIM
    pairs_t = atom_pairs.transpose(0, 1, 3, 2).reshape(windows, WIN_Q * features, WIN_K)
    eye = jnp.eye(WIN_Q, dtype=bool)
    spread = jnp.where(
        eye[None, :, :, None], atom_pw.T[:, None, None, :], jnp.zeros((), bf16)
    ).reshape(ATOM_HEADS * WIN_Q, WIN_Q * features)
    gather = WeightGather([part.shape for part in large], samp, seq) if kernels else None
    pooled, stored, fulls = atom_forward(
        ext,
        starts,
        pairs_t,
        spread,
        blocked,
        share,
        wide,
        down,
        atom_qb,
        gather,
        large if kernels else (),
    )
    if not kernels:
        fulls = [lax.all_gather(part, "samp", axis=0, tiled=True) for part in large]
    proj_w, up_w, down_w, cond_w, out_w = fulls
    block_in = token_input.astype(f32) + pooled

    noise_feature = 0.25 * jnp.log(noise_levels / sigma_data)
    cond_rows = (
        single_features.astype(f32)[None]
        + noise_feature[:, None, None] * noise_direction[None, None, :]
    )
    cond_low = norm_stats(cond_rows)[0].astype(bf16)
    cond_all = dot_last(cond_low, cond_w) + cond_b.astype(f32)
    parts = [cond_all[..., i * width : (i + 1) * width] for i in range(6)]

    pair_w = token_pw.T
    normed_in, inv_in = norm_stats(block_in)
    attn_in = (jax.nn.sigmoid(parts[0]) * normed_in + parts[1]).astype(bf16)
    mix = dot_last(attn_in, proj_w)
    queries = (mix[..., :width] + token_qb.astype(f32)).astype(bf16)
    keyval_own = mix[..., width : 3 * width].astype(bf16)
    gating = mix[..., 3 * width :]
    if kernels:
        (probs, keyval, stats), rows_out = gather_attend(
            queries,
            keyval_own,
            pair_features,
            pair_w,
            mix,
            block_in,
            cond_all,
            cotangent,
            out_w,
            up_w,
            down_w,
        )
        (
            block_out,
            ffn_in,
            upper_grad,
            hidden,
            branch_two_low,
            gated_low,
            branch_low,
            attend_low,
            gating_grad,
            mid_grad,
            cond_tail,
        ) = rows_out
        query_grad, keyval_grad, pairw_grad, ready = attend_back_scatter(
            queries,
            keyval,
            probs,
            attend_low.reshape(queries.shape),
            pair_features,
            stats,
            ffn_in,
            upper_grad,
            hidden,
            branch_two_low,
            gated_low,
            branch_low,
        )
        token_grad, token_qb_grad, cond_b_grad, grad_units = token_close(
            query_grad,
            keyval_grad,
            gating_grad,
            mid_grad,
            block_in,
            cond_all,
            cond_tail,
            proj_w,
            attn_in,
            cond_low,
            ready,
            samp,
            seq,
        )
        block_out = block_out.reshape(token_input.shape)
        token_grad = token_grad.reshape(token_input.shape)
        token_qb_grad, cond_b_grad = token_qb_grad.reshape(-1), cond_b_grad.reshape(-1)
    else:
        bias = pair_bias(pair_features, pair_w)
        keyval = lax.all_gather(keyval_own, "seq", axis=0, tiled=False)
        attend, probs = token_attention(queries, keyval, bias)
        sig_gate = jax.nn.sigmoid(gating)
        gated_low = (attend * sig_gate).astype(bf16)
        branch = dot_last(gated_low, out_w)
        gate_one = jax.nn.sigmoid(parts[2])
        mid = block_in + gate_one * branch
        normed_mid, inv_mid = norm_stats(mid)
        scale_two = jax.nn.sigmoid(parts[3])
        ffn_in = (scale_two * normed_mid + parts[4]).astype(bf16)
        upper = dot_last(ffn_in, up_w)
        hidden_width = down_w.shape[0]
        first_half, second_half = upper[..., :hidden_width], upper[..., hidden_width:]
        sig_first = jax.nn.sigmoid(first_half)
        hidden = (first_half * sig_first * second_half).astype(bf16)
        branch_two = dot_last(hidden, down_w)
        gate_two = jax.nn.sigmoid(parts[5])
        block_out = (mid + gate_two * branch_two).astype(bf16)

        out_grad = cotangent.astype(f32)
        branch_two_low = (out_grad * gate_two).astype(bf16)
        gate_two_grad = out_grad * branch_two * gate_two * (1.0 - gate_two)
        hidden_grad = dot_back(branch_two_low, down_w)
        first_grad = hidden_grad * second_half * sig_first * (1.0 + first_half * (1.0 - sig_first))
        second_grad = hidden_grad * first_half * sig_first
        upper_grad = jnp.concatenate([first_grad, second_grad], -1).astype(bf16)
        ffn_grad = dot_back(upper_grad, up_w)
        scale_two_grad = ffn_grad * normed_mid * scale_two * (1.0 - scale_two)
        mid_grad = out_grad + norm_back(normed_mid, inv_mid, ffn_grad * scale_two)
        branch_low = (mid_grad * gate_one).astype(bf16)
        gate_one_grad = mid_grad * branch * gate_one * (1.0 - gate_one)
        gated_grad = dot_back(branch_low, out_w)
        attend_low = (gated_grad * sig_gate).astype(bf16)
        gating_grad = gated_grad * attend * sig_gate * (1.0 - sig_gate)
        query_grad, keyval_part, bias_grad = token_attention_back(queries, keyval, probs, attend_low)
        keyval_grad = lax.psum_scatter(keyval_part, "seq", scatter_dimension=0, tiled=False)
        pairw_grad = pair_grad(pair_features, bias_grad, pair_w)
        mix_grad = jnp.concatenate(
            [query_grad.astype(bf16), keyval_grad, gating_grad.astype(bf16)], -1
        )
        token_qb_grad = jnp.sum(query_grad, (0, 1))
        attn_in_grad = dot_back(mix_grad, proj_w)
        scale_one = jax.nn.sigmoid(parts[0])
        scale_one_grad = attn_in_grad * normed_in * scale_one * (1.0 - scale_one)
        token_grad = mid_grad + norm_back(normed_in, inv_in, attn_in_grad * scale_one)
        cond_grad = jnp.concatenate(
            [scale_one_grad, attn_in_grad, gate_one_grad, scale_two_grad, ffn_grad, gate_two_grad], -1
        ).astype(bf16)
        cond_b_grad = jnp.sum(cond_grad.astype(f32), (0, 1))
    pairw_grad = pairw_grad.T

    if kernels:
        atom_grad, qb_grad, pairw_stack, pairw_mean, small, units = atom_backward_sum(
            token_grad,
            starts,
            stored,
            atom_input,
            pairs_t,
            share,
            wide,
            down,
            GradSum([part.shape for part in large]),
            grad_units,
        )
    else:
        mix_part, own, left, right, atom_mid_grad, *atom_totals = atom_backward(
            token_grad, starts, stored, pairs_t, share, wide, down
        )
        from_right = lax.ppermute(left, "seq", down_pairs)
        from_left = lax.ppermute(right, "seq", up_pairs)
        atom_grad, atom_proj_grad = atom_input_backward(
            atom_input, mix_part, own, from_left, from_right, atom_mid_grad, wide
        )
        qb_grad, outw_grad, upw_grad, downw_grad, pool_grad, pairw_stack, pairw_mean = atom_totals
    diagonal = pairw_stack.reshape(ATOM_HEADS, WIN_Q, WIN_Q, features)
    atom_pw_grad = (
        jnp.sum(jnp.where(eye[None, :, :, None], diagonal, 0.0), (1, 2)).T
        - jnp.sum(pairw_mean.reshape(ATOM_HEADS, -1), 1)[None, :]
    )

    rows = atom_width // samp
    tiny_parts = [qb_grad.reshape(-1), atom_pw_grad, cond_b_grad, token_qb_grad, pairw_grad]
    tiny_flat = jnp.concatenate([part.astype(bf16).reshape(samp, -1) for part in tiny_parts], 1)
    spare = atom_width
    tiny_flat = jnp.pad(tiny_flat, ((0, 0), (0, rows * spare - tiny_flat.shape[1])))
    tiny_rows = tiny_flat.reshape(samp, rows, spare)
    if kernels:
        total, units = small_sums(small, tiny_rows, units)
        *shares, pool_out, proj_out, downw_out, upw_out, outw_out, tiny_out = unpack(
            units, total, [part.shape for part in large], rows, atom_width
        )
    else:
        lanes = lambda part: part.astype(bf16).reshape(samp, rows, -1)
        downw_two = downw_grad.astype(bf16).reshape(samp, 2, rows, atom_width)
        small = jnp.stack(
            [
                lanes(pool_grad),
                jnp.concatenate([lanes(atom_proj_grad), downw_two[:, 0], downw_two[:, 1]], -1),
                jnp.concatenate([lanes(upw_grad), lanes(outw_grad), tiny_rows], -1),
                jnp.zeros((samp, rows, width), bf16),
            ],
            1,
        )
        factors = [
            (attn_in, mix_grad),
            (ffn_in, upper_grad),
            (hidden, branch_two_low),
            (cond_low, cond_grad),
            (gated_low, branch_low),
        ]
        shares, rest = sum_shares(
            [weight_grad(*pair) for pair in factors], small.reshape(-1, width)
        )
        rest = rest.reshape(-1, width)
        pool_out, second, third = rest[:rows], rest[rows : 2 * rows], rest[2 * rows : 3 * rows]
        low = 4 * atom_width
        proj_out = second[:, :low]
        downw_out = jnp.concatenate(
            [second[:, low : low + atom_width], second[:, low + atom_width :]], 0
        )
        upw_out, outw_out = third[:, :low], third[:, low : low + atom_width]
        tiny_out = third[:, low + atom_width :]
    tiny_out = tiny_out.reshape(-1)
    tiny_shares, cut = [], 0
    for part in tiny_parts:
        size = part.size // samp
        shape = (part.shape[0] // samp,) + part.shape[1:]
        tiny_shares.append(tiny_out[cut : cut + size].reshape(shape))
        cut += size
    return (
        block_out,
        atom_grad,
        token_grad,
        proj_out,
        tiny_shares[0],
        tiny_shares[1],
        outw_out,
        upw_out,
        downw_out,
        pool_out,
        shares[3],
        tiny_shares[2],
        shares[0],
        tiny_shares[3],
        tiny_shares[4],
        shares[4],
        shares[1],
        shares[2],
    )


def solution(mesh):
    in_specs = (
        P("samp", "seq", None),
        P("samp", "seq", None),
        P(),
        P("seq"),
        P("seq", None, None, None),
        P("seq", None, None),
        P("seq", None),
        P("samp"),
        P(),
        P("samp", None),
        P("samp"),
        P("samp", None),
        P("samp", None),
        P("samp", None),
        P("samp", None),
        P("samp", None),
        P("samp", None),
        P("samp"),
        P("samp", None),
        P("samp"),
        P("samp", None),
        P("samp", None),
        P("samp", None),
        P("samp", None),
        P("samp", "seq", None),
    )
    out_specs = (
        P("samp", "seq", None),
        P("samp", "seq", None),
        P("samp", "seq", None),
        P("samp", None),
        P("samp"),
        P("samp", None),
        P("samp", None),
        P("samp", None),
        P("samp", None),
        P("samp", None),
        P("samp", None),
        P("samp"),
        P("samp", None),
        P("samp"),
        P("samp", None),
        P("samp", None),
        P("samp", None),
        P("samp", None),
    )
    return jax.shard_map(local, mesh=mesh, in_specs=in_specs, out_specs=out_specs, check_vma=False)
```

```python
import functools

import jax
import jax.numpy as jnp
from jax import lax
from jax.experimental import pallas as pl
from jax.experimental.pallas import tpu as pltpu
from jax.sharding import PartitionSpec as P

MAX_ATOMS = 8
WIN_Q = 32
WIN_K = 128
ATOM_HEADS = 4
RIM = 96
LANES = 128

norm_eps = 1e-05
sigma_data = 16.0
masked_score = -1000000000.0
bf16 = jnp.bfloat16
f32 = jnp.float32
vmem_bytes = 56 << 20


def dot_last(left_op, right_op):
    return jnp.einsum("...k,kn->...n", left_op, right_op, preferred_element_type=f32)


def dot_back(grad_op, weight):
    return jnp.einsum("...n,kn->...k", grad_op, weight, preferred_element_type=f32)


def weight_grad(left_op, grad_op):
    flat_left = left_op.reshape(-1, left_op.shape[-1])
    flat_grad = grad_op.reshape(-1, grad_op.shape[-1])
    return jnp.einsum("rk,rn->kn", flat_left, flat_grad, preferred_element_type=f32)


def mm(left_op, right_op):
    return lax.dot_general(left_op, right_op, (((1,), (0,)), ((), ())), preferred_element_type=f32)


def mm_nt(left_op, right_op):
    return lax.dot_general(left_op, right_op, (((1,), (1,)), ((), ())), preferred_element_type=f32)


def mm_tn(left_op, right_op):
    return lax.dot_general(left_op, right_op, (((0,), (0,)), ((), ())), preferred_element_type=f32)


def norm_stats(operand):
    center = operand - jnp.mean(operand, -1, keepdims=True)
    inv_std = lax.rsqrt(jnp.mean(center * center, -1, keepdims=True) + norm_eps)
    return (center * inv_std, inv_std)


def norm_back(normed, inv_std, grad_op):
    return inv_std * (
        grad_op
        - jnp.mean(grad_op, -1, keepdims=True)
        - normed * jnp.mean(grad_op * normed, -1, keepdims=True)
    )


def sigmoid(operand):
    return 1.0 / (1.0 + jnp.exp(-operand))


def whole(shape):
    return pl.BlockSpec(shape, lambda *_: (0,) * len(shape))


def per_sample(shape):
    return pl.BlockSpec((1,) + shape, lambda b, *_: (b,) + (0,) * len(shape))


def params():
    return pltpu.CompilerParams(vmem_limit_bytes=vmem_bytes)


def square_sums(ones_op, squares):
    upper = squares.astype(bf16)
    lower = (squares - upper.astype(f32)).astype(bf16)
    return upper, lower


def head_masks(count, width, heads, head_dim, first):
    row = lax.broadcasted_iota(jnp.int32, (heads * count, width), 0)
    lane = lax.broadcasted_iota(jnp.int32, (heads * count, width), 1)
    inside = (lane - first) // head_dim == row // count
    return jnp.where(inside & (lane >= first), 1.0, 0.0).astype(bf16)


def head_stack(rows, heads, head_dim, first, masks=None):
    if masks is None:
        masks = head_masks(rows.shape[0], rows.shape[1], heads, head_dim, first)
    return jnp.concatenate([rows] * heads, 0) * masks


def head_fold(stacked, heads, head_dim, first):
    count = stacked.shape[0] // heads
    lane = lax.broadcasted_iota(jnp.int32, (count, stacked.shape[1]), 1)
    total = jnp.zeros((count, stacked.shape[1]), f32)
    for head in range(heads):
        low = first + head * head_dim
        part = stacked[head * count : (head + 1) * count]
        total = jnp.where((lane >= low) & (lane < low + head_dim), part, total)
    return total


MESH = pl.DeviceIdType.MESH


def places():
    samp_pos, seq_pos = lax.axis_index("samp"), lax.axis_index("seq")
    core, across, along = seq_pos % 2, seq_pos // 2 % 2, seq_pos // 4

    def index(along, across, core):
        return (along * 2 + across) * 2 + core

    return (
        samp_pos,
        seq_pos,
        index(along, across, 1 - core),
        index(along, 1 - across, core),
        index(1 - along, across, core),
        index(1 - along, 1 - across, core),
    )


def remote(source, target, send_sem, recv_sem, device):
    return pltpu.make_async_remote_copy(
        src_ref=source,
        dst_ref=target,
        send_sem=send_sem,
        recv_sem=recv_sem,
        device_id=device,
        device_id_type=MESH,
    )


def greet(devices):
    barrier = pltpu.get_barrier_semaphore()
    for device in devices:
        pl.semaphore_signal(barrier, inc=1, device_id=device, device_id_type=MESH)
    pl.semaphore_wait(barrier, len(devices))


def pick(position, values):
    chosen = values[0]
    for index, value in enumerate(values[1:], 1):
        chosen = jnp.where(position == index, value, chosen)
    return chosen


class WeightGather:
    def __init__(self, shapes, samp, seq):
        self.shapes, self.samp, self.seq = shapes, samp, seq
        self.splits = [self.split(shape, seq) for shape in shapes]

    @staticmethod
    def split(shape, parts):
        rows, columns = shape
        for down in (1, 2, 4, 8):
            across = parts // down
            if rows % (16 * down) == 0 and columns % (LANES * across) == 0:
                return (down, across)
        return None

    @staticmethod
    def fits(shapes, samp, seq):
        return (
            samp == 4
            and seq == 8
            and len(shapes) == 5
            and all(WeightGather.split(shape, seq) for shape in shapes)
        )

    def full_shapes(self):
        return [(rows * self.samp, columns) for rows, columns in self.shapes]

    def scratch(self):
        count = len(self.shapes)
        return [
            pltpu.SemaphoreType.DMA((9, self.samp, count)),
            pltpu.SemaphoreType.DMA((8, self.samp, count)),
            pltpu.SemaphoreType.DMA((2, count)),
        ] + [pltpu.VMEM(shape, bf16) for shape in self.shapes]

    def params(self):
        return pltpu.CompilerParams(
            vmem_limit_bytes=vmem_bytes, collective_id=1, has_side_effects=True
        )

    def cell(self, ref, weight, origin, part):
        rows, columns = self.shapes[weight]
        down, across = self.splits[weight]
        height, width = rows // down, columns // across
        low = origin * rows + part // across * height
        left = part % across * width
        return ref.at[
            pl.ds(pl.multiple_of(low, 16), height), pl.ds(pl.multiple_of(left, LANES), width)
        ]

    def origin(self, position, turn):
        order = [sorted(range(self.samp), key=lambda o: (abs(o - z), o)) for z in range(self.samp)]
        if isinstance(turn, int):
            return pick(position, [order[z][turn] for z in range(self.samp)])
        return pick(
            position, [pick(turn, [order[z][t] for t in range(self.samp)]) for z in range(self.samp)]
        )

    def own_copies(self, shards, fulls, own, held, stage):
        z = places()[0]
        copies = []
        for w, shard in enumerate(shards):
            rows = self.shapes[w][0]
            target = fulls[w].at[pl.ds(pl.multiple_of(z * rows, 16), rows), :]
            ends = (shard, held[w]) if stage == 0 else (held[w], target)
            copies.append(pltpu.make_async_copy(*ends, own.at[stage, w]))
        return copies

    def start(self, shards, fulls, send, recv, own, held):
        z, me, sib, xn, yn, dg = places()
        above, below = lax.rem(z + 1, self.samp), lax.rem(z + self.samp - 1, self.samp)
        greet([(z, sib), (z, xn), (z, yn), (above, me), (below, me)])
        for w, shard in enumerate(shards):
            source = self.cell(shard, w, 0, me)
            target = self.cell(fulls[w], w, z, me)

            @pl.when(z < self.samp - 1)
            def _():
                remote(source, target, send.at[0, 0, w], recv.at[0, z, w], (z + 1, me)).start()

            @pl.when(z > 0)
            def _():
                remote(source, target, send.at[1, 0, w], recv.at[0, z, w], (z - 1, me)).start()

        for copy in self.own_copies(shards, fulls, own, held, 0):
            copy.start()

    def place_own(self, shards, fulls, own, held):
        for copy in self.own_copies(shards, fulls, own, held, 0):
            copy.wait()
        for copy in self.own_copies(shards, fulls, own, held, 1):
            copy.start()

    def share_own(self, turn, origin, sources, fulls, send, recv):
        z, me, sib, xn, yn, dg = places()
        for kind, part in ((2, xn), (3, yn), (5, sib)):
            for w, source in enumerate(sources):
                target = self.cell(fulls[w], w, origin, me)
                arrival = {2: 1, 3: 2, 5: 4}[kind]
                remote(
                    source, target, send.at[kind, turn, w], recv.at[arrival, origin, w], (z, part)
                ).start()

    def wait_cell(self, fulls, recv, kind, w, origin, part, device):
        target = self.cell(fulls[w], w, origin, part)
        remote(target, target, recv.at[kind, origin, w], recv.at[kind, origin, w], device).wait_recv()

    def issue(self, turn, fulls, send, recv):
        z, me, sib, xn, yn, dg = places()
        origin = self.origin(z, turn)
        count = len(self.shapes)
        for w in range(count):
            self.wait_cell(fulls, recv, 0, w, origin, me, (z, sib))
        for w in range(count):
            cell = self.cell(fulls[w], w, origin, me)

            @pl.when((origin < z) & (z < self.samp - 1))
            def _():
                remote(cell, cell, send.at[0, turn, w], recv.at[0, origin, w], (z + 1, me)).start()

            @pl.when((origin > z) & (z > 0))
            def _():
                remote(cell, cell, send.at[1, turn, w], recv.at[0, origin, w], (z - 1, me)).start()

        cells = [self.cell(fulls[w], w, origin, me) for w in range(count)]
        self.share_own(turn, origin, cells, fulls, send, recv)

    def passed_on(self, w):
        return w in (0, 3)

    def finish(self, turn, fulls, send, recv):
        z, me, sib, xn, yn, dg = places()
        origin = self.origin(z, turn)
        count = len(self.shapes)
        for kind, part, other, by in ((1, xn, yn, True), (2, yn, xn, False)):
            for w in range(count):
                self.wait_cell(fulls, recv, kind, w, origin, part, (z, part))
                cell = self.cell(fulls[w], w, origin, part)
                if self.passed_on(w) == by:
                    remote(
                        cell, cell, send.at[4, turn, w], recv.at[3, origin, w], (z, other)
                    ).start()
                remote(
                    cell, cell, send.at[5 + kind, turn, w], recv.at[4 + kind, origin, w], (z, sib)
                ).start()

    def diagonal(self, turn, fulls, send, recv):
        z, me, sib, xn, yn, dg = places()
        origin = self.origin(z, turn)
        for w in range(len(self.shapes)):
            self.wait_cell(fulls, recv, 3, w, origin, dg, (z, yn))
            cell = self.cell(fulls[w], w, origin, dg)
            remote(cell, cell, send.at[8, turn, w], recv.at[7, origin, w], (z, sib)).start()

    def drain(self, shards, fulls, send, recv, own, held):
        z, me, sib, xn, yn, dg = places()
        count = len(self.shapes)

        def sent(kind, turn, w):
            cell = self.cell(fulls[w], w, 0, me)
            remote(cell, cell, send.at[kind, turn, w], recv.at[0, 0, w], (z, sib)).wait_send()

        def one(turn, carry):
            origin = self.origin(z, turn)
            for w in range(count):
                for kind in range(2, 9):
                    sent(kind, turn, w)

                @pl.when((z < self.samp - 1) & (origin < z))
                def _():
                    sent(0, turn, w)

                @pl.when((z > 0) & (origin > z))
                def _():
                    sent(1, turn, w)

                for kind in range(4, 8):
                    self.wait_cell(fulls, recv, kind, w, origin, sib, (z, sib))
            return carry

        lax.fori_loop(1, self.samp, one, 0)
        for w in range(count):

            @pl.when(z < self.samp - 1)
            def _():
                sent(0, 0, w)

            @pl.when(z > 0)
            def _():
                sent(1, 0, w)

        for copy in self.own_copies(shards, fulls, own, held, 1):
            copy.wait()

    def step(self, sample, shards, fulls, send, recv, own, *held):
        @pl.when(sample == 0)
        def _():
            self.start(shards, fulls, send, recv, own, held)

        @pl.when(sample == 1)
        def _():
            self.place_own(shards, fulls, own, held)

        for at, turn in ((2, 1), (3, 2), (5, 3)):

            @pl.when(sample == at)
            def _():
                self.issue(turn, fulls, send, recv)

        for at, turn in ((4, 1), (5, 2), (7, 3)):

            @pl.when(sample == at)
            def _():
                self.finish(turn, fulls, send, recv)

        for at, turn in ((5, 1), (7, 2)):

            @pl.when(sample == at)
            def _():
                self.diagonal(turn, fulls, send, recv)

    def last(self, sample, shards, fulls, send, recv, own, *held):
        @pl.when(sample == pl.num_programs(0) - 1)
        def _():
            self.diagonal(3, fulls, send, recv)
            self.drain(shards, fulls, send, recv, own, held)


def edge_kernel(
    samp,
    seq,
    proj_ref,
    upw_ref,
    pool_ref,
    outw_ref,
    down_ref,
    tiny_ref,
    rows_ref,
    wide_out,
    down_out,
    tiny_out,
    ext_out,
    held,
    send,
    recv,
):
    z, me = lax.axis_index("samp"), lax.axis_index("seq")
    sib = places()[2]
    core = me % 2
    samples, slots, width = rows_ref.shape
    right, left = lax.rem(me + 1, seq), lax.rem(me + seq - 1, seq)
    others = [lax.rem(z + hop, samp) for hop in range(1, samp)]
    greet([(other, me) for other in others] + [(z, sib), (z, right), (z, left)])
    low = 0
    for ref in (proj_ref, upw_ref, pool_ref, outw_ref):
        held[:, low : low + ref.shape[1]] = ref[...]
        low += ref.shape[1]

    def half(out, origin, part):
        rows = out.shape[0] // samp
        first = origin * rows + part * (rows // 2)
        return out.at[pl.ds(pl.multiple_of(first, 16), rows // 2), :]

    def own_half(ref):
        rows = ref.shape[0]
        return ref.at[pl.ds(pl.multiple_of(core * (rows // 2), 16), rows // 2), :]

    def tiny_place(origin):
        rows = tiny_ref.shape[0]
        return tiny_out.at[pl.ds(pl.multiple_of(origin * rows, 16), rows), :]

    copies = []
    for hop, other in enumerate(others):
        device = (other, me)
        copies.append(
            [
                remote(own_half(held), half(wide_out, z, core), send.at[0, hop], recv.at[0, hop], device),
                remote(own_half(down_ref), half(down_out, z, core), send.at[1, hop], recv.at[1, hop], device),
                remote(tiny_ref, tiny_place(z), send.at[2, hop], recv.at[2, hop], device),
            ]
        )
    for group in copies:
        for copy in group:
            copy.start()
    before, after = ext_out.at[:, :RIM, :], ext_out.at[:, RIM + slots :, :]
    to_right = remote(rows_ref.at[:, slots - RIM :, :], before, send.at[5, 0], recv.at[5, 0], (z, right))
    to_left = remote(rows_ref.at[:, :RIM, :], after, send.at[5, 1], recv.at[5, 1], (z, left))
    first, last = me == 0, me == seq - 1

    @pl.when(~last)
    def _():
        to_right.start()

    @pl.when(~first)
    def _():
        to_left.start()

    @pl.when(first)
    def _():
        ext_out[:, :RIM, :] = jnp.zeros((samples, RIM, width), bf16)

    @pl.when(last)
    def _():
        ext_out[:, RIM + slots :, :] = jnp.zeros((samples, RIM, width), bf16)

    def move(sample, carry):
        ext_out[sample, RIM : RIM + slots, :] = rows_ref[sample]
        return carry

    lax.fori_loop(0, samples, move, 0)
    for ref, out in ((held, wide_out), (down_ref, down_out), (tiny_ref, tiny_out)):
        rows = ref.shape[0]
        out[pl.ds(pl.multiple_of(z * rows, 16), rows), :] = ref[...]
    passed = []
    for hop in range(samp - 1):
        origin = lax.rem(z + samp - 1 - hop, samp)
        for kind, out in ((0, wide_out), (1, down_out)):
            copies[hop][kind].wait_recv()
            cell = half(out, origin, core)
            copy = remote(cell, cell, send.at[3 + kind, hop], recv.at[3 + kind, hop], (z, sib))
            copy.start()
            passed.append(copy)
    for hop in range(samp - 1):
        copies[hop][2].wait_recv()
        for copy in copies[hop]:
            copy.wait_send()
    for copy in passed:
        copy.wait()

    @pl.when(~last)
    def _():
        to_right.wait_send()
        to_left.wait_recv()

    @pl.when(~first)
    def _():
        to_left.wait_send()
        to_right.wait_recv()


def edges(weights, tiny_own, rows):
    samp, seq = lax.axis_size("samp"), lax.axis_size("seq")
    samples, slots, width = rows.shape
    place = pl.BlockSpec(memory_space=pltpu.VMEM)
    lanes = sum(part.shape[1] for part in weights[:4])
    return pl.pallas_call(
        functools.partial(edge_kernel, samp, seq),
        out_shape=[
            jax.ShapeDtypeStruct((samp * weights[0].shape[0], lanes), bf16),
            jax.ShapeDtypeStruct((samp * weights[4].shape[0], weights[4].shape[1]), bf16),
            jax.ShapeDtypeStruct((samp * tiny_own.shape[0], tiny_own.shape[1]), bf16),
            jax.ShapeDtypeStruct((samples, slots + 2 * RIM, width), bf16),
        ],
        in_specs=[place] * 7,
        out_specs=[place] * 4,
        scratch_shapes=[
            pltpu.VMEM((weights[0].shape[0], lanes), bf16),
            pltpu.SemaphoreType.DMA((6, samp)),
            pltpu.SemaphoreType.DMA((6, samp)),
        ],
        compiler_params=pltpu.CompilerParams(
            vmem_limit_bytes=vmem_bytes, collective_id=0, has_side_effects=True
        ),
        name="edges",
    )(*weights, tiny_own, rows)


UNIT = 336


def add_into(target, source, lanes=slice(None), rows=48):
    def one(step, carry):
        part = pl.ds(pl.multiple_of(step * rows, 16), rows)
        target[part, lanes] = target[part, lanes] + source[part, :]
        return carry

    lax.fori_loop(0, target.shape[0] // rows, one, 0)


class GradSum:
    head, tail, full = slice(0, 384), slice(384, 768), slice(0, 768)

    def __init__(self, shapes):
        self.shapes = list(shapes)

    def scratch(self):
        half = (UNIT, 384)
        dma = pltpu.SemaphoreType.DMA
        return [
            pltpu.VMEM((4, 4, UNIT, 768), bf16),
            pltpu.VMEM((4, 4, UNIT, 768), bf16),
            pltpu.VMEM((4, 2) + half, bf16),
            pltpu.VMEM((4, 2) + half, bf16),
            pltpu.VMEM((4,) + half, bf16),
            pltpu.VMEM((4,) + half, bf16),
            pltpu.VMEM((3, UNIT, 768), bf16),
            pltpu.VMEM((UNIT, 768), bf16),
            dma((4, 4)),
            dma((4, 4)),
            dma((4, 4)),
            dma((4, 4)),
            dma((4, 4)),
            dma((4, 2)),
            dma((4, 2)),
            dma((3,)),
            dma((3,)),
            dma((3,)),
            dma((3,)),
            dma,
        ]

    def params(self):
        return pltpu.CompilerParams(
            vmem_limit_bytes=vmem_bytes, collective_id=2, has_side_effects=True
        )

    def bind(
        self, grads, shares, mine, theirs, from_x, from_y, last_x, last_y, planes, own_share, *sems
    ):
        self.grads, self.shares, self.own_share = grads, shares, own_share
        self.mine, self.theirs, self.from_x, self.from_y = mine, theirs, from_x, from_y
        self.last_x, self.last_y, self.planes = last_x, last_y, planes
        (
            self.s_sib,
            self.r_sib,
            self.s_own,
            self.s_one,
            self.r_one,
            self.s_two,
            self.r_two,
            self.s_z,
            self.r_z,
            self.s_share,
            self.r_share,
            self.s_out,
        ) = sems
        self.z, self.me, self.sib, self.xn, self.yn, self.dg = places()
        self.core, self.chip = self.me % 2, self.me // 2
        self.chip_x, self.chip_y, self.chip_d = self.xn // 2, self.yn // 2, self.dg // 2
        order = [[p ^ hop for hop in (2, 3, 1, 0)] for p in range(4)]
        self.plane = [pick(self.z, [order[p][r] for p in range(4)]) for r in range(4)]

    def there(self, r, j):
        return remote(
            self.grads.at[2 * j + 1 - self.core, self.plane[r]],
            self.theirs.at[r, j],
            self.s_sib.at[r, j],
            self.r_sib.at[r, j],
            (self.z, self.sib),
        )

    def here(self, r, j):
        return pltpu.make_async_copy(
            self.grads.at[2 * j + self.core, self.plane[r]], self.mine.at[r, j], self.s_own.at[r, j]
        )

    def one(self, r, k):
        chip = (self.chip_x, self.chip_d, self.chip_y, self.chip_d)[k]
        lanes = self.head if k < 2 else self.tail
        target = (self.from_x if k < 2 else self.from_y).at[r, k % 2]
        device = (self.z, self.xn if k < 2 else self.yn)
        return remote(
            self.mine.at[r, chip, :, lanes], target, self.s_one.at[r, k], self.r_one.at[r, k], device
        )

    def two(self, r, k):
        chip, lanes, target, device = (
            (self.chip_y, self.head, self.last_y, self.yn),
            (self.chip_x, self.tail, self.last_x, self.xn),
        )[k]
        return remote(
            self.mine.at[r, chip, :, lanes],
            target.at[r],
            self.s_two.at[r, k],
            self.r_two.at[r, k],
            (self.z, device),
        )

    def across(self, r):
        return remote(
            self.mine.at[r, self.chip],
            self.planes.at[r],
            self.s_z.at[r],
            self.r_z.at[r],
            (self.plane[r], self.me),
        )

    def keep(self):
        return pltpu.make_async_copy(self.own_share, self.shares.at[self.me], self.s_out)

    def share(self, kind):
        device = (self.xn, self.yn, self.sib)[kind]
        return remote(
            self.own_share,
            self.shares.at[self.me],
            self.s_share.at[kind],
            self.r_share.at[kind],
            (self.z, device),
        )

    def shared(self, kind):
        part = self.shares.at[(self.xn, self.yn, self.sib)[kind]]
        return remote(part, part, self.s_share.at[kind], self.r_share.at[kind], (self.z, self.sib))

    def begin(self, r):
        for j in range(4):
            self.there(r, j).start()
            self.here(r, j).start()

    def pairs(self, r):
        for j in range(4):
            self.there(r, j).wait_recv()
            self.here(r, j).wait()
        for j in range(4):
            add_into(self.mine.at[r, j], self.theirs.at[r, j])
        for k in range(4):
            self.one(r, k).start()

    def middle(self, r):
        self.one(r, 1).wait_recv()
        add_into(self.mine.at[r, self.chip_y], self.from_x.at[r, 1], self.head)
        self.two(r, 0).start()
        self.one(r, 3).wait_recv()
        add_into(self.mine.at[r, self.chip_x], self.from_y.at[r, 1], self.tail)
        self.two(r, 1).start()
        self.one(r, 0).wait_recv()
        add_into(self.mine.at[r, self.chip], self.from_x.at[r, 0], self.head)
        self.one(r, 2).wait_recv()
        add_into(self.mine.at[r, self.chip], self.from_y.at[r, 0], self.tail)

    def finish(self, r):
        self.two(r, 0).wait_recv()
        add_into(self.mine.at[r, self.chip], self.last_y.at[r], self.head)
        self.two(r, 1).wait_recv()
        add_into(self.mine.at[r, self.chip], self.last_x.at[r], self.tail)
        if r < 3:
            self.across(r).start()

    def total(self):
        for r in range(3):
            self.across(r).wait_recv()

        def one(step, carry):
            rows = pl.ds(pl.multiple_of(step * 48, 16), 48)
            both = self.mine[3, self.chip, rows, :].astype(f32)
            for r in range(3):
                both += self.planes[r, rows, :].astype(f32)
            self.own_share[rows, :] = both.astype(bf16)
            return carry

        lax.fori_loop(0, UNIT // 48, one, 0)
        for kind in range(3):
            self.share(kind).start()
        self.keep().start()

    def collect(self):
        self.keep().wait()
        for kind in range(3):
            self.shared(kind).wait_recv()
        for kind in range(3):
            self.share(kind).wait_send()
        for r in range(4):
            for j in range(4):
                self.there(r, j).wait_send()
                self.one(r, j).wait_send()
            for k in range(2):
                self.two(r, k).wait_send()
            if r < 3:
                self.across(r).wait_send()

    def hello(self):
        greet(
            [(self.z, self.sib), (self.z, self.xn), (self.z, self.yn)]
            + [(self.plane[r], self.me) for r in range(3)]
            + [(self.z, lax.rem(self.me + 1, 8)), (self.z, lax.rem(self.me + 7, 8))]
        )
        self.begin(0)
        self.begin(1)

    def slot(self, index):
        plan = {
            0: [self.hello],
            1: [lambda: self.pairs(0), lambda: self.begin(2)],
            3: [lambda: self.pairs(1), lambda: self.begin(3)],
            4: [lambda: self.middle(0)],
            6: [lambda: self.pairs(2), lambda: self.finish(0)],
            7: [lambda: self.middle(1)],
            9: [lambda: self.pairs(3), lambda: self.finish(1)],
            10: [lambda: self.middle(2)],
            12: [lambda: self.finish(2)],
            13: [lambda: self.middle(3)],
            14: [lambda: self.finish(3)],
            16: [self.total],
        }
        for at, actions in plan.items():

            @pl.when(index == at)
            def _():
                for action in actions:
                    action()


def small_sum_kernel(
    main,
    tiny,
    own,
    out_ref,
    shares,
    grads,
    cores,
    chips,
    planes,
    share,
    total,
    s_one,
    r_one,
    s_two,
    r_two,
    s_z,
    r_z,
    s_all,
    r_all,
    s_share,
    r_share,
    s_own,
):
    z, me, sib, xn, yn, dg = places()
    core, chip = me % 2, me // 2
    near = (xn, yn, dg)
    parts, samp, rows = grads.shape[:3]
    for part in range(parts):
        for p in range(samp):
            grads[part, p] = main[p, part * rows : (part + 1) * rows, :]
    low, width = 2 * tiny.shape[1], tiny.shape[2]
    for part in range(tiny.shape[1] // rows):
        for p in range(samp):
            grads[low // rows + part, p, :, -width:] = tiny[p, part * rows : (part + 1) * rows, :]
    others = [lax.rem(z + hop, 4) for hop in (1, 2, 3)]
    greet(
        [(z, sib)]
        + [(z, part) for part in near]
        + [(z, part + 1 - 2 * core) for part in near]
        + [(other, me) for other in others]
    )

    def one(j):
        return remote(
            grads.at[2 * j + 1 - core], cores.at[j], s_one.at[j], r_one.at[j], (z, sib)
        )

    width = own.shape[2]
    head, tail, full = slice(0, width // 2), slice(width // 2, width), slice(0, width)

    def give(part, lanes, kind, device):
        target = shares.at[part, :, lanes]
        source = target if kind == 4 else own.at[part, :, lanes]
        return remote(source, target, s_share.at[kind], r_share.at[kind], (z, device))

    kept = [
        pltpu.make_async_copy(own.at[part], shares.at[part], s_own.at[k])
        for k, part in enumerate((me, xn, yn, sib))
    ]
    gifts = [
        give(xn, head, 0, yn),
        give(yn, tail, 1, xn),
        give(xn, full, 2, sib),
        give(yn, full, 3, sib),
    ]
    for copy in kept:
        copy.start()
    for j in range(4):
        one(j).start()
    for j in range(4):
        one(j).wait()
        both = cores[j].astype(f32) + grads[2 * j + core].astype(f32)
        cores[j] = both.astype(bf16)

    def two(k):
        return remote(cores.at[near[k] // 2], chips.at[k], s_two.at[k], r_two.at[k], (z, near[k]))

    for k in range(3):
        two(k).start()
    for gift in gifts:
        gift.start()
    both = cores[chip].astype(f32)
    for k in range(3):
        two(k).wait()
        both += chips[k].astype(f32)
    share[...] = both.astype(bf16)

    def three(k):
        return remote(share.at[others[k]], planes.at[k], s_z.at[k], r_z.at[k], (others[k], me))

    for k in range(3):
        three(k).start()
    give(dg, head, 0, yn).wait_recv()
    give(dg, tail, 1, xn).wait_recv()
    gifts.append(give(dg, full, 4, sib))
    gifts[-1].start()
    both = share[z].astype(f32)
    for k in range(3):
        three(k).wait()
        both += planes[k].astype(f32)
    total[me] = both.astype(bf16)

    receivers = [sib] + list(near) + [part + 1 - 2 * core for part in near]

    def four(k, part, device):
        return remote(total.at[part], total.at[part], s_all.at[k], r_all.at[k], (z, device))

    for k, device in enumerate(receivers):
        four(k, me, device).start()
    for k, device in enumerate(receivers):
        four(k, device, device).wait_recv()
    for k, device in enumerate(receivers):
        four(k, me, device).wait_send()
    for part in range(parts):
        out_ref[part * rows : (part + 1) * rows, :] = total[part]
    for kind in (2, 3, 4):
        give(sib, full, kind, sib).wait_recv()
    for copy in kept:
        copy.wait()
    for gift in gifts:
        gift.wait_send()


def small_sums(main, tiny, own):
    seq = lax.axis_size("seq")
    samp, rows, width = main.shape
    rows //= seq
    dma = pltpu.SemaphoreType.DMA
    return pl.pallas_call(
        small_sum_kernel,
        out_shape=[
            jax.ShapeDtypeStruct((seq * rows, width), bf16),
            jax.ShapeDtypeStruct(own.shape, bf16),
        ],
        in_specs=[pl.BlockSpec(memory_space=pltpu.VMEM)] * 3,
        out_specs=[
            pl.BlockSpec(memory_space=pltpu.VMEM),
            pl.BlockSpec(memory_space=pl.ANY),
        ],
        scratch_shapes=[
            pltpu.VMEM((seq, samp, rows, width), bf16),
            pltpu.VMEM((4, samp, rows, width), bf16),
            pltpu.VMEM((3, samp, rows, width), bf16),
            pltpu.VMEM((3, rows, width), bf16),
            pltpu.VMEM((samp, rows, width), bf16),
            pltpu.VMEM((seq, rows, width), bf16),
            dma((4,)),
            dma((4,)),
            dma((3,)),
            dma((3,)),
            dma((3,)),
            dma((3,)),
            dma((7,)),
            dma((7,)),
            dma((5,)),
            dma((5,)),
            dma((4,)),
        ],
        compiler_params=pltpu.CompilerParams(
            vmem_limit_bytes=vmem_bytes, collective_id=3, has_side_effects=True
        ),
        name="small_sums",
    )(main, tiny, own)


def pair_stats(pairs, fold):
    upper, lower = square_sums(fold, pairs.astype(f32) * pairs.astype(f32))
    features = pairs.shape[0] // WIN_Q
    mean = mm(fold, pairs) * (1.0 / features)
    square = (mm(fold, upper) + mm(fold, lower)) * (1.0 / features)
    var = jnp.maximum(square - mean * mean, 0.0)
    inv_std = lax.rsqrt(var + norm_eps)
    return mean, inv_std


def pair_fold(features):
    shape = (WIN_Q, WIN_Q * features)
    row = lax.broadcasted_iota(jnp.int32, shape, 0)
    column = lax.broadcasted_iota(jnp.int32, shape, 1)
    return jnp.where(column // features == row, 1.0, 0.0).astype(bf16)


def atom_fwd_kernel(
    gather,
    starts,
    ext_ref,
    pairs_ref,
    spread_ref,
    blocked_ref,
    share_ref,
    wide_ref,
    down_ref,
    qbias_ref,
    *refs,
):
    count = len(gather.shapes) if gather is not None else 0
    shards, refs = refs[:count], refs[count:]
    (
        pooled_ref,
        query_ref,
        keyval_ref,
        gate_ref,
        probs_ref,
        attend_ref,
        mid_ref,
    ), refs = refs[:7], refs[7:]
    fulls, refs = refs[:count], refs[count:]
    bias_s, sems = refs[0], refs[1:]
    width = ext_ref.shape[-1]
    head_dim = width // ATOM_HEADS
    scale = float(head_dim) ** (-0.5)
    slots = query_ref.shape[1]
    windows = slots // WIN_Q
    hidden_width = down_ref.shape[0]
    model_width = pooled_ref.shape[-1]
    features = pairs_ref.shape[1] // WIN_Q
    sample = pl.program_id(0)
    if gather is not None:
        gather.step(sample, shards, fulls, *sems)

    @pl.when(sample == 0)
    def _():
        fold = pair_fold(features)
        spread = spread_ref[...]
        spread_sum = jnp.sum(spread.astype(f32), -1, keepdims=True)
        first_lane = jnp.where(
            lax.broadcasted_iota(jnp.int32, (ATOM_HEADS * WIN_Q, LANES), 1) == 0, 1.0, 0.0
        ).astype(bf16)

        fill = jnp.full((ATOM_HEADS * WIN_Q, WIN_K), masked_score, f32)

        def one(duo, carry):
            base = pl.multiple_of(duo * 2 * WIN_Q, 2 * WIN_Q)
            blocked = mm_nt(first_lane, blocked_ref[pl.ds(base, 2 * WIN_K), :].astype(bf16))
            for part in range(2):
                win = duo * 2 + part
                pairs = pairs_ref[win]
                mean, inv_std = pair_stats(pairs, fold)
                mean = jnp.concatenate([mean] * ATOM_HEADS, 0)
                inv_std = jnp.concatenate([inv_std] * ATOM_HEADS, 0)
                bias = inv_std * (mm(spread, pairs) - mean * spread_sum)
                bias = pltpu.roll(jnp.concatenate([bias, fill], 1), starts[win] - base, 1) + blocked
                for head in range(ATOM_HEADS):
                    low = (head * 2 + part) * WIN_Q
                    bias_s[duo, low : low + WIN_Q, :] = bias[head * WIN_Q : (head + 1) * WIN_Q]
            return carry

        lax.fori_loop(0, windows // 2, one, 0)

    rows = ext_ref[0].astype(f32)
    normed_low = norm_stats(rows)[0].astype(bf16)
    key_val = mm(normed_low, wide_ref[:, width : 3 * width]).astype(bf16)
    keyval_ref[0] = key_val
    own_low = normed_low[RIM : RIM + slots]
    query_ref[0] = (mm(own_low, wide_ref[:, :width]) + qbias_ref[...]).astype(bf16)
    gate_ref[0] = mm(own_low, wide_ref[:, 3 * width : 4 * width])

    masks = head_masks(2 * WIN_Q, width, ATOM_HEADS, head_dim, 0)

    def two_windows(duo):
        first = pl.multiple_of(duo * 2 * WIN_Q, 2 * WIN_Q)
        span = pl.ds(first, 2 * WIN_K)
        own = pl.ds(first, 2 * WIN_Q)
        stacked = head_stack(query_ref[0, own, :], ATOM_HEADS, head_dim, 0, masks)
        scores = mm_nt(stacked, keyval_ref[0, span, :width]) * scale + bias_s[duo]
        exp_scores = jnp.exp(scores - jnp.max(scores, -1, keepdims=True))
        probs = exp_scores * (1.0 / jnp.sum(exp_scores, -1, keepdims=True))
        probs_low = probs.astype(bf16)
        probs_ref[0, duo] = probs_low
        attend_ref[0, own, :] = head_fold(
            mm(probs_low, keyval_ref[0, span, width:]), ATOM_HEADS, head_dim, 0
        )

    def some_windows(step, carry):
        for part in range(2):
            two_windows(step * 2 + part)
        return carry

    lax.fori_loop(0, windows // 4, some_windows, 0)

    gated_low = (attend_ref[0] * sigmoid(gate_ref[0])).astype(bf16)
    offset = 4 * width
    upw = wide_ref[:, offset : offset + 2 * hidden_width]
    offset += 2 * hidden_width
    pool_weight = wide_ref[:, offset : offset + model_width]
    outw = wide_ref[:, offset + model_width : offset + model_width + width]
    mid = rows[RIM : RIM + slots] + mm(gated_low, outw)
    mid_ref[0] = mid
    ffn_low = norm_stats(mid)[0].astype(bf16)
    upper = mm(ffn_low, upw)
    first_half, second_half = upper[:, :hidden_width], upper[:, hidden_width:]
    hidden = (first_half * sigmoid(first_half) * second_half).astype(bf16)
    final_low = (mid + mm(hidden, down_ref[...])).astype(bf16)
    pool_pre = mm(final_low, pool_weight)
    share = share_ref[...]
    for lane in range(0, model_width, LANES):
        part = pool_pre[:, lane : lane + LANES]
        part = part * sigmoid(part) * share
        pooled_ref[0, :, lane : lane + LANES] = jnp.sum(
            part.reshape(slots // MAX_ATOMS, MAX_ATOMS, LANES), 1
        )
    if gather is not None:
        gather.last(sample, shards, fulls, *sems)


def atom_forward(ext, starts, pairs, spread, blocked, share, wide, down, qbias, gather, shards):
    samples, ext_slots, width = ext.shape
    slots = ext_slots - 2 * RIM
    tokens = slots // MAX_ATOMS
    windows = slots // WIN_Q
    model_width = wide.shape[1] - 5 * width - 2 * down.shape[0]
    stack = ATOM_HEADS * WIN_Q
    outs = (
        ((tokens, model_width), f32),
        ((slots, width), bf16),
        ((ext_slots, 2 * width), bf16),
        ((slots, width), f32),
        ((windows // 2, 2 * stack, 2 * WIN_K), bf16),
        ((slots, width), f32),
        ((slots, width), f32),
    )
    place = pl.BlockSpec(memory_space=pl.ANY)
    results = pl.pallas_call(
        functools.partial(atom_fwd_kernel, gather),
        out_shape=[jax.ShapeDtypeStruct((samples,) + shape, kind) for shape, kind in outs]
        + [jax.ShapeDtypeStruct(shape, bf16) for shape in (gather.full_shapes() if gather else [])],
        grid=(samples,),
        in_specs=[
            pl.BlockSpec(memory_space=pltpu.SMEM),
            per_sample((ext_slots, width)),
            whole(pairs.shape),
            whole(spread.shape),
            whole(blocked.shape),
            whole(share.shape),
            whole(wide.shape),
            whole(down.shape),
            whole(qbias.shape),
        ]
        + [place] * len(shards),
        out_specs=[per_sample(shape) for shape, _ in outs] + [place] * len(shards),
        scratch_shapes=[pltpu.VMEM((windows // 2, 2 * stack, 2 * WIN_K), f32)]
        + (gather.scratch() if gather else []),
        compiler_params=gather.params() if gather else params(),
        name="atom_forward",
    )(starts, ext, pairs, spread, blocked, share, wide, down, qbias, *shards)
    return results[0], results[1:7], results[7:]


def atom_bwd_dense(sample_refs, consts, accs, attlow_s, gate_grad_at, mid_grad_at):
    grad_ref, query_ref, gate_ref, attend_ref, mid_ref = sample_refs
    share_ref, wide_ref, down_ref = consts
    outw_ref, upw_ref, downw_ref, pool_ref = accs
    width = query_ref.shape[-1]
    slots = query_ref.shape[1]
    hidden_width = down_ref.shape[0]
    model_width = grad_ref.shape[-1]
    tokens = grad_ref.shape[1]
    offset = 4 * width
    upw = wide_ref[:, offset : offset + 2 * hidden_width]
    offset += 2 * hidden_width
    pool_weight = wide_ref[:, offset : offset + model_width]
    outw = wide_ref[:, offset + model_width : offset + model_width + width]
    down = down_ref[...]

    mid = mid_ref[0]
    normed_mid, inv_mid = norm_stats(mid)
    ffn_low = normed_mid.astype(bf16)
    upper = mm(ffn_low, upw)
    first_half, second_half = upper[:, :hidden_width], upper[:, hidden_width:]
    sig_first = sigmoid(first_half)
    hidden = (first_half * sig_first * second_half).astype(bf16)
    final_low = (mid + mm(hidden, down)).astype(bf16)
    pool_pre = mm(final_low, pool_weight)
    share = share_ref[...]
    pool_parts = []
    for lane in range(0, model_width, LANES):
        part = pool_pre[:, lane : lane + LANES]
        grad = jnp.broadcast_to(
            grad_ref[0, :, lane : lane + LANES][:, None, :], (tokens, MAX_ATOMS, LANES)
        ).reshape(slots, LANES)
        sig_pool = sigmoid(part)
        pool_parts.append((grad * share * sig_pool * (1.0 + part * (1.0 - sig_pool))).astype(bf16))
    pool_grad = jnp.concatenate(pool_parts, 1)
    final_grad = mm_nt(pool_grad, pool_weight)
    pool_ref[...] += mm_tn(final_low, pool_grad)
    branch_low = final_grad.astype(bf16)
    hidden_grad = mm_nt(branch_low, down)
    first_grad = hidden_grad * second_half * sig_first * (1.0 + first_half * (1.0 - sig_first))
    second_grad = hidden_grad * first_half * sig_first
    upper_grad = jnp.concatenate([first_grad.astype(bf16), second_grad.astype(bf16)], 1)
    downw_ref[...] += mm_tn(hidden, branch_low)
    upw_ref[...] += mm_tn(ffn_low, upper_grad)
    mid_grad = final_grad + norm_back(normed_mid, inv_mid, mm_nt(upper_grad, upw))
    mid_grad_at[...] = mid_grad
    out_low = mid_grad.astype(bf16)
    gated_grad = mm_nt(out_low, outw)
    sig_gate = sigmoid(gate_ref[0])
    attend = attend_ref[0]
    gated_low = (attend * sig_gate).astype(bf16)
    outw_ref[...] += mm_tn(gated_low, out_low)
    attlow_s[...] = (gated_grad * sig_gate).astype(bf16)
    gate_grad_at[...] = (gated_grad * attend * sig_gate * (1.0 - sig_gate)).astype(bf16)


def atom_bwd_windows(sample_refs, scratch):
    query_ref, keyval_ref, probs_ref = sample_refs
    acck_s, accv_s, bias_s, attlow_s, dq_s = scratch
    width = query_ref.shape[-1]
    head_dim = width // ATOM_HEADS
    scale = float(head_dim) ** (-0.5)
    windows = query_ref.shape[1] // WIN_Q
    acck_s[...] = jnp.zeros_like(acck_s)
    accv_s[...] = jnp.zeros_like(accv_s)
    masks = head_masks(2 * WIN_Q, width, ATOM_HEADS, head_dim, 0)

    def two_windows(duo):
        first = pl.multiple_of(duo * 2 * WIN_Q, 2 * WIN_Q)
        span = pl.ds(first, 2 * WIN_K)
        own = pl.ds(first, 2 * WIN_Q)
        queries = head_stack(query_ref[0, own, :], ATOM_HEADS, head_dim, 0, masks)
        att = head_stack(attlow_s[own, :], ATOM_HEADS, head_dim, 0, masks)
        probs_low = probs_ref[0, duo]
        probs = probs_low.astype(f32)
        prob_grad = mm_nt(att, keyval_ref[0, span, width:])
        delta = jnp.sum(prob_grad * probs, -1, keepdims=True)
        score_low = (probs * (prob_grad - delta)).astype(bf16)
        bias_s[duo] += score_low.astype(f32)
        dq_s[own, :] = (
            head_fold(mm(score_low, keyval_ref[0, span, :width]), ATOM_HEADS, head_dim, 0) * scale
        )
        acck_s[span, :] += mm_tn(score_low, queries) * scale
        accv_s[span, :] += mm_tn(probs_low, att)

    def some_windows(step, carry):
        for part in range(2):
            two_windows(step * 2 + part)
        return carry

    lax.fori_loop(0, windows // 4, some_windows, 0)


def atom_bwd_pairs(starts, pairs_ref, bias_s, pairw_ref, pairm_ref):
    fold = pair_fold(pairs_ref.shape[1] // WIN_Q)

    def one(duo, carry):
        for part in range(2):
            win = duo * 2 + part
            pairs = pairs_ref[win]
            mean, inv_std = pair_stats(pairs, fold)
            lows = [(head * 2 + part) * WIN_Q for head in range(ATOM_HEADS)]
            placed = jnp.concatenate([bias_s[duo, low : low + WIN_Q, :] for low in lows], 0)
            shift = starts[win] - duo * 2 * WIN_Q
            grad = pltpu.roll(placed, lax.rem(2 * WIN_K - shift, 2 * WIN_K), 1)[:, :WIN_K]
            scaled = grad * jnp.concatenate([inv_std] * ATOM_HEADS, 0)
            pairm_ref[...] += scaled * jnp.concatenate([mean] * ATOM_HEADS, 0)
            upper = scaled.astype(bf16)
            lower = (scaled - upper.astype(f32)).astype(bf16)
            pairw_ref[...] += mm_nt(upper, pairs) + mm_nt(lower, pairs)
        return carry

    lax.fori_loop(0, pairs_ref.shape[0] // 2, one, 0)


def atom_bwd_kernel(
    starts,
    grad_ref,
    query_ref,
    keyval_ref,
    gate_ref,
    probs_ref,
    attend_ref,
    mid_ref,
    pairs_ref,
    share_ref,
    wide_ref,
    down_ref,
    mix_ref,
    own_ref,
    left_ref,
    right_ref,
    midgrad_ref,
    qbias_ref,
    outw_ref,
    upw_ref,
    downw_ref,
    pool_ref,
    pairw_ref,
    pairm_ref,
    *scratch,
):
    acck_s, accv_s, bias_s, attlow_s, dq_s = scratch
    width = query_ref.shape[-1]
    slots = query_ref.shape[1]
    sample = pl.program_id(0)

    @pl.when(sample == 0)
    def _():
        for ref in (qbias_ref, outw_ref, upw_ref, downw_ref, pool_ref, pairw_ref, pairm_ref, bias_s):
            ref[...] = jnp.zeros_like(ref)

    atom_bwd_dense(
        (grad_ref, query_ref, gate_ref, attend_ref, mid_ref),
        (share_ref, wide_ref, down_ref),
        (outw_ref, upw_ref, downw_ref, pool_ref),
        attlow_s,
        mix_ref.at[0, :, width:],
        midgrad_ref.at[0],
    )
    atom_bwd_windows((query_ref, keyval_ref, probs_ref), scratch)
    query_grad = dq_s[...]
    qbias_ref[...] += jnp.sum(query_grad, 0, keepdims=True)
    mix_ref[0, :, :width] = query_grad.astype(bf16)
    for ref, low, high in (
        (own_ref, RIM, RIM + slots),
        (left_ref, 0, RIM),
        (right_ref, RIM + slots, slots + 2 * RIM),
    ):
        ref[0, :, :width] = acck_s[low:high, :].astype(ref.dtype)
        ref[0, :, width:] = accv_s[low:high, :].astype(ref.dtype)

    @pl.when(sample == pl.num_programs(0) - 1)
    def _():
        atom_bwd_pairs(starts, pairs_ref, bias_s, pairw_ref, pairm_ref)


def atom_bwd_sum_kernel(
    summing,
    starts,
    grad_ref,
    query_ref,
    keyval_ref,
    gate_ref,
    probs_ref,
    attend_ref,
    mid_ref,
    rows_ref,
    pairs_ref,
    share_ref,
    wide_ref,
    down_ref,
    units_ref,
    atomgrad_ref,
    qbias_ref,
    pairw_ref,
    pairm_ref,
    small_ref,
    shares_ref,
    acck_s,
    accv_s,
    bias_s,
    attlow_s,
    dq_s,
    mix_s,
    midgrad_s,
    outw_s,
    upw_s,
    downw_s,
    pool_s,
    proj_s,
    own_s,
    to_left,
    to_right,
    from_left,
    from_right,
    s_rim,
    r_rim,
    *sums,
):
    summing.bind(units_ref, shares_ref, *sums)
    z, me = lax.axis_index("samp"), lax.axis_index("seq")
    seq = lax.axis_size("seq")
    first_place, last_place = me == 0, me == seq - 1
    width = query_ref.shape[-1]
    slots = query_ref.shape[1]
    step = pl.program_id(0)
    samples = pl.num_programs(0) - 1
    summing.slot(2 * step)

    def rim(b, side):
        ends = ((to_left, from_right, me - 1), (to_right, from_left, me + 1))[side]
        source, target, device = ends
        return remote(source.at[b], target.at[b], s_rim.at[side, b], r_rim.at[side, b], (z, device))

    def arrived(b, side):
        target = (from_right, from_left)[side]
        return remote(
            target.at[b], target.at[b], s_rim.at[side, b], r_rim.at[side, b], (z, lax.rem(me + 1, seq))
        )

    @pl.when(step == 0)
    def _():
        for ref in (qbias_ref, outw_s, upw_s, downw_s, pool_s, proj_s, pairw_ref, pairm_ref, bias_s):
            ref[...] = jnp.zeros_like(ref)

        @pl.when(first_place)
        def _():
            from_left[...] = jnp.zeros_like(from_left)

        @pl.when(last_place)
        def _():
            from_right[...] = jnp.zeros_like(from_right)

    slot_now = step % 2

    @pl.when(step < samples)
    def _():
        atom_bwd_dense(
            (grad_ref, query_ref, gate_ref, attend_ref, mid_ref),
            (share_ref, wide_ref, down_ref),
            (outw_s, upw_s, downw_s, pool_s),
            attlow_s,
            mix_s.at[slot_now, :, width:],
            midgrad_s.at[slot_now],
        )

    summing.slot(2 * step + 1)

    @pl.when(step < samples)
    def _():
        atom_bwd_windows(
            (query_ref, keyval_ref, probs_ref), (acck_s, accv_s, bias_s, attlow_s, dq_s)
        )
        query_grad = dq_s[...]
        qbias_ref[...] += jnp.sum(query_grad, 0, keepdims=True)
        mix_s[slot_now, :, :width] = query_grad.astype(bf16)
        for ref, low in ((to_left, 0), (to_right, RIM + slots)):
            ref[step, :, :width] = acck_s[low : low + RIM, :].astype(bf16)
            ref[step, :, width:] = accv_s[low : low + RIM, :].astype(bf16)

        @pl.when(~first_place)
        def _():
            rim(step, 0).start()

        @pl.when(~last_place)
        def _():
            rim(step, 1).start()

    @pl.when(step > 0)
    def _():
        b = step - 1

        @pl.when(~first_place)
        def _():
            arrived(b, 1).wait_recv()

        @pl.when(~last_place)
        def _():
            arrived(b, 0).wait_recv()

        normed, inv_std = norm_stats(rows_ref[0].astype(f32))
        parts = []
        for lanes in (slice(0, width), slice(width, 2 * width)):
            own = own_s[:, lanes]
            begin = own[:RIM] + from_left[b, :, lanes].astype(f32)
            end = own[slots - RIM :] + from_right[b, :, lanes].astype(f32)
            parts.append(jnp.concatenate([begin, own[RIM : slots - RIM], end], 0).astype(bf16))
        before = mix_s.at[1 - slot_now]
        mix = jnp.concatenate([before[:, :width], parts[0], parts[1], before[:, width:]], 1)
        proj_s[...] += mm_tn(normed.astype(bf16), mix)
        normed_grad = mm_nt(mix, wide_ref[:, : 4 * width])
        atomgrad_ref[0] = midgrad_s[1 - slot_now] + norm_back(normed, inv_std, normed_grad)

    @pl.when(step < samples)
    def _():
        own_s[:, :width] = acck_s[RIM : RIM + slots, :]
        own_s[:, width:] = accv_s[RIM : RIM + slots, :]

    @pl.when(step == samples)
    def _():
        atom_bwd_pairs(starts, pairs_ref, bias_s, pairw_ref, pairm_ref)
        samp = small_ref.shape[0]
        rows = width // samp
        for p in range(samp):
            span = slice(p * rows, (p + 1) * rows)
            small_ref[p, :rows, :] = pool_s[span, :].astype(bf16)
            small_ref[p, rows : 2 * rows, : 4 * width] = proj_s[span, :].astype(bf16)
            for part in range(2):
                low = (2 * p + part) * rows
                small_ref[p, rows : 2 * rows, (4 + part) * width : (5 + part) * width] = downw_s[
                    low : low + rows, :
                ].astype(bf16)
            small_ref[p, 2 * rows : 3 * rows, : 4 * width] = upw_s[span, :].astype(bf16)
            small_ref[p, 2 * rows : 3 * rows, 4 * width : 5 * width] = outw_s[span, :].astype(bf16)
            small_ref[p, 2 * rows : 3 * rows, 5 * width :] = jnp.zeros((rows, width), bf16)
            small_ref[p, 3 * rows :, :] = jnp.zeros((rows, 6 * width), bf16)
        summing.collect()

        def sent(b, carry):
            @pl.when(~first_place)
            def _():
                rim(b, 0).wait_send()

            @pl.when(~last_place)
            def _():
                rim(b, 1).wait_send()

            return carry

        lax.fori_loop(0, samples, sent, 0)


def atom_backward_sum(grad, starts, stored, rows, pairs, share, wide, down, summing, units):
    query = stored[0]
    samples, slots, width = query.shape
    samp = lax.axis_size("samp")
    ext_slots = slots + 2 * RIM
    windows = slots // WIN_Q
    model_width = grad.shape[-1]
    hidden_width = down.shape[0]
    stack = ATOM_HEADS * WIN_Q
    place = pl.BlockSpec(memory_space=pl.ANY)

    def now(shape):
        return pl.BlockSpec(
            (1,) + shape, lambda g: (jnp.minimum(g, samples - 1),) + (0,) * len(shape)
        )

    def late(shape):
        return pl.BlockSpec((1,) + shape, lambda g: (jnp.maximum(g - 1, 0),) + (0,) * len(shape))

    dma = pltpu.SemaphoreType.DMA
    rim_shape = (samples, RIM, 2 * width)
    small_shape = (samp, 4 * width // samp, model_width)
    return pl.pallas_call(
        functools.partial(atom_bwd_sum_kernel, summing),
        out_shape=[
            jax.ShapeDtypeStruct(rows.shape, f32),
            jax.ShapeDtypeStruct((1, width), f32),
            jax.ShapeDtypeStruct((stack, pairs.shape[1]), f32),
            jax.ShapeDtypeStruct((stack, WIN_K), f32),
            jax.ShapeDtypeStruct(small_shape, bf16),
            jax.ShapeDtypeStruct((8, UNIT, 768), bf16),
        ],
        grid=(samples + 1,),
        in_specs=[pl.BlockSpec(memory_space=pltpu.SMEM), now(grad.shape[1:])]
        + [now(part.shape[1:]) for part in stored]
        + [late(rows.shape[1:])]
        + [whole(part.shape) for part in (pairs, share, wide, down)]
        + [place],
        out_specs=[
            late(rows.shape[1:]),
            whole((1, width)),
            whole((stack, pairs.shape[1])),
            whole((stack, WIN_K)),
            whole(small_shape),
            place,
        ],
        scratch_shapes=[
            pltpu.VMEM((ext_slots, width), f32),
            pltpu.VMEM((ext_slots, width), f32),
            pltpu.VMEM((windows // 2, 2 * stack, 2 * WIN_K), f32),
            pltpu.VMEM((slots, width), bf16),
            pltpu.VMEM((slots, width), f32),
            pltpu.VMEM((2, slots, 2 * width), bf16),
            pltpu.VMEM((2, slots, width), f32),
            pltpu.VMEM((width, width), f32),
            pltpu.VMEM((width, 2 * hidden_width), f32),
            pltpu.VMEM((hidden_width, width), f32),
            pltpu.VMEM((width, model_width), f32),
            pltpu.VMEM((width, 4 * width), f32),
            pltpu.VMEM((slots, 2 * width), f32),
            pltpu.VMEM(rim_shape, bf16),
            pltpu.VMEM(rim_shape, bf16),
            pltpu.VMEM(rim_shape, bf16),
            pltpu.VMEM(rim_shape, bf16),
            dma((2, samples)),
            dma((2, samples)),
        ]
        + summing.scratch(),
        compiler_params=summing.params(),
        name="atom_backward",
    )(starts, grad, *stored, rows, pairs, share, wide, down, units)


def unpack_kernel(units_ref, small_ref, proj_ref, up_ref, down_ref, cond_ref, outw_ref, *atoms):
    proj_ref[...] = units_ref[0, :192, :384].astype(f32)
    up_ref[...] = units_ref[0, :192, 384:].astype(f32)
    down_ref[...] = units_ref[0, 192:240, :].astype(f32)
    cond_ref[:, :768] = units_ref[0, 240:288, :].astype(f32)
    cond_ref[:, 768:] = units_ref[0, 288:336, :384].astype(f32)
    outw_ref[...] = units_ref[0, 288:336, 384:].astype(f32)

    @pl.when(pl.program_id(0) == 0)
    def _():
        pool_ref, atomproj_ref, atomdown_ref, atomup_ref, atomout_ref, tiny_ref = atoms
        rows, width = atomout_ref.shape
        pool_ref[...] = small_ref[:rows, :].astype(f32)
        atomproj_ref[...] = small_ref[rows : 2 * rows, : 4 * width].astype(f32)
        for part in range(2):
            atomdown_ref[part * rows : (part + 1) * rows, :] = small_ref[
                rows : 2 * rows, (4 + part) * width : (5 + part) * width
            ].astype(f32)
        atomup_ref[...] = small_ref[2 * rows : 3 * rows, : 4 * width].astype(f32)
        atomout_ref[...] = small_ref[2 * rows : 3 * rows, 4 * width : 5 * width].astype(f32)
        tiny_ref[...] = small_ref[2 * rows : 3 * rows, 5 * width :].astype(f32)


def unpack(units, small, shapes, rows, width):
    outs = list(shapes) + [
        (rows, 6 * width),
        (rows, 4 * width),
        (2 * rows, width),
        (rows, 4 * width),
        (rows, width),
        (rows, width),
    ]
    specs = [
        pl.BlockSpec((192, 384), lambda s: (0, s)),
        pl.BlockSpec((192, 384), lambda s: (0, s)),
        pl.BlockSpec((48, 768), lambda s: (s, 0)),
        pl.BlockSpec((48, 1152), lambda s: (s // 4, s % 4)),
        pl.BlockSpec((48, 384), lambda s: (s // 2, s % 2)),
    ]
    return pl.pallas_call(
        unpack_kernel,
        out_shape=[jax.ShapeDtypeStruct(shape, f32) for shape in outs],
        grid=(8,),
        in_specs=[pl.BlockSpec((1, UNIT, 768), lambda s: (s, 0, 0)), whole(small.shape)],
        out_specs=specs + [whole(shape) for shape in outs[5:]],
        compiler_params=params(),
        name="unpack",
    )(units, small)


def atom_backward(grad, starts, stored, pairs, share, wide, down):
    query = stored[0]
    samples, slots, width = query.shape
    ext_slots = slots + 2 * RIM
    windows = slots // WIN_Q
    model_width = grad.shape[-1]
    hidden_width = down.shape[0]
    stack = ATOM_HEADS * WIN_Q
    outs = (
        ((slots, 2 * width), bf16),
        ((slots, 2 * width), f32),
        ((RIM, 2 * width), bf16),
        ((RIM, 2 * width), bf16),
        ((slots, width), f32),
    )
    totals = (
        (1, width),
        (width, width),
        (width, 2 * hidden_width),
        (hidden_width, width),
        (width, model_width),
        (stack, pairs.shape[1]),
        (stack, WIN_K),
    )
    return pl.pallas_call(
        atom_bwd_kernel,
        out_shape=[jax.ShapeDtypeStruct((samples,) + shape, kind) for shape, kind in outs]
        + [jax.ShapeDtypeStruct(shape, f32) for shape in totals],
        grid=(samples,),
        in_specs=[pl.BlockSpec(memory_space=pltpu.SMEM), per_sample(grad.shape[1:])]
        + [per_sample(part.shape[1:]) for part in stored]
        + [whole(part.shape) for part in (pairs, share, wide, down)],
        out_specs=[per_sample(shape) for shape, _ in outs] + [whole(shape) for shape in totals],
        scratch_shapes=[
            pltpu.VMEM((ext_slots, width), f32),
            pltpu.VMEM((ext_slots, width), f32),
            pltpu.VMEM((windows // 2, 2 * stack, 2 * WIN_K), f32),
            pltpu.VMEM((slots, width), bf16),
            pltpu.VMEM((slots, width), f32),
        ],
        compiler_params=params(),
        name="atom_backward",
    )(starts, grad, *stored, pairs, share, wide, down)


def atom_input_kernel(
    rows_ref, mix_ref, own_ref, left_ref, right_ref, midgrad_ref, wide_ref, grad_ref, proj_ref
):
    width = rows_ref.shape[-1]

    @pl.when(pl.program_id(0) == 0)
    def _():
        proj_ref[...] = jnp.zeros_like(proj_ref)

    normed, inv_std = norm_stats(rows_ref[0].astype(f32))
    slots = normed.shape[0]
    own = own_ref[0]
    head = own[:RIM] + left_ref[0].astype(f32)
    tail = own[slots - RIM :] + right_ref[0].astype(f32)
    own = jnp.concatenate([head, own[RIM : slots - RIM], tail], 0).astype(bf16)
    mix = jnp.concatenate([mix_ref[0, :, :width], own, mix_ref[0, :, width:]], 1)
    proj_ref[...] += mm_tn(normed.astype(bf16), mix)
    normed_grad = mm_nt(mix, wide_ref[:, : 4 * width])
    grad_ref[0] = midgrad_ref[0] + norm_back(normed, inv_std, normed_grad)


def atom_input_backward(rows, mix, own, left, right, midgrad, wide):
    samples, slots, width = rows.shape
    return pl.pallas_call(
        atom_input_kernel,
        out_shape=[
            jax.ShapeDtypeStruct(rows.shape, f32),
            jax.ShapeDtypeStruct((width, 4 * width), f32),
        ],
        grid=(samples,),
        in_specs=[per_sample(part.shape[1:]) for part in (rows, mix, own, left, right, midgrad)]
        + [whole(wide.shape)],
        out_specs=[per_sample((slots, width)), whole((width, 4 * width))],
        compiler_params=params(),
        name="atom_input_backward",
    )(rows, mix, own, left, right, midgrad, wide)


def row_stats(pairs, ones_op, weights):
    count = weights.shape[0]
    both = mm_nt(jnp.concatenate([weights, ones_op], 0), pairs)
    upper, lower = square_sums(ones_op, pairs.astype(f32) * pairs.astype(f32))
    features = pairs.shape[1]
    mean = both[count : count + 1] * (1.0 / features)
    square = (mm_nt(ones_op, upper) + mm_nt(ones_op, lower))[:1] * (1.0 / features)
    var = jnp.maximum(square - mean * mean, 0.0)
    return both[:count], mean, lax.rsqrt(var + norm_eps)


def pair_bias_kernel(pair_ref, weight_ref, bias_ref):
    weights = weight_ref[...]
    ones_op = jnp.ones((16, weights.shape[1]), bf16)
    weight_sum = jnp.sum(weights.astype(f32), -1, keepdims=True)
    for row in range(pair_ref.shape[0]):
        product, mean, inv_std = row_stats(pair_ref[row], ones_op, weights)
        bias_ref[:, row, :] = inv_std * (product - mean * weight_sum)


def pair_bias(pairs, weights):
    rows, keys, features = pairs.shape
    heads = weights.shape[0]
    return pl.pallas_call(
        pair_bias_kernel,
        out_shape=jax.ShapeDtypeStruct((heads, rows, keys), f32),
        grid=(rows // 8,),
        in_specs=[pl.BlockSpec((8, keys, features), lambda i: (i, 0, 0)), whole(weights.shape)],
        out_specs=pl.BlockSpec((heads, 8, keys), lambda i: (0, i, 0)),
        compiler_params=params(),
        name="pair_bias",
    )(pairs, weights)


def pair_grad_kernel(pair_ref, grad_ref, weight_ref, total_ref, mean_ref):
    @pl.when(pl.program_id(0) == 0)
    def _():
        total_ref[...] = jnp.zeros_like(total_ref)
        mean_ref[...] = jnp.zeros_like(mean_ref)

    heads = grad_ref.shape[0]
    ones_op = jnp.ones((16, pair_ref.shape[2]), bf16)
    total = jnp.zeros(total_ref.shape, f32)
    means = jnp.zeros(mean_ref.shape, f32)
    for row in range(pair_ref.shape[0]):
        pairs = pair_ref[row]
        _, mean, inv_std = row_stats(pairs, ones_op, weight_ref[...])
        scaled = grad_ref[:, row, :] * inv_std
        means += scaled * mean
        upper = scaled.astype(bf16)
        lower = (scaled - upper.astype(f32)).astype(bf16)
        both = mm(jnp.concatenate([upper, lower], 0), pairs)
        total += both[:heads] + both[heads:]
    total_ref[...] += total
    mean_ref[...] += means


def pair_grad(pairs, grads, weights):
    rows, keys, features = pairs.shape
    heads = grads.shape[0]
    total, means = pl.pallas_call(
        pair_grad_kernel,
        out_shape=[
            jax.ShapeDtypeStruct((heads, features), f32),
            jax.ShapeDtypeStruct((heads, keys), f32),
        ],
        grid=(rows // 8,),
        in_specs=[
            pl.BlockSpec((8, keys, features), lambda i: (i, 0, 0)),
            pl.BlockSpec((heads, 8, keys), lambda i: (0, i, 0)),
            whole(weights.shape),
        ],
        out_specs=[whole((heads, features)), whole((heads, keys))],
        compiler_params=params(),
        name="pair_grad",
    )(pairs, grads, weights)
    return total - jnp.sum(means, -1, keepdims=True)


def head_groups(width, heads):
    head_dim = width // heads
    groups = []
    for head in range(0, heads, 4):
        low = head * head_dim
        base = low // LANES * LANES
        groups.append((head, base, low - base))
    return head_dim, groups


def token_fwd_kernel(query_ref, keyval_ref, bias_ref, attend_ref, probs_ref, fold_s):
    tokens, width = query_ref.shape[1:]
    heads = bias_ref.shape[0]
    keys = bias_ref.shape[2]
    head_dim, groups = head_groups(width, heads)
    scale = float(head_dim) ** (-0.5)
    fold_s[...] = jnp.zeros_like(fold_s)
    for head, base, first in groups:
        span = slice(base, base + 256)
        key_rows = keyval_ref[:, 0, :, base : base + 256].reshape(keys, 256)
        value_rows = keyval_ref[:, 0, :, width + base : width + base + 256].reshape(keys, 256)
        stacked = head_stack(query_ref[0, :, span], 4, head_dim, first)
        bias = bias_ref[head : head + 4].reshape(4 * tokens, keys)
        scores = mm_nt(stacked, key_rows) * scale + bias
        exp_scores = jnp.exp(scores - jnp.max(scores, -1, keepdims=True))
        probs = exp_scores * (1.0 / jnp.sum(exp_scores, -1, keepdims=True))
        probs_low = probs.astype(bf16)
        probs_ref[0, head : head + 4] = probs_low.reshape(4, tokens, keys)
        fold_s[:, span] += head_fold(mm(probs_low, value_rows), 4, head_dim, first)
    attend_ref[0] = fold_s[...]


def token_attention(query, keyval, bias):
    samples, tokens, width = query.shape
    heads, _, keys = bias.shape
    devices = keyval.shape[0]
    return pl.pallas_call(
        token_fwd_kernel,
        out_shape=[
            jax.ShapeDtypeStruct(query.shape, f32),
            jax.ShapeDtypeStruct((samples, heads, tokens, keys), bf16),
        ],
        grid=(samples,),
        in_specs=[
            per_sample((tokens, width)),
            pl.BlockSpec((devices, 1, tokens, 2 * width), lambda b: (0, b, 0, 0)),
            whole(bias.shape),
        ],
        out_specs=[per_sample((tokens, width)), per_sample((heads, tokens, keys))],
        scratch_shapes=[pltpu.VMEM((tokens, width), f32)],
        compiler_params=params(),
        name="token_attention",
    )(query, keyval, bias)


def token_bwd_kernel(
    query_ref, keyval_ref, probs_ref, att_ref, dq_ref, dkv_ref, bias_ref, fold_s, grad_s
):
    tokens, width = query_ref.shape[1:]
    heads, _, keys = bias_ref.shape
    devices = keyval_ref.shape[0]
    head_dim, groups = head_groups(width, heads)
    scale = float(head_dim) ** (-0.5)

    @pl.when(pl.program_id(0) == 0)
    def _():
        bias_ref[...] = jnp.zeros_like(bias_ref)

    fold_s[...] = jnp.zeros_like(fold_s)
    grad_s[...] = jnp.zeros_like(grad_s)
    for head, base, first in groups:
        span = slice(base, base + 256)
        key_rows = keyval_ref[:, 0, :, base : base + 256].reshape(keys, 256)
        value_rows = keyval_ref[:, 0, :, width + base : width + base + 256].reshape(keys, 256)
        queries = head_stack(query_ref[0, :, span], 4, head_dim, first)
        att = head_stack(att_ref[0, :, span], 4, head_dim, first)
        probs_low = probs_ref[0, head : head + 4].reshape(4 * tokens, keys)
        probs = probs_low.astype(f32)
        prob_grad = mm_nt(att, value_rows)
        delta = jnp.sum(prob_grad * probs, -1, keepdims=True)
        score_low = (probs * (prob_grad - delta)).astype(bf16)
        bias_ref[head : head + 4] += score_low.astype(f32).reshape(4, tokens, keys)
        fold_s[:, span] += head_fold(mm(score_low, key_rows), 4, head_dim, first) * scale
        grad_s[:, span] += mm_tn(score_low, queries) * scale
        grad_s[:, width + base : width + base + 256] += mm_tn(probs_low, att)
    dq_ref[0] = fold_s[...]
    dkv_ref[:, 0] = grad_s[...].astype(bf16).reshape(devices, tokens, 2 * width)


def token_attention_back(query, keyval, probs, att):
    samples, tokens, width = query.shape
    heads, _, keys = probs.shape[1:]
    devices = keyval.shape[0]
    return pl.pallas_call(
        token_bwd_kernel,
        out_shape=[
            jax.ShapeDtypeStruct(query.shape, f32),
            jax.ShapeDtypeStruct(keyval.shape, bf16),
            jax.ShapeDtypeStruct((heads, tokens, keys), f32),
        ],
        grid=(samples,),
        in_specs=[
            per_sample((tokens, width)),
            pl.BlockSpec((devices, 1, tokens, 2 * width), lambda b: (0, b, 0, 0)),
            per_sample((heads, tokens, keys)),
            per_sample((tokens, width)),
        ],
        out_specs=[
            per_sample((tokens, width)),
            pl.BlockSpec((devices, 1, tokens, 2 * width), lambda b: (0, b, 0, 0)),
            whole((heads, tokens, keys)),
        ],
        scratch_shapes=[
            pltpu.VMEM((tokens, width), f32),
            pltpu.VMEM((keys, 2 * width), f32),
        ],
        compiler_params=params(),
        name="token_attention_back",
    )(query, keyval, probs, att)


def token_open_kernel(
    noise,
    direction_ref,
    single_ref,
    pooled_ref,
    tokens_ref,
    condw_ref,
    condb_ref,
    proj_ref,
    qbias_ref,
    block_ref,
    condlow_ref,
    cond_ref,
    attn_ref,
    query_ref,
    keyval_ref,
    gating_ref,
):
    width = tokens_ref.shape[1]
    count = single_ref.shape[0]
    step = pl.program_id(0)
    single = single_ref[...].astype(f32)
    direction = direction_ref[...]
    for part in range(tokens_ref.shape[0] // count):
        level = jnp.full(direction.shape, noise[step * (tokens_ref.shape[0] // count) + part], f32)
        shifted = single + 0.25 * jnp.log(level / sigma_data) * direction
        condlow_ref[part * count : (part + 1) * count, :] = norm_stats(shifted)[0].astype(bf16)
    cond_low = condlow_ref[...]
    for part in range(6):
        lanes = slice(part * width, (part + 1) * width)
        cond_ref[:, lanes] = mm(cond_low, condw_ref[:, lanes]) + condb_ref[:, lanes]
    block_in = tokens_ref[...].astype(f32) + pooled_ref[...]
    block_ref[...] = block_in
    normed = norm_stats(block_in)[0]
    attn_in = (sigmoid(cond_ref[:, :width]) * normed + cond_ref[:, width : 2 * width]).astype(bf16)
    attn_ref[...] = attn_in
    query_ref[...] = (mm(attn_in, proj_ref[:, :width]) + qbias_ref[...]).astype(bf16)
    keyval_ref[...] = mm(attn_in, proj_ref[:, width : 3 * width]).astype(bf16)
    gating_ref[...] = mm(attn_in, proj_ref[:, 3 * width :])


def token_open(noise, direction, single, pooled, tokens, condw, condb, proj, qbias):
    samples, count, width = tokens.shape
    rows = samples * count
    block = 2 * count
    lanes = lambda size: pl.BlockSpec((block, size), lambda i: (i, 0))
    inner = single.shape[1]
    outs = (
        (width, f32),
        (inner, bf16),
        (6 * width, f32),
        (width, bf16),
        (width, bf16),
        (2 * width, bf16),
        (width, f32),
    )
    return pl.pallas_call(
        token_open_kernel,
        out_shape=[jax.ShapeDtypeStruct((rows, size), kind) for size, kind in outs],
        grid=(rows // block,),
        in_specs=[
            pl.BlockSpec(memory_space=pltpu.SMEM),
            whole((1, inner)),
            whole(single.shape),
            lanes(width),
            lanes(width),
            whole(condw.shape),
            whole((1, 6 * width)),
            whole(proj.shape),
            whole((1, width)),
        ],
        out_specs=[lanes(size) for size, _ in outs],
        compiler_params=params(),
        name="token_open",
    )(
        noise,
        direction.reshape(1, -1),
        single,
        pooled.reshape(rows, width),
        tokens.reshape(rows, width),
        condw,
        condb.reshape(1, -1),
        proj,
        qbias.reshape(1, -1),
    )


def token_middle_rows(
    attend,
    gating_ref,
    block_ref,
    gate1_ref,
    scale2_ref,
    shift2_ref,
    gate2_ref,
    cotangent_ref,
    outw_ref,
    upw_ref,
    downw_ref,
    result_ref,
    ffn_ref,
    upper_ref,
    hidden_ref,
    two_ref,
    gated_ref,
    branch_ref,
    att_ref,
    gategrad_ref,
    midgrad_ref,
    condgrad_ref,
):
    width = attend.shape[1]
    hidden_width = downw_ref.shape[0]
    outw, upw, downw = outw_ref[...], upw_ref[...], downw_ref[...]
    sig_gate = sigmoid(gating_ref[...])
    gated_low = (attend * sig_gate).astype(bf16)
    gated_ref[...] = gated_low
    branch = mm(gated_low, outw)
    gate_one = sigmoid(gate1_ref[...])
    mid = block_ref[...] + gate_one * branch
    normed, inv_std = norm_stats(mid)
    scale_two = sigmoid(scale2_ref[...])
    ffn_in = (scale_two * normed + shift2_ref[...]).astype(bf16)
    ffn_ref[...] = ffn_in
    first_half = mm(ffn_in, upw[:, :hidden_width])
    second_half = mm(ffn_in, upw[:, hidden_width:])
    sig_first = sigmoid(first_half)
    hidden = (first_half * sig_first * second_half).astype(bf16)
    hidden_ref[...] = hidden
    branch_two = mm(hidden, downw)
    gate_two = sigmoid(gate2_ref[...])
    result_ref[...] = (mid + gate_two * branch_two).astype(bf16)

    out_grad = cotangent_ref[...].astype(f32)
    two_low = (out_grad * gate_two).astype(bf16)
    two_ref[...] = two_low
    condgrad_ref[:, 3 * width :] = (
        out_grad * branch_two * gate_two * (1.0 - gate_two)
    ).astype(bf16)
    hidden_grad = mm_nt(two_low, downw)
    first_grad = (
        hidden_grad * second_half * sig_first * (1.0 + first_half * (1.0 - sig_first))
    ).astype(bf16)
    second_grad = (hidden_grad * first_half * sig_first).astype(bf16)
    upper_ref[:, :hidden_width] = first_grad
    upper_ref[:, hidden_width:] = second_grad
    ffn_grad = mm_nt(first_grad, upw[:, :hidden_width]) + mm_nt(second_grad, upw[:, hidden_width:])
    condgrad_ref[:, 2 * width : 3 * width] = ffn_grad.astype(bf16)
    condgrad_ref[:, width : 2 * width] = (
        ffn_grad * normed * scale_two * (1.0 - scale_two)
    ).astype(bf16)
    mid_grad = out_grad + norm_back(normed, inv_std, ffn_grad * scale_two)
    midgrad_ref[...] = mid_grad
    branch_low = (mid_grad * gate_one).astype(bf16)
    branch_ref[...] = branch_low
    condgrad_ref[:, :width] = (mid_grad * branch * gate_one * (1.0 - gate_one)).astype(bf16)
    gated_grad = mm_nt(branch_low, outw)
    att_ref[...] = (gated_grad * sig_gate).astype(bf16)
    gategrad_ref[...] = (gated_grad * attend * sig_gate * (1.0 - sig_gate)).astype(bf16)


def attend_groups(heads, width, tokens, query, keyval, bias, probs_ref, fold_s):
    head_dim, groups = head_groups(width, heads)
    scale = float(head_dim) ** (-0.5)
    fold_s[...] = jnp.zeros_like(fold_s)
    for head, base, first in groups:
        span = slice(base, base + 256)
        stacked = head_stack(query[:, span], 4, head_dim, first)
        scores = mm_nt(stacked, keyval(base)) * scale + bias(head)
        exp_scores = jnp.exp(scores - jnp.max(scores, -1, keepdims=True))
        probs = exp_scores * (1.0 / jnp.sum(exp_scores, -1, keepdims=True))
        probs_low = probs.astype(bf16)
        probs_ref[0, head : head + 4] = probs_low.reshape(4, tokens, -1)
        fold_s[:, span] += head_fold(mm(probs_low, keyval(width + base)), 4, head_dim, first)


def gather_attend_kernel(
    query_ref,
    own_ref,
    pair_ref,
    weight_ref,
    gating_ref,
    block_ref,
    gate1_ref,
    scale2_ref,
    shift2_ref,
    gate2_ref,
    cotangent_ref,
    outw_ref,
    upw_ref,
    downw_ref,
    probs_ref,
    keyval_ref,
    stats_ref,
    *refs,
):
    middle, (all_s, bias_s, fold_s, attend_s, send, recv, load) = refs[:11], refs[11:]
    z, me, sib, xn, yn, dg = places()
    step = pl.program_id(0)
    tokens, width = query_ref.shape[1:]
    heads = weight_ref.shape[0]
    devices, samples = all_s.shape[:2]
    keys = devices * tokens
    head, tail, full = slice(0, width), slice(width, 2 * width), slice(0, 2 * width)

    def unit(part, sample, lanes, kind, device):
        ref = all_s.at[part, sample, :, lanes]
        return remote(ref, ref, send.at[kind, sample], recv.at[kind, sample], (z, device))

    def issue(sample):
        unit(me, sample, full, 0, xn).start()
        unit(me, sample, full, 1, yn).start()
        unit(me, sample, full, 4, sib).start()

    def relay(sample):
        unit(xn, sample, full, 0, xn).wait_recv()
        unit(xn, sample, head, 2, yn).start()
        unit(xn, sample, full, 5, sib).start()
        unit(yn, sample, full, 1, yn).wait_recv()
        unit(yn, sample, tail, 3, xn).start()
        unit(yn, sample, full, 6, sib).start()

    def collect(sample):
        unit(dg, sample, head, 2, yn).wait_recv()
        unit(dg, sample, tail, 3, xn).wait_recv()
        unit(dg, sample, full, 7, sib).start()

    @pl.when(step == 0)
    def _():
        copy = pltpu.make_async_copy(own_ref, all_s.at[me], load)
        copy.start()
        greet([(z, sib), (z, xn), (z, yn)])
        copy.wait()
        issue(0)
        issue(1)

    @pl.when((step >= 1) & (step - 1 < samples))
    def _():
        relay(step - 1)

    @pl.when((step >= 1) & (step + 1 < samples))
    def _():
        issue(step + 1)

    @pl.when((step >= 2) & (step - 2 < samples))
    def _():
        collect(step - 2)

    @pl.when(step < 2)
    def _():
        weights = weight_ref[...]
        ones_op = jnp.ones((16, weights.shape[1]), bf16)
        weight_sum = jnp.sum(weights.astype(f32), -1, keepdims=True)
        groups = pair_ref.shape[0] // 8

        def one(group, carry):
            for row in range(8):
                product, mean, inv_std = row_stats(pair_ref[group * 8 + row], ones_op, weights)
                place = step * groups + group
                bias_s[:, place, row, :] = inv_std * (product - mean * weight_sum)
                stats_ref[0, place, row : row + 1, :] = mean
                stats_ref[1, place, row : row + 1, :] = inv_std
            return carry

        lax.fori_loop(0, groups, one, 0)

    @pl.when(step >= 3)
    def _():
        sample = step - 3
        for kind, part in ((4, sib), (5, sib), (6, sib), (7, sib)):
            unit(part, sample, full, kind, sib).wait_recv()
        for part in range(devices):
            keyval_ref[part, 0] = all_s[part, sample]
        attend_groups(
            heads,
            width,
            tokens,
            query_ref[0],
            lambda base: keyval_ref[:, 0, :, base : base + 256].reshape(keys, 256),
            lambda head: bias_s[head : head + 4].reshape(4 * tokens, keys),
            probs_ref,
            fold_s,
        )
        attend_s[pl.ds(pl.multiple_of(sample % 2 * tokens, 16), tokens), :] = fold_s[...]

    @pl.when((step >= 3) & (step % 2 == 0))
    def _():
        token_middle_rows(
            attend_s[...],
            gating_ref,
            block_ref,
            gate1_ref,
            scale2_ref,
            shift2_ref,
            gate2_ref,
            cotangent_ref,
            outw_ref,
            upw_ref,
            downw_ref,
            *middle,
        )

    @pl.when(step == pl.num_programs(0) - 1)
    def _():
        def sent(sample, carry):
            for kind in (0, 1, 4, 5, 6, 7):
                unit(me, sample, full, kind, sib).wait_send()
            unit(me, sample, head, 2, sib).wait_send()
            unit(me, sample, tail, 3, sib).wait_send()
            return carry

        lax.fori_loop(0, samples, sent, 0)


def held_once(shape):
    return pl.BlockSpec(shape, lambda *_: (0,) * len(shape), pipeline_mode=pl.Buffered(1))


def gather_attend(
    query, own, pairs, weights, gating, block_in, cond_all, cotangent, outw, upw, downw
):
    samples, tokens, width = query.shape
    heads, features = weights.shape
    seq = lax.axis_size("seq")
    keys = seq * tokens
    hidden_width = downw.shape[0]
    rows, block = samples * tokens, 2 * tokens
    late = lambda g: jnp.maximum(g - 3, 0)
    sample_block = lambda shape: pl.BlockSpec((1,) + shape, lambda g: (late(g),) + (0,) * len(shape))
    duo_block = lambda lanes, column=0: pl.BlockSpec((block, lanes), lambda g: (late(g) // 2, column))
    flat = lambda part: part.reshape(rows, part.shape[-1])
    cond = flat(cond_all)
    dma = pltpu.SemaphoreType.DMA
    outs = (
        (width, bf16),
        (width, bf16),
        (2 * hidden_width, bf16),
        (hidden_width, bf16),
        (width, bf16),
        (width, bf16),
        (width, bf16),
        (width, bf16),
        (width, bf16),
        (width, f32),
        (4 * width, bf16),
    )
    results = pl.pallas_call(
        gather_attend_kernel,
        out_shape=[
            jax.ShapeDtypeStruct((samples, heads, tokens, keys), bf16),
            jax.ShapeDtypeStruct((seq, samples, tokens, 2 * width), bf16),
            jax.ShapeDtypeStruct((2, tokens // 8, 8, keys), f32),
        ]
        + [jax.ShapeDtypeStruct((rows, lanes), kind) for lanes, kind in outs],
        grid=(samples + 3,),
        in_specs=[
            sample_block((tokens, width)),
            pl.BlockSpec(memory_space=pl.ANY),
            pl.BlockSpec((tokens // 2, keys, features), lambda g: (jnp.minimum(g, 1), 0, 0)),
            whole(weights.shape),
            duo_block(width),
            duo_block(width),
            duo_block(width, 2),
            duo_block(width, 3),
            duo_block(width, 4),
            duo_block(width, 5),
            duo_block(width),
        ]
        + [held_once(part.shape) for part in (outw, upw, downw)],
        out_specs=[
            sample_block((heads, tokens, keys)),
            pl.BlockSpec((seq, 1, tokens, 2 * width), lambda g: (0, late(g), 0, 0)),
            whole((2, tokens // 8, 8, keys)),
        ]
        + [duo_block(lanes) for lanes, _ in outs],
        scratch_shapes=[
            pltpu.VMEM((seq, samples, tokens, 2 * width), bf16),
            pltpu.VMEM((heads, tokens // 8, 8, keys), f32),
            pltpu.VMEM((tokens, width), f32),
            pltpu.VMEM((block, width), f32),
            dma((8, samples)),
            dma((8, samples)),
            dma,
        ],
        compiler_params=pltpu.CompilerParams(
            vmem_limit_bytes=60 << 20, collective_id=4, has_side_effects=True
        ),
        name="gather_attend",
    )(
        query,
        own,
        pairs,
        weights,
        flat(gating),
        flat(block_in),
        cond,
        cond,
        cond,
        cond,
        flat(cotangent),
        outw,
        upw,
        downw,
    )
    return results[:3], results[3:]


def attend_back_scatter_kernel(
    query_ref,
    keyval_ref,
    probs_ref,
    att_ref,
    pair_ref,
    stats_ref,
    ffn_ref,
    upper_ref,
    hidden_ref,
    two_ref,
    gated_ref,
    branch_ref,
    dq_ref,
    dkv_ref,
    pairw_ref,
    pairm_ref,
    upw_ref,
    downw_ref,
    outw_ref,
    fold_s,
    grad_s,
    bias_s,
    mine,
    theirs,
    from_x,
    from_y,
    last_x,
    last_y,
    s_sib,
    r_sib,
    s_one,
    r_one,
    s_two,
    r_two,
):
    z, me, sib, xn, yn, dg = places()
    core, chip = me % 2, me // 2
    chip_x, chip_y, chip_d = xn // 2, yn // 2, dg // 2
    step = pl.program_id(0)
    tokens, width = query_ref.shape[1:]
    samples = mine.shape[0]
    heads, keys = probs_ref.shape[1], probs_ref.shape[3]
    head_dim, groups = head_groups(width, heads)
    scale = float(head_dim) ** (-0.5)
    head, tail = slice(0, width), slice(width, 2 * width)

    def there(b):
        return remote(
            mine.at[b, :, 1 - core], theirs.at[b], s_sib.at[b], r_sib.at[b], (z, sib)
        )

    def one(b, k):
        part = (chip_x, chip_d, chip_y, chip_d)[k]
        lanes = head if k < 2 else tail
        target = (from_x if k < 2 else from_y).at[b, k % 2]
        device = xn if k < 2 else yn
        source = mine.at[b, part, core, :, lanes]
        return remote(source, target, s_one.at[b, k], r_one.at[b, k], (z, device))

    def two(b, k):
        part, lanes, target, device = ((chip_y, head, last_y, yn), (chip_x, tail, last_x, xn))[k]
        source = mine.at[b, part, core, :, lanes]
        return remote(source, target.at[b], s_two.at[b, k], r_two.at[b, k], (z, device))

    def add(b, part, lanes, source):
        both = mine[b, part, core, :, lanes].astype(f32) + source.astype(f32)
        mine[b, part, core, :, lanes] = both.astype(bf16)

    @pl.when(step == 0)
    def _():
        greet([(z, sib), (z, xn), (z, yn)])
        bias_s[...] = jnp.zeros_like(bias_s)
        pairw_ref[...] = jnp.zeros_like(pairw_ref)
        pairm_ref[...] = jnp.zeros_like(pairm_ref)

    @pl.when((step >= 1) & (step - 1 < samples))
    def _():
        b = step - 1
        there(b).wait_recv()

        def chips(j, carry):
            add(b, j, slice(0, 2 * width), theirs[b, j])
            return carry

        lax.fori_loop(0, 4, chips, 0)
        for k in range(4):
            one(b, k).start()

    @pl.when((step >= 2) & (step - 2 < samples))
    def _():
        b = step - 2
        one(b, 1).wait_recv()
        add(b, chip_y, head, from_x[b, 1])
        two(b, 0).start()
        one(b, 3).wait_recv()
        add(b, chip_x, tail, from_y[b, 1])
        two(b, 1).start()
        one(b, 0).wait_recv()
        add(b, chip, head, from_x[b, 0])
        one(b, 2).wait_recv()
        add(b, chip, tail, from_y[b, 0])

    @pl.when((step >= 3) & (step - 3 < samples))
    def _():
        b = step - 3
        two(b, 0).wait_recv()
        add(b, chip, head, last_y[b])
        two(b, 1).wait_recv()
        add(b, chip, tail, last_x[b])
        dkv_ref[0] = mine[b, chip, core]

    @pl.when(step < samples)
    def _():
        fold_s[...] = jnp.zeros_like(fold_s)
        grad_s[...] = jnp.zeros_like(grad_s)
        for first_head, base, first in groups:
            span = slice(base, base + 256)
            key_rows = keyval_ref[:, 0, :, base : base + 256].reshape(keys, 256)
            value_rows = keyval_ref[:, 0, :, width + base : width + base + 256].reshape(keys, 256)
            queries = head_stack(query_ref[0, :, span], 4, head_dim, first)
            att = head_stack(att_ref[0, :, span], 4, head_dim, first)
            probs_low = probs_ref[0, first_head : first_head + 4].reshape(4 * tokens, keys)
            probs = probs_low.astype(f32)
            prob_grad = mm_nt(att, value_rows)
            delta = jnp.sum(prob_grad * probs, -1, keepdims=True)
            score_low = (probs * (prob_grad - delta)).astype(bf16)
            bias_s[first_head : first_head + 4] += score_low.astype(f32).reshape(
                4, tokens // 8, 8, keys
            )
            fold_s[:, span] += head_fold(mm(score_low, key_rows), 4, head_dim, first) * scale
            grad_s[:, span] += mm_tn(score_low, queries) * scale
            grad_s[:, width + base : width + base + 256] += mm_tn(probs_low, att)
        dq_ref[0] = fold_s[...]
        mine[step] = grad_s[...].astype(bf16).reshape(mine.shape[1:])
        there(step).start()
        upw_ref[...] = mm_tn(ffn_ref[...], upper_ref[...]).astype(bf16)

    @pl.when(step < 6)
    def _():
        downw_ref[...] = mm_tn(hidden_ref[...], two_ref[...]).astype(bf16)

    @pl.when((step >= 6) & (step < 8))
    def _():
        outw_ref[...] = mm_tn(gated_ref[...], branch_ref[...]).astype(bf16)

    @pl.when((step >= samples) & (step < samples + 2))
    def _():
        rows = pair_ref.shape[0] // 8

        def some(group, carry):
            total, means = carry
            place = (step - samples) * rows + group
            for row in range(8):
                inv_std = stats_ref[1, place, row : row + 1, :]
                scaled = bias_s[:, place, row, :] * inv_std
                means += scaled * stats_ref[0, place, row : row + 1, :]
                upper = scaled.astype(bf16)
                lower = (scaled - upper.astype(f32)).astype(bf16)
                both = mm(jnp.concatenate([upper, lower], 0), pair_ref[group * 8 + row])
                total += both[:heads] + both[heads:]
            return total, means

        zeros = (jnp.zeros(pairw_ref.shape, f32), jnp.zeros(pairm_ref.shape, f32))
        total, means = lax.fori_loop(0, rows, some, zeros)
        pairw_ref[...] += total
        pairm_ref[...] += means

    @pl.when(step == pl.num_programs(0) - 1)
    def _():
        def sent(b, carry):
            there(b).wait_send()
            for k in range(4):
                one(b, k).wait_send()
            for k in range(2):
                two(b, k).wait_send()
            return carry

        lax.fori_loop(0, samples, sent, 0)


def attend_back_scatter(query, keyval, probs, att, pairs, stats, ffn, upper, hidden, two, gated, branch):
    samples, tokens, width = query.shape
    heads, _, keys = probs.shape[1:]
    seq = keyval.shape[0]
    features = pairs.shape[-1]
    flat = [part.reshape(-1, part.shape[-1]) for part in (ffn, upper, hidden, two, gated, branch)]
    rows = flat[0].shape[0]
    held = lambda g: jnp.minimum(g, samples - 1)
    late = lambda g: jnp.clip(g - 3, 0, samples - 1)
    pair_step = lambda g: jnp.clip(g - samples, 0, 1)
    up_step = lambda g: jnp.minimum(g, seq - 1)
    down_step = lambda g: jnp.minimum(g, 5)
    out_step = lambda g: jnp.clip(g - 6, 0, 1)
    sample_block = lambda shape, at: pl.BlockSpec((1,) + shape, lambda g: (at(g),) + (0,) * len(shape))
    keyval_block = pl.BlockSpec((seq, 1, tokens, 2 * width), lambda g: (0, held(g), 0, 0))
    up_width = flat[1].shape[1] // seq
    hidden_width = flat[2].shape[1]
    dma = pltpu.SemaphoreType.DMA
    results = pl.pallas_call(
        attend_back_scatter_kernel,
        out_shape=[
            jax.ShapeDtypeStruct(query.shape, f32),
            jax.ShapeDtypeStruct((samples, tokens, 2 * width), bf16),
            jax.ShapeDtypeStruct((heads, features), f32),
            jax.ShapeDtypeStruct((heads, keys), f32),
            jax.ShapeDtypeStruct((width, flat[1].shape[1]), bf16),
            jax.ShapeDtypeStruct((hidden_width, width), bf16),
            jax.ShapeDtypeStruct((width, width), bf16),
        ],
        grid=(samples + 3,),
        in_specs=[
            sample_block((tokens, width), held),
            keyval_block,
            sample_block((heads, tokens, keys), held),
            sample_block((tokens, width), held),
            pl.BlockSpec((tokens // 2, keys, features), lambda g: (pair_step(g), 0, 0)),
            whole(stats.shape),
            whole(flat[0].shape),
            pl.BlockSpec((rows, up_width), lambda g: (0, up_step(g))),
            pl.BlockSpec((rows, 256), lambda g: (0, down_step(g))),
            whole(flat[3].shape),
            pl.BlockSpec((rows, width // 2), lambda g: (0, out_step(g))),
            whole(flat[5].shape),
        ],
        out_specs=[
            sample_block((tokens, width), held),
            sample_block((tokens, 2 * width), late),
            whole((heads, features)),
            whole((heads, keys)),
            pl.BlockSpec((width, up_width), lambda g: (0, up_step(g))),
            pl.BlockSpec((256, width), lambda g: (down_step(g), 0)),
            pl.BlockSpec((width // 2, width), lambda g: (out_step(g), 0)),
        ],
        scratch_shapes=[
            pltpu.VMEM((tokens, width), f32),
            pltpu.VMEM((keys, 2 * width), f32),
            pltpu.VMEM((heads, tokens // 8, 8, keys), f32),
            pltpu.VMEM((samples, seq // 2, 2, tokens, 2 * width), bf16),
            pltpu.VMEM((samples, seq // 2, tokens, 2 * width), bf16),
            pltpu.VMEM((samples, 2, tokens, width), bf16),
            pltpu.VMEM((samples, 2, tokens, width), bf16),
            pltpu.VMEM((samples, tokens, width), bf16),
            pltpu.VMEM((samples, tokens, width), bf16),
            dma((samples,)),
            dma((samples,)),
            dma((samples, 4)),
            dma((samples, 4)),
            dma((samples, 2)),
            dma((samples, 2)),
        ],
        compiler_params=pltpu.CompilerParams(
            vmem_limit_bytes=60 << 20, collective_id=5, has_side_effects=True
        ),
        name="attend_back_scatter",
    )(query, keyval, probs, att, pairs, stats, *flat)
    dq, dkv, total, means, upw, downw, outw = results
    return dq, dkv, total - jnp.sum(means, -1, keepdims=True), (upw, downw, outw)


def token_close_kernel(
    dq_ref,
    dkv_ref,
    gategrad_ref,
    midgrad_ref,
    block_ref,
    scale1_ref,
    tail_ref,
    proj_ref,
    attn_ref,
    cond_ref,
    upw_ref,
    downw_ref,
    outw_ref,
    tokengrad_ref,
    qbias_ref,
    cbias_ref,
    units_ref,
    mix_s,
    condgrad_s,
    cond_s,
    proj_s,
):
    step = pl.program_id(0)
    block, width = dq_ref.shape
    blocks = mix_s.shape[0] // block
    samp = units_ref.shape[1]

    @pl.when(step == 0)
    def _():
        qbias_ref[...] = jnp.zeros_like(qbias_ref)
        cbias_ref[...] = jnp.zeros_like(cbias_ref)

    @pl.when(step < blocks)
    def _():
        rows = pl.ds(pl.multiple_of(step * block, block), block)
        dq = dq_ref[...]
        qbias_ref[...] += jnp.sum(dq, 0, keepdims=True)
        mix = jnp.concatenate([dq.astype(bf16), dkv_ref[...], gategrad_ref[...]], 1)
        mix_s[rows, :] = mix
        attn_grad = mm_nt(mix, proj_ref[...])
        normed, inv_std = norm_stats(block_ref[...])
        scale_one = sigmoid(scale1_ref[...])
        scale_grad = (attn_grad * normed * scale_one * (1.0 - scale_one)).astype(bf16)
        tokengrad_ref[...] = midgrad_ref[...] + norm_back(normed, inv_std, attn_grad * scale_one)
        shift_grad = attn_grad.astype(bf16)
        tail = tail_ref[...]
        condgrad_s[rows, :width] = scale_grad
        condgrad_s[rows, width : 2 * width] = shift_grad
        condgrad_s[rows, 2 * width :] = tail
        for part, low in ((scale_grad, 0), (shift_grad, width), (tail, 2 * width)):
            cbias_ref[:, low : low + part.shape[1]] += jnp.sum(
                part.astype(f32), 0, keepdims=True
            )

    @pl.when(step == blocks)
    def _():
        cond_rows = cond_ref[...].T
        for low in range(0, cond_s.shape[1], 768):
            cond_s[:, low : low + 768] = mm(cond_rows, condgrad_s[:, low : low + 768]).astype(bf16)
        attn_rows = attn_ref[...].T
        for low in range(0, proj_s.shape[1], 768):
            proj_s[:, low : low + 768] = mm(attn_rows, mix_s[:, low : low + 768]).astype(bf16)

    @pl.when(step >= blocks)
    def _():
        part = step - blocks
        left = pl.multiple_of(part * 384, LANES)
        proj = proj_s[:, pl.ds(left, 384)]
        rows = proj.shape[0] // samp
        for z in range(samp):
            units_ref[0, z, :rows, :384] = proj[z * rows : (z + 1) * rows]
            units_ref[0, z, :rows, 384:] = upw_ref[z * rows : (z + 1) * rows, :]
            units_ref[0, z, 192:240, :] = downw_ref[
                pl.ds(pl.multiple_of(z * 384 + part * 48, 16), 48), :
            ]
            low = pl.multiple_of(z * 96 + part // 4 * 48, 16)
            left = pl.multiple_of(part % 4 * 1152, LANES)
            units_ref[0, z, 240:288, :] = cond_s[pl.ds(low, 48), pl.ds(left, 768)]
            left = pl.multiple_of(part % 4 * 1152 + 768, LANES)
            units_ref[0, z, 288:336, :384] = cond_s[pl.ds(low, 48), pl.ds(left, 384)]
            low = pl.multiple_of(z * 192 + part // 2 * 48, 16)
            left = pl.multiple_of(part % 2 * 384, LANES)
            units_ref[0, z, 288:336, 384:] = outw_ref[pl.ds(low, 48), pl.ds(left, 384)]


def token_close(dq, dkv, gategrad, midgrad, block_in, cond_all, tail, proj, attn_in, cond_low, ready, samp, seq):
    samples, tokens, width = dq.shape
    rows = samples * tokens
    blocks = 4
    block = rows // blocks
    flat = lambda part: part.reshape(rows, part.shape[-1])
    upw, downw, outw = ready
    attn, cond = flat(attn_in), flat(cond_low)

    def early(lanes, column=0):
        return pl.BlockSpec((block, lanes), lambda g: (jnp.minimum(g, blocks - 1), column))

    late = lambda g: jnp.maximum(g - blocks, 0)
    return pl.pallas_call(
        token_close_kernel,
        out_shape=[
            jax.ShapeDtypeStruct((rows, width), f32),
            jax.ShapeDtypeStruct((1, width), f32),
            jax.ShapeDtypeStruct((1, 6 * width), f32),
            jax.ShapeDtypeStruct((seq, samp, UNIT, 768), bf16),
        ],
        grid=(blocks + seq,),
        in_specs=[
            early(width),
            early(2 * width),
            early(width),
            early(width),
            early(width),
            early(width),
            early(4 * width),
            whole(proj.shape),
            whole(attn.shape),
            whole(cond.shape),
            pl.BlockSpec((width, 384), lambda g: (0, late(g))),
            whole(downw.shape),
            whole(outw.shape),
        ],
        out_specs=[
            early(width),
            whole((1, width)),
            whole((1, 6 * width)),
            pl.BlockSpec((1, samp, UNIT, 768), lambda g: (late(g), 0, 0, 0)),
        ],
        scratch_shapes=[
            pltpu.VMEM((rows, 4 * width), bf16),
            pltpu.VMEM((rows, 6 * width), bf16),
            pltpu.VMEM((cond.shape[1], 6 * width), bf16),
            pltpu.VMEM((width, 4 * width), bf16),
        ],
        compiler_params=params(),
        name="token_close",
    )(
        flat(dq),
        flat(dkv),
        gategrad,
        midgrad,
        flat(block_in),
        flat(cond_all),
        tail,
        proj,
        attn,
        cond,
        upw,
        downw,
        outw,
    )


def to_blocks(array, width):
    return [array[:, low : low + width] for low in range(0, array.shape[1], width)]


def pack_blocks(arrays, width):
    parts = []
    for array in arrays:
        parts += to_blocks(array, width)
    return jnp.concatenate(parts, 0)


def unpack_blocks(packed, shapes, width):
    arrays, low = [], 0
    for rows, columns in shapes:
        parts = []
        for _ in range(columns // width):
            parts.append(packed[low : low + rows])
            low += rows
        arrays.append(jnp.concatenate(parts, 1) if len(parts) > 1 else parts[0])
    return arrays


def sum_shares(grads, extra):
    samp, seq = lax.axis_size("samp"), lax.axis_size("seq")
    width = grads[2].shape[1]
    shapes = [(grad.shape[0] // samp, grad.shape[1]) for grad in grads]
    packed = jnp.concatenate(
        [
            block.astype(bf16).reshape(samp, -1, width)
            for grad in grads
            for block in to_blocks(grad, width)
        ]
        + [extra.astype(bf16).reshape(samp, -1, width)],
        1,
    )
    rows = packed.shape[1]
    packed = packed.reshape(samp, seq, rows // seq, width).transpose(1, 0, 2, 3)
    part = lax.psum_scatter(packed, "seq", scatter_dimension=0, tiled=False)
    part = lax.psum_scatter(part, "samp", scatter_dimension=0, tiled=False)
    packed = lax.all_gather(part, "seq", axis=0, tiled=True).astype(f32)
    shares = unpack_blocks(packed, shapes, width)
    return shares, packed[sum(r * (c // width) for r, c in shapes) :]


def local(
    atom_input,
    token_input,
    atom_counts,
    key_offsets,
    atom_pairs,
    pair_features,
    single_features,
    noise_levels,
    noise_direction,
    atom_proj,
    atom_qbias,
    atom_pairw,
    atom_outw,
    atom_upw,
    atom_downw,
    pool_weight,
    cond_weight,
    cond_bias,
    token_proj,
    token_qbias,
    token_pairw,
    token_outw,
    token_upw,
    token_downw,
    cotangent,
):
    samp, seq = lax.axis_size("samp"), lax.axis_size("seq")
    seq_pos = lax.axis_index("seq")
    samples, slots, atom_width = atom_input.shape
    tokens, width = token_input.shape[1:]
    features = atom_pairs.shape[-1]

    tiny_own = jnp.concatenate(
        [
            atom_qbias,
            cond_bias,
            token_qbias,
            atom_pairw.reshape(-1),
            token_pairw.reshape(-1),
        ]
    )
    tiny_own = jnp.pad(tiny_own, (0, -tiny_own.size % (16 * LANES))).reshape(-1, LANES)
    large = (token_proj, token_upw, token_downw, cond_weight, token_outw)
    kernels = samples == 8 and WeightGather.fits([part.shape for part in large], samp, seq)
    up_pairs = [(i, i + 1) for i in range(seq - 1)]
    down_pairs = [(i + 1, i) for i in range(seq - 1)]
    if kernels:
        wide, down, tiny_all, ext = edges(
            (atom_proj, atom_upw, pool_weight, atom_outw, atom_downw), tiny_own, atom_input
        )
    else:
        wide_own = jnp.concatenate([atom_proj, atom_upw, pool_weight, atom_outw], 1)
        wide = lax.all_gather(wide_own, "samp", axis=0, tiled=True)
        down = lax.all_gather(atom_downw, "samp", axis=0, tiled=True)
        tiny_all = lax.all_gather(tiny_own, "samp", axis=0, tiled=True)
        before = lax.ppermute(atom_input[:, slots - RIM :], "seq", up_pairs)
        after = lax.ppermute(atom_input[:, :RIM], "seq", down_pairs)
        ext = jnp.concatenate([before, atom_input, after], 1)
    tiny_all = tiny_all.reshape(samp, -1)
    sizes = [atom_qbias.size, cond_bias.size, token_qbias.size, atom_pairw.size, token_pairw.size]
    cuts = [sum(sizes[:i]) for i in range(6)]
    tiny = [tiny_all[:, cuts[i] : cuts[i + 1]] for i in range(5)]
    atom_qb = tiny[0].reshape(1, -1).astype(f32)
    cond_b = tiny[1].reshape(-1)
    token_qb = tiny[2].reshape(-1)
    atom_pw = tiny[3].reshape(features, ATOM_HEADS)
    token_pw = tiny[4].reshape(-1, token_pairw.shape[1])

    rim_tokens = RIM // MAX_ATOMS
    counts = lax.dynamic_slice_in_dim(
        jnp.pad(atom_counts, (rim_tokens, rim_tokens)), seq_pos * tokens, tokens + 2 * rim_tokens
    )
    place = jnp.arange(MAX_ATOMS, dtype=jnp.int32)
    used = place[None, :] < counts[:, None]
    blocked = jnp.where(used, 0.0, masked_score).astype(f32).reshape(-1, 1)
    blocked = jnp.broadcast_to(blocked, (blocked.shape[0], LANES))
    own_counts = counts[rim_tokens : rim_tokens + tokens]
    share = used[rim_tokens : rim_tokens + tokens].astype(f32) / own_counts[:, None].astype(f32)
    share = jnp.broadcast_to(share.reshape(-1, 1), (slots, LANES))
    windows = slots // WIN_Q
    starts = jnp.arange(windows, dtype=jnp.int32) * WIN_Q + key_offsets + RIM
    pairs_t = atom_pairs.transpose(0, 1, 3, 2).reshape(windows, WIN_Q * features, WIN_K)
    eye = jnp.eye(WIN_Q, dtype=bool)
    spread = jnp.where(
        eye[None, :, :, None], atom_pw.T[:, None, None, :], jnp.zeros((), bf16)
    ).reshape(ATOM_HEADS * WIN_Q, WIN_Q * features)
    gather = WeightGather([part.shape for part in large], samp, seq) if kernels else None
    pooled, stored, fulls = atom_forward(
        ext,
        starts,
        pairs_t,
        spread,
        blocked,
        share,
        wide,
        down,
        atom_qb,
        gather,
        large if kernels else (),
    )
    if not kernels:
        fulls = [lax.all_gather(part, "samp", axis=0, tiled=True) for part in large]
    proj_w, up_w, down_w, cond_w, out_w = fulls
    pair_w = token_pw.T
    if kernels:
        block_in, cond_low, cond_all, attn_in, queries, keyval_own, gating = token_open(
            noise_levels,
            noise_direction,
            single_features,
            pooled,
            token_input,
            cond_w,
            cond_b.astype(f32),
            proj_w,
            token_qb.astype(f32),
        )
        queries = queries.reshape(token_input.shape)
        keyval_own = keyval_own.reshape(samples, tokens, 2 * width)
    else:
        block_in = token_input.astype(f32) + pooled

        noise_feature = 0.25 * jnp.log(noise_levels / sigma_data)
        cond_rows = (
            single_features.astype(f32)[None]
            + noise_feature[:, None, None] * noise_direction[None, None, :]
        )
        cond_low = norm_stats(cond_rows)[0].astype(bf16)
        cond_all = dot_last(cond_low, cond_w) + cond_b.astype(f32)
        parts = [cond_all[..., i * width : (i + 1) * width] for i in range(6)]

        normed_in, inv_in = norm_stats(block_in)
        attn_in = (jax.nn.sigmoid(parts[0]) * normed_in + parts[1]).astype(bf16)
        mix = dot_last(attn_in, proj_w)
        queries = (mix[..., :width] + token_qb.astype(f32)).astype(bf16)
        keyval_own = mix[..., width : 3 * width].astype(bf16)
        gating = mix[..., 3 * width :]

    if kernels:
        (probs, keyval, stats), rows_out = gather_attend(
            queries,
            keyval_own,
            pair_features,
            pair_w,
            gating,
            block_in,
            cond_all,
            cotangent,
            out_w,
            up_w,
            down_w,
        )
        (
            block_out,
            ffn_in,
            upper_grad,
            hidden,
            branch_two_low,
            gated_low,
            branch_low,
            attend_low,
            gating_grad,
            mid_grad,
            cond_tail,
        ) = rows_out
        query_grad, keyval_grad, pairw_grad, ready = attend_back_scatter(
            queries,
            keyval,
            probs,
            attend_low.reshape(queries.shape),
            pair_features,
            stats,
            ffn_in,
            upper_grad,
            hidden,
            branch_two_low,
            gated_low,
            branch_low,
        )
        token_grad, token_qb_grad, cond_b_grad, grad_units = token_close(
            query_grad,
            keyval_grad,
            gating_grad,
            mid_grad,
            block_in,
            cond_all,
            cond_tail,
            proj_w,
            attn_in,
            cond_low,
            ready,
            samp,
            seq,
        )
        block_out = block_out.reshape(token_input.shape)
        token_grad = token_grad.reshape(token_input.shape)
        token_qb_grad, cond_b_grad = token_qb_grad.reshape(-1), cond_b_grad.reshape(-1)
    else:
        bias = pair_bias(pair_features, pair_w)
        keyval = lax.all_gather(keyval_own, "seq", axis=0, tiled=False)
        attend, probs = token_attention(queries, keyval, bias)
        sig_gate = jax.nn.sigmoid(gating)
        gated_low = (attend * sig_gate).astype(bf16)
        branch = dot_last(gated_low, out_w)
        gate_one = jax.nn.sigmoid(parts[2])
        mid = block_in + gate_one * branch
        normed_mid, inv_mid = norm_stats(mid)
        scale_two = jax.nn.sigmoid(parts[3])
        ffn_in = (scale_two * normed_mid + parts[4]).astype(bf16)
        upper = dot_last(ffn_in, up_w)
        hidden_width = down_w.shape[0]
        first_half, second_half = upper[..., :hidden_width], upper[..., hidden_width:]
        sig_first = jax.nn.sigmoid(first_half)
        hidden = (first_half * sig_first * second_half).astype(bf16)
        branch_two = dot_last(hidden, down_w)
        gate_two = jax.nn.sigmoid(parts[5])
        block_out = (mid + gate_two * branch_two).astype(bf16)

        out_grad = cotangent.astype(f32)
        branch_two_low = (out_grad * gate_two).astype(bf16)
        gate_two_grad = out_grad * branch_two * gate_two * (1.0 - gate_two)
        hidden_grad = dot_back(branch_two_low, down_w)
        first_grad = hidden_grad * second_half * sig_first * (1.0 + first_half * (1.0 - sig_first))
        second_grad = hidden_grad * first_half * sig_first
        upper_grad = jnp.concatenate([first_grad, second_grad], -1).astype(bf16)
        ffn_grad = dot_back(upper_grad, up_w)
        scale_two_grad = ffn_grad * normed_mid * scale_two * (1.0 - scale_two)
        mid_grad = out_grad + norm_back(normed_mid, inv_mid, ffn_grad * scale_two)
        branch_low = (mid_grad * gate_one).astype(bf16)
        gate_one_grad = mid_grad * branch * gate_one * (1.0 - gate_one)
        gated_grad = dot_back(branch_low, out_w)
        attend_low = (gated_grad * sig_gate).astype(bf16)
        gating_grad = gated_grad * attend * sig_gate * (1.0 - sig_gate)
        query_grad, keyval_part, bias_grad = token_attention_back(queries, keyval, probs, attend_low)
        keyval_grad = lax.psum_scatter(keyval_part, "seq", scatter_dimension=0, tiled=False)
        pairw_grad = pair_grad(pair_features, bias_grad, pair_w)
        mix_grad = jnp.concatenate(
            [query_grad.astype(bf16), keyval_grad, gating_grad.astype(bf16)], -1
        )
        token_qb_grad = jnp.sum(query_grad, (0, 1))
        attn_in_grad = dot_back(mix_grad, proj_w)
        scale_one = jax.nn.sigmoid(parts[0])
        scale_one_grad = attn_in_grad * normed_in * scale_one * (1.0 - scale_one)
        token_grad = mid_grad + norm_back(normed_in, inv_in, attn_in_grad * scale_one)
        cond_grad = jnp.concatenate(
            [scale_one_grad, attn_in_grad, gate_one_grad, scale_two_grad, ffn_grad, gate_two_grad], -1
        ).astype(bf16)
        cond_b_grad = jnp.sum(cond_grad.astype(f32), (0, 1))
    pairw_grad = pairw_grad.T

    if kernels:
        atom_grad, qb_grad, pairw_stack, pairw_mean, small, units = atom_backward_sum(
            token_grad,
            starts,
            stored,
            atom_input,
            pairs_t,
            share,
            wide,
            down,
            GradSum([part.shape for part in large]),
            grad_units,
        )
    else:
        mix_part, own, left, right, atom_mid_grad, *atom_totals = atom_backward(
            token_grad, starts, stored, pairs_t, share, wide, down
        )
        from_right = lax.ppermute(left, "seq", down_pairs)
        from_left = lax.ppermute(right, "seq", up_pairs)
        atom_grad, atom_proj_grad = atom_input_backward(
            atom_input, mix_part, own, from_left, from_right, atom_mid_grad, wide
        )
        qb_grad, outw_grad, upw_grad, downw_grad, pool_grad, pairw_stack, pairw_mean = atom_totals
    diagonal = pairw_stack.reshape(ATOM_HEADS, WIN_Q, WIN_Q, features)
    atom_pw_grad = (
        jnp.sum(jnp.where(eye[None, :, :, None], diagonal, 0.0), (1, 2)).T
        - jnp.sum(pairw_mean.reshape(ATOM_HEADS, -1), 1)[None, :]
    )

    rows = atom_width // samp
    tiny_parts = [qb_grad.reshape(-1), atom_pw_grad, cond_b_grad, token_qb_grad, pairw_grad]
    tiny_flat = jnp.concatenate([part.astype(bf16).reshape(samp, -1) for part in tiny_parts], 1)
    spare = atom_width
    tiny_flat = jnp.pad(tiny_flat, ((0, 0), (0, rows * spare - tiny_flat.shape[1])))
    tiny_rows = tiny_flat.reshape(samp, rows, spare)
    if kernels:
        total, units = small_sums(small, tiny_rows, units)
        *shares, pool_out, proj_out, downw_out, upw_out, outw_out, tiny_out = unpack(
            units, total, [part.shape for part in large], rows, atom_width
        )
    else:
        lanes = lambda part: part.astype(bf16).reshape(samp, rows, -1)
        downw_two = downw_grad.astype(bf16).reshape(samp, 2, rows, atom_width)
        small = jnp.stack(
            [
                lanes(pool_grad),
                jnp.concatenate([lanes(atom_proj_grad), downw_two[:, 0], downw_two[:, 1]], -1),
                jnp.concatenate([lanes(upw_grad), lanes(outw_grad), tiny_rows], -1),
                jnp.zeros((samp, rows, width), bf16),
            ],
            1,
        )
        factors = [
            (attn_in, mix_grad),
            (ffn_in, upper_grad),
            (hidden, branch_two_low),
            (cond_low, cond_grad),
            (gated_low, branch_low),
        ]
        shares, rest = sum_shares(
            [weight_grad(*pair) for pair in factors], small.reshape(-1, width)
        )
        rest = rest.reshape(-1, width)
        pool_out, second, third = rest[:rows], rest[rows : 2 * rows], rest[2 * rows : 3 * rows]
        low = 4 * atom_width
        proj_out = second[:, :low]
        downw_out = jnp.concatenate(
            [second[:, low : low + atom_width], second[:, low + atom_width :]], 0
        )
        upw_out, outw_out = third[:, :low], third[:, low : low + atom_width]
        tiny_out = third[:, low + atom_width :]
    tiny_out = tiny_out.reshape(-1)
    tiny_shares, cut = [], 0
    for part in tiny_parts:
        size = part.size // samp
        shape = (part.shape[0] // samp,) + part.shape[1:]
        tiny_shares.append(tiny_out[cut : cut + size].reshape(shape))
        cut += size
    return (
        block_out,
        atom_grad,
        token_grad,
        proj_out,
        tiny_shares[0],
        tiny_shares[1],
        outw_out,
        upw_out,
        downw_out,
        pool_out,
        shares[3],
        tiny_shares[2],
        shares[0],
        tiny_shares[3],
        tiny_shares[4],
        shares[4],
        shares[1],
        shares[2],
    )


def solution(mesh):
    in_specs = (
        P("samp", "seq", None),
        P("samp", "seq", None),
        P(),
        P("seq"),
        P("seq", None, None, None),
        P("seq", None, None),
        P("seq", None),
        P("samp"),
        P(),
        P("samp", None),
        P("samp"),
        P("samp", None),
        P("samp", None),
        P("samp", None),
        P("samp", None),
        P("samp", None),
        P("samp", None),
        P("samp"),
        P("samp", None),
        P("samp"),
        P("samp", None),
        P("samp", None),
        P("samp", None),
        P("samp", None),
        P("samp", "seq", None),
    )
    out_specs = (
        P("samp", "seq", None),
        P("samp", "seq", None),
        P("samp", "seq", None),
        P("samp", None),
        P("samp"),
        P("samp", None),
        P("samp", None),
        P("samp", None),
        P("samp", None),
        P("samp", None),
        P("samp", None),
        P("samp"),
        P("samp", None),
        P("samp"),
        P("samp", None),
        P("samp", None),
        P("samp", None),
        P("samp", None),
    )
    return jax.shard_map(local, mesh=mesh, in_specs=in_specs, out_specs=out_specs, check_vma=False)
```

```python
import functools

import jax
import jax.numpy as jnp
from jax import lax
from jax.experimental import pallas as pl
from jax.experimental.pallas import tpu as pltpu
from jax.sharding import PartitionSpec as P

MAX_ATOMS = 8
WIN_Q = 32
WIN_K = 128
ATOM_HEADS = 4
RIM = 96
LANES = 128

norm_eps = 1e-05
sigma_data = 16.0
masked_score = -1000000000.0
bf16 = jnp.bfloat16
f32 = jnp.float32
vmem_bytes = 56 << 20


def dot_last(left_op, right_op):
    return jnp.einsum("...k,kn->...n", left_op, right_op, preferred_element_type=f32)


def dot_back(grad_op, weight):
    return jnp.einsum("...n,kn->...k", grad_op, weight, preferred_element_type=f32)


def weight_grad(left_op, grad_op):
    flat_left = left_op.reshape(-1, left_op.shape[-1])
    flat_grad = grad_op.reshape(-1, grad_op.shape[-1])
    return jnp.einsum("rk,rn->kn", flat_left, flat_grad, preferred_element_type=f32)


def mm(left_op, right_op):
    return lax.dot_general(left_op, right_op, (((1,), (0,)), ((), ())), preferred_element_type=f32)


def mm_nt(left_op, right_op):
    return lax.dot_general(left_op, right_op, (((1,), (1,)), ((), ())), preferred_element_type=f32)


def mm_tn(left_op, right_op):
    return lax.dot_general(left_op, right_op, (((0,), (0,)), ((), ())), preferred_element_type=f32)


def norm_stats(operand):
    center = operand - jnp.mean(operand, -1, keepdims=True)
    inv_std = lax.rsqrt(jnp.mean(center * center, -1, keepdims=True) + norm_eps)
    return (center * inv_std, inv_std)


def norm_back(normed, inv_std, grad_op):
    return inv_std * (
        grad_op
        - jnp.mean(grad_op, -1, keepdims=True)
        - normed * jnp.mean(grad_op * normed, -1, keepdims=True)
    )


def sigmoid(operand):
    return 1.0 / (1.0 + jnp.exp(-operand))


def whole(shape):
    return pl.BlockSpec(shape, lambda *_: (0,) * len(shape))


def per_sample(shape):
    return pl.BlockSpec((1,) + shape, lambda b, *_: (b,) + (0,) * len(shape))


def params():
    return pltpu.CompilerParams(vmem_limit_bytes=vmem_bytes)


def square_sums(ones_op, squares):
    upper = squares.astype(bf16)
    lower = (squares - upper.astype(f32)).astype(bf16)
    return upper, lower


def head_masks(count, width, heads, head_dim, first):
    row = lax.broadcasted_iota(jnp.int32, (heads * count, width), 0)
    lane = lax.broadcasted_iota(jnp.int32, (heads * count, width), 1)
    inside = (lane - first) // head_dim == row // count
    return jnp.where(inside & (lane >= first), 1.0, 0.0).astype(bf16)


def head_stack(rows, heads, head_dim, first, masks=None):
    if masks is None:
        masks = head_masks(rows.shape[0], rows.shape[1], heads, head_dim, first)
    return jnp.concatenate([rows] * heads, 0) * masks


def head_fold(stacked, heads, head_dim, first):
    count = stacked.shape[0] // heads
    lane = lax.broadcasted_iota(jnp.int32, (count, stacked.shape[1]), 1)
    total = jnp.zeros((count, stacked.shape[1]), f32)
    for head in range(heads):
        low = first + head * head_dim
        part = stacked[head * count : (head + 1) * count]
        total = jnp.where((lane >= low) & (lane < low + head_dim), part, total)
    return total


MESH = pl.DeviceIdType.MESH


def places():
    samp_pos, seq_pos = lax.axis_index("samp"), lax.axis_index("seq")
    core, across, along = seq_pos % 2, seq_pos // 2 % 2, seq_pos // 4

    def index(along, across, core):
        return (along * 2 + across) * 2 + core

    return (
        samp_pos,
        seq_pos,
        index(along, across, 1 - core),
        index(along, 1 - across, core),
        index(1 - along, across, core),
        index(1 - along, 1 - across, core),
    )


def remote(source, target, send_sem, recv_sem, device):
    return pltpu.make_async_remote_copy(
        src_ref=source,
        dst_ref=target,
        send_sem=send_sem,
        recv_sem=recv_sem,
        device_id=device,
        device_id_type=MESH,
    )


def greet(devices):
    barrier = pltpu.get_barrier_semaphore()
    for device in devices:
        pl.semaphore_signal(barrier, inc=1, device_id=device, device_id_type=MESH)
    pl.semaphore_wait(barrier, len(devices))


def pick(position, values):
    chosen = values[0]
    for index, value in enumerate(values[1:], 1):
        chosen = jnp.where(position == index, value, chosen)
    return chosen


class WeightGather:
    def __init__(self, shapes, samp, seq):
        self.shapes, self.samp, self.seq = shapes, samp, seq
        self.splits = [self.split(shape, seq) for shape in shapes]

    @staticmethod
    def split(shape, parts):
        rows, columns = shape
        for down in (1, 2, 4, 8):
            across = parts // down
            if rows % (16 * down) == 0 and columns % (LANES * across) == 0:
                return (down, across)
        return None

    @staticmethod
    def fits(shapes, samp, seq):
        return (
            samp == 4
            and seq == 8
            and len(shapes) == 5
            and all(WeightGather.split(shape, seq) for shape in shapes)
        )

    def full_shapes(self):
        return [(rows * self.samp, columns) for rows, columns in self.shapes]

    def scratch(self):
        count = len(self.shapes)
        return [
            pltpu.SemaphoreType.DMA((9, self.samp, count)),
            pltpu.SemaphoreType.DMA((8, self.samp, count)),
            pltpu.SemaphoreType.DMA((2, count)),
        ] + [pltpu.VMEM(shape, bf16) for shape in self.shapes]

    def params(self):
        return pltpu.CompilerParams(
            vmem_limit_bytes=vmem_bytes, collective_id=1, has_side_effects=True
        )

    def cell(self, ref, weight, origin, part):
        rows, columns = self.shapes[weight]
        down, across = self.splits[weight]
        height, width = rows // down, columns // across
        low = origin * rows + part // across * height
        left = part % across * width
        return ref.at[
            pl.ds(pl.multiple_of(low, 16), height), pl.ds(pl.multiple_of(left, LANES), width)
        ]

    def origin(self, position, turn):
        order = [sorted(range(self.samp), key=lambda o: (abs(o - z), o)) for z in range(self.samp)]
        if isinstance(turn, int):
            return pick(position, [order[z][turn] for z in range(self.samp)])
        return pick(
            position, [pick(turn, [order[z][t] for t in range(self.samp)]) for z in range(self.samp)]
        )

    def own_copies(self, shards, fulls, own, held, stage):
        z = places()[0]
        copies = []
        for w, shard in enumerate(shards):
            rows = self.shapes[w][0]
            target = fulls[w].at[pl.ds(pl.multiple_of(z * rows, 16), rows), :]
            ends = (shard, held[w]) if stage == 0 else (held[w], target)
            copies.append(pltpu.make_async_copy(*ends, own.at[stage, w]))
        return copies

    def start(self, shards, fulls, send, recv, own, held):
        z, me, sib, xn, yn, dg = places()
        above, below = lax.rem(z + 1, self.samp), lax.rem(z + self.samp - 1, self.samp)
        greet([(z, sib), (z, xn), (z, yn), (above, me), (below, me)])
        for w, shard in enumerate(shards):
            source = self.cell(shard, w, 0, me)
            target = self.cell(fulls[w], w, z, me)

            @pl.when(z < self.samp - 1)
            def _():
                remote(source, target, send.at[0, 0, w], recv.at[0, z, w], (z + 1, me)).start()

            @pl.when(z > 0)
            def _():
                remote(source, target, send.at[1, 0, w], recv.at[0, z, w], (z - 1, me)).start()

        for copy in self.own_copies(shards, fulls, own, held, 0):
            copy.start()

    def place_own(self, shards, fulls, own, held):
        for copy in self.own_copies(shards, fulls, own, held, 0):
            copy.wait()
        for copy in self.own_copies(shards, fulls, own, held, 1):
            copy.start()

    def share_own(self, turn, origin, sources, fulls, send, recv):
        z, me, sib, xn, yn, dg = places()
        for kind, part in ((2, xn), (3, yn), (5, sib)):
            for w, source in enumerate(sources):
                target = self.cell(fulls[w], w, origin, me)
                arrival = {2: 1, 3: 2, 5: 4}[kind]
                remote(
                    source, target, send.at[kind, turn, w], recv.at[arrival, origin, w], (z, part)
                ).start()

    def wait_cell(self, fulls, recv, kind, w, origin, part, device):
        target = self.cell(fulls[w], w, origin, part)
        remote(target, target, recv.at[kind, origin, w], recv.at[kind, origin, w], device).wait_recv()

    def issue(self, turn, fulls, send, recv):
        z, me, sib, xn, yn, dg = places()
        origin = self.origin(z, turn)
        count = len(self.shapes)
        for w in range(count):
            self.wait_cell(fulls, recv, 0, w, origin, me, (z, sib))
        for w in range(count):
            cell = self.cell(fulls[w], w, origin, me)

            @pl.when((origin < z) & (z < self.samp - 1))
            def _():
                remote(cell, cell, send.at[0, turn, w], recv.at[0, origin, w], (z + 1, me)).start()

            @pl.when((origin > z) & (z > 0))
            def _():
                remote(cell, cell, send.at[1, turn, w], recv.at[0, origin, w], (z - 1, me)).start()

        cells = [self.cell(fulls[w], w, origin, me) for w in range(count)]
        self.share_own(turn, origin, cells, fulls, send, recv)

    def passed_on(self, w):
        return w in (0, 3)

    def finish(self, turn, fulls, send, recv):
        z, me, sib, xn, yn, dg = places()
        origin = self.origin(z, turn)
        count = len(self.shapes)
        for kind, part, other, by in ((1, xn, yn, True), (2, yn, xn, False)):
            for w in range(count):
                self.wait_cell(fulls, recv, kind, w, origin, part, (z, part))
                cell = self.cell(fulls[w], w, origin, part)
                if self.passed_on(w) == by:
                    remote(
                        cell, cell, send.at[4, turn, w], recv.at[3, origin, w], (z, other)
                    ).start()
                remote(
                    cell, cell, send.at[5 + kind, turn, w], recv.at[4 + kind, origin, w], (z, sib)
                ).start()

    def diagonal(self, turn, fulls, send, recv):
        z, me, sib, xn, yn, dg = places()
        origin = self.origin(z, turn)
        for w in range(len(self.shapes)):
            self.wait_cell(fulls, recv, 3, w, origin, dg, (z, yn))
            cell = self.cell(fulls[w], w, origin, dg)
            remote(cell, cell, send.at[8, turn, w], recv.at[7, origin, w], (z, sib)).start()

    def drain(self, shards, fulls, send, recv, own, held):
        z, me, sib, xn, yn, dg = places()
        count = len(self.shapes)

        def sent(kind, turn, w):
            cell = self.cell(fulls[w], w, 0, me)
            remote(cell, cell, send.at[kind, turn, w], recv.at[0, 0, w], (z, sib)).wait_send()

        def one(turn, carry):
            origin = self.origin(z, turn)
            for w in range(count):
                for kind in range(2, 9):
                    sent(kind, turn, w)

                @pl.when((z < self.samp - 1) & (origin < z))
                def _():
                    sent(0, turn, w)

                @pl.when((z > 0) & (origin > z))
                def _():
                    sent(1, turn, w)

                for kind in range(4, 8):
                    self.wait_cell(fulls, recv, kind, w, origin, sib, (z, sib))
            return carry

        lax.fori_loop(1, self.samp, one, 0)
        for w in range(count):

            @pl.when(z < self.samp - 1)
            def _():
                sent(0, 0, w)

            @pl.when(z > 0)
            def _():
                sent(1, 0, w)

        for copy in self.own_copies(shards, fulls, own, held, 1):
            copy.wait()

    def step(self, sample, shards, fulls, send, recv, own, *held):
        @pl.when(sample == 0)
        def _():
            self.start(shards, fulls, send, recv, own, held)

        @pl.when(sample == 1)
        def _():
            self.place_own(shards, fulls, own, held)

        for at, turn in ((2, 1), (3, 2), (5, 3)):

            @pl.when(sample == at)
            def _():
                self.issue(turn, fulls, send, recv)

        for at, turn in ((4, 1), (5, 2), (7, 3)):

            @pl.when(sample == at)
            def _():
                self.finish(turn, fulls, send, recv)

        for at, turn in ((5, 1), (7, 2)):

            @pl.when(sample == at)
            def _():
                self.diagonal(turn, fulls, send, recv)

    def last(self, sample, shards, fulls, send, recv, own, *held):
        @pl.when(sample == pl.num_programs(0) - 1)
        def _():
            self.diagonal(3, fulls, send, recv)
            self.drain(shards, fulls, send, recv, own, held)


def edge_kernel(
    samp,
    seq,
    proj_ref,
    upw_ref,
    pool_ref,
    outw_ref,
    down_ref,
    tiny_ref,
    rows_ref,
    wide_out,
    down_out,
    tiny_out,
    ext_out,
    held,
    send,
    recv,
):
    z, me = lax.axis_index("samp"), lax.axis_index("seq")
    sib = places()[2]
    core = me % 2
    samples, slots, width = rows_ref.shape
    right, left = lax.rem(me + 1, seq), lax.rem(me + seq - 1, seq)
    others = [lax.rem(z + hop, samp) for hop in range(1, samp)]
    greet([(other, me) for other in others] + [(z, sib), (z, right), (z, left)])
    low = 0
    for ref in (proj_ref, upw_ref, pool_ref, outw_ref):
        held[:, low : low + ref.shape[1]] = ref[...]
        low += ref.shape[1]

    def half(out, origin, part):
        rows = out.shape[0] // samp
        first = origin * rows + part * (rows // 2)
        return out.at[pl.ds(pl.multiple_of(first, 16), rows // 2), :]

    def own_half(ref):
        rows = ref.shape[0]
        return ref.at[pl.ds(pl.multiple_of(core * (rows // 2), 16), rows // 2), :]

    def tiny_place(origin):
        rows = tiny_ref.shape[0]
        return tiny_out.at[pl.ds(pl.multiple_of(origin * rows, 16), rows), :]

    copies = []
    for hop, other in enumerate(others):
        device = (other, me)
        copies.append(
            [
                remote(own_half(held), half(wide_out, z, core), send.at[0, hop], recv.at[0, hop], device),
                remote(own_half(down_ref), half(down_out, z, core), send.at[1, hop], recv.at[1, hop], device),
                remote(tiny_ref, tiny_place(z), send.at[2, hop], recv.at[2, hop], device),
            ]
        )
    for group in copies:
        for copy in group:
            copy.start()
    before, after = ext_out.at[:, :RIM, :], ext_out.at[:, RIM + slots :, :]
    to_right = remote(rows_ref.at[:, slots - RIM :, :], before, send.at[5, 0], recv.at[5, 0], (z, right))
    to_left = remote(rows_ref.at[:, :RIM, :], after, send.at[5, 1], recv.at[5, 1], (z, left))
    first, last = me == 0, me == seq - 1

    @pl.when(~last)
    def _():
        to_right.start()

    @pl.when(~first)
    def _():
        to_left.start()

    @pl.when(first)
    def _():
        ext_out[:, :RIM, :] = jnp.zeros((samples, RIM, width), bf16)

    @pl.when(last)
    def _():
        ext_out[:, RIM + slots :, :] = jnp.zeros((samples, RIM, width), bf16)

    def move(sample, carry):
        ext_out[sample, RIM : RIM + slots, :] = rows_ref[sample]
        return carry

    lax.fori_loop(0, samples, move, 0)
    for ref, out in ((held, wide_out), (down_ref, down_out), (tiny_ref, tiny_out)):
        rows = ref.shape[0]
        out[pl.ds(pl.multiple_of(z * rows, 16), rows), :] = ref[...]
    passed = []
    for hop in range(samp - 1):
        origin = lax.rem(z + samp - 1 - hop, samp)
        for kind, out in ((0, wide_out), (1, down_out)):
            copies[hop][kind].wait_recv()
            cell = half(out, origin, core)
            copy = remote(cell, cell, send.at[3 + kind, hop], recv.at[3 + kind, hop], (z, sib))
            copy.start()
            passed.append(copy)
    for hop in range(samp - 1):
        copies[hop][2].wait_recv()
        for copy in copies[hop]:
            copy.wait_send()
    for copy in passed:
        copy.wait()

    @pl.when(~last)
    def _():
        to_right.wait_send()
        to_left.wait_recv()

    @pl.when(~first)
    def _():
        to_left.wait_send()
        to_right.wait_recv()


def edges(weights, tiny_own, rows):
    samp, seq = lax.axis_size("samp"), lax.axis_size("seq")
    samples, slots, width = rows.shape
    place = pl.BlockSpec(memory_space=pltpu.VMEM)
    lanes = sum(part.shape[1] for part in weights[:4])
    return pl.pallas_call(
        functools.partial(edge_kernel, samp, seq),
        out_shape=[
            jax.ShapeDtypeStruct((samp * weights[0].shape[0], lanes), bf16),
            jax.ShapeDtypeStruct((samp * weights[4].shape[0], weights[4].shape[1]), bf16),
            jax.ShapeDtypeStruct((samp * tiny_own.shape[0], tiny_own.shape[1]), bf16),
            jax.ShapeDtypeStruct((samples, slots + 2 * RIM, width), bf16),
        ],
        in_specs=[place] * 7,
        out_specs=[place] * 4,
        scratch_shapes=[
            pltpu.VMEM((weights[0].shape[0], lanes), bf16),
            pltpu.SemaphoreType.DMA((6, samp)),
            pltpu.SemaphoreType.DMA((6, samp)),
        ],
        compiler_params=pltpu.CompilerParams(
            vmem_limit_bytes=vmem_bytes, collective_id=0, has_side_effects=True
        ),
        name="edges",
    )(*weights, tiny_own, rows)


UNIT = 336


def add_into(target, source, lanes=slice(None), rows=48):
    def one(step, carry):
        part = pl.ds(pl.multiple_of(step * rows, 16), rows)
        target[part, lanes] = target[part, lanes] + source[part, :]
        return carry

    lax.fori_loop(0, target.shape[0] // rows, one, 0)


class GradSum:
    head, tail, full = slice(0, 384), slice(384, 768), slice(0, 768)

    def __init__(self, shapes):
        self.shapes = list(shapes)

    def scratch(self):
        half = (UNIT, 384)
        dma = pltpu.SemaphoreType.DMA
        return [
            pltpu.VMEM((4, 4, UNIT, 768), bf16),
            pltpu.VMEM((4, 4, UNIT, 768), bf16),
            pltpu.VMEM((4, 2) + half, bf16),
            pltpu.VMEM((4, 2) + half, bf16),
            pltpu.VMEM((4,) + half, bf16),
            pltpu.VMEM((4,) + half, bf16),
            pltpu.VMEM((3, UNIT, 768), bf16),
            pltpu.VMEM((UNIT, 768), bf16),
            dma((4, 4)),
            dma((4, 4)),
            dma((4, 4)),
            dma((4, 4)),
            dma((4, 4)),
            dma((4, 2)),
            dma((4, 2)),
            dma((3,)),
            dma((3,)),
            dma((3,)),
            dma((3,)),
            dma,
        ]

    def params(self):
        return pltpu.CompilerParams(
            vmem_limit_bytes=vmem_bytes, collective_id=2, has_side_effects=True
        )

    def bind(
        self, grads, shares, mine, theirs, from_x, from_y, last_x, last_y, planes, own_share, *sems
    ):
        self.grads, self.shares, self.own_share = grads, shares, own_share
        self.mine, self.theirs, self.from_x, self.from_y = mine, theirs, from_x, from_y
        self.last_x, self.last_y, self.planes = last_x, last_y, planes
        (
            self.s_sib,
            self.r_sib,
            self.s_own,
            self.s_one,
            self.r_one,
            self.s_two,
            self.r_two,
            self.s_z,
            self.r_z,
            self.s_share,
            self.r_share,
            self.s_out,
        ) = sems
        self.z, self.me, self.sib, self.xn, self.yn, self.dg = places()
        self.core, self.chip = self.me % 2, self.me // 2
        self.chip_x, self.chip_y, self.chip_d = self.xn // 2, self.yn // 2, self.dg // 2
        order = [[p ^ hop for hop in (2, 3, 1, 0)] for p in range(4)]
        self.plane = [pick(self.z, [order[p][r] for p in range(4)]) for r in range(4)]

    def there(self, r, j):
        return remote(
            self.grads.at[2 * j + 1 - self.core, self.plane[r]],
            self.theirs.at[r, j],
            self.s_sib.at[r, j],
            self.r_sib.at[r, j],
            (self.z, self.sib),
        )

    def here(self, r, j):
        return pltpu.make_async_copy(
            self.grads.at[2 * j + self.core, self.plane[r]], self.mine.at[r, j], self.s_own.at[r, j]
        )

    def one(self, r, k):
        chip = (self.chip_x, self.chip_d, self.chip_y, self.chip_d)[k]
        lanes = self.head if k < 2 else self.tail
        target = (self.from_x if k < 2 else self.from_y).at[r, k % 2]
        device = (self.z, self.xn if k < 2 else self.yn)
        return remote(
            self.mine.at[r, chip, :, lanes], target, self.s_one.at[r, k], self.r_one.at[r, k], device
        )

    def two(self, r, k):
        chip, lanes, target, device = (
            (self.chip_y, self.head, self.last_y, self.yn),
            (self.chip_x, self.tail, self.last_x, self.xn),
        )[k]
        return remote(
            self.mine.at[r, chip, :, lanes],
            target.at[r],
            self.s_two.at[r, k],
            self.r_two.at[r, k],
            (self.z, device),
        )

    def across(self, r):
        return remote(
            self.mine.at[r, self.chip],
            self.planes.at[r],
            self.s_z.at[r],
            self.r_z.at[r],
            (self.plane[r], self.me),
        )

    def keep(self):
        return pltpu.make_async_copy(self.own_share, self.shares.at[self.me], self.s_out)

    def share(self, kind):
        device = (self.xn, self.yn, self.sib)[kind]
        return remote(
            self.own_share,
            self.shares.at[self.me],
            self.s_share.at[kind],
            self.r_share.at[kind],
            (self.z, device),
        )

    def shared(self, kind):
        part = self.shares.at[(self.xn, self.yn, self.sib)[kind]]
        return remote(part, part, self.s_share.at[kind], self.r_share.at[kind], (self.z, self.sib))

    def begin(self, r):
        for j in range(4):
            self.there(r, j).start()
            self.here(r, j).start()

    def pairs(self, r):
        for j in range(4):
            self.there(r, j).wait_recv()
            self.here(r, j).wait()
        for j in range(4):
            add_into(self.mine.at[r, j], self.theirs.at[r, j])
        for k in range(4):
            self.one(r, k).start()

    def middle(self, r):
        self.one(r, 1).wait_recv()
        add_into(self.mine.at[r, self.chip_y], self.from_x.at[r, 1], self.head)
        self.two(r, 0).start()
        self.one(r, 3).wait_recv()
        add_into(self.mine.at[r, self.chip_x], self.from_y.at[r, 1], self.tail)
        self.two(r, 1).start()
        self.one(r, 0).wait_recv()
        add_into(self.mine.at[r, self.chip], self.from_x.at[r, 0], self.head)
        self.one(r, 2).wait_recv()
        add_into(self.mine.at[r, self.chip], self.from_y.at[r, 0], self.tail)

    def finish(self, r):
        self.two(r, 0).wait_recv()
        add_into(self.mine.at[r, self.chip], self.last_y.at[r], self.head)
        self.two(r, 1).wait_recv()
        add_into(self.mine.at[r, self.chip], self.last_x.at[r], self.tail)
        if r < 3:
            self.across(r).start()

    def total(self):
        for r in range(3):
            self.across(r).wait_recv()

        def one(step, carry):
            rows = pl.ds(pl.multiple_of(step * 48, 16), 48)
            both = self.mine[3, self.chip, rows, :].astype(f32)
            for r in range(3):
                both += self.planes[r, rows, :].astype(f32)
            self.own_share[rows, :] = both.astype(bf16)
            return carry

        lax.fori_loop(0, UNIT // 48, one, 0)
        for kind in range(3):
            self.share(kind).start()
        self.keep().start()

    def collect(self):
        self.keep().wait()
        for kind in range(3):
            self.shared(kind).wait_recv()
        for kind in range(3):
            self.share(kind).wait_send()
        for r in range(4):
            for j in range(4):
                self.there(r, j).wait_send()
                self.one(r, j).wait_send()
            for k in range(2):
                self.two(r, k).wait_send()
            if r < 3:
                self.across(r).wait_send()

    def hello(self):
        greet(
            [(self.z, self.sib), (self.z, self.xn), (self.z, self.yn)]
            + [(self.plane[r], self.me) for r in range(3)]
            + [(self.z, lax.rem(self.me + 1, 8)), (self.z, lax.rem(self.me + 7, 8))]
        )
        self.begin(0)
        self.begin(1)

    def slot(self, index):
        plan = {
            0: [self.hello],
            1: [lambda: self.pairs(0), lambda: self.begin(2)],
            3: [lambda: self.pairs(1), lambda: self.begin(3)],
            4: [lambda: self.middle(0)],
            6: [lambda: self.pairs(2), lambda: self.finish(0)],
            7: [lambda: self.middle(1)],
            9: [lambda: self.pairs(3), lambda: self.finish(1)],
            10: [lambda: self.middle(2)],
            12: [lambda: self.finish(2)],
            13: [lambda: self.middle(3)],
            14: [lambda: self.finish(3)],
            16: [self.total],
        }
        for at, actions in plan.items():

            @pl.when(index == at)
            def _():
                for action in actions:
                    action()


def small_sum_kernel(
    main,
    tiny,
    own,
    out_ref,
    shares,
    grads,
    cores,
    chips,
    planes,
    share,
    total,
    s_one,
    r_one,
    s_two,
    r_two,
    s_z,
    r_z,
    s_all,
    r_all,
    s_share,
    r_share,
    s_own,
):
    z, me, sib, xn, yn, dg = places()
    core, chip = me % 2, me // 2
    near = (xn, yn, dg)
    parts, samp, rows = grads.shape[:3]
    for part in range(parts):
        for p in range(samp):
            grads[part, p] = main[p, part * rows : (part + 1) * rows, :]
    low, width = 2 * tiny.shape[1], tiny.shape[2]
    for part in range(tiny.shape[1] // rows):
        for p in range(samp):
            grads[low // rows + part, p, :, -width:] = tiny[p, part * rows : (part + 1) * rows, :]
    others = [lax.rem(z + hop, 4) for hop in (1, 2, 3)]
    greet(
        [(z, sib)]
        + [(z, part) for part in near]
        + [(z, part + 1 - 2 * core) for part in near]
        + [(other, me) for other in others]
    )

    def one(j):
        return remote(
            grads.at[2 * j + 1 - core], cores.at[j], s_one.at[j], r_one.at[j], (z, sib)
        )

    width = own.shape[2]
    head, tail, full = slice(0, width // 2), slice(width // 2, width), slice(0, width)

    def give(part, lanes, kind, device):
        target = shares.at[part, :, lanes]
        source = target if kind == 4 else own.at[part, :, lanes]
        return remote(source, target, s_share.at[kind], r_share.at[kind], (z, device))

    kept = [
        pltpu.make_async_copy(own.at[part], shares.at[part], s_own.at[k])
        for k, part in enumerate((me, xn, yn, sib))
    ]
    gifts = [
        give(xn, head, 0, yn),
        give(yn, tail, 1, xn),
        give(xn, full, 2, sib),
        give(yn, full, 3, sib),
    ]
    for copy in kept:
        copy.start()
    for j in range(4):
        one(j).start()
    for j in range(4):
        one(j).wait()
        both = cores[j].astype(f32) + grads[2 * j + core].astype(f32)
        cores[j] = both.astype(bf16)

    def two(k):
        return remote(cores.at[near[k] // 2], chips.at[k], s_two.at[k], r_two.at[k], (z, near[k]))

    for k in range(3):
        two(k).start()
    for gift in gifts:
        gift.start()
    both = cores[chip].astype(f32)
    for k in range(3):
        two(k).wait()
        both += chips[k].astype(f32)
    share[...] = both.astype(bf16)

    def three(k):
        return remote(share.at[others[k]], planes.at[k], s_z.at[k], r_z.at[k], (others[k], me))

    for k in range(3):
        three(k).start()
    give(dg, head, 0, yn).wait_recv()
    give(dg, tail, 1, xn).wait_recv()
    gifts.append(give(dg, full, 4, sib))
    gifts[-1].start()
    both = share[z].astype(f32)
    for k in range(3):
        three(k).wait()
        both += planes[k].astype(f32)
    total[me] = both.astype(bf16)

    receivers = [sib] + list(near) + [part + 1 - 2 * core for part in near]

    def four(k, part, device):
        return remote(total.at[part], total.at[part], s_all.at[k], r_all.at[k], (z, device))

    for k, device in enumerate(receivers):
        four(k, me, device).start()
    for k, device in enumerate(receivers):
        four(k, device, device).wait_recv()
    for k, device in enumerate(receivers):
        four(k, me, device).wait_send()
    for part in range(parts):
        out_ref[part * rows : (part + 1) * rows, :] = total[part]
    for kind in (2, 3, 4):
        give(sib, full, kind, sib).wait_recv()
    for copy in kept:
        copy.wait()
    for gift in gifts:
        gift.wait_send()


def small_sums(main, tiny, own):
    seq = lax.axis_size("seq")
    samp, rows, width = main.shape
    rows //= seq
    dma = pltpu.SemaphoreType.DMA
    return pl.pallas_call(
        small_sum_kernel,
        out_shape=[
            jax.ShapeDtypeStruct((seq * rows, width), bf16),
            jax.ShapeDtypeStruct(own.shape, bf16),
        ],
        in_specs=[pl.BlockSpec(memory_space=pltpu.VMEM)] * 3,
        out_specs=[
            pl.BlockSpec(memory_space=pltpu.VMEM),
            pl.BlockSpec(memory_space=pl.ANY),
        ],
        scratch_shapes=[
            pltpu.VMEM((seq, samp, rows, width), bf16),
            pltpu.VMEM((4, samp, rows, width), bf16),
            pltpu.VMEM((3, samp, rows, width), bf16),
            pltpu.VMEM((3, rows, width), bf16),
            pltpu.VMEM((samp, rows, width), bf16),
            pltpu.VMEM((seq, rows, width), bf16),
            dma((4,)),
            dma((4,)),
            dma((3,)),
            dma((3,)),
            dma((3,)),
            dma((3,)),
            dma((7,)),
            dma((7,)),
            dma((5,)),
            dma((5,)),
            dma((4,)),
        ],
        compiler_params=pltpu.CompilerParams(
            vmem_limit_bytes=vmem_bytes, collective_id=3, has_side_effects=True
        ),
        name="small_sums",
    )(main, tiny, own)


def pair_stats(pairs, fold):
    upper, lower = square_sums(fold, pairs.astype(f32) * pairs.astype(f32))
    features = pairs.shape[0] // WIN_Q
    mean = mm(fold, pairs) * (1.0 / features)
    square = (mm(fold, upper) + mm(fold, lower)) * (1.0 / features)
    var = jnp.maximum(square - mean * mean, 0.0)
    inv_std = lax.rsqrt(var + norm_eps)
    return mean, inv_std


def pair_fold(features):
    shape = (WIN_Q, WIN_Q * features)
    row = lax.broadcasted_iota(jnp.int32, shape, 0)
    column = lax.broadcasted_iota(jnp.int32, shape, 1)
    return jnp.where(column // features == row, 1.0, 0.0).astype(bf16)


def atom_fwd_kernel(
    gather,
    starts,
    ext_ref,
    pairs_ref,
    spread_ref,
    blocked_ref,
    share_ref,
    wide_ref,
    down_ref,
    qbias_ref,
    *refs,
):
    count = len(gather.shapes) if gather is not None else 0
    shards, refs = refs[:count], refs[count:]
    (
        pooled_ref,
        query_ref,
        keyval_ref,
        gate_ref,
        probs_ref,
        attend_ref,
        mid_ref,
    ), refs = refs[:7], refs[7:]
    fulls, refs = refs[:count], refs[count:]
    bias_s, sems = refs[0], refs[1:]
    width = ext_ref.shape[-1]
    head_dim = width // ATOM_HEADS
    scale = float(head_dim) ** (-0.5)
    slots = query_ref.shape[1]
    windows = slots // WIN_Q
    hidden_width = down_ref.shape[0]
    model_width = pooled_ref.shape[-1]
    features = pairs_ref.shape[1] // WIN_Q
    sample = pl.program_id(0)
    if gather is not None:
        gather.step(sample, shards, fulls, *sems)

    @pl.when(sample == 0)
    def _():
        fold = pair_fold(features)
        spread = spread_ref[...]
        spread_sum = jnp.sum(spread.astype(f32), -1, keepdims=True)
        first_lane = jnp.where(
            lax.broadcasted_iota(jnp.int32, (ATOM_HEADS * WIN_Q, LANES), 1) == 0, 1.0, 0.0
        ).astype(bf16)

        fill = jnp.full((ATOM_HEADS * WIN_Q, WIN_K), masked_score, f32)

        def one(duo, carry):
            base = pl.multiple_of(duo * 2 * WIN_Q, 2 * WIN_Q)
            blocked = mm_nt(first_lane, blocked_ref[pl.ds(base, 2 * WIN_K), :].astype(bf16))
            for part in range(2):
                win = duo * 2 + part
                pairs = pairs_ref[win]
                mean, inv_std = pair_stats(pairs, fold)
                mean = jnp.concatenate([mean] * ATOM_HEADS, 0)
                inv_std = jnp.concatenate([inv_std] * ATOM_HEADS, 0)
                bias = inv_std * (mm(spread, pairs) - mean * spread_sum)
                bias = pltpu.roll(jnp.concatenate([bias, fill], 1), starts[win] - base, 1) + blocked
                for head in range(ATOM_HEADS):
                    low = (head * 2 + part) * WIN_Q
                    bias_s[duo, low : low + WIN_Q, :] = bias[head * WIN_Q : (head + 1) * WIN_Q]
            return carry

        lax.fori_loop(0, windows // 2, one, 0)

    rows = ext_ref[0].astype(f32)
    normed_low = norm_stats(rows)[0].astype(bf16)
    key_val = mm(normed_low, wide_ref[:, width : 3 * width]).astype(bf16)
    keyval_ref[0] = key_val
    own_low = normed_low[RIM : RIM + slots]
    query_ref[0] = (mm(own_low, wide_ref[:, :width]) + qbias_ref[...]).astype(bf16)
    gate_ref[0] = mm(own_low, wide_ref[:, 3 * width : 4 * width])

    masks = head_masks(2 * WIN_Q, width, ATOM_HEADS, head_dim, 0)

    def two_windows(duo):
        first = pl.multiple_of(duo * 2 * WIN_Q, 2 * WIN_Q)
        span = pl.ds(first, 2 * WIN_K)
        own = pl.ds(first, 2 * WIN_Q)
        stacked = head_stack(query_ref[0, own, :], ATOM_HEADS, head_dim, 0, masks)
        scores = mm_nt(stacked, keyval_ref[0, span, :width]) * scale + bias_s[duo]
        exp_scores = jnp.exp(scores - jnp.max(scores, -1, keepdims=True))
        probs = exp_scores * (1.0 / jnp.sum(exp_scores, -1, keepdims=True))
        probs_low = probs.astype(bf16)
        probs_ref[0, duo] = probs_low
        attend_ref[0, own, :] = head_fold(
            mm(probs_low, keyval_ref[0, span, width:]), ATOM_HEADS, head_dim, 0
        )

    def some_windows(step, carry):
        for part in range(2):
            two_windows(step * 2 + part)
        return carry

    lax.fori_loop(0, windows // 4, some_windows, 0)

    gated_low = (attend_ref[0] * sigmoid(gate_ref[0])).astype(bf16)
    offset = 4 * width
    upw = wide_ref[:, offset : offset + 2 * hidden_width]
    offset += 2 * hidden_width
    pool_weight = wide_ref[:, offset : offset + model_width]
    outw = wide_ref[:, offset + model_width : offset + model_width + width]
    mid = rows[RIM : RIM + slots] + mm(gated_low, outw)
    mid_ref[0] = mid
    ffn_low = norm_stats(mid)[0].astype(bf16)
    upper = mm(ffn_low, upw)
    first_half, second_half = upper[:, :hidden_width], upper[:, hidden_width:]
    hidden = (first_half * sigmoid(first_half) * second_half).astype(bf16)
    final_low = (mid + mm(hidden, down_ref[...])).astype(bf16)
    pool_pre = mm(final_low, pool_weight)
    share = share_ref[...]
    for lane in range(0, model_width, LANES):
        part = pool_pre[:, lane : lane + LANES]
        part = part * sigmoid(part) * share
        pooled_ref[0, :, lane : lane + LANES] = jnp.sum(
            part.reshape(slots // MAX_ATOMS, MAX_ATOMS, LANES), 1
        )
    if gather is not None:
        gather.last(sample, shards, fulls, *sems)


def atom_forward(ext, starts, pairs, spread, blocked, share, wide, down, qbias, gather, shards):
    samples, ext_slots, width = ext.shape
    slots = ext_slots - 2 * RIM
    tokens = slots // MAX_ATOMS
    windows = slots // WIN_Q
    model_width = wide.shape[1] - 5 * width - 2 * down.shape[0]
    stack = ATOM_HEADS * WIN_Q
    outs = (
        ((tokens, model_width), f32),
        ((slots, width), bf16),
        ((ext_slots, 2 * width), bf16),
        ((slots, width), f32),
        ((windows // 2, 2 * stack, 2 * WIN_K), bf16),
        ((slots, width), f32),
        ((slots, width), f32),
    )
    place = pl.BlockSpec(memory_space=pl.ANY)
    results = pl.pallas_call(
        functools.partial(atom_fwd_kernel, gather),
        out_shape=[jax.ShapeDtypeStruct((samples,) + shape, kind) for shape, kind in outs]
        + [jax.ShapeDtypeStruct(shape, bf16) for shape in (gather.full_shapes() if gather else [])],
        grid=(samples,),
        in_specs=[
            pl.BlockSpec(memory_space=pltpu.SMEM),
            per_sample((ext_slots, width)),
            whole(pairs.shape),
            whole(spread.shape),
            whole(blocked.shape),
            whole(share.shape),
            whole(wide.shape),
            whole(down.shape),
            whole(qbias.shape),
        ]
        + [place] * len(shards),
        out_specs=[per_sample(shape) for shape, _ in outs] + [place] * len(shards),
        scratch_shapes=[pltpu.VMEM((windows // 2, 2 * stack, 2 * WIN_K), f32)]
        + (gather.scratch() if gather else []),
        compiler_params=gather.params() if gather else params(),
        name="atom_forward",
    )(starts, ext, pairs, spread, blocked, share, wide, down, qbias, *shards)
    return results[0], results[1:7], results[7:]


def atom_bwd_dense(sample_refs, consts, accs, attlow_s, gate_grad_at, mid_grad_at):
    grad_ref, query_ref, gate_ref, attend_ref, mid_ref = sample_refs
    share_ref, wide_ref, down_ref = consts
    outw_ref, upw_ref, downw_ref, pool_ref = accs
    width = query_ref.shape[-1]
    slots = query_ref.shape[1]
    hidden_width = down_ref.shape[0]
    model_width = grad_ref.shape[-1]
    tokens = grad_ref.shape[1]
    offset = 4 * width
    upw = wide_ref[:, offset : offset + 2 * hidden_width]
    offset += 2 * hidden_width
    pool_weight = wide_ref[:, offset : offset + model_width]
    outw = wide_ref[:, offset + model_width : offset + model_width + width]
    down = down_ref[...]

    mid = mid_ref[0]
    normed_mid, inv_mid = norm_stats(mid)
    ffn_low = normed_mid.astype(bf16)
    upper = mm(ffn_low, upw)
    first_half, second_half = upper[:, :hidden_width], upper[:, hidden_width:]
    sig_first = sigmoid(first_half)
    hidden = (first_half * sig_first * second_half).astype(bf16)
    final_low = (mid + mm(hidden, down)).astype(bf16)
    pool_pre = mm(final_low, pool_weight)
    share = share_ref[...]
    pool_parts = []
    for lane in range(0, model_width, LANES):
        part = pool_pre[:, lane : lane + LANES]
        grad = jnp.broadcast_to(
            grad_ref[0, :, lane : lane + LANES][:, None, :], (tokens, MAX_ATOMS, LANES)
        ).reshape(slots, LANES)
        sig_pool = sigmoid(part)
        pool_parts.append((grad * share * sig_pool * (1.0 + part * (1.0 - sig_pool))).astype(bf16))
    pool_grad = jnp.concatenate(pool_parts, 1)
    final_grad = mm_nt(pool_grad, pool_weight)
    pool_ref[...] += mm_tn(final_low, pool_grad)
    branch_low = final_grad.astype(bf16)
    hidden_grad = mm_nt(branch_low, down)
    first_grad = hidden_grad * second_half * sig_first * (1.0 + first_half * (1.0 - sig_first))
    second_grad = hidden_grad * first_half * sig_first
    upper_grad = jnp.concatenate([first_grad.astype(bf16), second_grad.astype(bf16)], 1)
    downw_ref[...] += mm_tn(hidden, branch_low)
    upw_ref[...] += mm_tn(ffn_low, upper_grad)
    mid_grad = final_grad + norm_back(normed_mid, inv_mid, mm_nt(upper_grad, upw))
    mid_grad_at[...] = mid_grad
    out_low = mid_grad.astype(bf16)
    gated_grad = mm_nt(out_low, outw)
    sig_gate = sigmoid(gate_ref[0])
    attend = attend_ref[0]
    gated_low = (attend * sig_gate).astype(bf16)
    outw_ref[...] += mm_tn(gated_low, out_low)
    attlow_s[...] = (gated_grad * sig_gate).astype(bf16)
    gate_grad_at[...] = (gated_grad * attend * sig_gate * (1.0 - sig_gate)).astype(bf16)


def atom_bwd_windows(sample_refs, scratch):
    query_ref, keyval_ref, probs_ref = sample_refs
    acck_s, accv_s, bias_s, attlow_s, dq_s = scratch
    width = query_ref.shape[-1]
    head_dim = width // ATOM_HEADS
    scale = float(head_dim) ** (-0.5)
    windows = query_ref.shape[1] // WIN_Q
    acck_s[...] = jnp.zeros_like(acck_s)
    accv_s[...] = jnp.zeros_like(accv_s)
    masks = head_masks(2 * WIN_Q, width, ATOM_HEADS, head_dim, 0)

    def two_windows(duo):
        first = pl.multiple_of(duo * 2 * WIN_Q, 2 * WIN_Q)
        span = pl.ds(first, 2 * WIN_K)
        own = pl.ds(first, 2 * WIN_Q)
        queries = head_stack(query_ref[0, own, :], ATOM_HEADS, head_dim, 0, masks)
        att = head_stack(attlow_s[own, :], ATOM_HEADS, head_dim, 0, masks)
        probs_low = probs_ref[0, duo]
        probs = probs_low.astype(f32)
        prob_grad = mm_nt(att, keyval_ref[0, span, width:])
        delta = jnp.sum(prob_grad * probs, -1, keepdims=True)
        score_low = (probs * (prob_grad - delta)).astype(bf16)
        bias_s[duo] += score_low.astype(f32)
        dq_s[own, :] = (
            head_fold(mm(score_low, keyval_ref[0, span, :width]), ATOM_HEADS, head_dim, 0) * scale
        )
        acck_s[span, :] += mm_tn(score_low, queries) * scale
        accv_s[span, :] += mm_tn(probs_low, att)

    def some_windows(step, carry):
        for part in range(2):
            two_windows(step * 2 + part)
        return carry

    lax.fori_loop(0, windows // 4, some_windows, 0)


def atom_bwd_pairs(starts, pairs_ref, bias_s, pairw_ref, pairm_ref):
    fold = pair_fold(pairs_ref.shape[1] // WIN_Q)

    def one(duo, carry):
        for part in range(2):
            win = duo * 2 + part
            pairs = pairs_ref[win]
            mean, inv_std = pair_stats(pairs, fold)
            lows = [(head * 2 + part) * WIN_Q for head in range(ATOM_HEADS)]
            placed = jnp.concatenate([bias_s[duo, low : low + WIN_Q, :] for low in lows], 0)
            shift = starts[win] - duo * 2 * WIN_Q
            grad = pltpu.roll(placed, lax.rem(2 * WIN_K - shift, 2 * WIN_K), 1)[:, :WIN_K]
            scaled = grad * jnp.concatenate([inv_std] * ATOM_HEADS, 0)
            pairm_ref[...] += scaled * jnp.concatenate([mean] * ATOM_HEADS, 0)
            upper = scaled.astype(bf16)
            lower = (scaled - upper.astype(f32)).astype(bf16)
            pairw_ref[...] += mm_nt(upper, pairs) + mm_nt(lower, pairs)
        return carry

    lax.fori_loop(0, pairs_ref.shape[0] // 2, one, 0)


def atom_bwd_kernel(
    starts,
    grad_ref,
    query_ref,
    keyval_ref,
    gate_ref,
    probs_ref,
    attend_ref,
    mid_ref,
    pairs_ref,
    share_ref,
    wide_ref,
    down_ref,
    mix_ref,
    own_ref,
    left_ref,
    right_ref,
    midgrad_ref,
    qbias_ref,
    outw_ref,
    upw_ref,
    downw_ref,
    pool_ref,
    pairw_ref,
    pairm_ref,
    *scratch,
):
    acck_s, accv_s, bias_s, attlow_s, dq_s = scratch
    width = query_ref.shape[-1]
    slots = query_ref.shape[1]
    sample = pl.program_id(0)

    @pl.when(sample == 0)
    def _():
        for ref in (qbias_ref, outw_ref, upw_ref, downw_ref, pool_ref, pairw_ref, pairm_ref, bias_s):
            ref[...] = jnp.zeros_like(ref)

    atom_bwd_dense(
        (grad_ref, query_ref, gate_ref, attend_ref, mid_ref),
        (share_ref, wide_ref, down_ref),
        (outw_ref, upw_ref, downw_ref, pool_ref),
        attlow_s,
        mix_ref.at[0, :, width:],
        midgrad_ref.at[0],
    )
    atom_bwd_windows((query_ref, keyval_ref, probs_ref), scratch)
    query_grad = dq_s[...]
    qbias_ref[...] += jnp.sum(query_grad, 0, keepdims=True)
    mix_ref[0, :, :width] = query_grad.astype(bf16)
    for ref, low, high in (
        (own_ref, RIM, RIM + slots),
        (left_ref, 0, RIM),
        (right_ref, RIM + slots, slots + 2 * RIM),
    ):
        ref[0, :, :width] = acck_s[low:high, :].astype(ref.dtype)
        ref[0, :, width:] = accv_s[low:high, :].astype(ref.dtype)

    @pl.when(sample == pl.num_programs(0) - 1)
    def _():
        atom_bwd_pairs(starts, pairs_ref, bias_s, pairw_ref, pairm_ref)


def atom_bwd_sum_kernel(
    summing,
    starts,
    grad_ref,
    query_ref,
    keyval_ref,
    gate_ref,
    probs_ref,
    attend_ref,
    mid_ref,
    rows_ref,
    pairs_ref,
    share_ref,
    wide_ref,
    down_ref,
    units_ref,
    atomgrad_ref,
    qbias_ref,
    pairw_ref,
    pairm_ref,
    small_ref,
    shares_ref,
    acck_s,
    accv_s,
    bias_s,
    attlow_s,
    dq_s,
    mix_s,
    midgrad_s,
    outw_s,
    upw_s,
    downw_s,
    pool_s,
    proj_s,
    own_s,
    to_left,
    to_right,
    from_left,
    from_right,
    s_rim,
    r_rim,
    *sums,
):
    summing.bind(units_ref, shares_ref, *sums)
    z, me = lax.axis_index("samp"), lax.axis_index("seq")
    seq = lax.axis_size("seq")
    first_place, last_place = me == 0, me == seq - 1
    width = query_ref.shape[-1]
    slots = query_ref.shape[1]
    step = pl.program_id(0)
    samples = pl.num_programs(0) - 1
    summing.slot(2 * step)

    def rim(b, side):
        ends = ((to_left, from_right, me - 1), (to_right, from_left, me + 1))[side]
        source, target, device = ends
        return remote(source.at[b], target.at[b], s_rim.at[side, b], r_rim.at[side, b], (z, device))

    def arrived(b, side):
        target = (from_right, from_left)[side]
        return remote(
            target.at[b], target.at[b], s_rim.at[side, b], r_rim.at[side, b], (z, lax.rem(me + 1, seq))
        )

    @pl.when(step == 0)
    def _():
        for ref in (qbias_ref, outw_s, upw_s, downw_s, pool_s, proj_s, pairw_ref, pairm_ref, bias_s):
            ref[...] = jnp.zeros_like(ref)

        @pl.when(first_place)
        def _():
            from_left[...] = jnp.zeros_like(from_left)

        @pl.when(last_place)
        def _():
            from_right[...] = jnp.zeros_like(from_right)

    slot_now = step % 2

    @pl.when(step < samples)
    def _():
        atom_bwd_dense(
            (grad_ref, query_ref, gate_ref, attend_ref, mid_ref),
            (share_ref, wide_ref, down_ref),
            (outw_s, upw_s, downw_s, pool_s),
            attlow_s,
            mix_s.at[slot_now, :, width:],
            midgrad_s.at[slot_now],
        )

    summing.slot(2 * step + 1)

    @pl.when(step < samples)
    def _():
        atom_bwd_windows(
            (query_ref, keyval_ref, probs_ref), (acck_s, accv_s, bias_s, attlow_s, dq_s)
        )
        query_grad = dq_s[...]
        qbias_ref[...] += jnp.sum(query_grad, 0, keepdims=True)
        mix_s[slot_now, :, :width] = query_grad.astype(bf16)
        for ref, low in ((to_left, 0), (to_right, RIM + slots)):
            ref[step, :, :width] = acck_s[low : low + RIM, :].astype(bf16)
            ref[step, :, width:] = accv_s[low : low + RIM, :].astype(bf16)

        @pl.when(~first_place)
        def _():
            rim(step, 0).start()

        @pl.when(~last_place)
        def _():
            rim(step, 1).start()

    @pl.when(step > 0)
    def _():
        b = step - 1

        @pl.when(~first_place)
        def _():
            arrived(b, 1).wait_recv()

        @pl.when(~last_place)
        def _():
            arrived(b, 0).wait_recv()

        normed, inv_std = norm_stats(rows_ref[0].astype(f32))
        parts = []
        for lanes in (slice(0, width), slice(width, 2 * width)):
            own = own_s[:, lanes]
            begin = own[:RIM] + from_left[b, :, lanes].astype(f32)
            end = own[slots - RIM :] + from_right[b, :, lanes].astype(f32)
            parts.append(jnp.concatenate([begin, own[RIM : slots - RIM], end], 0).astype(bf16))
        before = mix_s.at[1 - slot_now]
        mix = jnp.concatenate([before[:, :width], parts[0], parts[1], before[:, width:]], 1)
        proj_s[...] += mm_tn(normed.astype(bf16), mix)
        normed_grad = mm_nt(mix, wide_ref[:, : 4 * width])
        atomgrad_ref[0] = midgrad_s[1 - slot_now] + norm_back(normed, inv_std, normed_grad)

    @pl.when(step < samples)
    def _():
        own_s[:, :width] = acck_s[RIM : RIM + slots, :]
        own_s[:, width:] = accv_s[RIM : RIM + slots, :]

    @pl.when(step == samples)
    def _():
        atom_bwd_pairs(starts, pairs_ref, bias_s, pairw_ref, pairm_ref)
        samp = small_ref.shape[0]
        rows = width // samp
        for p in range(samp):
            span = slice(p * rows, (p + 1) * rows)
            small_ref[p, :rows, :] = pool_s[span, :].astype(bf16)
            small_ref[p, rows : 2 * rows, : 4 * width] = proj_s[span, :].astype(bf16)
            for part in range(2):
                low = (2 * p + part) * rows
                small_ref[p, rows : 2 * rows, (4 + part) * width : (5 + part) * width] = downw_s[
                    low : low + rows, :
                ].astype(bf16)
            small_ref[p, 2 * rows : 3 * rows, : 4 * width] = upw_s[span, :].astype(bf16)
            small_ref[p, 2 * rows : 3 * rows, 4 * width : 5 * width] = outw_s[span, :].astype(bf16)
            small_ref[p, 2 * rows : 3 * rows, 5 * width :] = jnp.zeros((rows, width), bf16)
            small_ref[p, 3 * rows :, :] = jnp.zeros((rows, 6 * width), bf16)
        summing.collect()

        def sent(b, carry):
            @pl.when(~first_place)
            def _():
                rim(b, 0).wait_send()

            @pl.when(~last_place)
            def _():
                rim(b, 1).wait_send()

            return carry

        lax.fori_loop(0, samples, sent, 0)


def atom_backward_sum(grad, starts, stored, rows, pairs, share, wide, down, summing, units):
    query = stored[0]
    samples, slots, width = query.shape
    samp = lax.axis_size("samp")
    ext_slots = slots + 2 * RIM
    windows = slots // WIN_Q
    model_width = grad.shape[-1]
    hidden_width = down.shape[0]
    stack = ATOM_HEADS * WIN_Q
    place = pl.BlockSpec(memory_space=pl.ANY)

    def now(shape):
        return pl.BlockSpec(
            (1,) + shape, lambda g: (jnp.minimum(g, samples - 1),) + (0,) * len(shape)
        )

    def late(shape):
        return pl.BlockSpec((1,) + shape, lambda g: (jnp.maximum(g - 1, 0),) + (0,) * len(shape))

    dma = pltpu.SemaphoreType.DMA
    rim_shape = (samples, RIM, 2 * width)
    small_shape = (samp, 4 * width // samp, model_width)
    return pl.pallas_call(
        functools.partial(atom_bwd_sum_kernel, summing),
        out_shape=[
            jax.ShapeDtypeStruct(rows.shape, f32),
            jax.ShapeDtypeStruct((1, width), f32),
            jax.ShapeDtypeStruct((stack, pairs.shape[1]), f32),
            jax.ShapeDtypeStruct((stack, WIN_K), f32),
            jax.ShapeDtypeStruct(small_shape, bf16),
            jax.ShapeDtypeStruct((8, UNIT, 768), bf16),
        ],
        grid=(samples + 1,),
        in_specs=[pl.BlockSpec(memory_space=pltpu.SMEM), now(grad.shape[1:])]
        + [now(part.shape[1:]) for part in stored]
        + [late(rows.shape[1:])]
        + [whole(part.shape) for part in (pairs, share, wide, down)]
        + [place],
        out_specs=[
            late(rows.shape[1:]),
            whole((1, width)),
            whole((stack, pairs.shape[1])),
            whole((stack, WIN_K)),
            whole(small_shape),
            place,
        ],
        scratch_shapes=[
            pltpu.VMEM((ext_slots, width), f32),
            pltpu.VMEM((ext_slots, width), f32),
            pltpu.VMEM((windows // 2, 2 * stack, 2 * WIN_K), f32),
            pltpu.VMEM((slots, width), bf16),
            pltpu.VMEM((slots, width), f32),
            pltpu.VMEM((2, slots, 2 * width), bf16),
            pltpu.VMEM((2, slots, width), f32),
            pltpu.VMEM((width, width), f32),
            pltpu.VMEM((width, 2 * hidden_width), f32),
            pltpu.VMEM((hidden_width, width), f32),
            pltpu.VMEM((width, model_width), f32),
            pltpu.VMEM((width, 4 * width), f32),
            pltpu.VMEM((slots, 2 * width), f32),
            pltpu.VMEM(rim_shape, bf16),
            pltpu.VMEM(rim_shape, bf16),
            pltpu.VMEM(rim_shape, bf16),
            pltpu.VMEM(rim_shape, bf16),
            dma((2, samples)),
            dma((2, samples)),
        ]
        + summing.scratch(),
        compiler_params=summing.params(),
        name="atom_backward",
    )(starts, grad, *stored, rows, pairs, share, wide, down, units)


def unpack_kernel(units_ref, small_ref, proj_ref, up_ref, down_ref, cond_ref, outw_ref, *atoms):
    proj_ref[...] = units_ref[0, :192, :384].astype(f32)
    up_ref[...] = units_ref[0, :192, 384:].astype(f32)
    down_ref[...] = units_ref[0, 192:240, :].astype(f32)
    cond_ref[:, :768] = units_ref[0, 240:288, :].astype(f32)
    cond_ref[:, 768:] = units_ref[0, 288:336, :384].astype(f32)
    outw_ref[...] = units_ref[0, 288:336, 384:].astype(f32)

    @pl.when(pl.program_id(0) == 0)
    def _():
        pool_ref, atomproj_ref, atomdown_ref, atomup_ref, atomout_ref, tiny_ref = atoms
        rows, width = atomout_ref.shape
        pool_ref[...] = small_ref[:rows, :].astype(f32)
        atomproj_ref[...] = small_ref[rows : 2 * rows, : 4 * width].astype(f32)
        for part in range(2):
            atomdown_ref[part * rows : (part + 1) * rows, :] = small_ref[
                rows : 2 * rows, (4 + part) * width : (5 + part) * width
            ].astype(f32)
        atomup_ref[...] = small_ref[2 * rows : 3 * rows, : 4 * width].astype(f32)
        atomout_ref[...] = small_ref[2 * rows : 3 * rows, 4 * width : 5 * width].astype(f32)
        tiny_ref[...] = small_ref[2 * rows : 3 * rows, 5 * width :].astype(f32)


def unpack(units, small, shapes, rows, width):
    outs = list(shapes) + [
        (rows, 6 * width),
        (rows, 4 * width),
        (2 * rows, width),
        (rows, 4 * width),
        (rows, width),
        (rows, width),
    ]
    specs = [
        pl.BlockSpec((192, 384), lambda s: (0, s)),
        pl.BlockSpec((192, 384), lambda s: (0, s)),
        pl.BlockSpec((48, 768), lambda s: (s, 0)),
        pl.BlockSpec((48, 1152), lambda s: (s // 4, s % 4)),
        pl.BlockSpec((48, 384), lambda s: (s // 2, s % 2)),
    ]
    return pl.pallas_call(
        unpack_kernel,
        out_shape=[jax.ShapeDtypeStruct(shape, f32) for shape in outs],
        grid=(8,),
        in_specs=[pl.BlockSpec((1, UNIT, 768), lambda s: (s, 0, 0)), whole(small.shape)],
        out_specs=specs + [whole(shape) for shape in outs[5:]],
        compiler_params=params(),
        name="unpack",
    )(units, small)


def atom_backward(grad, starts, stored, pairs, share, wide, down):
    query = stored[0]
    samples, slots, width = query.shape
    ext_slots = slots + 2 * RIM
    windows = slots // WIN_Q
    model_width = grad.shape[-1]
    hidden_width = down.shape[0]
    stack = ATOM_HEADS * WIN_Q
    outs = (
        ((slots, 2 * width), bf16),
        ((slots, 2 * width), f32),
        ((RIM, 2 * width), bf16),
        ((RIM, 2 * width), bf16),
        ((slots, width), f32),
    )
    totals = (
        (1, width),
        (width, width),
        (width, 2 * hidden_width),
        (hidden_width, width),
        (width, model_width),
        (stack, pairs.shape[1]),
        (stack, WIN_K),
    )
    return pl.pallas_call(
        atom_bwd_kernel,
        out_shape=[jax.ShapeDtypeStruct((samples,) + shape, kind) for shape, kind in outs]
        + [jax.ShapeDtypeStruct(shape, f32) for shape in totals],
        grid=(samples,),
        in_specs=[pl.BlockSpec(memory_space=pltpu.SMEM), per_sample(grad.shape[1:])]
        + [per_sample(part.shape[1:]) for part in stored]
        + [whole(part.shape) for part in (pairs, share, wide, down)],
        out_specs=[per_sample(shape) for shape, _ in outs] + [whole(shape) for shape in totals],
        scratch_shapes=[
            pltpu.VMEM((ext_slots, width), f32),
            pltpu.VMEM((ext_slots, width), f32),
            pltpu.VMEM((windows // 2, 2 * stack, 2 * WIN_K), f32),
            pltpu.VMEM((slots, width), bf16),
            pltpu.VMEM((slots, width), f32),
        ],
        compiler_params=params(),
        name="atom_backward",
    )(starts, grad, *stored, pairs, share, wide, down)


def atom_input_kernel(
    rows_ref, mix_ref, own_ref, left_ref, right_ref, midgrad_ref, wide_ref, grad_ref, proj_ref
):
    width = rows_ref.shape[-1]

    @pl.when(pl.program_id(0) == 0)
    def _():
        proj_ref[...] = jnp.zeros_like(proj_ref)

    normed, inv_std = norm_stats(rows_ref[0].astype(f32))
    slots = normed.shape[0]
    own = own_ref[0]
    head = own[:RIM] + left_ref[0].astype(f32)
    tail = own[slots - RIM :] + right_ref[0].astype(f32)
    own = jnp.concatenate([head, own[RIM : slots - RIM], tail], 0).astype(bf16)
    mix = jnp.concatenate([mix_ref[0, :, :width], own, mix_ref[0, :, width:]], 1)
    proj_ref[...] += mm_tn(normed.astype(bf16), mix)
    normed_grad = mm_nt(mix, wide_ref[:, : 4 * width])
    grad_ref[0] = midgrad_ref[0] + norm_back(normed, inv_std, normed_grad)


def atom_input_backward(rows, mix, own, left, right, midgrad, wide):
    samples, slots, width = rows.shape
    return pl.pallas_call(
        atom_input_kernel,
        out_shape=[
            jax.ShapeDtypeStruct(rows.shape, f32),
            jax.ShapeDtypeStruct((width, 4 * width), f32),
        ],
        grid=(samples,),
        in_specs=[per_sample(part.shape[1:]) for part in (rows, mix, own, left, right, midgrad)]
        + [whole(wide.shape)],
        out_specs=[per_sample((slots, width)), whole((width, 4 * width))],
        compiler_params=params(),
        name="atom_input_backward",
    )(rows, mix, own, left, right, midgrad, wide)


def row_stats(pairs, ones_op, weights):
    count = weights.shape[0]
    both = mm_nt(jnp.concatenate([weights, ones_op], 0), pairs)
    upper, lower = square_sums(ones_op, pairs.astype(f32) * pairs.astype(f32))
    features = pairs.shape[1]
    mean = both[count : count + 1] * (1.0 / features)
    square = (mm_nt(ones_op, upper) + mm_nt(ones_op, lower))[:1] * (1.0 / features)
    var = jnp.maximum(square - mean * mean, 0.0)
    return both[:count], mean, lax.rsqrt(var + norm_eps)


def pair_bias_kernel(pair_ref, weight_ref, bias_ref):
    weights = weight_ref[...]
    ones_op = jnp.ones((16, weights.shape[1]), bf16)
    weight_sum = jnp.sum(weights.astype(f32), -1, keepdims=True)
    for row in range(pair_ref.shape[0]):
        product, mean, inv_std = row_stats(pair_ref[row], ones_op, weights)
        bias_ref[:, row, :] = inv_std * (product - mean * weight_sum)


def pair_bias(pairs, weights):
    rows, keys, features = pairs.shape
    heads = weights.shape[0]
    return pl.pallas_call(
        pair_bias_kernel,
        out_shape=jax.ShapeDtypeStruct((heads, rows, keys), f32),
        grid=(rows // 8,),
        in_specs=[pl.BlockSpec((8, keys, features), lambda i: (i, 0, 0)), whole(weights.shape)],
        out_specs=pl.BlockSpec((heads, 8, keys), lambda i: (0, i, 0)),
        compiler_params=params(),
        name="pair_bias",
    )(pairs, weights)


def pair_grad_kernel(pair_ref, grad_ref, weight_ref, total_ref, mean_ref):
    @pl.when(pl.program_id(0) == 0)
    def _():
        total_ref[...] = jnp.zeros_like(total_ref)
        mean_ref[...] = jnp.zeros_like(mean_ref)

    heads = grad_ref.shape[0]
    ones_op = jnp.ones((16, pair_ref.shape[2]), bf16)
    total = jnp.zeros(total_ref.shape, f32)
    means = jnp.zeros(mean_ref.shape, f32)
    for row in range(pair_ref.shape[0]):
        pairs = pair_ref[row]
        _, mean, inv_std = row_stats(pairs, ones_op, weight_ref[...])
        scaled = grad_ref[:, row, :] * inv_std
        means += scaled * mean
        upper = scaled.astype(bf16)
        lower = (scaled - upper.astype(f32)).astype(bf16)
        both = mm(jnp.concatenate([upper, lower], 0), pairs)
        total += both[:heads] + both[heads:]
    total_ref[...] += total
    mean_ref[...] += means


def pair_grad(pairs, grads, weights):
    rows, keys, features = pairs.shape
    heads = grads.shape[0]
    total, means = pl.pallas_call(
        pair_grad_kernel,
        out_shape=[
            jax.ShapeDtypeStruct((heads, features), f32),
            jax.ShapeDtypeStruct((heads, keys), f32),
        ],
        grid=(rows // 8,),
        in_specs=[
            pl.BlockSpec((8, keys, features), lambda i: (i, 0, 0)),
            pl.BlockSpec((heads, 8, keys), lambda i: (0, i, 0)),
            whole(weights.shape),
        ],
        out_specs=[whole((heads, features)), whole((heads, keys))],
        compiler_params=params(),
        name="pair_grad",
    )(pairs, grads, weights)
    return total - jnp.sum(means, -1, keepdims=True)


def head_groups(width, heads):
    head_dim = width // heads
    groups = []
    for head in range(0, heads, 4):
        low = head * head_dim
        base = low // LANES * LANES
        groups.append((head, base, low - base))
    return head_dim, groups


def token_fwd_kernel(query_ref, keyval_ref, bias_ref, attend_ref, probs_ref, fold_s):
    tokens, width = query_ref.shape[1:]
    heads = bias_ref.shape[0]
    keys = bias_ref.shape[2]
    head_dim, groups = head_groups(width, heads)
    scale = float(head_dim) ** (-0.5)
    fold_s[...] = jnp.zeros_like(fold_s)
    for head, base, first in groups:
        span = slice(base, base + 256)
        key_rows = keyval_ref[:, 0, :, base : base + 256].reshape(keys, 256)
        value_rows = keyval_ref[:, 0, :, width + base : width + base + 256].reshape(keys, 256)
        stacked = head_stack(query_ref[0, :, span], 4, head_dim, first)
        bias = bias_ref[head : head + 4].reshape(4 * tokens, keys)
        scores = mm_nt(stacked, key_rows) * scale + bias
        exp_scores = jnp.exp(scores - jnp.max(scores, -1, keepdims=True))
        probs = exp_scores * (1.0 / jnp.sum(exp_scores, -1, keepdims=True))
        probs_low = probs.astype(bf16)
        probs_ref[0, head : head + 4] = probs_low.reshape(4, tokens, keys)
        fold_s[:, span] += head_fold(mm(probs_low, value_rows), 4, head_dim, first)
    attend_ref[0] = fold_s[...]


def token_attention(query, keyval, bias):
    samples, tokens, width = query.shape
    heads, _, keys = bias.shape
    devices = keyval.shape[0]
    return pl.pallas_call(
        token_fwd_kernel,
        out_shape=[
            jax.ShapeDtypeStruct(query.shape, f32),
            jax.ShapeDtypeStruct((samples, heads, tokens, keys), bf16),
        ],
        grid=(samples,),
        in_specs=[
            per_sample((tokens, width)),
            pl.BlockSpec((devices, 1, tokens, 2 * width), lambda b: (0, b, 0, 0)),
            whole(bias.shape),
        ],
        out_specs=[per_sample((tokens, width)), per_sample((heads, tokens, keys))],
        scratch_shapes=[pltpu.VMEM((tokens, width), f32)],
        compiler_params=params(),
        name="token_attention",
    )(query, keyval, bias)


def token_bwd_kernel(
    query_ref, keyval_ref, probs_ref, att_ref, dq_ref, dkv_ref, bias_ref, fold_s, grad_s
):
    tokens, width = query_ref.shape[1:]
    heads, _, keys = bias_ref.shape
    devices = keyval_ref.shape[0]
    head_dim, groups = head_groups(width, heads)
    scale = float(head_dim) ** (-0.5)

    @pl.when(pl.program_id(0) == 0)
    def _():
        bias_ref[...] = jnp.zeros_like(bias_ref)

    fold_s[...] = jnp.zeros_like(fold_s)
    grad_s[...] = jnp.zeros_like(grad_s)
    for head, base, first in groups:
        span = slice(base, base + 256)
        key_rows = keyval_ref[:, 0, :, base : base + 256].reshape(keys, 256)
        value_rows = keyval_ref[:, 0, :, width + base : width + base + 256].reshape(keys, 256)
        queries = head_stack(query_ref[0, :, span], 4, head_dim, first)
        att = head_stack(att_ref[0, :, span], 4, head_dim, first)
        probs_low = probs_ref[0, head : head + 4].reshape(4 * tokens, keys)
        probs = probs_low.astype(f32)
        prob_grad = mm_nt(att, value_rows)
        delta = jnp.sum(prob_grad * probs, -1, keepdims=True)
        score_low = (probs * (prob_grad - delta)).astype(bf16)
        bias_ref[head : head + 4] += score_low.astype(f32).reshape(4, tokens, keys)
        fold_s[:, span] += head_fold(mm(score_low, key_rows), 4, head_dim, first) * scale
        grad_s[:, span] += mm_tn(score_low, queries) * scale
        grad_s[:, width + base : width + base + 256] += mm_tn(probs_low, att)
    dq_ref[0] = fold_s[...]
    dkv_ref[:, 0] = grad_s[...].astype(bf16).reshape(devices, tokens, 2 * width)


def token_attention_back(query, keyval, probs, att):
    samples, tokens, width = query.shape
    heads, _, keys = probs.shape[1:]
    devices = keyval.shape[0]
    return pl.pallas_call(
        token_bwd_kernel,
        out_shape=[
            jax.ShapeDtypeStruct(query.shape, f32),
            jax.ShapeDtypeStruct(keyval.shape, bf16),
            jax.ShapeDtypeStruct((heads, tokens, keys), f32),
        ],
        grid=(samples,),
        in_specs=[
            per_sample((tokens, width)),
            pl.BlockSpec((devices, 1, tokens, 2 * width), lambda b: (0, b, 0, 0)),
            per_sample((heads, tokens, keys)),
            per_sample((tokens, width)),
        ],
        out_specs=[
            per_sample((tokens, width)),
            pl.BlockSpec((devices, 1, tokens, 2 * width), lambda b: (0, b, 0, 0)),
            whole((heads, tokens, keys)),
        ],
        scratch_shapes=[
            pltpu.VMEM((tokens, width), f32),
            pltpu.VMEM((keys, 2 * width), f32),
        ],
        compiler_params=params(),
        name="token_attention_back",
    )(query, keyval, probs, att)


def token_open_kernel(
    noise,
    direction_ref,
    single_ref,
    pooled_ref,
    tokens_ref,
    condw_ref,
    condb_ref,
    proj_ref,
    qbias_ref,
    block_ref,
    condlow_ref,
    cond_ref,
    attn_ref,
    query_ref,
    keyval_ref,
    gating_ref,
):
    width = tokens_ref.shape[1]
    count = single_ref.shape[0]
    step = pl.program_id(0)
    single = single_ref[...].astype(f32)
    direction = direction_ref[...]
    for part in range(tokens_ref.shape[0] // count):
        level = jnp.full(direction.shape, noise[step * (tokens_ref.shape[0] // count) + part], f32)
        shifted = single + 0.25 * jnp.log(level / sigma_data) * direction
        condlow_ref[part * count : (part + 1) * count, :] = norm_stats(shifted)[0].astype(bf16)
    cond_low = condlow_ref[...]
    for part in range(6):
        lanes = slice(part * width, (part + 1) * width)
        cond_ref[:, lanes] = mm(cond_low, condw_ref[:, lanes]) + condb_ref[:, lanes]
    block_in = tokens_ref[...].astype(f32) + pooled_ref[...]
    block_ref[...] = block_in
    normed = norm_stats(block_in)[0]
    attn_in = (sigmoid(cond_ref[:, :width]) * normed + cond_ref[:, width : 2 * width]).astype(bf16)
    attn_ref[...] = attn_in
    query_ref[...] = (mm(attn_in, proj_ref[:, :width]) + qbias_ref[...]).astype(bf16)
    keyval_ref[...] = mm(attn_in, proj_ref[:, width : 3 * width]).astype(bf16)
    gating_ref[...] = mm(attn_in, proj_ref[:, 3 * width :])


def token_open(noise, direction, single, pooled, tokens, condw, condb, proj, qbias):
    samples, count, width = tokens.shape
    rows = samples * count
    block = 4 * count
    lanes = lambda size: pl.BlockSpec((block, size), lambda i: (i, 0))
    inner = single.shape[1]
    outs = (
        (width, f32),
        (inner, bf16),
        (6 * width, f32),
        (width, bf16),
        (width, bf16),
        (2 * width, bf16),
        (width, f32),
    )
    return pl.pallas_call(
        token_open_kernel,
        out_shape=[jax.ShapeDtypeStruct((rows, size), kind) for size, kind in outs],
        grid=(rows // block,),
        in_specs=[
            pl.BlockSpec(memory_space=pltpu.SMEM),
            whole((1, inner)),
            whole(single.shape),
            lanes(width),
            lanes(width),
            whole(condw.shape),
            whole((1, 6 * width)),
            whole(proj.shape),
            whole((1, width)),
        ],
        out_specs=[lanes(size) for size, _ in outs],
        compiler_params=params(),
        name="token_open",
    )(
        noise,
        direction.reshape(1, -1),
        single,
        pooled.reshape(rows, width),
        tokens.reshape(rows, width),
        condw,
        condb.reshape(1, -1),
        proj,
        qbias.reshape(1, -1),
    )


def token_middle_rows(
    attend,
    gating_ref,
    block_ref,
    gate1_ref,
    scale2_ref,
    shift2_ref,
    gate2_ref,
    cotangent_ref,
    outw_ref,
    upw_ref,
    downw_ref,
    result_ref,
    ffn_ref,
    upper_ref,
    hidden_ref,
    two_ref,
    gated_ref,
    branch_ref,
    att_ref,
    gategrad_ref,
    midgrad_ref,
    condgrad_ref,
):
    width = attend.shape[1]
    hidden_width = downw_ref.shape[0]
    outw, upw, downw = outw_ref[...], upw_ref[...], downw_ref[...]
    sig_gate = sigmoid(gating_ref[...])
    gated_low = (attend * sig_gate).astype(bf16)
    gated_ref[...] = gated_low
    branch = mm(gated_low, outw)
    gate_one = sigmoid(gate1_ref[...])
    mid = block_ref[...] + gate_one * branch
    normed, inv_std = norm_stats(mid)
    scale_two = sigmoid(scale2_ref[...])
    ffn_in = (scale_two * normed + shift2_ref[...]).astype(bf16)
    ffn_ref[...] = ffn_in
    first_half = mm(ffn_in, upw[:, :hidden_width])
    second_half = mm(ffn_in, upw[:, hidden_width:])
    sig_first = sigmoid(first_half)
    hidden = (first_half * sig_first * second_half).astype(bf16)
    hidden_ref[...] = hidden
    branch_two = mm(hidden, downw)
    gate_two = sigmoid(gate2_ref[...])
    result_ref[...] = (mid + gate_two * branch_two).astype(bf16)

    out_grad = cotangent_ref[...].astype(f32)
    two_low = (out_grad * gate_two).astype(bf16)
    two_ref[...] = two_low
    condgrad_ref[:, 3 * width :] = (
        out_grad * branch_two * gate_two * (1.0 - gate_two)
    ).astype(bf16)
    hidden_grad = mm_nt(two_low, downw)
    first_grad = (
        hidden_grad * second_half * sig_first * (1.0 + first_half * (1.0 - sig_first))
    ).astype(bf16)
    second_grad = (hidden_grad * first_half * sig_first).astype(bf16)
    upper_ref[:, :hidden_width] = first_grad
    upper_ref[:, hidden_width:] = second_grad
    ffn_grad = mm_nt(first_grad, upw[:, :hidden_width]) + mm_nt(second_grad, upw[:, hidden_width:])
    condgrad_ref[:, 2 * width : 3 * width] = ffn_grad.astype(bf16)
    condgrad_ref[:, width : 2 * width] = (
        ffn_grad * normed * scale_two * (1.0 - scale_two)
    ).astype(bf16)
    mid_grad = out_grad + norm_back(normed, inv_std, ffn_grad * scale_two)
    midgrad_ref[...] = mid_grad
    branch_low = (mid_grad * gate_one).astype(bf16)
    branch_ref[...] = branch_low
    condgrad_ref[:, :width] = (mid_grad * branch * gate_one * (1.0 - gate_one)).astype(bf16)
    gated_grad = mm_nt(branch_low, outw)
    att_ref[...] = (gated_grad * sig_gate).astype(bf16)
    gategrad_ref[...] = (gated_grad * attend * sig_gate * (1.0 - sig_gate)).astype(bf16)


def attend_groups(heads, width, tokens, query, keyval, bias, probs_ref, fold_s):
    head_dim, groups = head_groups(width, heads)
    scale = float(head_dim) ** (-0.5)
    fold_s[...] = jnp.zeros_like(fold_s)
    for head, base, first in groups:
        span = slice(base, base + 256)
        stacked = head_stack(query[:, span], 4, head_dim, first)
        scores = mm_nt(stacked, keyval(base)) * scale + bias(head)
        exp_scores = jnp.exp(scores - jnp.max(scores, -1, keepdims=True))
        probs = exp_scores * (1.0 / jnp.sum(exp_scores, -1, keepdims=True))
        probs_low = probs.astype(bf16)
        probs_ref[0, head : head + 4] = probs_low.reshape(4, tokens, -1)
        fold_s[:, span] += head_fold(mm(probs_low, keyval(width + base)), 4, head_dim, first)


def gather_attend_kernel(
    query_ref,
    own_ref,
    pair_ref,
    weight_ref,
    gating_ref,
    block_ref,
    gate1_ref,
    scale2_ref,
    shift2_ref,
    gate2_ref,
    cotangent_ref,
    outw_ref,
    upw_ref,
    downw_ref,
    probs_ref,
    keyval_ref,
    stats_ref,
    *refs,
):
    middle, (all_s, bias_s, fold_s, attend_s, send, recv, load) = refs[:11], refs[11:]
    z, me, sib, xn, yn, dg = places()
    step = pl.program_id(0)
    tokens, width = query_ref.shape[1:]
    heads = weight_ref.shape[0]
    devices, samples = all_s.shape[:2]
    keys = devices * tokens
    head, tail, full = slice(0, width), slice(width, 2 * width), slice(0, 2 * width)

    def unit(part, sample, lanes, kind, device):
        ref = all_s.at[part, sample, :, lanes]
        return remote(ref, ref, send.at[kind, sample], recv.at[kind, sample], (z, device))

    def issue(sample):
        unit(me, sample, full, 0, xn).start()
        unit(me, sample, full, 1, yn).start()
        unit(me, sample, full, 4, sib).start()

    def relay(sample):
        unit(xn, sample, full, 0, xn).wait_recv()
        unit(xn, sample, head, 2, yn).start()
        unit(xn, sample, full, 5, sib).start()
        unit(yn, sample, full, 1, yn).wait_recv()
        unit(yn, sample, tail, 3, xn).start()
        unit(yn, sample, full, 6, sib).start()

    def collect(sample):
        unit(dg, sample, head, 2, yn).wait_recv()
        unit(dg, sample, tail, 3, xn).wait_recv()
        unit(dg, sample, full, 7, sib).start()

    @pl.when(step == 0)
    def _():
        copy = pltpu.make_async_copy(own_ref, all_s.at[me], load)
        copy.start()
        greet([(z, sib), (z, xn), (z, yn)])
        copy.wait()
        issue(0)
        issue(1)

    @pl.when((step >= 1) & (step - 1 < samples))
    def _():
        relay(step - 1)

    @pl.when((step >= 1) & (step + 1 < samples))
    def _():
        issue(step + 1)

    @pl.when((step >= 2) & (step - 2 < samples))
    def _():
        collect(step - 2)

    @pl.when(step < 2)
    def _():
        weights = weight_ref[...]
        ones_op = jnp.ones((16, weights.shape[1]), bf16)
        weight_sum = jnp.sum(weights.astype(f32), -1, keepdims=True)
        groups = pair_ref.shape[0] // 8

        def one(group, carry):
            for row in range(8):
                product, mean, inv_std = row_stats(pair_ref[group * 8 + row], ones_op, weights)
                place = step * groups + group
                bias_s[:, place, row, :] = inv_std * (product - mean * weight_sum)
                stats_ref[0, place, row : row + 1, :] = mean
                stats_ref[1, place, row : row + 1, :] = inv_std
            return carry

        lax.fori_loop(0, groups, one, 0)

    @pl.when(step >= 3)
    def _():
        sample = step - 3
        for kind, part in ((4, sib), (5, sib), (6, sib), (7, sib)):
            unit(part, sample, full, kind, sib).wait_recv()
        for part in range(devices):
            keyval_ref[part, 0] = all_s[part, sample]
        attend_groups(
            heads,
            width,
            tokens,
            query_ref[0],
            lambda base: keyval_ref[:, 0, :, base : base + 256].reshape(keys, 256),
            lambda head: bias_s[head : head + 4].reshape(4 * tokens, keys),
            probs_ref,
            fold_s,
        )
        attend_s[pl.ds(pl.multiple_of(sample % 2 * tokens, 16), tokens), :] = fold_s[...]

    @pl.when((step >= 3) & (step % 2 == 0))
    def _():
        token_middle_rows(
            attend_s[...],
            gating_ref,
            block_ref,
            gate1_ref,
            scale2_ref,
            shift2_ref,
            gate2_ref,
            cotangent_ref,
            outw_ref,
            upw_ref,
            downw_ref,
            *middle,
        )

    @pl.when(step == pl.num_programs(0) - 1)
    def _():
        def sent(sample, carry):
            for kind in (0, 1, 4, 5, 6, 7):
                unit(me, sample, full, kind, sib).wait_send()
            unit(me, sample, head, 2, sib).wait_send()
            unit(me, sample, tail, 3, sib).wait_send()
            return carry

        lax.fori_loop(0, samples, sent, 0)


def held_once(shape):
    return pl.BlockSpec(shape, lambda *_: (0,) * len(shape), pipeline_mode=pl.Buffered(1))


def gather_attend(
    query, own, pairs, weights, gating, block_in, cond_all, cotangent, outw, upw, downw
):
    samples, tokens, width = query.shape
    heads, features = weights.shape
    seq = lax.axis_size("seq")
    keys = seq * tokens
    hidden_width = downw.shape[0]
    rows, block = samples * tokens, 2 * tokens
    late = lambda g: jnp.maximum(g - 3, 0)
    sample_block = lambda shape: pl.BlockSpec((1,) + shape, lambda g: (late(g),) + (0,) * len(shape))
    duo_block = lambda lanes, column=0: pl.BlockSpec((block, lanes), lambda g: (late(g) // 2, column))
    flat = lambda part: part.reshape(rows, part.shape[-1])
    cond = flat(cond_all)
    dma = pltpu.SemaphoreType.DMA
    outs = (
        (width, bf16),
        (width, bf16),
        (2 * hidden_width, bf16),
        (hidden_width, bf16),
        (width, bf16),
        (width, bf16),
        (width, bf16),
        (width, bf16),
        (width, bf16),
        (width, f32),
        (4 * width, bf16),
    )
    results = pl.pallas_call(
        gather_attend_kernel,
        out_shape=[
            jax.ShapeDtypeStruct((samples, heads, tokens, keys), bf16),
            jax.ShapeDtypeStruct((seq, samples, tokens, 2 * width), bf16),
            jax.ShapeDtypeStruct((2, tokens // 8, 8, keys), f32),
        ]
        + [jax.ShapeDtypeStruct((rows, lanes), kind) for lanes, kind in outs],
        grid=(samples + 3,),
        in_specs=[
            sample_block((tokens, width)),
            pl.BlockSpec(memory_space=pl.ANY),
            pl.BlockSpec((tokens // 2, keys, features), lambda g: (jnp.minimum(g, 1), 0, 0)),
            whole(weights.shape),
            duo_block(width),
            duo_block(width),
            duo_block(width, 2),
            duo_block(width, 3),
            duo_block(width, 4),
            duo_block(width, 5),
            duo_block(width),
        ]
        + [held_once(part.shape) for part in (outw, upw, downw)],
        out_specs=[
            sample_block((heads, tokens, keys)),
            pl.BlockSpec((seq, 1, tokens, 2 * width), lambda g: (0, late(g), 0, 0)),
            whole((2, tokens // 8, 8, keys)),
        ]
        + [duo_block(lanes) for lanes, _ in outs],
        scratch_shapes=[
            pltpu.VMEM((seq, samples, tokens, 2 * width), bf16),
            pltpu.VMEM((heads, tokens // 8, 8, keys), f32),
            pltpu.VMEM((tokens, width), f32),
            pltpu.VMEM((block, width), f32),
            dma((8, samples)),
            dma((8, samples)),
            dma,
        ],
        compiler_params=pltpu.CompilerParams(
            vmem_limit_bytes=60 << 20, collective_id=4, has_side_effects=True
        ),
        name="gather_attend",
    )(
        query,
        own,
        pairs,
        weights,
        flat(gating),
        flat(block_in),
        cond,
        cond,
        cond,
        cond,
        flat(cotangent),
        outw,
        upw,
        downw,
    )
    return results[:3], results[3:]


def attend_back_scatter_kernel(
    query_ref,
    keyval_ref,
    probs_ref,
    att_ref,
    pair_ref,
    stats_ref,
    ffn_ref,
    upper_ref,
    hidden_ref,
    two_ref,
    gated_ref,
    branch_ref,
    dq_ref,
    dkv_ref,
    pairw_ref,
    pairm_ref,
    upw_ref,
    downw_ref,
    outw_ref,
    fold_s,
    grad_s,
    bias_s,
    mine,
    theirs,
    from_x,
    from_y,
    last_x,
    last_y,
    s_sib,
    r_sib,
    s_one,
    r_one,
    s_two,
    r_two,
):
    z, me, sib, xn, yn, dg = places()
    core, chip = me % 2, me // 2
    chip_x, chip_y, chip_d = xn // 2, yn // 2, dg // 2
    step = pl.program_id(0)
    tokens, width = query_ref.shape[1:]
    samples = mine.shape[0]
    heads, keys = probs_ref.shape[1], probs_ref.shape[3]
    head_dim, groups = head_groups(width, heads)
    scale = float(head_dim) ** (-0.5)
    head, tail = slice(0, width), slice(width, 2 * width)

    def there(b):
        return remote(
            mine.at[b, :, 1 - core], theirs.at[b], s_sib.at[b], r_sib.at[b], (z, sib)
        )

    def one(b, k):
        part = (chip_x, chip_d, chip_y, chip_d)[k]
        lanes = head if k < 2 else tail
        target = (from_x if k < 2 else from_y).at[b, k % 2]
        device = xn if k < 2 else yn
        source = mine.at[b, part, core, :, lanes]
        return remote(source, target, s_one.at[b, k], r_one.at[b, k], (z, device))

    def two(b, k):
        part, lanes, target, device = ((chip_y, head, last_y, yn), (chip_x, tail, last_x, xn))[k]
        source = mine.at[b, part, core, :, lanes]
        return remote(source, target.at[b], s_two.at[b, k], r_two.at[b, k], (z, device))

    def add(b, part, lanes, source):
        both = mine[b, part, core, :, lanes].astype(f32) + source.astype(f32)
        mine[b, part, core, :, lanes] = both.astype(bf16)

    @pl.when(step == 0)
    def _():
        greet([(z, sib), (z, xn), (z, yn)])
        bias_s[...] = jnp.zeros_like(bias_s)
        pairw_ref[...] = jnp.zeros_like(pairw_ref)
        pairm_ref[...] = jnp.zeros_like(pairm_ref)

    @pl.when((step >= 1) & (step - 1 < samples))
    def _():
        b = step - 1
        there(b).wait_recv()

        def chips(j, carry):
            add(b, j, slice(0, 2 * width), theirs[b, j])
            return carry

        lax.fori_loop(0, 4, chips, 0)
        for k in range(4):
            one(b, k).start()

    @pl.when((step >= 2) & (step - 2 < samples))
    def _():
        b = step - 2
        one(b, 1).wait_recv()
        add(b, chip_y, head, from_x[b, 1])
        two(b, 0).start()
        one(b, 3).wait_recv()
        add(b, chip_x, tail, from_y[b, 1])
        two(b, 1).start()
        one(b, 0).wait_recv()
        add(b, chip, head, from_x[b, 0])
        one(b, 2).wait_recv()
        add(b, chip, tail, from_y[b, 0])

    @pl.when((step >= 3) & (step - 3 < samples))
    def _():
        b = step - 3
        two(b, 0).wait_recv()
        add(b, chip, head, last_y[b])
        two(b, 1).wait_recv()
        add(b, chip, tail, last_x[b])
        dkv_ref[0] = mine[b, chip, core]

    @pl.when(step < samples)
    def _():
        fold_s[...] = jnp.zeros_like(fold_s)
        grad_s[...] = jnp.zeros_like(grad_s)
        for first_head, base, first in groups:
            span = slice(base, base + 256)
            key_rows = keyval_ref[:, 0, :, base : base + 256].reshape(keys, 256)
            value_rows = keyval_ref[:, 0, :, width + base : width + base + 256].reshape(keys, 256)
            queries = head_stack(query_ref[0, :, span], 4, head_dim, first)
            att = head_stack(att_ref[0, :, span], 4, head_dim, first)
            probs_low = probs_ref[0, first_head : first_head + 4].reshape(4 * tokens, keys)
            probs = probs_low.astype(f32)
            prob_grad = mm_nt(att, value_rows)
            delta = jnp.sum(prob_grad * probs, -1, keepdims=True)
            score_low = (probs * (prob_grad - delta)).astype(bf16)
            bias_s[first_head : first_head + 4] += score_low.astype(f32).reshape(
                4, tokens // 8, 8, keys
            )
            fold_s[:, span] += head_fold(mm(score_low, key_rows), 4, head_dim, first) * scale
            grad_s[:, span] += mm_tn(score_low, queries) * scale
            grad_s[:, width + base : width + base + 256] += mm_tn(probs_low, att)
        dq_ref[0] = fold_s[...]
        mine[step] = grad_s[...].astype(bf16).reshape(mine.shape[1:])
        there(step).start()
        upw_ref[...] = mm_tn(ffn_ref[...], upper_ref[...]).astype(bf16)

    @pl.when(step < 6)
    def _():
        downw_ref[...] = mm_tn(hidden_ref[...], two_ref[...]).astype(bf16)

    @pl.when((step >= 6) & (step < 8))
    def _():
        outw_ref[...] = mm_tn(gated_ref[...], branch_ref[...]).astype(bf16)

    @pl.when((step >= samples) & (step < samples + 2))
    def _():
        rows = pair_ref.shape[0] // 8

        def some(group, carry):
            total, means = carry
            place = (step - samples) * rows + group
            for row in range(8):
                inv_std = stats_ref[1, place, row : row + 1, :]
                scaled = bias_s[:, place, row, :] * inv_std
                means += scaled * stats_ref[0, place, row : row + 1, :]
                upper = scaled.astype(bf16)
                lower = (scaled - upper.astype(f32)).astype(bf16)
                both = mm(jnp.concatenate([upper, lower], 0), pair_ref[group * 8 + row])
                total += both[:heads] + both[heads:]
            return total, means

        zeros = (jnp.zeros(pairw_ref.shape, f32), jnp.zeros(pairm_ref.shape, f32))
        total, means = lax.fori_loop(0, rows, some, zeros)
        pairw_ref[...] += total
        pairm_ref[...] += means

    @pl.when(step == pl.num_programs(0) - 1)
    def _():
        def sent(b, carry):
            there(b).wait_send()
            for k in range(4):
                one(b, k).wait_send()
            for k in range(2):
                two(b, k).wait_send()
            return carry

        lax.fori_loop(0, samples, sent, 0)


def attend_back_scatter(query, keyval, probs, att, pairs, stats, ffn, upper, hidden, two, gated, branch):
    samples, tokens, width = query.shape
    heads, _, keys = probs.shape[1:]
    seq = keyval.shape[0]
    features = pairs.shape[-1]
    flat = [part.reshape(-1, part.shape[-1]) for part in (ffn, upper, hidden, two, gated, branch)]
    rows = flat[0].shape[0]
    held = lambda g: jnp.minimum(g, samples - 1)
    late = lambda g: jnp.clip(g - 3, 0, samples - 1)
    pair_step = lambda g: jnp.clip(g - samples, 0, 1)
    up_step = lambda g: jnp.minimum(g, seq - 1)
    down_step = lambda g: jnp.minimum(g, 5)
    out_step = lambda g: jnp.clip(g - 6, 0, 1)
    sample_block = lambda shape, at: pl.BlockSpec((1,) + shape, lambda g: (at(g),) + (0,) * len(shape))
    keyval_block = pl.BlockSpec((seq, 1, tokens, 2 * width), lambda g: (0, held(g), 0, 0))
    up_width = flat[1].shape[1] // seq
    hidden_width = flat[2].shape[1]
    dma = pltpu.SemaphoreType.DMA
    results = pl.pallas_call(
        attend_back_scatter_kernel,
        out_shape=[
            jax.ShapeDtypeStruct(query.shape, f32),
            jax.ShapeDtypeStruct((samples, tokens, 2 * width), bf16),
            jax.ShapeDtypeStruct((heads, features), f32),
            jax.ShapeDtypeStruct((heads, keys), f32),
            jax.ShapeDtypeStruct((width, flat[1].shape[1]), bf16),
            jax.ShapeDtypeStruct((hidden_width, width), bf16),
            jax.ShapeDtypeStruct((width, width), bf16),
        ],
        grid=(samples + 3,),
        in_specs=[
            sample_block((tokens, width), held),
            keyval_block,
            sample_block((heads, tokens, keys), held),
            sample_block((tokens, width), held),
            pl.BlockSpec((tokens // 2, keys, features), lambda g: (pair_step(g), 0, 0)),
            whole(stats.shape),
            whole(flat[0].shape),
            pl.BlockSpec((rows, up_width), lambda g: (0, up_step(g))),
            pl.BlockSpec((rows, 256), lambda g: (0, down_step(g))),
            whole(flat[3].shape),
            pl.BlockSpec((rows, width // 2), lambda g: (0, out_step(g))),
            whole(flat[5].shape),
        ],
        out_specs=[
            sample_block((tokens, width), held),
            sample_block((tokens, 2 * width), late),
            whole((heads, features)),
            whole((heads, keys)),
            pl.BlockSpec((width, up_width), lambda g: (0, up_step(g))),
            pl.BlockSpec((256, width), lambda g: (down_step(g), 0)),
            pl.BlockSpec((width // 2, width), lambda g: (out_step(g), 0)),
        ],
        scratch_shapes=[
            pltpu.VMEM((tokens, width), f32),
            pltpu.VMEM((keys, 2 * width), f32),
            pltpu.VMEM((heads, tokens // 8, 8, keys), f32),
            pltpu.VMEM((samples, seq // 2, 2, tokens, 2 * width), bf16),
            pltpu.VMEM((samples, seq // 2, tokens, 2 * width), bf16),
            pltpu.VMEM((samples, 2, tokens, width), bf16),
            pltpu.VMEM((samples, 2, tokens, width), bf16),
            pltpu.VMEM((samples, tokens, width), bf16),
            pltpu.VMEM((samples, tokens, width), bf16),
            dma((samples,)),
            dma((samples,)),
            dma((samples, 4)),
            dma((samples, 4)),
            dma((samples, 2)),
            dma((samples, 2)),
        ],
        compiler_params=pltpu.CompilerParams(
            vmem_limit_bytes=60 << 20, collective_id=5, has_side_effects=True
        ),
        name="attend_back_scatter",
    )(query, keyval, probs, att, pairs, stats, *flat)
    dq, dkv, total, means, upw, downw, outw = results
    return dq, dkv, total - jnp.sum(means, -1, keepdims=True), (upw, downw, outw)


def token_close_kernel(
    dq_ref,
    dkv_ref,
    gategrad_ref,
    midgrad_ref,
    block_ref,
    scale1_ref,
    tail_ref,
    proj_ref,
    attn_ref,
    cond_ref,
    upw_ref,
    downw_ref,
    outw_ref,
    tokengrad_ref,
    qbias_ref,
    cbias_ref,
    units_ref,
    mix_s,
    condgrad_s,
    cond_s,
    proj_s,
):
    step = pl.program_id(0)
    block, width = dq_ref.shape
    blocks = mix_s.shape[0] // block
    samp = units_ref.shape[1]

    @pl.when(step == 0)
    def _():
        qbias_ref[...] = jnp.zeros_like(qbias_ref)
        cbias_ref[...] = jnp.zeros_like(cbias_ref)

    @pl.when(step < blocks)
    def _():
        rows = pl.ds(pl.multiple_of(step * block, block), block)
        dq = dq_ref[...]
        qbias_ref[...] += jnp.sum(dq, 0, keepdims=True)
        mix = jnp.concatenate([dq.astype(bf16), dkv_ref[...], gategrad_ref[...]], 1)
        mix_s[rows, :] = mix
        attn_grad = mm_nt(mix, proj_ref[...])
        normed, inv_std = norm_stats(block_ref[...])
        scale_one = sigmoid(scale1_ref[...])
        scale_grad = (attn_grad * normed * scale_one * (1.0 - scale_one)).astype(bf16)
        tokengrad_ref[...] = midgrad_ref[...] + norm_back(normed, inv_std, attn_grad * scale_one)
        shift_grad = attn_grad.astype(bf16)
        tail = tail_ref[...]
        condgrad_s[rows, :width] = scale_grad
        condgrad_s[rows, width : 2 * width] = shift_grad
        condgrad_s[rows, 2 * width :] = tail
        for part, low in ((scale_grad, 0), (shift_grad, width), (tail, 2 * width)):
            cbias_ref[:, low : low + part.shape[1]] += jnp.sum(
                part.astype(f32), 0, keepdims=True
            )

    @pl.when(step == blocks)
    def _():
        cond_rows = cond_ref[...].T
        for low in range(0, cond_s.shape[1], 768):
            cond_s[:, low : low + 768] = mm(cond_rows, condgrad_s[:, low : low + 768]).astype(bf16)
        attn_rows = attn_ref[...].T
        for low in range(0, proj_s.shape[1], 768):
            proj_s[:, low : low + 768] = mm(attn_rows, mix_s[:, low : low + 768]).astype(bf16)

    @pl.when(step >= blocks)
    def _():
        part = step - blocks
        left = pl.multiple_of(part * 384, LANES)
        proj = proj_s[:, pl.ds(left, 384)]
        rows = proj.shape[0] // samp
        for z in range(samp):
            units_ref[0, z, :rows, :384] = proj[z * rows : (z + 1) * rows]
            units_ref[0, z, :rows, 384:] = upw_ref[z * rows : (z + 1) * rows, :]
            units_ref[0, z, 192:240, :] = downw_ref[
                pl.ds(pl.multiple_of(z * 384 + part * 48, 16), 48), :
            ]
            low = pl.multiple_of(z * 96 + part // 4 * 48, 16)
            left = pl.multiple_of(part % 4 * 1152, LANES)
            units_ref[0, z, 240:288, :] = cond_s[pl.ds(low, 48), pl.ds(left, 768)]
            left = pl.multiple_of(part % 4 * 1152 + 768, LANES)
            units_ref[0, z, 288:336, :384] = cond_s[pl.ds(low, 48), pl.ds(left, 384)]
            low = pl.multiple_of(z * 192 + part // 2 * 48, 16)
            left = pl.multiple_of(part % 2 * 384, LANES)
            units_ref[0, z, 288:336, 384:] = outw_ref[pl.ds(low, 48), pl.ds(left, 384)]


def token_close(dq, dkv, gategrad, midgrad, block_in, cond_all, tail, proj, attn_in, cond_low, ready, samp, seq):
    samples, tokens, width = dq.shape
    rows = samples * tokens
    blocks = 2
    block = rows // blocks
    flat = lambda part: part.reshape(rows, part.shape[-1])
    upw, downw, outw = ready
    attn, cond = flat(attn_in), flat(cond_low)

    def early(lanes, column=0):
        return pl.BlockSpec((block, lanes), lambda g: (jnp.minimum(g, blocks - 1), column))

    late = lambda g: jnp.maximum(g - blocks, 0)
    return pl.pallas_call(
        token_close_kernel,
        out_shape=[
            jax.ShapeDtypeStruct((rows, width), f32),
            jax.ShapeDtypeStruct((1, width), f32),
            jax.ShapeDtypeStruct((1, 6 * width), f32),
            jax.ShapeDtypeStruct((seq, samp, UNIT, 768), bf16),
        ],
        grid=(blocks + seq,),
        in_specs=[
            early(width),
            early(2 * width),
            early(width),
            early(width),
            early(width),
            early(width),
            early(4 * width),
            whole(proj.shape),
            whole(attn.shape),
            whole(cond.shape),
            pl.BlockSpec((width, 384), lambda g: (0, late(g))),
            whole(downw.shape),
            whole(outw.shape),
        ],
        out_specs=[
            early(width),
            whole((1, width)),
            whole((1, 6 * width)),
            pl.BlockSpec((1, samp, UNIT, 768), lambda g: (late(g), 0, 0, 0)),
        ],
        scratch_shapes=[
            pltpu.VMEM((rows, 4 * width), bf16),
            pltpu.VMEM((rows, 6 * width), bf16),
            pltpu.VMEM((cond.shape[1], 6 * width), bf16),
            pltpu.VMEM((width, 4 * width), bf16),
        ],
        compiler_params=params(),
        name="token_close",
    )(
        flat(dq),
        flat(dkv),
        gategrad,
        midgrad,
        flat(block_in),
        flat(cond_all),
        tail,
        proj,
        attn,
        cond,
        upw,
        downw,
        outw,
    )


def to_blocks(array, width):
    return [array[:, low : low + width] for low in range(0, array.shape[1], width)]


def pack_blocks(arrays, width):
    parts = []
    for array in arrays:
        parts += to_blocks(array, width)
    return jnp.concatenate(parts, 0)


def unpack_blocks(packed, shapes, width):
    arrays, low = [], 0
    for rows, columns in shapes:
        parts = []
        for _ in range(columns // width):
            parts.append(packed[low : low + rows])
            low += rows
        arrays.append(jnp.concatenate(parts, 1) if len(parts) > 1 else parts[0])
    return arrays


def sum_shares(grads, extra):
    samp, seq = lax.axis_size("samp"), lax.axis_size("seq")
    width = grads[2].shape[1]
    shapes = [(grad.shape[0] // samp, grad.shape[1]) for grad in grads]
    packed = jnp.concatenate(
        [
            block.astype(bf16).reshape(samp, -1, width)
            for grad in grads
            for block in to_blocks(grad, width)
        ]
        + [extra.astype(bf16).reshape(samp, -1, width)],
        1,
    )
    rows = packed.shape[1]
    packed = packed.reshape(samp, seq, rows // seq, width).transpose(1, 0, 2, 3)
    part = lax.psum_scatter(packed, "seq", scatter_dimension=0, tiled=False)
    part = lax.psum_scatter(part, "samp", scatter_dimension=0, tiled=False)
    packed = lax.all_gather(part, "seq", axis=0, tiled=True).astype(f32)
    shares = unpack_blocks(packed, shapes, width)
    return shares, packed[sum(r * (c // width) for r, c in shapes) :]


def local(
    atom_input,
    token_input,
    atom_counts,
    key_offsets,
    atom_pairs,
    pair_features,
    single_features,
    noise_levels,
    noise_direction,
    atom_proj,
    atom_qbias,
    atom_pairw,
    atom_outw,
    atom_upw,
    atom_downw,
    pool_weight,
    cond_weight,
    cond_bias,
    token_proj,
    token_qbias,
    token_pairw,
    token_outw,
    token_upw,
    token_downw,
    cotangent,
):
    samp, seq = lax.axis_size("samp"), lax.axis_size("seq")
    seq_pos = lax.axis_index("seq")
    samples, slots, atom_width = atom_input.shape
    tokens, width = token_input.shape[1:]
    features = atom_pairs.shape[-1]

    tiny_own = jnp.concatenate(
        [
            atom_qbias,
            cond_bias,
            token_qbias,
            atom_pairw.reshape(-1),
            token_pairw.reshape(-1),
        ]
    )
    tiny_own = jnp.pad(tiny_own, (0, -tiny_own.size % (16 * LANES))).reshape(-1, LANES)
    large = (token_proj, token_upw, token_downw, cond_weight, token_outw)
    kernels = samples == 8 and WeightGather.fits([part.shape for part in large], samp, seq)
    up_pairs = [(i, i + 1) for i in range(seq - 1)]
    down_pairs = [(i + 1, i) for i in range(seq - 1)]
    if kernels:
        wide, down, tiny_all, ext = edges(
            (atom_proj, atom_upw, pool_weight, atom_outw, atom_downw), tiny_own, atom_input
        )
    else:
        wide_own = jnp.concatenate([atom_proj, atom_upw, pool_weight, atom_outw], 1)
        wide = lax.all_gather(wide_own, "samp", axis=0, tiled=True)
        down = lax.all_gather(atom_downw, "samp", axis=0, tiled=True)
        tiny_all = lax.all_gather(tiny_own, "samp", axis=0, tiled=True)
        before = lax.ppermute(atom_input[:, slots - RIM :], "seq", up_pairs)
        after = lax.ppermute(atom_input[:, :RIM], "seq", down_pairs)
        ext = jnp.concatenate([before, atom_input, after], 1)
    tiny_all = tiny_all.reshape(samp, -1)
    sizes = [atom_qbias.size, cond_bias.size, token_qbias.size, atom_pairw.size, token_pairw.size]
    cuts = [sum(sizes[:i]) for i in range(6)]
    tiny = [tiny_all[:, cuts[i] : cuts[i + 1]] for i in range(5)]
    atom_qb = tiny[0].reshape(1, -1).astype(f32)
    cond_b = tiny[1].reshape(-1)
    token_qb = tiny[2].reshape(-1)
    atom_pw = tiny[3].reshape(features, ATOM_HEADS)
    token_pw = tiny[4].reshape(-1, token_pairw.shape[1])

    rim_tokens = RIM // MAX_ATOMS
    counts = lax.dynamic_slice_in_dim(
        jnp.pad(atom_counts, (rim_tokens, rim_tokens)), seq_pos * tokens, tokens + 2 * rim_tokens
    )
    place = jnp.arange(MAX_ATOMS, dtype=jnp.int32)
    used = place[None, :] < counts[:, None]
    blocked = jnp.where(used, 0.0, masked_score).astype(f32).reshape(-1, 1)
    blocked = jnp.broadcast_to(blocked, (blocked.shape[0], LANES))
    own_counts = counts[rim_tokens : rim_tokens + tokens]
    share = used[rim_tokens : rim_tokens + tokens].astype(f32) / own_counts[:, None].astype(f32)
    share = jnp.broadcast_to(share.reshape(-1, 1), (slots, LANES))
    windows = slots // WIN_Q
    starts = jnp.arange(windows, dtype=jnp.int32) * WIN_Q + key_offsets + RIM
    pairs_t = atom_pairs.transpose(0, 1, 3, 2).reshape(windows, WIN_Q * features, WIN_K)
    eye = jnp.eye(WIN_Q, dtype=bool)
    spread = jnp.where(
        eye[None, :, :, None], atom_pw.T[:, None, None, :], jnp.zeros((), bf16)
    ).reshape(ATOM_HEADS * WIN_Q, WIN_Q * features)
    gather = WeightGather([part.shape for part in large], samp, seq) if kernels else None
    pooled, stored, fulls = atom_forward(
        ext,
        starts,
        pairs_t,
        spread,
        blocked,
        share,
        wide,
        down,
        atom_qb,
        gather,
        large if kernels else (),
    )
    if not kernels:
        fulls = [lax.all_gather(part, "samp", axis=0, tiled=True) for part in large]
    proj_w, up_w, down_w, cond_w, out_w = fulls
    pair_w = token_pw.T
    if kernels:
        block_in, cond_low, cond_all, attn_in, queries, keyval_own, gating = token_open(
            noise_levels,
            noise_direction,
            single_features,
            pooled,
            token_input,
            cond_w,
            cond_b.astype(f32),
            proj_w,
            token_qb.astype(f32),
        )
        queries = queries.reshape(token_input.shape)
        keyval_own = keyval_own.reshape(samples, tokens, 2 * width)
    else:
        block_in = token_input.astype(f32) + pooled

        noise_feature = 0.25 * jnp.log(noise_levels / sigma_data)
        cond_rows = (
            single_features.astype(f32)[None]
            + noise_feature[:, None, None] * noise_direction[None, None, :]
        )
        cond_low = norm_stats(cond_rows)[0].astype(bf16)
        cond_all = dot_last(cond_low, cond_w) + cond_b.astype(f32)
        parts = [cond_all[..., i * width : (i + 1) * width] for i in range(6)]

        normed_in, inv_in = norm_stats(block_in)
        attn_in = (jax.nn.sigmoid(parts[0]) * normed_in + parts[1]).astype(bf16)
        mix = dot_last(attn_in, proj_w)
        queries = (mix[..., :width] + token_qb.astype(f32)).astype(bf16)
        keyval_own = mix[..., width : 3 * width].astype(bf16)
        gating = mix[..., 3 * width :]

    if kernels:
        (probs, keyval, stats), rows_out = gather_attend(
            queries,
            keyval_own,
            pair_features,
            pair_w,
            gating,
            block_in,
            cond_all,
            cotangent,
            out_w,
            up_w,
            down_w,
        )
        (
            block_out,
            ffn_in,
            upper_grad,
            hidden,
            branch_two_low,
            gated_low,
            branch_low,
            attend_low,
            gating_grad,
            mid_grad,
            cond_tail,
        ) = rows_out
        query_grad, keyval_grad, pairw_grad, ready = attend_back_scatter(
            queries,
            keyval,
            probs,
            attend_low.reshape(queries.shape),
            pair_features,
            stats,
            ffn_in,
            upper_grad,
            hidden,
            branch_two_low,
            gated_low,
            branch_low,
        )
        token_grad, token_qb_grad, cond_b_grad, grad_units = token_close(
            query_grad,
            keyval_grad,
            gating_grad,
            mid_grad,
            block_in,
            cond_all,
            cond_tail,
            proj_w,
            attn_in,
            cond_low,
            ready,
            samp,
            seq,
        )
        block_out = block_out.reshape(token_input.shape)
        token_grad = token_grad.reshape(token_input.shape)
        token_qb_grad, cond_b_grad = token_qb_grad.reshape(-1), cond_b_grad.reshape(-1)
    else:
        bias = pair_bias(pair_features, pair_w)
        keyval = lax.all_gather(keyval_own, "seq", axis=0, tiled=False)
        attend, probs = token_attention(queries, keyval, bias)
        sig_gate = jax.nn.sigmoid(gating)
        gated_low = (attend * sig_gate).astype(bf16)
        branch = dot_last(gated_low, out_w)
        gate_one = jax.nn.sigmoid(parts[2])
        mid = block_in + gate_one * branch
        normed_mid, inv_mid = norm_stats(mid)
        scale_two = jax.nn.sigmoid(parts[3])
        ffn_in = (scale_two * normed_mid + parts[4]).astype(bf16)
        upper = dot_last(ffn_in, up_w)
        hidden_width = down_w.shape[0]
        first_half, second_half = upper[..., :hidden_width], upper[..., hidden_width:]
        sig_first = jax.nn.sigmoid(first_half)
        hidden = (first_half * sig_first * second_half).astype(bf16)
        branch_two = dot_last(hidden, down_w)
        gate_two = jax.nn.sigmoid(parts[5])
        block_out = (mid + gate_two * branch_two).astype(bf16)

        out_grad = cotangent.astype(f32)
        branch_two_low = (out_grad * gate_two).astype(bf16)
        gate_two_grad = out_grad * branch_two * gate_two * (1.0 - gate_two)
        hidden_grad = dot_back(branch_two_low, down_w)
        first_grad = hidden_grad * second_half * sig_first * (1.0 + first_half * (1.0 - sig_first))
        second_grad = hidden_grad * first_half * sig_first
        upper_grad = jnp.concatenate([first_grad, second_grad], -1).astype(bf16)
        ffn_grad = dot_back(upper_grad, up_w)
        scale_two_grad = ffn_grad * normed_mid * scale_two * (1.0 - scale_two)
        mid_grad = out_grad + norm_back(normed_mid, inv_mid, ffn_grad * scale_two)
        branch_low = (mid_grad * gate_one).astype(bf16)
        gate_one_grad = mid_grad * branch * gate_one * (1.0 - gate_one)
        gated_grad = dot_back(branch_low, out_w)
        attend_low = (gated_grad * sig_gate).astype(bf16)
        gating_grad = gated_grad * attend * sig_gate * (1.0 - sig_gate)
        query_grad, keyval_part, bias_grad = token_attention_back(queries, keyval, probs, attend_low)
        keyval_grad = lax.psum_scatter(keyval_part, "seq", scatter_dimension=0, tiled=False)
        pairw_grad = pair_grad(pair_features, bias_grad, pair_w)
        mix_grad = jnp.concatenate(
            [query_grad.astype(bf16), keyval_grad, gating_grad.astype(bf16)], -1
        )
        token_qb_grad = jnp.sum(query_grad, (0, 1))
        attn_in_grad = dot_back(mix_grad, proj_w)
        scale_one = jax.nn.sigmoid(parts[0])
        scale_one_grad = attn_in_grad * normed_in * scale_one * (1.0 - scale_one)
        token_grad = mid_grad + norm_back(normed_in, inv_in, attn_in_grad * scale_one)
        cond_grad = jnp.concatenate(
            [scale_one_grad, attn_in_grad, gate_one_grad, scale_two_grad, ffn_grad, gate_two_grad], -1
        ).astype(bf16)
        cond_b_grad = jnp.sum(cond_grad.astype(f32), (0, 1))
    pairw_grad = pairw_grad.T

    if kernels:
        atom_grad, qb_grad, pairw_stack, pairw_mean, small, units = atom_backward_sum(
            token_grad,
            starts,
            stored,
            atom_input,
            pairs_t,
            share,
            wide,
            down,
            GradSum([part.shape for part in large]),
            grad_units,
        )
    else:
        mix_part, own, left, right, atom_mid_grad, *atom_totals = atom_backward(
            token_grad, starts, stored, pairs_t, share, wide, down
        )
        from_right = lax.ppermute(left, "seq", down_pairs)
        from_left = lax.ppermute(right, "seq", up_pairs)
        atom_grad, atom_proj_grad = atom_input_backward(
            atom_input, mix_part, own, from_left, from_right, atom_mid_grad, wide
        )
        qb_grad, outw_grad, upw_grad, downw_grad, pool_grad, pairw_stack, pairw_mean = atom_totals
    diagonal = pairw_stack.reshape(ATOM_HEADS, WIN_Q, WIN_Q, features)
    atom_pw_grad = (
        jnp.sum(jnp.where(eye[None, :, :, None], diagonal, 0.0), (1, 2)).T
        - jnp.sum(pairw_mean.reshape(ATOM_HEADS, -1), 1)[None, :]
    )

    rows = atom_width // samp
    tiny_parts = [qb_grad.reshape(-1), atom_pw_grad, cond_b_grad, token_qb_grad, pairw_grad]
    tiny_flat = jnp.concatenate([part.astype(bf16).reshape(samp, -1) for part in tiny_parts], 1)
    spare = atom_width
    tiny_flat = jnp.pad(tiny_flat, ((0, 0), (0, rows * spare - tiny_flat.shape[1])))
    tiny_rows = tiny_flat.reshape(samp, rows, spare)
    if kernels:
        total, units = small_sums(small, tiny_rows, units)
        *shares, pool_out, proj_out, downw_out, upw_out, outw_out, tiny_out = unpack(
            units, total, [part.shape for part in large], rows, atom_width
        )
    else:
        lanes = lambda part: part.astype(bf16).reshape(samp, rows, -1)
        downw_two = downw_grad.astype(bf16).reshape(samp, 2, rows, atom_width)
        small = jnp.stack(
            [
                lanes(pool_grad),
                jnp.concatenate([lanes(atom_proj_grad), downw_two[:, 0], downw_two[:, 1]], -1),
                jnp.concatenate([lanes(upw_grad), lanes(outw_grad), tiny_rows], -1),
                jnp.zeros((samp, rows, width), bf16),
            ],
            1,
        )
        factors = [
            (attn_in, mix_grad),
            (ffn_in, upper_grad),
            (hidden, branch_two_low),
            (cond_low, cond_grad),
            (gated_low, branch_low),
        ]
        shares, rest = sum_shares(
            [weight_grad(*pair) for pair in factors], small.reshape(-1, width)
        )
        rest = rest.reshape(-1, width)
        pool_out, second, third = rest[:rows], rest[rows : 2 * rows], rest[2 * rows : 3 * rows]
        low = 4 * atom_width
        proj_out = second[:, :low]
        downw_out = jnp.concatenate(
            [second[:, low : low + atom_width], second[:, low + atom_width :]], 0
        )
        upw_out, outw_out = third[:, :low], third[:, low : low + atom_width]
        tiny_out = third[:, low + atom_width :]
    tiny_out = tiny_out.reshape(-1)
    tiny_shares, cut = [], 0
    for part in tiny_parts:
        size = part.size // samp
        shape = (part.shape[0] // samp,) + part.shape[1:]
        tiny_shares.append(tiny_out[cut : cut + size].reshape(shape))
        cut += size
    return (
        block_out,
        atom_grad,
        token_grad,
        proj_out,
        tiny_shares[0],
        tiny_shares[1],
        outw_out,
        upw_out,
        downw_out,
        pool_out,
        shares[3],
        tiny_shares[2],
        shares[0],
        tiny_shares[3],
        tiny_shares[4],
        shares[4],
        shares[1],
        shares[2],
    )


def solution(mesh):
    in_specs = (
        P("samp", "seq", None),
        P("samp", "seq", None),
        P(),
        P("seq"),
        P("seq", None, None, None),
        P("seq", None, None),
        P("seq", None),
        P("samp"),
        P(),
        P("samp", None),
        P("samp"),
        P("samp", None),
        P("samp", None),
        P("samp", None),
        P("samp", None),
        P("samp", None),
        P("samp", None),
        P("samp"),
        P("samp", None),
        P("samp"),
        P("samp", None),
        P("samp", None),
        P("samp", None),
        P("samp", None),
        P("samp", "seq", None),
    )
    out_specs = (
        P("samp", "seq", None),
        P("samp", "seq", None),
        P("samp", "seq", None),
        P("samp", None),
        P("samp"),
        P("samp", None),
        P("samp", None),
        P("samp", None),
        P("samp", None),
        P("samp", None),
        P("samp", None),
        P("samp"),
        P("samp", None),
        P("samp"),
        P("samp", None),
        P("samp", None),
        P("samp", None),
        P("samp", None),
    )
    return jax.shard_map(local, mesh=mesh, in_specs=in_specs, out_specs=out_specs, check_vma=False)
```
